32 devices in a mesh: gx: 4 (over x, core), gy: 4 (over z), gz: 2 (over y).
Axes of the slice: x: 2, y: 2, z: 4, core: 2. Of those that a mesh axis runs over, the one named last changes fastest.
Arguments:
- cells: bfloat16 [4, 16, 256, 256], P(None, 'gx', 'gy', 'gz'), may hold values from -6 to 6
- weight: bfloat16 [32, 4, 3, 3, 3], replicated, may hold values from -0.625 to 0.625
- bias: float32 [32], replicated, may hold values from -3 to 3
- cotangent: bfloat16 [32, 8, 128, 128], P(None, 'gx', 'gy', 'gz'), may hold values from -6 to 6
Outputs:
- pooled: bfloat16 [32, 8, 128, 128], P(None, 'gx', 'gy', 'gz')
- weight_grad: float32 [32, 4, 3, 3, 3], replicated
- bias_grad: float32 [32], replicated
- input_grad: float32 [4, 16, 256, 256], P(None, 'gx', 'gy', 'gz')
The draws below stay inside these ranges and needn't reach their ends.
All inputs are finite; a program needn't handle non-finite values.
Results may differ from the reference program's by a relative error of at most 0.0029.
Values may be sent and summed in bfloat16 or wider, within the bound.
No kernel may reach another device: no remote copies, remote signals or barrier semaphores. Data moves between devices by JAX's collectives and lax.ppermute only.
A program may use at most 128 MiB of HBM per device.

```python
import jax
import jax.numpy as jnp
from jax import lax

CIN = 4
COUT = 32
CX = 4
NX = 16
NY = 256
NZ = 256
N_GX = 4


def block_levels(rng, dims, split, least, top_value):
    loudness = 1.0
    for axis_at, parts in split:
        draws = jax.random.uniform(jax.random.fold_in(jax.random.fold_in(rng, 6), axis_at), (parts,), jnp.float32, least / len(split), top_value / len(split))
        loudness = loudness * jnp.repeat(jnp.exp(draws), dims[axis_at] // parts).reshape((-1,) + (1,) * (len(dims) - 1 - axis_at))
    return loudness


def scatter_about(rng, extent, scale, limit, split=(), kind=jnp.bfloat16):
    factor_of = block_levels(rng, extent, split, -0.22, 0.18) if split else 1.0
    entries = jax.random.normal(rng, extent, jnp.float32) * scale * factor_of
    return jnp.minimum(jnp.maximum(entries, -limit), limit).astype(kind)


def setup_inputs(seed: int = 0) -> dict:
    seeds = jax.random.split(jax.random.key(seed), 5)
    cells = scatter_about(seeds[0], (CIN, NX, NY, NZ), 1.0, 6.0, ((1, 4), (2, 4), (3, 2)))
    weight = scatter_about(seeds[1], (COUT, CIN, 3, 3, 3), (CIN * 27) ** -0.5, 0.625)
    bias = scatter_about(seeds[2], (COUT,), 0.5, 3.0, (), jnp.float32)
    cotangent = scatter_about(seeds[3], (COUT, NX // 2, NY // 2, NZ // 2), 1.0, 6.0, ((1, 4), (2, 4), (3, 2)))
    return {"cells": cells, "weight": weight, "bias": bias, "cotangent": cotangent}


leak_slope = 0.3
soft_scale = 10.0


def activate(preact):
    return leak_slope * preact + (1.0 - leak_slope) / soft_scale * jax.nn.softplus(soft_scale * preact)


def slope_of(preact):
    return leak_slope + (1.0 - leak_slope) * jax.nn.sigmoid(soft_scale * preact)


def correlate(volume, kernel):
    return lax.conv_general_dilated(volume[None], kernel, (1, 1, 1), "VALID", dimension_numbers=("NCDHW", "OIDHW", "NCDHW"), precision=lax.Precision.HIGHEST)[0]


def reference(cells, weight, bias, cotangent):
    kernel = weight.astype(jnp.float32)
    flipped = jnp.transpose(kernel[:, :, ::-1, ::-1, ::-1], (1, 0, 2, 3, 4))
    wrapped = jnp.pad(cells.astype(jnp.float32), ((0, 0), (0, 0), (1, 1), (1, 1)), mode="wrap")
    cot_full = cotangent.astype(jnp.float32)

    def one_slab(index):
        start = index * CX
        rows_in = (start - 2 + jnp.arange(CX + 4, dtype=jnp.int32)) % NX
        slab_in = jnp.take(wrapped, rows_in, axis=1)
        preact = correlate(slab_in, kernel) + bias.astype(jnp.float32)[:, None, None, None]
        activated = activate(preact)[:, 1:CX + 1]
        pooled = activated.reshape(COUT, CX // 2, 2, NY // 2, 2, NZ // 2, 2).mean(axis=(2, 4, 6)).astype(jnp.bfloat16)
        rows_pre = (start - 1 + jnp.arange(CX + 2, dtype=jnp.int32)) % NX
        spread = jnp.take(cot_full, rows_pre // 2, axis=1)
        spread = jnp.repeat(jnp.repeat(spread, 2, axis=2), 2, axis=3)
        delta = (slope_of(preact) * spread * 0.125).astype(jnp.bfloat16).astype(jnp.float32)
        delta_pad = jnp.pad(delta, ((0, 0), (0, 0), (1, 1), (1, 1)), mode="wrap")
        grad_slab = correlate(delta_pad, flipped)
        central = delta[:, 1:CX + 1]
        padded_central = slab_in[:, 1:CX + 3]
        terms = []
        for shift_a in range(3):
            for shift_b in range(3):
                for shift_e in range(3):
                    window = padded_central[:, shift_a:shift_a + CX, shift_b:shift_b + NY, shift_e:shift_e + NZ]
                    terms.append(jnp.einsum("oxyz,cxyz->oc", central, window, precision=lax.Precision.HIGHEST))
        weight_part = jnp.stack(terms, axis=2).reshape(COUT, CIN, 3, 3, 3)
        bias_part = jnp.sum(central, axis=(1, 2, 3))
        return pooled, grad_slab, weight_part, bias_part

    pooled, grads, weight_parts, bias_parts = lax.map(one_slab, jnp.arange(N_GX, dtype=jnp.int32))
    pooled = jnp.moveaxis(pooled, 0, 1).reshape(COUT, NX // 2, NY // 2, NZ // 2)
    input_grad = jnp.moveaxis(grads, 0, 1).reshape(CIN, NX, NY, NZ)
    return pooled, jnp.sum(weight_parts, axis=0), jnp.sum(bias_parts, axis=0), input_grad
```

```python
import functools

import jax
import jax.numpy as jnp
import numpy as np
from jax import lax
from jax.experimental import pallas as pl
from jax.experimental.pallas import tpu as pltpu
from jax.sharding import PartitionSpec as P

axes = ("gx", "gy", "gz")
f32, bf16 = jnp.float32, jnp.bfloat16
log_scale = 0.07
lanes = 128
limit = 48 * 1024 * 1024


def dot(a, b, contract=((1,), (0,))):
    return lax.dot_general(a, b, (contract, ((), ())), preferred_element_type=f32)


def iota(shape, dim):
    return lax.broadcasted_iota(jnp.int32, shape, dim)


def taken_from(array, offset):
    sizes = [lax.axis_size(axis) for axis in axes]
    pairs = []
    for place in np.ndindex(*sizes):
        source = [(p + o) % n for p, o, n in zip(place, offset, sizes)]
        pairs.append(
            (int(np.ravel_multi_index(source, sizes)), int(np.ravel_multi_index(place, sizes)))
        )
    return lax.ppermute(array, axes, pairs)


def pack_kernel(cells, edges, first, last, low, high, rows):
    chan, count_x, count_y, _ = cells.shape
    count = chan * count_x
    planes = [cells[c, x] for x in range(count_x) for c in range(chan)]
    wide = jnp.concatenate(planes, axis=1)
    row = iota((2 * count, count * lanes), 0)
    lane = iota((2 * count, count * lanes), 1)
    want = jnp.where(row < count, row * lanes, (row - count) * lanes + lanes - 1)
    pick = (lane == want).astype(f32).astype(bf16)
    found = dot(pick, wide, ((1,), (1,)))
    found = jnp.concatenate([found, jnp.zeros((2 * count, lanes - count_y), f32)], axis=1)
    edges[...] = pltpu.roll(found, 1, 1).astype(bf16)
    for at, plane in enumerate(planes):
        wide_plane = plane.astype(f32)
        rows[at : at + 1, :] = wide_plane[0:1]
        rows[count + at : count + at + 1, :] = wide_plane[count_y - 1 : count_y]
    first[...] = rows[0:count, :].astype(bf16)
    last[...] = rows[count : 2 * count, :].astype(bf16)
    low[...] = cells[:, 0]
    high[...] = cells[:, count_x - 1]


def main_kernel(
    cells, low, high, above, below, edges, cot, wbig, wback,
    pooled, wsum, grad, face_low, face_high, row_low, row_high, cols,
    stage, patches, left, right, spread, sums, field, outer, carry, gram,
):
    chan, count_x, count_y, _ = cells.shape
    chan_out = cot.shape[0]
    own = chan * count_x
    wide = own + 2 * chan
    depth = 3 * wide + 8
    lane = iota((wide, lanes), 1)

    for x in range(count_x + 2):
        for c in range(chan):
            if x == 0:
                plane = low[c]
            elif x == count_x + 1:
                plane = high[c]
            else:
                plane = cells[c, x - 1]
            stage[pl.ds(wide + x * chan + c, count_y, stride=wide), :] = plane.astype(f32)
    for ref, base in ((above, 0), (below, (count_y + 1) * wide)):
        stage[base : base + chan, :] = ref[0].astype(f32)[own - chan : own]
        stage[base + chan : base + chan + own, :] = ref[1].astype(f32)
        stage[base + chan + own : base + wide, :] = ref[2].astype(f32)[0:chan]
    for side, ref in ((1, left), (0, right)):
        at = slice(side * own, side * own + own)
        spot = iota((own, lanes), 1)
        whole = []
        for dx in range(3):
            mid = edges[dx, 1].astype(f32)[at]
            before = pltpu.roll(edges[dx, 0].astype(f32)[at], count_y, 1)
            after = pltpu.roll(edges[dx, 2].astype(f32)[at], lanes - count_y, 1)
            whole.append(jnp.where(spot == 0, before, jnp.where(spot == count_y + 1, after, mid)))
        ref[0:chan, :] = whole[0][own - chan : own]
        ref[chan : chan + own, :] = whole[1]
        ref[chan + own : wide, :] = whole[2][0:chan]
    left_cols, right_cols = left[...], right[...]
    for y in range(count_y + 2):
        mid = stage[y * wide : (y + 1) * wide, :]
        low_col = pltpu.roll(left_cols, (lanes - y) % lanes, 1)
        high_col = pltpu.roll(right_cols, (lanes - 1 - y) % lanes, 1)
        before = jnp.where(lane == 0, low_col, pltpu.roll(mid, 1, 1))
        after = jnp.where(lane == lanes - 1, high_col, pltpu.roll(mid, lanes - 1, 1))
        whole = jnp.concatenate([before, mid, after, jnp.ones((8, lanes), f32)], axis=0)
        patches[y * depth : (y + 1) * depth, :] = whole.astype(bf16)

    pool_x, pool_y, pool_z = cot.shape[1:]
    twice = jnp.where(
        iota((pool_z, lanes), 1) // 2 == iota((pool_z, lanes), 0), 0.125, 0.0
    ).astype(bf16)
    for o in range(chan_out):
        part = dot(cot[o].reshape(pool_x * pool_y, pool_z), twice)
        for x in range(pool_x):
            spread[pl.ds(x * chan_out + o, pool_y, stride=pool_x * chan_out), :] = part[
                x * pool_y : (x + 1) * pool_y
            ]

    carry[...] = jnp.zeros_like(carry)
    gram[...] = jnp.zeros_like(gram)
    pairs = 4

    def finish(y, whole):
        before = pltpu.roll(whole[0:wide], lanes - 1, 1)
        after = pltpu.roll(whole[2 * wide : 3 * wide], 1, 1)
        zero = jnp.zeros_like(before)
        inner = (
            whole[wide : 2 * wide]
            + jnp.where(lane == lanes - 1, zero, before)
            + jnp.where(lane == 0, zero, after)
        )
        rest = jnp.where(lane == lanes - 1, before, jnp.where(lane == 0, after, zero))
        place = pl.ds(pl.multiple_of(y * wide, 8), wide)
        field[place, :] = inner
        outer[place, :] = rest

    def step(i, _):
        deltas, blocks = [], []
        weights = wbig[...]
        for k in range(pairs):
            j = i * pairs + k
            block = jnp.concatenate(
                [
                    patches[pl.ds(pl.multiple_of((2 * j + h) * depth, 16), 3 * depth), :]
                    for h in range(2)
                ],
                axis=1,
            )
            preact = dot(weights, block)
            slope = jnp.tanh(5.0 * preact)
            linear = jnp.maximum(preact, 0.3 * preact)
            factor = 1.0 + jnp.abs(slope)
            here = spread[pl.ds(pl.multiple_of(j * pool_x * chan_out, 8), pool_x * chan_out), :]
            slope = 0.65 + 0.35 * slope
            delta = []
            for x in range(pool_x):
                top, mid = 2 * x * chan_out, (2 * x + 1) * chan_out
                end = mid + chan_out
                times = here[x * chan_out : (x + 1) * chan_out]
                times = jnp.concatenate([times, times], axis=1)
                delta.append((slope[top:mid] * times).astype(bf16))
                delta.append((slope[mid:end] * times).astype(bf16))
                total = linear[top:mid] + linear[mid:end]
                total = total[:, :lanes] + total[:, lanes:]
                prod = factor[top:mid] * factor[mid:end]
                prod = prod[:, :lanes] * prod[:, lanes:]
                total = total - log_scale * jnp.log(prod)
                sums[pl.ds(x * pool_y + j, chan_out, stride=pool_x * pool_y), :] = total
            deltas.append(jnp.concatenate(delta, axis=0))
            blocks.append(block)
        gram[...] += dot(
            jnp.concatenate(deltas, axis=1), jnp.concatenate(blocks, axis=1), ((1,), (1,))
        )
        back = wback[...]
        size = 3 * wide
        carry_a, carry_b = carry[0:size, :], carry[size : 2 * size, :]
        for k in range(pairs):
            j = i * pairs + k
            parts = dot(back, deltas[k])
            part = lambda b, h: parts[b * size : (b + 1) * size, h * lanes : (h + 1) * lanes]
            finish(2 * j, carry_a + part(0, 0))
            finish(2 * j + 1, carry_b + part(1, 0) + part(0, 1))
            carry_a = part(2, 0) + part(1, 1)
            carry_b = part(2, 1)
        carry[0:size, :] = carry_a
        carry[size : 2 * size, :] = carry_b
        return 0

    lax.fori_loop(0, count_y // (2 * pairs), step, 0)
    size = 3 * wide
    finish(count_y, carry[0:size, :])
    finish(count_y + 1, carry[size : 2 * size, :])

    span = gram.shape[1]
    straight, turned = 0.0, 0.0
    for x in range(count_x):
        part = gram[x * chan_out : (x + 1) * chan_out, :]
        part = jnp.concatenate([part, jnp.zeros((chan_out, 2 * lanes - span), f32)], axis=1)
        straight = straight + part
        turned = turned + (pltpu.roll(part, 2 * lanes - chan * x, 1) if x else part)
    wsum[...] = jnp.where(iota((chan_out, 2 * lanes), 1) == 3 * wide, straight, turned)

    halves = jnp.where(
        iota((2 * lanes, pool_z), 0) % lanes // 2 == iota((2 * lanes, pool_z), 1), 0.125, 0.0
    ).astype(bf16)
    for o in range(0, chan_out, 4):
        rows = 4 * pool_x * pool_y
        part = sums[o * pool_x * pool_y : o * pool_x * pool_y + rows, :]
        coarse = part.astype(bf16)
        fine = (part - coarse.astype(f32)).astype(bf16)
        mean = dot(jnp.concatenate([coarse, fine], axis=1), halves) + log_scale * float(np.log(2.0))
        pooled[o : o + 4] = mean.astype(bf16).reshape(4, pool_x, pool_y, pool_z)

    for x in range(count_x + 2):
        for c in range(chan):
            plane = field[pl.ds(wide + x * chan + c, count_y, stride=wide), :]
            if x == 0:
                face_low[c] = plane.astype(bf16)
            elif x == count_x + 1:
                face_high[c] = plane.astype(bf16)
            else:
                grad[c, x - 1] = plane
    row_low[...] = field[0:wide, :]
    row_high[...] = field[(count_y + 1) * wide : (count_y + 2) * wide, :]
    tall = cols.shape[0]
    outer[(count_y + 2) * wide :, :] = jnp.zeros((outer.shape[0] - (count_y + 2) * wide, lanes), f32)
    planes = [outer[pl.ds(r, tall, stride=wide), :].astype(bf16) for r in range(wide)]
    row = iota((wide * lanes, lanes), 0)
    spot = iota((wide * lanes, lanes), 1)
    want = jnp.where(spot < wide, spot * lanes + lanes - 1, (spot - wide) * lanes)
    pick = ((row == want) & (spot < 2 * wide)).astype(f32).astype(bf16)
    cols[...] = dot(jnp.concatenate(planes, axis=1), pick).astype(bf16)


def final_kernel(grad, low, high, above, below, cols, out):
    chan, count_x, count_y, _ = grad.shape
    own = chan * count_x
    wide = own + 2 * chan
    spot = iota((count_y, lanes), 1)
    row = iota((count_y, lanes), 0)
    total = 0.0
    for dx, turn, start in ((1, 0, chan), (0, lanes - own, chan), (2, own, own)):
        mid = cols[dx, 1].astype(f32)
        mid = mid[1 : count_y + 1]
        before = cols[dx, 0].astype(f32)[count_y + 1 : count_y + 2]
        after = cols[dx, 2].astype(f32)[0:1]
        mid = mid + jnp.where(row == 0, before, 0.0) + jnp.where(row == count_y - 1, after, 0.0)
        if turn:
            mid = pltpu.roll(mid, turn, 1)
            near = (spot >= start) & (spot < start + chan)
            near = near | ((spot >= wide + start) & (spot < wide + start + chan))
            mid = jnp.where(near, mid, 0.0)
        total = total + mid
    for x in range(count_x):
        for c in range(chan):
            r = chan + x * chan + c
            plane = grad[c, x]
            first = above[1][r : r + 1]
            final = below[1][r : r + 1]
            if x == 0:
                plane = plane + low[c].astype(f32)
                first = first + above[0][chan + own + c : chan + own + c + 1]
                final = final + below[0][chan + own + c : chan + own + c + 1]
            if x == count_x - 1:
                plane = plane + high[c].astype(f32)
                first = first + above[2][c : c + 1]
                final = final + below[2][c : c + 1]
            plane = plane + jnp.where(row == 0, first, 0.0)
            plane = plane + jnp.where(row == count_y - 1, final, 0.0)
            plane = plane + jnp.where(spot == lanes - 1, total[:, r : r + 1], 0.0)
            plane = plane + jnp.where(spot == 0, total[:, wide + r : wide + r + 1], 0.0)
            out[c, x] = plane


def call(kernel, outs, scratch=()):
    return pl.pallas_call(
        kernel,
        out_shape=outs,
        scratch_shapes=list(scratch),
        compiler_params=pltpu.CompilerParams(vmem_limit_bytes=limit),
    )


def summed(array, axis):
    count = lax.axis_size(axis)
    if count > 4:
        return lax.psum(array, axis)
    moved = [array] + [
        lax.ppermute(array, axis, [((i + k) % count, i) for i in range(count)])
        for k in range(1, count)
    ]
    if count == 4:
        return (moved[0] + moved[2]) + (moved[1] + moved[3])
    return sum(moved[1:], moved[0])


def on_device(cells, weight, bias, cotangent):
    chan, count_x, count_y, count_z = cells.shape
    chan_out = weight.shape[0]
    own = chan * count_x
    wide = own + 2 * chan
    depth = 3 * wide + 8
    shape = jax.ShapeDtypeStruct

    kernel = weight.transpose(0, 3, 4, 2, 1)
    placed = jnp.stack(
        [
            jnp.pad(kernel, ((0, 0), (0, 0), (0, 0), (x, count_x - 1 - x), (0, 0)))
            for x in range(count_x)
        ]
    ).reshape(count_x * chan_out, 3, 3 * wide)
    coarse = lax.reduce_precision(bias, 8, 7)
    middle = lax.reduce_precision(bias - coarse, 8, 7)
    fine = bias - coarse - middle
    pieces = jnp.stack([coarse, middle, fine], axis=1).astype(bf16)
    pieces = jnp.pad(jnp.tile(pieces, (count_x, 1))[:, None], ((0, 0), (0, 2), (0, 5)))
    wbig = jnp.concatenate([placed, pieces], axis=2).reshape(count_x * chan_out, 3 * depth)
    wback = placed.reshape(count_x * chan_out, 9 * wide).T

    edges, first, last, low, high = call(
        pack_kernel,
        [
            shape((2 * own, lanes), bf16),
            shape((own, lanes), bf16),
            shape((own, lanes), bf16),
            shape((chan, count_y, lanes), bf16),
            shape((chan, count_y, lanes), bf16),
        ],
        [pltpu.VMEM((2 * own, lanes), f32)],
    )(cells)
    steps = (-1, 0, 1)
    edges_in = jnp.stack(
        [jnp.stack([taken_from(edges, (dx, dy, 1)) for dy in steps]) for dx in steps]
    )
    above = jnp.stack([taken_from(last, (dx, -1, 0)) for dx in steps])
    below = jnp.stack([taken_from(first, (dx, 1, 0)) for dx in steps])
    low_in = taken_from(high, (-1, 0, 0))
    high_in = taken_from(low, (1, 0, 0))

    pool_x, pool_y, pool_z = cotangent.shape[1:]
    tall = 80
    pooled, wsum, grad, face_low, face_high, row_low, row_high, cols = call(
        main_kernel,
        [
            shape(cotangent.shape, bf16),
            shape((chan_out, 2 * lanes), f32),
            shape(cells.shape, f32),
            shape((chan, count_y, lanes), bf16),
            shape((chan, count_y, lanes), bf16),
            shape((wide, lanes), f32),
            shape((wide, lanes), f32),
            shape((tall, lanes), bf16),
        ],
        [
            pltpu.VMEM(((count_y + 2) * wide, lanes), f32),
            pltpu.VMEM(((count_y + 2) * depth, lanes), bf16),
            pltpu.VMEM((wide, lanes), f32),
            pltpu.VMEM((wide, lanes), f32),
            pltpu.VMEM((pool_y * pool_x * chan_out, lanes), f32),
            pltpu.VMEM((pool_y * pool_x * chan_out, lanes), f32),
            pltpu.VMEM(((count_y + 2) * wide, lanes), f32),
            pltpu.VMEM((tall * wide, lanes), f32),
            pltpu.VMEM((6 * wide, lanes), f32),
            pltpu.VMEM((count_x * chan_out, 3 * depth), f32),
        ],
    )(cells, low_in, high_in, above, below, edges_in, cotangent, wbig, wback)

    low_back = taken_from(face_high, (-1, 0, 0))
    high_back = taken_from(face_low, (1, 0, 0))
    above_back = jnp.stack([taken_from(row_high, (dx, -1, 0)) for dx in steps])
    below_back = jnp.stack([taken_from(row_low, (dx, 1, 0)) for dx in steps])
    cols_back = jnp.stack(
        [jnp.stack([taken_from(cols, (dx, dy, 1)) for dy in steps]) for dx in steps]
    )
    input_grad = call(final_kernel, shape(cells.shape, f32))(
        grad, low_back, high_back, above_back, below_back, cols_back
    )

    for axis in axes:
        wsum = summed(wsum, axis)
    bias_grad = wsum[:, 3 * wide]
    weight_grad = wsum[:, : 3 * depth].reshape(chan_out, 3, depth)[:, :, : 3 * wide]
    weight_grad = weight_grad.reshape(chan_out, 3, 3, count_x + 2, chan)[:, :, :, :3]
    return (pooled, weight_grad.transpose(0, 4, 3, 1, 2), bias_grad, input_grad)


def solution(mesh):
    in_specs = (P(None, "gx", "gy", "gz"), P(), P(), P(None, "gx", "gy", "gz"))
    out_specs = (P(None, "gx", "gy", "gz"), P(), P(), P(None, "gx", "gy", "gz"))
    return jax.shard_map(
        on_device, mesh=mesh, in_specs=in_specs, out_specs=out_specs, check_vma=False
    )
```

```python
import functools

import jax
import jax.numpy as jnp
import numpy as np
from jax import lax
from jax.experimental import pallas as pl
from jax.experimental.pallas import tpu as pltpu
from jax.sharding import PartitionSpec as P

axes = ("gx", "gy", "gz")
f32, bf16 = jnp.float32, jnp.bfloat16
log_scale = 0.07
lanes = 128
limit = 48 * 1024 * 1024


def dot(a, b, contract=((1,), (0,))):
    return lax.dot_general(a, b, (contract, ((), ())), preferred_element_type=f32)


def iota(shape, dim):
    return lax.broadcasted_iota(jnp.int32, shape, dim)


def taken_from(array, offset):
    sizes = [lax.axis_size(axis) for axis in axes]
    pairs = []
    for place in np.ndindex(*sizes):
        source = [(p + o) % n for p, o, n in zip(place, offset, sizes)]
        pairs.append(
            (int(np.ravel_multi_index(source, sizes)), int(np.ravel_multi_index(place, sizes)))
        )
    return lax.ppermute(array, axes, pairs)


def place_of(offset, sizes):
    at = 0
    for axis, step, size in zip(axes, offset, sizes):
        at = at * size + lax.rem(lax.axis_index(axis) + step + size, size)
    return at


def pack_kernel(cells, frame, low, high, rows):
    chan, count_x, count_y, _ = cells.shape
    count = chan * count_x
    planes = [cells[c, x] for x in range(count_x) for c in range(chan)]
    wide = jnp.concatenate(planes, axis=1)
    row = iota((2 * count, count * lanes), 0)
    lane = iota((2 * count, count * lanes), 1)
    want = jnp.where(row < count, row * lanes, (row - count) * lanes + lanes - 1)
    pick = (lane == want).astype(f32).astype(bf16)
    found = dot(pick, wide, ((1,), (1,)))
    found = jnp.concatenate([found, jnp.zeros((2 * count, lanes - count_y), f32)], axis=1)
    frame[0 : 2 * count, :] = pltpu.roll(found, 1, 1).astype(bf16)
    for at, plane in enumerate(planes):
        wide_plane = plane.astype(f32)
        rows[at : at + 1, :] = wide_plane[0:1]
        rows[count + at : count + at + 1, :] = wide_plane[count_y - 1 : count_y]
    frame[2 * count :, :] = rows[...].astype(bf16)
    low[...] = cells[:, 0]
    high[...] = cells[:, count_x - 1]


def main_kernel(
    sizes,
    cells, low, high, frames, cot, wbig, wback,
    pooled, grad, face_low, face_high, frame_out,
    stage, patches, left, right, spread, sums, field, outer, carry, gram,
):
    chan, count_x, count_y, _ = cells.shape
    chan_out = cot.shape[0]
    own = chan * count_x
    wide = own + 2 * chan
    depth = 3 * wide + 8
    lane = iota((wide, lanes), 1)

    for x in range(count_x + 2):
        for c in range(chan):
            if x == 0:
                plane = low[c]
            elif x == count_x + 1:
                plane = high[c]
            else:
                plane = cells[c, x - 1]
            stage[pl.ds(wide + x * chan + c, count_y, stride=wide), :] = plane.astype(f32)
    for dy, base in ((-1, 0), (1, (count_y + 1) * wide)):
        top = (3 if dy < 0 else 2) * own
        rows = [
            frames[place_of((dx, dy, 0), sizes), top : top + own, :].astype(f32)
            for dx in (-1, 0, 1)
        ]
        stage[base : base + chan, :] = rows[0][own - chan : own]
        stage[base + chan : base + chan + own, :] = rows[1]
        stage[base + chan + own : base + wide, :] = rows[2][0:chan]
    for side, ref in ((1, left), (0, right)):
        at = slice(side * own, side * own + own)
        spot = iota((own, lanes), 1)
        whole = []
        for dx in range(3):
            before, mid, after = [
                frames[place_of((dx - 1, dy, 1), sizes), at, :].astype(f32) for dy in (-1, 0, 1)
            ]
            before = pltpu.roll(before, count_y, 1)
            after = pltpu.roll(after, lanes - count_y, 1)
            whole.append(jnp.where(spot == 0, before, jnp.where(spot == count_y + 1, after, mid)))
        ref[0:chan, :] = whole[0][own - chan : own]
        ref[chan : chan + own, :] = whole[1]
        ref[chan + own : wide, :] = whole[2][0:chan]
    left_cols, right_cols = left[...], right[...]
    for y in range(count_y + 2):
        mid = stage[y * wide : (y + 1) * wide, :]
        low_col = pltpu.roll(left_cols, (lanes - y) % lanes, 1)
        high_col = pltpu.roll(right_cols, (lanes - 1 - y) % lanes, 1)
        before = jnp.where(lane == 0, low_col, pltpu.roll(mid, 1, 1))
        after = jnp.where(lane == lanes - 1, high_col, pltpu.roll(mid, lanes - 1, 1))
        whole = jnp.concatenate([before, mid, after, jnp.ones((8, lanes), f32)], axis=0)
        patches[y * depth : (y + 1) * depth, :] = whole.astype(bf16)

    pool_x, pool_y, pool_z = cot.shape[1:]
    twice = jnp.where(
        iota((pool_z, lanes), 1) // 2 == iota((pool_z, lanes), 0), 0.125, 0.0
    ).astype(bf16)
    for o in range(chan_out):
        part = dot(cot[o].reshape(pool_x * pool_y, pool_z), twice)
        for x in range(pool_x):
            spread[pl.ds(x * chan_out + o, pool_y, stride=pool_x * chan_out), :] = part[
                x * pool_y : (x + 1) * pool_y
            ]

    carry[...] = jnp.zeros_like(carry)
    gram[...] = jnp.zeros_like(gram)
    pairs = 4

    def finish(y, whole):
        before = pltpu.roll(whole[0:wide], lanes - 1, 1)
        after = pltpu.roll(whole[2 * wide : 3 * wide], 1, 1)
        zero = jnp.zeros_like(before)
        inner = (
            whole[wide : 2 * wide]
            + jnp.where(lane == lanes - 1, zero, before)
            + jnp.where(lane == 0, zero, after)
        )
        rest = jnp.where(lane == lanes - 1, before, jnp.where(lane == 0, after, zero))
        place = pl.ds(pl.multiple_of(y * wide, 8), wide)
        field[place, :] = inner
        outer[place, :] = rest

    def step(i, _):
        deltas, blocks = [], []
        weights = wbig[...]
        for k in range(pairs):
            j = i * pairs + k
            block = jnp.concatenate(
                [
                    patches[pl.ds(pl.multiple_of((2 * j + h) * depth, 16), 3 * depth), :]
                    for h in range(2)
                ],
                axis=1,
            )
            preact = dot(weights, block)
            slope = jnp.tanh(5.0 * preact)
            linear = jnp.maximum(preact, 0.3 * preact)
            factor = 1.0 + jnp.abs(slope)
            here = spread[pl.ds(pl.multiple_of(j * pool_x * chan_out, 8), pool_x * chan_out), :]
            slope = 0.65 + 0.35 * slope
            delta = []
            for x in range(pool_x):
                top, mid = 2 * x * chan_out, (2 * x + 1) * chan_out
                end = mid + chan_out
                times = here[x * chan_out : (x + 1) * chan_out]
                times = jnp.concatenate([times, times], axis=1)
                delta.append((slope[top:mid] * times).astype(bf16))
                delta.append((slope[mid:end] * times).astype(bf16))
                total = linear[top:mid] + linear[mid:end]
                total = total[:, :lanes] + total[:, lanes:]
                prod = factor[top:mid] * factor[mid:end]
                prod = prod[:, :lanes] * prod[:, lanes:]
                total = total - log_scale * jnp.log(prod)
                sums[pl.ds(x * pool_y + j, chan_out, stride=pool_x * pool_y), :] = total
            deltas.append(jnp.concatenate(delta, axis=0))
            blocks.append(block)
        gram[...] += dot(
            jnp.concatenate(deltas, axis=1), jnp.concatenate(blocks, axis=1), ((1,), (1,))
        )
        back = wback[...]
        size = 3 * wide
        carry_a, carry_b = carry[0:size, :], carry[size : 2 * size, :]
        for k in range(pairs):
            j = i * pairs + k
            parts = dot(back, deltas[k])
            part = lambda b, h: parts[b * size : (b + 1) * size, h * lanes : (h + 1) * lanes]
            finish(2 * j, carry_a + part(0, 0))
            finish(2 * j + 1, carry_b + part(1, 0) + part(0, 1))
            carry_a = part(2, 0) + part(1, 1)
            carry_b = part(2, 1)
        carry[0:size, :] = carry_a
        carry[size : 2 * size, :] = carry_b
        return 0

    lax.fori_loop(0, count_y // (2 * pairs), step, 0)
    size = 3 * wide
    finish(count_y, carry[0:size, :])
    finish(count_y + 1, carry[size : 2 * size, :])

    span = gram.shape[1]
    straight, turned = 0.0, 0.0
    for x in range(count_x):
        part = gram[x * chan_out : (x + 1) * chan_out, :]
        part = jnp.concatenate([part, jnp.zeros((chan_out, 2 * lanes - span), f32)], axis=1)
        straight = straight + part
        turned = turned + (pltpu.roll(part, 2 * lanes - chan * x, 1) if x else part)
    spot = iota((chan_out, lanes), 1)
    tight = 0.0
    group = 3 * chan
    for b in range(3):
        for e in range(3):
            shift = (b * depth + e * wide) - (b * 3 + e) * group
            part = pltpu.roll(turned, 2 * lanes - shift, 1)[:, :lanes] if shift else turned[:, :lanes]
            tight = jnp.where(spot // group == b * 3 + e, part, tight)
    part = pltpu.roll(straight, 2 * lanes + 9 * group - 3 * wide, 1)[:, :lanes]
    tight = jnp.where(spot == 9 * group, part, tight)
    coarse = tight.astype(bf16)
    frame_out[0:chan_out, :] = coarse
    frame_out[chan_out : 2 * chan_out, :] = (tight - coarse.astype(f32)).astype(bf16)

    halves = jnp.where(
        iota((2 * lanes, pool_z), 0) % lanes // 2 == iota((2 * lanes, pool_z), 1), 0.125, 0.0
    ).astype(bf16)
    for o in range(0, chan_out, 4):
        rows = 4 * pool_x * pool_y
        part = sums[o * pool_x * pool_y : o * pool_x * pool_y + rows, :]
        coarse = part.astype(bf16)
        fine = (part - coarse.astype(f32)).astype(bf16)
        mean = dot(jnp.concatenate([coarse, fine], axis=1), halves) + log_scale * float(np.log(2.0))
        pooled[o : o + 4] = mean.astype(bf16).reshape(4, pool_x, pool_y, pool_z)

    for x in range(count_x + 2):
        for c in range(chan):
            plane = field[pl.ds(wide + x * chan + c, count_y, stride=wide), :]
            if x == 0:
                face_low[c] = plane.astype(bf16)
            elif x == count_x + 1:
                face_high[c] = plane.astype(bf16)
            else:
                grad[c, x - 1] = plane
    top = 2 * chan_out
    ends = [field[0:wide, :], field[(count_y + 1) * wide : (count_y + 2) * wide, :]]
    frame_out[top : top + 2 * wide, :] = jnp.concatenate(ends, axis=0).astype(bf16)
    top = top + 2 * wide
    tall = frame_out.shape[0] - top
    outer[(count_y + 2) * wide :, :] = jnp.zeros((outer.shape[0] - (count_y + 2) * wide, lanes), f32)
    planes = [outer[pl.ds(r, tall, stride=wide), :].astype(bf16) for r in range(wide)]
    row = iota((wide * lanes, lanes), 0)
    spot = iota((wide * lanes, lanes), 1)
    want = jnp.where(spot < wide, spot * lanes + lanes - 1, (spot - wide) * lanes)
    pick = ((row == want) & (spot < 2 * wide)).astype(f32).astype(bf16)
    frame_out[top:, :] = dot(jnp.concatenate(planes, axis=1), pick).astype(bf16)


def final_kernel(sizes, grad, low, high, frames, out, wout):
    chan, count_x, count_y, _ = grad.shape
    chan_out = wout.shape[0]
    own = chan * count_x
    wide = own + 2 * chan
    coarse, fine = 0.0, 0.0
    for at in range(frames.shape[0]):
        coarse = coarse + frames[at, 0:chan_out, :].astype(f32)
        fine = fine + frames[at, chan_out : 2 * chan_out, :].astype(f32)
    wout[...] = coarse + fine
    top = 2 * chan_out
    above, below = [], []
    for dx in (-1, 0, 1):
        rows = frames[place_of((dx, -1, 0), sizes), top : top + 2 * wide, :]
        above.append(rows.astype(f32)[wide:])
        rows = frames[place_of((dx, 1, 0), sizes), top : top + 2 * wide, :]
        below.append(rows.astype(f32)[:wide])
    top = top + 2 * wide
    spot = iota((count_y, lanes), 1)
    row = iota((count_y, lanes), 0)
    total = 0.0
    for dx, turn, start in ((1, 0, chan), (0, lanes - own, chan), (2, own, own)):
        before, mid, after = [
            frames[place_of((dx - 1, dy, 1), sizes), top:, :].astype(f32) for dy in (-1, 0, 1)
        ]
        mid = mid[1 : count_y + 1]
        before = before[count_y + 1 : count_y + 2]
        after = after[0:1]
        mid = mid + jnp.where(row == 0, before, 0.0) + jnp.where(row == count_y - 1, after, 0.0)
        if turn:
            mid = pltpu.roll(mid, turn, 1)
            near = (spot >= start) & (spot < start + chan)
            near = near | ((spot >= wide + start) & (spot < wide + start + chan))
            mid = jnp.where(near, mid, 0.0)
        total = total + mid
    for x in range(count_x):
        for c in range(chan):
            r = chan + x * chan + c
            plane = grad[c, x]
            first = above[1][r : r + 1]
            final = below[1][r : r + 1]
            if x == 0:
                plane = plane + low[c].astype(f32)
                first = first + above[0][chan + own + c : chan + own + c + 1]
                final = final + below[0][chan + own + c : chan + own + c + 1]
            if x == count_x - 1:
                plane = plane + high[c].astype(f32)
                first = first + above[2][c : c + 1]
                final = final + below[2][c : c + 1]
            plane = plane + jnp.where(row == 0, first, 0.0)
            plane = plane + jnp.where(row == count_y - 1, final, 0.0)
            plane = plane + jnp.where(spot == lanes - 1, total[:, r : r + 1], 0.0)
            plane = plane + jnp.where(spot == 0, total[:, wide + r : wide + r + 1], 0.0)
            out[c, x] = plane


def call(kernel, outs, scratch=()):
    return pl.pallas_call(
        kernel,
        out_shape=outs,
        scratch_shapes=list(scratch),
        compiler_params=pltpu.CompilerParams(vmem_limit_bytes=limit),
    )


def on_device(cells, weight, bias, cotangent):
    chan, count_x, count_y, count_z = cells.shape
    chan_out = weight.shape[0]
    own = chan * count_x
    wide = own + 2 * chan
    depth = 3 * wide + 8
    shape = jax.ShapeDtypeStruct

    kernel = weight.transpose(0, 3, 4, 2, 1)
    placed = jnp.stack(
        [
            jnp.pad(kernel, ((0, 0), (0, 0), (0, 0), (x, count_x - 1 - x), (0, 0)))
            for x in range(count_x)
        ]
    ).reshape(count_x * chan_out, 3, 3 * wide)
    coarse = lax.reduce_precision(bias, 8, 7)
    middle = lax.reduce_precision(bias - coarse, 8, 7)
    fine = bias - coarse - middle
    pieces = jnp.stack([coarse, middle, fine], axis=1).astype(bf16)
    pieces = jnp.pad(jnp.tile(pieces, (count_x, 1))[:, None], ((0, 0), (0, 2), (0, 5)))
    wbig = jnp.concatenate([placed, pieces], axis=2).reshape(count_x * chan_out, 3 * depth)
    wback = placed.reshape(count_x * chan_out, 9 * wide).T

    sizes = [lax.axis_size(axis) for axis in axes]
    frame, low, high = call(
        pack_kernel,
        [
            shape((4 * own, lanes), bf16),
            shape((chan, count_y, lanes), bf16),
            shape((chan, count_y, lanes), bf16),
        ],
        [pltpu.VMEM((2 * own, lanes), f32)],
    )(cells)
    frames = lax.all_gather(frame, axes)
    low_in = taken_from(high, (-1, 0, 0))
    high_in = taken_from(low, (1, 0, 0))

    pool_x, pool_y, pool_z = cotangent.shape[1:]
    tall = 80
    pooled, grad, face_low, face_high, frame = call(
        functools.partial(main_kernel, sizes),
        [
            shape(cotangent.shape, bf16),
            shape(cells.shape, f32),
            shape((chan, count_y, lanes), bf16),
            shape((chan, count_y, lanes), bf16),
            shape((2 * chan_out + 2 * wide + tall, lanes), bf16),
        ],
        [
            pltpu.VMEM(((count_y + 2) * wide, lanes), f32),
            pltpu.VMEM(((count_y + 2) * depth, lanes), bf16),
            pltpu.VMEM((wide, lanes), f32),
            pltpu.VMEM((wide, lanes), f32),
            pltpu.VMEM((pool_y * pool_x * chan_out, lanes), f32),
            pltpu.VMEM((pool_y * pool_x * chan_out, lanes), f32),
            pltpu.VMEM(((count_y + 2) * wide, lanes), f32),
            pltpu.VMEM((tall * wide, lanes), f32),
            pltpu.VMEM((6 * wide, lanes), f32),
            pltpu.VMEM((count_x * chan_out, 3 * depth), f32),
        ],
    )(cells, low_in, high_in, frames, cotangent, wbig, wback)

    frames = lax.all_gather(frame, axes)
    low_back = taken_from(face_high, (-1, 0, 0))
    high_back = taken_from(face_low, (1, 0, 0))
    input_grad, wsum = call(
        functools.partial(final_kernel, sizes),
        [shape(cells.shape, f32), shape((chan_out, lanes), f32)],
    )(grad, low_back, high_back, frames)
    group = 3 * chan
    bias_grad = wsum[:, 9 * group]
    weight_grad = wsum[:, : 9 * group].reshape(chan_out, 3, 3, 3, chan)
    return (pooled, weight_grad.transpose(0, 4, 3, 1, 2), bias_grad, input_grad)


def solution(mesh):
    in_specs = (P(None, "gx", "gy", "gz"), P(), P(), P(None, "gx", "gy", "gz"))
    out_specs = (P(None, "gx", "gy", "gz"), P(), P(), P(None, "gx", "gy", "gz"))
    return jax.shard_map(
        on_device, mesh=mesh, in_specs=in_specs, out_specs=out_specs, check_vma=False
    )
```

```python
import functools

import jax
import jax.numpy as jnp
import numpy as np
from jax import lax
from jax.experimental import pallas as pl
from jax.experimental.pallas import tpu as pltpu
from jax.sharding import PartitionSpec as P

axes = ("gx", "gy", "gz")
f32, bf16 = jnp.float32, jnp.bfloat16
log_scale = 0.07
lanes = 128
limit = 48 * 1024 * 1024


def dot(a, b, contract=((1,), (0,))):
    return lax.dot_general(a, b, (contract, ((), ())), preferred_element_type=f32)


def iota(shape, dim):
    return lax.broadcasted_iota(jnp.int32, shape, dim)


def taken_from(array, offset):
    sizes = [lax.axis_size(axis) for axis in axes]
    pairs = []
    for place in np.ndindex(*sizes):
        source = [(p + o) % n for p, o, n in zip(place, offset, sizes)]
        pairs.append(
            (int(np.ravel_multi_index(source, sizes)), int(np.ravel_multi_index(place, sizes)))
        )
    return lax.ppermute(array, axes, pairs)


def split(value):
    coarse = value.astype(bf16)
    return coarse, (value - coarse.astype(f32)).astype(bf16)


def joined(pair):
    half = pair.shape[0] // 2
    return pair[:half].astype(f32) + pair[half:].astype(f32)


def pack_kernel(cells, edges, first, last, rows):
    chan, count_x, count_y, _ = cells.shape
    count = chan * count_x
    planes = [cells[c, x] for x in range(count_x) for c in range(chan)]
    wide = jnp.concatenate(planes, axis=1)
    row = iota((2 * count, count * lanes), 0)
    lane = iota((2 * count, count * lanes), 1)
    want = jnp.where(row < count, row * lanes, (row - count) * lanes + lanes - 1)
    pick = (lane == want).astype(f32).astype(bf16)
    found = dot(pick, wide, ((1,), (1,)))
    found = jnp.concatenate([found, jnp.zeros((2 * count, lanes - count_y), f32)], axis=1)
    edges[...] = pltpu.roll(found, 1, 1).astype(bf16)
    for at, plane in enumerate(planes):
        wide_plane = plane.astype(f32)
        rows[at : at + 1, :] = wide_plane[0:1]
        rows[count + at : count + at + 1, :] = wide_plane[count_y - 1 : count_y]
    first[...] = rows[0:count, :].astype(bf16)
    last[...] = rows[count : 2 * count, :].astype(bf16)


def bundle_kernel(cells, edges, above, below, low, high, left, right):
    chan, count_x, count_y, _ = cells.shape
    own = chan * count_x
    spot = iota((2 * own, lanes), 1)
    before = pltpu.roll(above[own:, :].astype(f32), count_y, 1)
    after = pltpu.roll(below[own:, :].astype(f32), lanes - count_y, 1)
    whole = jnp.where(
        spot == 0, before, jnp.where(spot == count_y + 1, after, edges[...].astype(f32))
    )
    right[...] = whole[0:own]
    left[...] = whole[own : 2 * own]
    rows_above = above[0:own, :].astype(f32)
    rows_below = below[0:own, :].astype(f32)
    zero = jnp.zeros((8, lanes), f32)
    body = chan * count_y
    for ref, x in ((low, 0), (high, count_x - 1)):
        for c in range(chan):
            ref[c * count_y : (c + 1) * count_y, :] = cells[c, x]
        at = slice(x * chan, x * chan + chan)
        frame = [rows_above[at], rows_below[at], zero]
        frame += [whole[own + x * chan : own + (x + 1) * chan], whole[at], zero]
        ref[body : body + 32, :] = jnp.concatenate(frame, axis=0).astype(bf16)


def spread_kernel(cot, spread):
    chan_out, pool_x, pool_y, pool_z = cot.shape
    twice = jnp.where(
        iota((pool_z, lanes), 1) // 2 == iota((pool_z, lanes), 0), 0.125, 0.0
    ).astype(bf16)
    for o in range(chan_out):
        part = dot(cot[o].reshape(pool_x * pool_y, pool_z), twice)
        for x in range(pool_x):
            spread[pl.ds(x * chan_out + o, pool_y, stride=pool_x * chan_out), :] = part[
                x * pool_y : (x + 1) * pool_y
            ]


def pool_kernel(sums, pooled):
    chan_out, pool_x, pool_y, pool_z = pooled.shape
    halves = jnp.where(
        iota((2 * lanes, pool_z), 0) % lanes // 2 == iota((2 * lanes, pool_z), 1), 0.125, 0.0
    ).astype(bf16)
    for o in range(0, chan_out, 4):
        rows = 4 * pool_x * pool_y
        part = sums[o * pool_x * pool_y : o * pool_x * pool_y + rows, :]
        mean = dot(jnp.concatenate(split(part), axis=1), halves) + log_scale * float(np.log(2.0))
        pooled[o : o + 4] = mean.astype(bf16).reshape(4, pool_x, pool_y, pool_z)


def main_kernel(
    cells, low, high, above, below, left_in, right_in, spread, wbig, wback,
    sums, field, bundle_low, bundle_high, wpart, wframe, rows_out, cols,
    stage, patches, left, right, outer, carry, gram,
):
    chan, count_x, count_y, _ = cells.shape
    pool_x, pool_y = count_x // 2, count_y // 2
    chan_out = wbig.shape[0] // count_x
    own = chan * count_x
    wide = own + 2 * chan
    depth = 3 * wide + 8
    body = chan * count_y
    lane = iota((wide, lanes), 1)

    for x in range(count_x + 2):
        for c in range(chan):
            if x == 0:
                plane = low[c * count_y : (c + 1) * count_y, :]
            elif x == count_x + 1:
                plane = high[c * count_y : (c + 1) * count_y, :]
            else:
                plane = cells[c, x - 1]
            stage[pl.ds(wide + x * chan + c, count_y, stride=wide), :] = plane.astype(f32)
    rest_low = low[body : body + 32, :].astype(f32)
    rest_high = high[body : body + 32, :].astype(f32)
    for base, ref, at in ((0, above, 0), ((count_y + 1) * wide, below, chan)):
        stage[base : base + chan, :] = rest_low[at : at + chan]
        stage[base + chan : base + chan + own, :] = ref[0:own, :].astype(f32)
        stage[base + chan + own : base + wide, :] = rest_high[at : at + chan]
    for ref, mine, at in ((left, left_in, 16), (right, right_in, 16 + chan)):
        ref[0:chan, :] = rest_low[at : at + chan]
        ref[chan : chan + own, :] = mine[...]
        ref[chan + own : wide, :] = rest_high[at : at + chan]
    left_cols, right_cols = left[...], right[...]
    for y in range(count_y + 2):
        mid = stage[y * wide : (y + 1) * wide, :]
        low_col = pltpu.roll(left_cols, (lanes - y) % lanes, 1)
        high_col = pltpu.roll(right_cols, (lanes - 1 - y) % lanes, 1)
        before = jnp.where(lane == 0, low_col, pltpu.roll(mid, 1, 1))
        after = jnp.where(lane == lanes - 1, high_col, pltpu.roll(mid, lanes - 1, 1))
        whole = jnp.concatenate([before, mid, after, jnp.ones((8, lanes), f32)], axis=0)
        patches[y * depth : (y + 1) * depth, :] = whole.astype(bf16)

    carry[...] = jnp.zeros_like(carry)
    gram[...] = jnp.zeros_like(gram)
    pairs = 4

    def finish(y, whole):
        before = pltpu.roll(whole[0:wide], lanes - 1, 1)
        after = pltpu.roll(whole[2 * wide : 3 * wide], 1, 1)
        zero = jnp.zeros_like(before)
        inner = (
            whole[wide : 2 * wide]
            + jnp.where(lane == lanes - 1, zero, before)
            + jnp.where(lane == 0, zero, after)
        )
        rest = jnp.where(lane == lanes - 1, before, jnp.where(lane == 0, after, zero))
        place = pl.ds(pl.multiple_of(y * wide, 8), wide)
        field[place, :] = inner
        outer[place, :] = rest

    def step(i, _):
        deltas, blocks = [], []
        weights = wbig[...]
        for k in range(pairs):
            j = i * pairs + k
            block = jnp.concatenate(
                [
                    patches[pl.ds(pl.multiple_of((2 * j + h) * depth, 16), 3 * depth), :]
                    for h in range(2)
                ],
                axis=1,
            )
            preact = dot(weights, block)
            slope = jnp.tanh(5.0 * preact)
            linear = jnp.maximum(preact, 0.3 * preact)
            factor = 1.0 + jnp.abs(slope)
            here = spread[pl.ds(pl.multiple_of(j * pool_x * chan_out, 8), pool_x * chan_out), :]
            slope = 0.65 + 0.35 * slope
            delta = []
            for x in range(pool_x):
                top, mid = 2 * x * chan_out, (2 * x + 1) * chan_out
                end = mid + chan_out
                times = here[x * chan_out : (x + 1) * chan_out]
                times = jnp.concatenate([times, times], axis=1)
                delta.append((slope[top:mid] * times).astype(bf16))
                delta.append((slope[mid:end] * times).astype(bf16))
                total = linear[top:mid] + linear[mid:end]
                total = total[:, :lanes] + total[:, lanes:]
                prod = factor[top:mid] * factor[mid:end]
                prod = prod[:, :lanes] * prod[:, lanes:]
                total = total - log_scale * jnp.log(prod)
                sums[pl.ds(x * pool_y + j, chan_out, stride=pool_x * pool_y), :] = total
            deltas.append(jnp.concatenate(delta, axis=0))
            blocks.append(block)
        gram[...] += dot(
            jnp.concatenate(deltas, axis=1), jnp.concatenate(blocks, axis=1), ((1,), (1,))
        )
        back = wback[...]
        size = 3 * wide
        carry_a, carry_b = carry[0:size, :], carry[size : 2 * size, :]
        for k in range(pairs):
            j = i * pairs + k
            parts = dot(back, deltas[k])
            part = lambda b, h: parts[b * size : (b + 1) * size, h * lanes : (h + 1) * lanes]
            finish(2 * j, carry_a + part(0, 0))
            finish(2 * j + 1, carry_b + part(1, 0) + part(0, 1))
            carry_a = part(2, 0) + part(1, 1)
            carry_b = part(2, 1)
        carry[0:size, :] = carry_a
        carry[size : 2 * size, :] = carry_b
        return 0

    lax.fori_loop(0, count_y // (2 * pairs), step, 0)
    size = 3 * wide
    finish(count_y, carry[0:size, :])
    finish(count_y + 1, carry[size : 2 * size, :])

    span = gram.shape[1]
    straight, turned = 0.0, 0.0
    for x in range(count_x):
        part = gram[x * chan_out : (x + 1) * chan_out, :]
        part = jnp.concatenate([part, jnp.zeros((chan_out, 2 * lanes - span), f32)], axis=1)
        straight = straight + part
        turned = turned + (pltpu.roll(part, 2 * lanes - chan * x, 1) if x else part)
    spot = iota((chan_out, lanes), 1)
    tight = 0.0
    group = 3 * chan
    for b in range(3):
        for e in range(3):
            shift = (b * depth + e * wide) - (b * 3 + e) * group
            part = pltpu.roll(turned, 2 * lanes - shift, 1)[:, :lanes] if shift else turned[:, :lanes]
            tight = jnp.where(spot // group == b * 3 + e, part, tight)
    part = pltpu.roll(straight, 2 * lanes + 9 * group - 3 * wide, 1)[:, :lanes]
    tight = jnp.where(spot == 9 * group, part, tight)
    coarse = tight.astype(bf16)
    wpart[...] = tight
    sides = jnp.concatenate(split(tight), axis=0)
    wframe[...] = sides

    ends = [field[0:wide, :], field[(count_y + 1) * wide : (count_y + 2) * wide, :]]
    rows_out[...] = jnp.concatenate([end[chan : chan + own] for end in ends], axis=0)
    tall = cols.shape[0]
    outer[(count_y + 2) * wide :, :] = jnp.zeros((outer.shape[0] - (count_y + 2) * wide, lanes), f32)
    planes = [outer[pl.ds(r, tall, stride=wide), :].astype(bf16) for r in range(wide)]
    row = iota((wide * lanes, lanes), 0)
    spot = iota((wide * lanes, lanes), 1)
    want = jnp.where(spot < wide, spot * lanes + lanes - 1, (spot - wide) * lanes)
    pick = ((row == want) & (spot < 2 * wide)).astype(f32).astype(bf16)
    found = dot(jnp.concatenate(planes, axis=1), pick)
    cols[...] = found
    found = found.astype(bf16)
    zero = jnp.zeros((8, lanes), f32)
    for ref, x in ((bundle_low, 0), (bundle_high, count_x + 1)):
        for c in range(chan):
            plane = field[pl.ds(wide + x * chan + c, count_y, stride=wide), :]
            ref[c * count_y : (c + 1) * count_y, :] = plane.astype(bf16)
        frame = [end[x * chan : (x + 1) * chan] for end in ends] + [zero]
        ref[body : body + 16, :] = jnp.concatenate(frame, axis=0).astype(bf16)
        ref[body + 16 : body + 16 + tall, :] = found
        ref[body + 16 + tall :, :] = sides


def x_kernel(alone, wpart, wframe, rows, cols, from_low, from_high, far, wsum, up, down, cols_out):
    tall = cols.shape[0]
    chan_out = wpart.shape[0]
    own = rows.shape[0] // 2
    body = from_low.shape[0] - 16 - tall - 2 * chan_out
    chan = 4
    wide = own + 2 * chan
    if alone:
        total = joined(jnp.concatenate(split(wpart[...]), axis=0))
    else:
        total = joined(wframe[...]) + joined(far[...])
        sides = [ref[body + 16 + tall :, :] for ref in (from_low, from_high)]
        total = total + (joined(sides[0]) + joined(sides[1]))
    wsum[...] = total
    sides = jnp.concatenate(split(total), axis=0)
    spot = iota((tall, lanes), 1)
    found = cols[...]
    for ref, turn, start in ((from_low, lanes - own, chan), (from_high, own, own)):
        part = pltpu.roll(ref[body + 16 : body + 16 + tall, :].astype(f32), turn, 1)
        near = (spot >= start) & (spot < start + chan)
        near = near | ((spot >= wide + start) & (spot < wide + start + chan))
        found = found + jnp.where(near, part, 0.0)
    cols_out[...] = found
    low_rows = from_low[body : body + 16, :].astype(f32)
    high_rows = from_high[body : body + 16, :].astype(f32)
    count_y = body // chan
    mid = jnp.zeros((own - 2 * chan, lanes), f32)
    for ref, at, line in ((down, 0, 0), (up, 1, count_y + 1)):
        more = [low_rows[at * chan : (at + 1) * chan], mid, high_rows[at * chan : (at + 1) * chan]]
        total = rows[at * own : (at + 1) * own, :] + jnp.concatenate(more, axis=0)
        extra = jnp.broadcast_to(found[line : line + 1], (16, lanes))
        ref[0 : own + 16, :] = jnp.concatenate([total, extra], axis=0).astype(bf16)
        ref[own + 16 :, :] = sides


def y_kernel(alone, count_y, wsum, cols, above, below, far, wout, frame):
    tall = cols.shape[0]
    chan_out = wsum.shape[0]
    top = above.shape[0] - 2 * chan_out
    if alone:
        total = joined(jnp.concatenate(split(wsum[...]), axis=0))
    else:
        total = joined(jnp.concatenate(split(wsum[...]), axis=0)) + joined(far[...])
        total = total + (joined(above[top:, :]) + joined(below[top:, :]))
    wout[...] = total
    frame[tall:, :] = jnp.concatenate(split(total), axis=0)
    row = iota((tall, lanes), 0)
    found = cols[...]
    found = found + jnp.where(row == 1, above[top - 16 : top, :].astype(f32)[0:1], 0.0)
    found = found + jnp.where(row == count_y, below[top - 16 : top, :].astype(f32)[0:1], 0.0)
    frame[0:tall, :] = found.astype(bf16)


def grad_kernel(field, from_low, from_high, grad):
    chan, count_x, count_y, _ = grad.shape
    wide = chan * (count_x + 2)
    for x in range(count_x):
        for c in range(chan):
            plane = field[pl.ds(wide + (x + 1) * chan + c, count_y, stride=wide), :]
            if x == 0:
                plane = plane + from_low[c * count_y : (c + 1) * count_y, :].astype(f32)
            if x == count_x - 1:
                plane = plane + from_high[c * count_y : (c + 1) * count_y, :].astype(f32)
            grad[c, x] = plane


def final_kernel(grad, wsum, above, below, frame, out, wout, bout):
    chan, count_x, count_y, _ = grad.shape
    chan_out = wsum.shape[0]
    own = chan * count_x
    wide = own + 2 * chan
    tall = frame.shape[0] - 2 * chan_out
    total = joined(jnp.concatenate(split(wsum[...]), axis=0)) + joined(frame[tall:, :])
    total = jnp.concatenate([total, jnp.zeros((lanes - chan_out, lanes), f32)], axis=0)
    total = total.T
    for a in range(3):
        for be in range(9):
            at = (be * 3 + a) * chan
            wout[a * 9 + be] = total[at : at + chan, :chan_out]
    bout[...] = total[27 * chan : 27 * chan + 1, :chan_out]
    spot = iota((count_y, lanes), 1)
    row = iota((count_y, lanes), 0)
    cols = frame[0:tall, :].astype(f32)[1 : count_y + 1]
    first = above[0:own, :].astype(f32)
    final = below[0:own, :].astype(f32)
    for x in range(count_x):
        for c in range(chan):
            at = x * chan + c
            r = chan + at
            more = jnp.where(spot == lanes - 1, cols[:, r : r + 1], 0.0)
            more = jnp.where(spot == 0, cols[:, wide + r : wide + r + 1], more)
            more = more + jnp.where(row == 0, first[at : at + 1], 0.0)
            more = more + jnp.where(row == count_y - 1, final[at : at + 1], 0.0)
            out[c, x] = grad[c, x] + more


def call(kernel, outs, scratch=(), cost=None):
    return pl.pallas_call(
        kernel,
        out_shape=outs,
        scratch_shapes=list(scratch),
        cost_estimate=cost,
        compiler_params=pltpu.CompilerParams(vmem_limit_bytes=limit),
    )


def on_device(cells, weight, bias, cotangent):
    chan, count_x, count_y, count_z = cells.shape
    chan_out = weight.shape[0]
    own = chan * count_x
    wide = own + 2 * chan
    depth = 3 * wide + 8
    shape = jax.ShapeDtypeStruct

    kernel = weight.transpose(0, 3, 4, 2, 1)
    placed = jnp.stack(
        [
            jnp.pad(kernel, ((0, 0), (0, 0), (0, 0), (x, count_x - 1 - x), (0, 0)))
            for x in range(count_x)
        ]
    ).reshape(count_x * chan_out, 3, 3 * wide)
    coarse = lax.reduce_precision(bias, 8, 7)
    middle = lax.reduce_precision(bias - coarse, 8, 7)
    fine = bias - coarse - middle
    pieces = jnp.stack([coarse, middle, fine], axis=1).astype(bf16)
    pieces = jnp.pad(jnp.tile(pieces, (count_x, 1))[:, None], ((0, 0), (0, 2), (0, 5)))
    wbig = jnp.concatenate([placed, pieces], axis=2).reshape(count_x * chan_out, 3 * depth)
    wback = placed.reshape(count_x * chan_out, 9 * wide).T

    own_block = shape((own, lanes), bf16)
    edges, first, last = call(
        pack_kernel,
        [shape((2 * own, lanes), bf16), own_block, own_block],
        [pltpu.VMEM((2 * own, lanes), f32)],
    )(cells)
    pool_x, pool_y, pool_z = cotangent.shape[1:]
    pooled_rows = shape((pool_y * pool_x * chan_out, lanes), f32)
    spread = call(spread_kernel, pooled_rows)(cotangent)
    edges = taken_from(edges, (0, 0, 1))
    above = taken_from(jnp.concatenate([last, edges]), (0, -1, 0))
    below = taken_from(jnp.concatenate([first, edges]), (0, 1, 0))
    body = chan * count_y
    bundle = shape((body + 32, lanes), bf16)
    low, high, left, right = call(
        bundle_kernel, [bundle, bundle, shape((own, lanes), f32), shape((own, lanes), f32)]
    )(cells, edges, above, below)
    low, high = taken_from(high, (-1, 0, 0)), taken_from(low, (1, 0, 0))

    tall = 80
    bundle = shape((body + 16 + tall + 2 * chan_out, lanes), bf16)
    sums, field, low, high, wpart, wframe, rows, cols = call(
        main_kernel,
        [
            pooled_rows,
            shape(((count_y + 2) * wide, lanes), f32),
            bundle,
            bundle,
            shape((chan_out, lanes), f32),
            shape((2 * chan_out, lanes), bf16),
            shape((2 * own, lanes), f32),
            shape((tall, lanes), f32),
        ],
        [
            pltpu.VMEM(((count_y + 2) * wide, lanes), f32),
            pltpu.VMEM(((count_y + 2) * depth, lanes), bf16),
            pltpu.VMEM((wide, lanes), f32),
            pltpu.VMEM((wide, lanes), f32),
            pltpu.VMEM((tall * wide, lanes), f32),
            pltpu.VMEM((6 * wide, lanes), f32),
            pltpu.VMEM((count_x * chan_out, 3 * depth), f32),
        ],
    )(cells, low, high, above, below, left, right, spread, wbig, wback)

    alone_x = lax.axis_size("gx") != 4
    alone_y = lax.axis_size("gy") != 4
    if alone_x:
        wpart, far = lax.psum(wpart, "gx"), wframe
    else:
        far = taken_from(wframe, (2, 0, 0))
    low, high = taken_from(high, (-1, 0, 0)), taken_from(low, (1, 0, 0))
    pooled = call(pool_kernel, shape(cotangent.shape, bf16))(sums)
    rows_out = shape((own + 16 + 2 * chan_out, lanes), bf16)
    wsum, up, down, cols = call(
        functools.partial(x_kernel, alone_x),
        [shape((chan_out, lanes), f32), rows_out, rows_out, shape((tall, lanes), f32)],
    )(wpart, wframe, rows, cols, low, high, far)
    grad = call(grad_kernel, shape(cells.shape, f32))(field, low, high)
    if alone_y:
        far, wsum = wframe, lax.psum(wsum, "gy")
    else:
        far = taken_from(up[own + 16 :], (0, 2, 0))
    above, below = taken_from(up, (0, -1, 0)), taken_from(down, (0, 1, 0))
    wsum, frame = call(
        functools.partial(y_kernel, alone_y, count_y),
        [shape((chan_out, lanes), f32), shape((tall + 2 * chan_out, lanes), bf16)],
    )(wsum, cols, above, below, far)
    frame = taken_from(frame, (0, 0, 1))
    input_grad, wsum, bias_grad = call(
        final_kernel,
        [
            shape(cells.shape, f32),
            shape((27, chan, chan_out), f32),
            shape((1, chan_out), f32),
        ],
    )(grad, wsum, above, below, frame)
    weight_grad = wsum.reshape(3, 3, 3, chan, chan_out).transpose(4, 3, 0, 1, 2)
    return (pooled, weight_grad, bias_grad.reshape(chan_out), input_grad)


def solution(mesh):
    in_specs = (P(None, "gx", "gy", "gz"), P(), P(), P(None, "gx", "gy", "gz"))
    out_specs = (P(None, "gx", "gy", "gz"), P(), P(), P(None, "gx", "gy", "gz"))
    return jax.shard_map(
        on_device, mesh=mesh, in_specs=in_specs, out_specs=out_specs, check_vma=False
    )
```

```python
import functools

import jax
import jax.numpy as jnp
import numpy as np
from jax import lax
from jax.experimental import pallas as pl
from jax.experimental.pallas import tpu as pltpu
from jax.sharding import PartitionSpec as P

axes = ("gx", "gy", "gz")
f32, bf16 = jnp.float32, jnp.bfloat16
log_scale = 0.07
lanes = 128
limit = 48 * 1024 * 1024


def dot(a, b, contract=((1,), (0,))):
    return lax.dot_general(a, b, (contract, ((), ())), preferred_element_type=f32)


def iota(shape, dim):
    return lax.broadcasted_iota(jnp.int32, shape, dim)


def taken_from(array, offset):
    sizes = [lax.axis_size(axis) for axis in axes]
    pairs = []
    for place in np.ndindex(*sizes):
        source = [(p + o) % n for p, o, n in zip(place, offset, sizes)]
        pairs.append(
            (int(np.ravel_multi_index(source, sizes)), int(np.ravel_multi_index(place, sizes)))
        )
    return lax.ppermute(array, axes, pairs)


def split(value):
    coarse = value.astype(bf16)
    return coarse, (value - coarse.astype(f32)).astype(bf16)


def joined(pair):
    half = pair.shape[0] // 2
    return pair[:half].astype(f32) + pair[half:].astype(f32)


def pack_kernel(cells, edges, first, last, rows):
    chan, count_x, count_y, _ = cells.shape
    count = chan * count_x
    planes = [cells[c, x] for x in range(count_x) for c in range(chan)]
    wide = jnp.concatenate(planes, axis=1)
    row = iota((2 * count, count * lanes), 0)
    lane = iota((2 * count, count * lanes), 1)
    want = jnp.where(row < count, row * lanes, (row - count) * lanes + lanes - 1)
    pick = (lane == want).astype(f32).astype(bf16)
    found = dot(pick, wide, ((1,), (1,)))
    found = jnp.concatenate([found, jnp.zeros((2 * count, lanes - count_y), f32)], axis=1)
    edges[...] = pltpu.roll(found, 1, 1).astype(bf16)
    for at, plane in enumerate(planes):
        wide_plane = plane.astype(f32)
        rows[at : at + 1, :] = wide_plane[0:1]
        rows[count + at : count + at + 1, :] = wide_plane[count_y - 1 : count_y]
    first[...] = rows[0:count, :].astype(bf16)
    last[...] = rows[count : 2 * count, :].astype(bf16)


def beside(axis, step, count):
    return lax.rem(lax.axis_index(axis) + (step + count), count)


def send_kernel(first, last, edges, blocks):
    count = blocks.shape[0]
    own = first.shape[0]
    blocks[...] = jnp.zeros_like(blocks)
    for step, ref in ((1, last), (-1, first)):
        to = beside("gy", step, count)
        blocks[to, 0:own, :] = ref[...]
        blocks[to, own : 3 * own, :] = edges[...]


def bundle_kernel(cells, edges, blocks, low, high, left, right, rows):
    chan, count_x, count_y, _ = cells.shape
    count = blocks.shape[0]
    above = blocks.at[beside("gy", -1, count)]
    below = blocks.at[beside("gy", 1, count)]
    own = chan * count_x
    spot = iota((2 * own, lanes), 1)
    before = pltpu.roll(above[own:, :].astype(f32), count_y, 1)
    after = pltpu.roll(below[own:, :].astype(f32), lanes - count_y, 1)
    whole = jnp.where(
        spot == 0, before, jnp.where(spot == count_y + 1, after, edges[...].astype(f32))
    )
    right[...] = whole[0:own]
    left[...] = whole[own : 2 * own]
    rows_above = above[0:own, :].astype(f32)
    rows_below = below[0:own, :].astype(f32)
    rows[0:own, :] = rows_above
    rows[own : 2 * own, :] = rows_below
    zero = jnp.zeros((8, lanes), f32)
    body = chan * count_y
    for ref, x in ((low, 0), (high, count_x - 1)):
        for c in range(chan):
            ref[c * count_y : (c + 1) * count_y, :] = cells[c, x]
        at = slice(x * chan, x * chan + chan)
        frame = [rows_above[at], rows_below[at], zero]
        frame += [whole[own + x * chan : own + (x + 1) * chan], whole[at], zero]
        ref[body : body + 32, :] = jnp.concatenate(frame, axis=0).astype(bf16)


def spread_kernel(cot, spread):
    chan_out, pool_x, pool_y, pool_z = cot.shape
    twice = jnp.where(
        iota((pool_z, lanes), 1) // 2 == iota((pool_z, lanes), 0), 0.125, 0.0
    ).astype(bf16)
    for o in range(chan_out):
        part = dot(cot[o].reshape(pool_x * pool_y, pool_z), twice)
        for x in range(pool_x):
            spread[pl.ds(x * chan_out + o, pool_y, stride=pool_x * chan_out), :] = part[
                x * pool_y : (x + 1) * pool_y
            ]


def pool_kernel(sums, pooled):
    chan_out, pool_x, pool_y, pool_z = pooled.shape
    halves = jnp.where(
        iota((2 * lanes, pool_z), 0) % lanes // 2 == iota((2 * lanes, pool_z), 1), 0.125, 0.0
    ).astype(bf16)
    for o in range(0, chan_out, 4):
        rows = 4 * pool_x * pool_y
        part = sums[o * pool_x * pool_y : o * pool_x * pool_y + rows, :]
        mean = dot(jnp.concatenate(split(part), axis=1), halves) + log_scale * float(np.log(2.0))
        pooled[o : o + 4] = mean.astype(bf16).reshape(4, pool_x, pool_y, pool_z)


def main_kernel(
    cells, low, high, rows_in, left_in, right_in, spread, wbig, wback,
    sums, field, bundle_low, bundle_high, wpart, wframe, rows_out, cols,
    stage, patches, left, right, outer, carry, gram,
):
    chan, count_x, count_y, _ = cells.shape
    pool_x, pool_y = count_x // 2, count_y // 2
    chan_out = wbig.shape[0] // count_x
    own = chan * count_x
    wide = own + 2 * chan
    depth = 3 * wide + 8
    body = chan * count_y
    lane = iota((wide, lanes), 1)

    for x in range(count_x + 2):
        for c in range(chan):
            if x == 0:
                plane = low[c * count_y : (c + 1) * count_y, :]
            elif x == count_x + 1:
                plane = high[c * count_y : (c + 1) * count_y, :]
            else:
                plane = cells[c, x - 1]
            stage[pl.ds(wide + x * chan + c, count_y, stride=wide), :] = plane.astype(f32)
    rest_low = low[body : body + 32, :].astype(f32)
    rest_high = high[body : body + 32, :].astype(f32)
    for base, top, at in ((0, 0, 0), ((count_y + 1) * wide, own, chan)):
        stage[base : base + chan, :] = rest_low[at : at + chan]
        stage[base + chan : base + chan + own, :] = rows_in[top : top + own, :]
        stage[base + chan + own : base + wide, :] = rest_high[at : at + chan]
    for ref, mine, at in ((left, left_in, 16), (right, right_in, 16 + chan)):
        ref[0:chan, :] = rest_low[at : at + chan]
        ref[chan : chan + own, :] = mine[...]
        ref[chan + own : wide, :] = rest_high[at : at + chan]
    left_cols, right_cols = left[...], right[...]
    for y in range(count_y + 2):
        mid = stage[y * wide : (y + 1) * wide, :]
        low_col = pltpu.roll(left_cols, (lanes - y) % lanes, 1)
        high_col = pltpu.roll(right_cols, (lanes - 1 - y) % lanes, 1)
        before = jnp.where(lane == 0, low_col, pltpu.roll(mid, 1, 1))
        after = jnp.where(lane == lanes - 1, high_col, pltpu.roll(mid, lanes - 1, 1))
        whole = jnp.concatenate([before, mid, after, jnp.ones((8, lanes), f32)], axis=0)
        patches[y * depth : (y + 1) * depth, :] = whole.astype(bf16)

    carry[...] = jnp.zeros_like(carry)
    gram[...] = jnp.zeros_like(gram)
    pairs = 4

    def finish(y, whole):
        before = pltpu.roll(whole[0:wide], lanes - 1, 1)
        after = pltpu.roll(whole[2 * wide : 3 * wide], 1, 1)
        zero = jnp.zeros_like(before)
        inner = (
            whole[wide : 2 * wide]
            + jnp.where(lane == lanes - 1, zero, before)
            + jnp.where(lane == 0, zero, after)
        )
        rest = jnp.where(lane == lanes - 1, before, jnp.where(lane == 0, after, zero))
        place = pl.ds(pl.multiple_of(y * wide, 8), wide)
        field[place, :] = inner
        outer[place, :] = rest

    def step(i, _):
        deltas, blocks = [], []
        weights = wbig[...]
        for k in range(pairs):
            j = i * pairs + k
            block = jnp.concatenate(
                [
                    patches[pl.ds(pl.multiple_of((2 * j + h) * depth, 16), 3 * depth), :]
                    for h in range(2)
                ],
                axis=1,
            )
            preact = dot(weights, block)
            slope = jnp.tanh(5.0 * preact)
            linear = jnp.maximum(preact, 0.3 * preact)
            factor = 1.0 + jnp.abs(slope)
            here = spread[pl.ds(pl.multiple_of(j * pool_x * chan_out, 8), pool_x * chan_out), :]
            slope = 0.65 + 0.35 * slope
            delta = []
            for x in range(pool_x):
                top, mid = 2 * x * chan_out, (2 * x + 1) * chan_out
                end = mid + chan_out
                times = here[x * chan_out : (x + 1) * chan_out]
                times = jnp.concatenate([times, times], axis=1)
                delta.append((slope[top:mid] * times).astype(bf16))
                delta.append((slope[mid:end] * times).astype(bf16))
                total = linear[top:mid] + linear[mid:end]
                total = total[:, :lanes] + total[:, lanes:]
                prod = factor[top:mid] * factor[mid:end]
                prod = prod[:, :lanes] * prod[:, lanes:]
                total = total - log_scale * jnp.log(prod)
                sums[pl.ds(x * pool_y + j, chan_out, stride=pool_x * pool_y), :] = total
            deltas.append(jnp.concatenate(delta, axis=0))
            blocks.append(block)
        gram[...] += dot(
            jnp.concatenate(deltas, axis=1), jnp.concatenate(blocks, axis=1), ((1,), (1,))
        )
        back = wback[...]
        size = 3 * wide
        carry_a, carry_b = carry[0:size, :], carry[size : 2 * size, :]
        for k in range(pairs):
            j = i * pairs + k
            parts = dot(back, deltas[k])
            part = lambda b, h: parts[b * size : (b + 1) * size, h * lanes : (h + 1) * lanes]
            finish(2 * j, carry_a + part(0, 0))
            finish(2 * j + 1, carry_b + part(1, 0) + part(0, 1))
            carry_a = part(2, 0) + part(1, 1)
            carry_b = part(2, 1)
        carry[0:size, :] = carry_a
        carry[size : 2 * size, :] = carry_b
        return 0

    lax.fori_loop(0, count_y // (2 * pairs), step, 0)
    size = 3 * wide
    finish(count_y, carry[0:size, :])
    finish(count_y + 1, carry[size : 2 * size, :])

    span = gram.shape[1]
    straight, turned = 0.0, 0.0
    for x in range(count_x):
        part = gram[x * chan_out : (x + 1) * chan_out, :]
        part = jnp.concatenate([part, jnp.zeros((chan_out, 2 * lanes - span), f32)], axis=1)
        straight = straight + part
        turned = turned + (pltpu.roll(part, 2 * lanes - chan * x, 1) if x else part)
    spot = iota((chan_out, lanes), 1)
    tight = 0.0
    group = 3 * chan
    for b in range(3):
        for e in range(3):
            shift = (b * depth + e * wide) - (b * 3 + e) * group
            part = pltpu.roll(turned, 2 * lanes - shift, 1)[:, :lanes] if shift else turned[:, :lanes]
            tight = jnp.where(spot // group == b * 3 + e, part, tight)
    part = pltpu.roll(straight, 2 * lanes + 9 * group - 3 * wide, 1)[:, :lanes]
    tight = jnp.where(spot == 9 * group, part, tight)
    coarse = tight.astype(bf16)
    wpart[...] = tight
    sides = jnp.concatenate(split(tight), axis=0)
    wframe[...] = sides

    ends = [field[0:wide, :], field[(count_y + 1) * wide : (count_y + 2) * wide, :]]
    rows_out[...] = jnp.concatenate([end[chan : chan + own] for end in ends], axis=0)
    tall = cols.shape[0]
    outer[(count_y + 2) * wide :, :] = jnp.zeros((outer.shape[0] - (count_y + 2) * wide, lanes), f32)
    planes = [outer[pl.ds(r, tall, stride=wide), :].astype(bf16) for r in range(wide)]
    row = iota((wide * lanes, lanes), 0)
    spot = iota((wide * lanes, lanes), 1)
    want = jnp.where(spot < wide, spot * lanes + lanes - 1, (spot - wide) * lanes)
    pick = ((row == want) & (spot < 2 * wide)).astype(f32).astype(bf16)
    found = dot(jnp.concatenate(planes, axis=1), pick)
    cols[...] = found
    found = found.astype(bf16)
    zero = jnp.zeros((8, lanes), f32)
    for ref, x in ((bundle_low, 0), (bundle_high, count_x + 1)):
        for c in range(chan):
            plane = field[pl.ds(wide + x * chan + c, count_y, stride=wide), :]
            ref[c * count_y : (c + 1) * count_y, :] = plane.astype(bf16)
        frame = [end[x * chan : (x + 1) * chan] for end in ends] + [zero]
        ref[body : body + 16, :] = jnp.concatenate(frame, axis=0).astype(bf16)
        ref[body + 16 : body + 16 + tall, :] = found
        ref[body + 16 + tall :, :] = sides


def x_kernel(alone, wpart, wframe, rows, cols, from_low, from_high, far, blocks, cols_out):
    tall = cols.shape[0]
    chan_out = wpart.shape[0]
    own = rows.shape[0] // 2
    body = from_low.shape[0] - 16 - tall - 2 * chan_out
    chan = 4
    wide = own + 2 * chan
    if alone:
        total = joined(jnp.concatenate(split(wpart[...]), axis=0))
    else:
        total = joined(wframe[...]) + joined(far[...])
        sides = [ref[body + 16 + tall :, :] for ref in (from_low, from_high)]
        total = total + (joined(sides[0]) + joined(sides[1]))
    sides = jnp.concatenate(split(total), axis=0)
    spot = iota((tall, lanes), 1)
    found = cols[...]
    for ref, turn, start in ((from_low, lanes - own, chan), (from_high, own, own)):
        part = pltpu.roll(ref[body + 16 : body + 16 + tall, :].astype(f32), turn, 1)
        near = (spot >= start) & (spot < start + chan)
        near = near | ((spot >= wide + start) & (spot < wide + start + chan))
        found = found + jnp.where(near, part, 0.0)
    cols_out[...] = found
    low_rows = from_low[body : body + 16, :].astype(f32)
    high_rows = from_high[body : body + 16, :].astype(f32)
    count_y = body // chan
    mid = jnp.zeros((own - 2 * chan, lanes), f32)
    count = blocks.shape[0]
    for to in range(count):
        blocks[to, 0 : own + 16, :] = jnp.zeros((own + 16, lanes), bf16)
        blocks[to, own + 16 :, :] = sides
    for step, at, line in ((-1, 0, 0), (1, 1, count_y + 1)):
        more = [low_rows[at * chan : (at + 1) * chan], mid, high_rows[at * chan : (at + 1) * chan]]
        total = rows[at * own : (at + 1) * own, :] + jnp.concatenate(more, axis=0)
        extra = jnp.broadcast_to(found[line : line + 1], (16, lanes))
        to = beside("gy", step, count)
        blocks[to, 0 : own + 16, :] = jnp.concatenate([total, extra], axis=0).astype(bf16)


def y_kernel(count_y, cols, blocks, wout, rows, frame):
    tall = cols.shape[0]
    chan_out = wout.shape[0]
    count = blocks.shape[0]
    top = blocks.shape[1] - 2 * chan_out
    above = blocks.at[beside("gy", -1, count)]
    below = blocks.at[beside("gy", 1, count)]
    rows[...] = jnp.concatenate([above[0:16, :], below[0:16, :]], axis=0).astype(f32)
    total = joined(blocks[0, top:, :])
    for at in range(1, count):
        total = total + joined(blocks[at, top:, :])
    wout[...] = total
    frame[tall:, :] = jnp.concatenate(split(total), axis=0)
    row = iota((tall, lanes), 0)
    found = cols[...]
    found = found + jnp.where(row == 1, above[top - 16 : top, :].astype(f32)[0:1], 0.0)
    found = found + jnp.where(row == count_y, below[top - 16 : top, :].astype(f32)[0:1], 0.0)
    frame[0:tall, :] = found.astype(bf16)


def grad_kernel(field, from_low, from_high, grad):
    chan, count_x, count_y, _ = grad.shape
    wide = chan * (count_x + 2)
    for x in range(count_x):
        for c in range(chan):
            plane = field[pl.ds(wide + (x + 1) * chan + c, count_y, stride=wide), :]
            if x == 0:
                plane = plane + from_low[c * count_y : (c + 1) * count_y, :].astype(f32)
            if x == count_x - 1:
                plane = plane + from_high[c * count_y : (c + 1) * count_y, :].astype(f32)
            grad[c, x] = plane


def final_kernel(grad, wsum, rows, frame, out, wout, bout):
    chan, count_x, count_y, _ = grad.shape
    chan_out = wsum.shape[0]
    own = chan * count_x
    wide = own + 2 * chan
    tall = frame.shape[0] - 2 * chan_out
    total = joined(jnp.concatenate(split(wsum[...]), axis=0)) + joined(frame[tall:, :])
    total = jnp.concatenate([total, jnp.zeros((lanes - chan_out, lanes), f32)], axis=0)
    total = total.T
    for a in range(3):
        for be in range(9):
            at = (be * 3 + a) * chan
            wout[a * 9 + be] = total[at : at + chan, :chan_out]
    bout[...] = total[27 * chan : 27 * chan + 1, :chan_out]
    spot = iota((count_y, lanes), 1)
    row = iota((count_y, lanes), 0)
    cols = frame[0:tall, :].astype(f32)[1 : count_y + 1]
    first = rows[0:own, :]
    final = rows[own : 2 * own, :]
    for x in range(count_x):
        for c in range(chan):
            at = x * chan + c
            r = chan + at
            more = jnp.where(spot == lanes - 1, cols[:, r : r + 1], 0.0)
            more = jnp.where(spot == 0, cols[:, wide + r : wide + r + 1], more)
            more = more + jnp.where(row == 0, first[at : at + 1], 0.0)
            more = more + jnp.where(row == count_y - 1, final[at : at + 1], 0.0)
            out[c, x] = grad[c, x] + more


def call(kernel, outs, scratch=(), cost=None):
    return pl.pallas_call(
        kernel,
        out_shape=outs,
        scratch_shapes=list(scratch),
        cost_estimate=cost,
        compiler_params=pltpu.CompilerParams(vmem_limit_bytes=limit),
    )


def on_device(cells, weight, bias, cotangent):
    chan, count_x, count_y, count_z = cells.shape
    chan_out = weight.shape[0]
    own = chan * count_x
    wide = own + 2 * chan
    depth = 3 * wide + 8
    shape = jax.ShapeDtypeStruct

    kernel = weight.transpose(0, 3, 4, 2, 1)
    placed = jnp.stack(
        [
            jnp.pad(kernel, ((0, 0), (0, 0), (0, 0), (x, count_x - 1 - x), (0, 0)))
            for x in range(count_x)
        ]
    ).reshape(count_x * chan_out, 3, 3 * wide)
    coarse = lax.reduce_precision(bias, 8, 7)
    middle = lax.reduce_precision(bias - coarse, 8, 7)
    fine = bias - coarse - middle
    pieces = jnp.stack([coarse, middle, fine], axis=1).astype(bf16)
    pieces = jnp.pad(jnp.tile(pieces, (count_x, 1))[:, None], ((0, 0), (0, 2), (0, 5)))
    wbig = jnp.concatenate([placed, pieces], axis=2).reshape(count_x * chan_out, 3 * depth)
    wback = placed.reshape(count_x * chan_out, 9 * wide).T

    own_block = shape((own, lanes), bf16)
    edges, first, last = call(
        pack_kernel,
        [shape((2 * own, lanes), bf16), own_block, own_block],
        [pltpu.VMEM((2 * own, lanes), f32)],
    )(cells)
    pool_x, pool_y, pool_z = cotangent.shape[1:]
    pooled_rows = shape((pool_y * pool_x * chan_out, lanes), f32)
    spread = call(spread_kernel, pooled_rows)(cotangent)
    edges = taken_from(edges, (0, 0, 1))
    count_gy = lax.axis_size("gy")
    blocks = call(send_kernel, shape((count_gy, 3 * own, lanes), bf16))(first, last, edges)
    blocks = lax.all_to_all(blocks, "gy", 0, 0)
    body = chan * count_y
    bundle = shape((body + 32, lanes), bf16)
    side = shape((own, lanes), f32)
    low, high, left, right, rows = call(
        bundle_kernel, [bundle, bundle, side, side, shape((2 * own, lanes), f32)]
    )(cells, edges, blocks)
    low, high = taken_from(high, (-1, 0, 0)), taken_from(low, (1, 0, 0))

    tall = 80
    bundle = shape((body + 16 + tall + 2 * chan_out, lanes), bf16)
    sums, field, low, high, wpart, wframe, rows, cols = call(
        main_kernel,
        [
            pooled_rows,
            shape(((count_y + 2) * wide, lanes), f32),
            bundle,
            bundle,
            shape((chan_out, lanes), f32),
            shape((2 * chan_out, lanes), bf16),
            shape((2 * own, lanes), f32),
            shape((tall, lanes), f32),
        ],
        [
            pltpu.VMEM(((count_y + 2) * wide, lanes), f32),
            pltpu.VMEM(((count_y + 2) * depth, lanes), bf16),
            pltpu.VMEM((wide, lanes), f32),
            pltpu.VMEM((wide, lanes), f32),
            pltpu.VMEM((tall * wide, lanes), f32),
            pltpu.VMEM((6 * wide, lanes), f32),
            pltpu.VMEM((count_x * chan_out, 3 * depth), f32),
        ],
    )(cells, low, high, rows, left, right, spread, wbig, wback)

    alone_x = lax.axis_size("gx") != 4
    if alone_x:
        wpart, far = lax.psum(wpart, "gx"), wframe
    else:
        far = taken_from(wframe, (2, 0, 0))
    low, high = taken_from(high, (-1, 0, 0)), taken_from(low, (1, 0, 0))
    pooled = call(pool_kernel, shape(cotangent.shape, bf16))(sums)
    blocks, cols = call(
        functools.partial(x_kernel, alone_x),
        [
            shape((count_gy, own + 16 + 2 * chan_out, lanes), bf16),
            shape((tall, lanes), f32),
        ],
    )(wpart, wframe, rows, cols, low, high, far)
    grad = call(grad_kernel, shape(cells.shape, f32))(field, low, high)
    blocks = lax.all_to_all(blocks, "gy", 0, 0)
    wsum, rows, frame = call(
        functools.partial(y_kernel, count_y),
        [
            shape((chan_out, lanes), f32),
            shape((2 * own, lanes), f32),
            shape((tall + 2 * chan_out, lanes), bf16),
        ],
    )(cols, blocks)
    frame = taken_from(frame, (0, 0, 1))
    input_grad, wsum, bias_grad = call(
        final_kernel,
        [
            shape(cells.shape, f32),
            shape((27, chan, chan_out), f32),
            shape((1, chan_out), f32),
        ],
    )(grad, wsum, rows, frame)
    weight_grad = wsum.reshape(3, 3, 3, chan, chan_out).transpose(4, 3, 0, 1, 2)
    return (pooled, weight_grad, bias_grad.reshape(chan_out), input_grad)


def solution(mesh):
    in_specs = (P(None, "gx", "gy", "gz"), P(), P(), P(None, "gx", "gy", "gz"))
    out_specs = (P(None, "gx", "gy", "gz"), P(), P(), P(None, "gx", "gy", "gz"))
    return jax.shard_map(
        on_device, mesh=mesh, in_specs=in_specs, out_specs=out_specs, check_vma=False
    )
```

```python
import functools

import jax
import jax.numpy as jnp
import numpy as np
from jax import lax
from jax.experimental import pallas as pl
from jax.experimental.pallas import tpu as pltpu
from jax.sharding import PartitionSpec as P

axes = ("gx", "gy", "gz")
f32, bf16 = jnp.float32, jnp.bfloat16
log_scale = 0.07
lanes = 128
limit = 48 * 1024 * 1024


def dot(a, b, contract=((1,), (0,))):
    return lax.dot_general(a, b, (contract, ((), ())), preferred_element_type=f32)


def iota(shape, dim):
    return lax.broadcasted_iota(jnp.int32, shape, dim)


def swapped(array, axis, pairing):
    count = lax.axis_size(axis)
    pairs = []
    for i in range(count):
        if pairing == 2:
            partner = i + count // 2
        else:
            partner = i + 1 if i % 2 == pairing else i - 1
        pairs.append((i, partner % count))
    return lax.ppermute(array, axis, pairs)


def is_even(axis):
    return lax.rem(lax.axis_index(axis), 2) == 0


def pick(axis, if_even, if_odd):
    return jnp.where(is_even(axis), if_even, if_odd)


def split(value):
    coarse = value.astype(bf16)
    return coarse, (value - coarse.astype(f32)).astype(bf16)


def joined(pair):
    half = pair.shape[0] // 2
    return pair[:half].astype(f32) + pair[half:].astype(f32)


def pack_kernel(cells, edges, sent_0, sent_1, rows):
    chan, count_x, count_y, _ = cells.shape
    count = chan * count_x
    planes = [cells[c, x] for x in range(count_x) for c in range(chan)]
    wide = jnp.concatenate(planes, axis=1)
    row = iota((2 * count, count * lanes), 0)
    lane = iota((2 * count, count * lanes), 1)
    want = jnp.where(row < count, row * lanes, (row - count) * lanes + lanes - 1)
    chosen = (lane == want).astype(f32).astype(bf16)
    found = dot(chosen, wide, ((1,), (1,)))
    found = jnp.concatenate([found, jnp.zeros((2 * count, lanes - count_y), f32)], axis=1)
    edges[...] = pltpu.roll(found, 1, 1).astype(bf16)
    for at, plane in enumerate(planes):
        wide_plane = plane.astype(f32)
        rows[at : at + 1, :] = wide_plane[0:1]
        rows[count + at : count + at + 1, :] = wide_plane[count_y - 1 : count_y]
    first, last = rows[0:count, :], rows[count : 2 * count, :]
    sent_0[...] = pick("gy", last, first).astype(bf16)
    sent_1[...] = pick("gy", first, last).astype(bf16)


def bundle_kernel(cells, edges, got_0, got_1, sent_0, sent_1, left, right, rows):
    chan, count_x, count_y, _ = cells.shape
    own = chan * count_x
    above = pick("gy", got_1[...].astype(f32), got_0[...].astype(f32))
    below = pick("gy", got_0[...].astype(f32), got_1[...].astype(f32))
    spot = iota((2 * own, lanes), 1)
    before = pltpu.roll(above[own:], count_y, 1)
    after = pltpu.roll(below[own:], lanes - count_y, 1)
    whole = jnp.where(
        spot == 0, before, jnp.where(spot == count_y + 1, after, edges[...].astype(f32))
    )
    right[...] = whole[0:own]
    left[...] = whole[own : 2 * own]
    rows_above, rows_below = above[0:own], below[0:own]
    rows[0:own, :] = rows_above
    rows[own : 2 * own, :] = rows_below
    zero = jnp.zeros((8, lanes), f32)
    body = chan * count_y
    frames = []
    for x in (0, count_x - 1):
        at = slice(x * chan, x * chan + chan)
        frame = [rows_above[at], rows_below[at], zero]
        frame += [whole[own + x * chan : own + (x + 1) * chan], whole[at], zero]
        frames.append(jnp.concatenate(frame, axis=0))
    even = is_even("gx")
    for ref, odd in ((sent_0, 0), (sent_1, 1)):
        high = even != (odd == 1)
        x = jnp.where(high, count_x - 1, 0)
        for c in range(chan):
            ref[c * count_y : (c + 1) * count_y, :] = cells[c, x]
        ref[body : body + 32, :] = jnp.where(high, frames[1], frames[0]).astype(bf16)


def spread_kernel(cot, spread):
    chan_out, pool_x, pool_y, pool_z = cot.shape
    twice = jnp.where(
        iota((pool_z, lanes), 1) // 2 == iota((pool_z, lanes), 0), 0.125, 0.0
    ).astype(bf16)
    for o in range(chan_out):
        part = dot(cot[o].reshape(pool_x * pool_y, pool_z), twice)
        for x in range(pool_x):
            spread[pl.ds(x * chan_out + o, pool_y, stride=pool_x * chan_out), :] = part[
                x * pool_y : (x + 1) * pool_y
            ]


def pool_kernel(sums, pooled):
    chan_out, pool_x, pool_y, pool_z = pooled.shape
    halves = jnp.where(
        iota((2 * lanes, pool_z), 0) % lanes // 2 == iota((2 * lanes, pool_z), 1), 0.125, 0.0
    ).astype(bf16)
    for o in range(0, chan_out, 4):
        rows = 4 * pool_x * pool_y
        part = sums[o * pool_x * pool_y : o * pool_x * pool_y + rows, :]
        mean = dot(jnp.concatenate(split(part), axis=1), halves) + log_scale * float(np.log(2.0))
        pooled[o : o + 4] = mean.astype(bf16).reshape(4, pool_x, pool_y, pool_z)


def main_kernel(
    cells, got_0, got_1, rows_in, left_in, right_in, spread, wbig, wback,
    sums, field, sent_0, sent_1, wpart, wframe, rows_out, cols,
    stage, patches, left, right, outer, carry, gram,
):
    chan, count_x, count_y, _ = cells.shape
    pool_x, pool_y = count_x // 2, count_y // 2
    chan_out = wbig.shape[0] // count_x
    own = chan * count_x
    wide = own + 2 * chan
    depth = 3 * wide + 8
    body = chan * count_y
    lane = iota((wide, lanes), 1)
    even = is_even("gx")

    def got(up, start, size):
        one = got_0[start : start + size, :].astype(f32)
        two = got_1[start : start + size, :].astype(f32)
        return jnp.where(even, one, two) if up else jnp.where(even, two, one)

    for x in range(count_x + 2):
        for c in range(chan):
            if x == 0:
                plane = got(False, c * count_y, count_y)
            elif x == count_x + 1:
                plane = got(True, c * count_y, count_y)
            else:
                plane = cells[c, x - 1]
            stage[pl.ds(wide + x * chan + c, count_y, stride=wide), :] = plane.astype(f32)
    rest_low, rest_high = got(False, body, 32), got(True, body, 32)
    for base, top, at in ((0, 0, 0), ((count_y + 1) * wide, own, chan)):
        stage[base : base + chan, :] = rest_low[at : at + chan]
        stage[base + chan : base + chan + own, :] = rows_in[top : top + own, :]
        stage[base + chan + own : base + wide, :] = rest_high[at : at + chan]
    for ref, mine, at in ((left, left_in, 16), (right, right_in, 16 + chan)):
        ref[0:chan, :] = rest_low[at : at + chan]
        ref[chan : chan + own, :] = mine[...]
        ref[chan + own : wide, :] = rest_high[at : at + chan]
    left_cols, right_cols = left[...], right[...]
    for y in range(count_y + 2):
        mid = stage[y * wide : (y + 1) * wide, :]
        low_col = pltpu.roll(left_cols, (lanes - y) % lanes, 1)
        high_col = pltpu.roll(right_cols, (lanes - 1 - y) % lanes, 1)
        before = jnp.where(lane == 0, low_col, pltpu.roll(mid, 1, 1))
        after = jnp.where(lane == lanes - 1, high_col, pltpu.roll(mid, lanes - 1, 1))
        whole = jnp.concatenate([before, mid, after, jnp.ones((8, lanes), f32)], axis=0)
        patches[y * depth : (y + 1) * depth, :] = whole.astype(bf16)

    carry[...] = jnp.zeros_like(carry)
    gram[...] = jnp.zeros_like(gram)
    pairs = 4

    def finish(y, whole):
        before = pltpu.roll(whole[0:wide], lanes - 1, 1)
        after = pltpu.roll(whole[2 * wide : 3 * wide], 1, 1)
        zero = jnp.zeros_like(before)
        inner = (
            whole[wide : 2 * wide]
            + jnp.where(lane == lanes - 1, zero, before)
            + jnp.where(lane == 0, zero, after)
        )
        rest = jnp.where(lane == lanes - 1, before, jnp.where(lane == 0, after, zero))
        place = pl.ds(pl.multiple_of(y * wide, 8), wide)
        field[place, :] = inner
        outer[place, :] = rest

    def step(i, _):
        deltas, blocks = [], []
        weights = wbig[...]
        for k in range(pairs):
            j = i * pairs + k
            block = jnp.concatenate(
                [
                    patches[pl.ds(pl.multiple_of((2 * j + h) * depth, 16), 3 * depth), :]
                    for h in range(2)
                ],
                axis=1,
            )
            preact = dot(weights, block)
            slope = jnp.tanh(5.0 * preact)
            linear = jnp.maximum(preact, 0.3 * preact)
            factor = 1.0 + jnp.abs(slope)
            here = spread[pl.ds(pl.multiple_of(j * pool_x * chan_out, 8), pool_x * chan_out), :]
            slope = 0.65 + 0.35 * slope
            delta = []
            for x in range(pool_x):
                top, mid = 2 * x * chan_out, (2 * x + 1) * chan_out
                end = mid + chan_out
                times = here[x * chan_out : (x + 1) * chan_out]
                times = jnp.concatenate([times, times], axis=1)
                delta.append((slope[top:mid] * times).astype(bf16))
                delta.append((slope[mid:end] * times).astype(bf16))
                total = linear[top:mid] + linear[mid:end]
                total = total[:, :lanes] + total[:, lanes:]
                prod = factor[top:mid] * factor[mid:end]
                prod = prod[:, :lanes] * prod[:, lanes:]
                total = total - log_scale * jnp.log(prod)
                sums[pl.ds(x * pool_y + j, chan_out, stride=pool_x * pool_y), :] = total
            deltas.append(jnp.concatenate(delta, axis=0))
            blocks.append(block)
        gram[...] += dot(
            jnp.concatenate(deltas, axis=1), jnp.concatenate(blocks, axis=1), ((1,), (1,))
        )
        back = wback[...]
        size = 3 * wide
        carry_a, carry_b = carry[0:size, :], carry[size : 2 * size, :]
        for k in range(pairs):
            j = i * pairs + k
            parts = dot(back, deltas[k])
            part = lambda b, h: parts[b * size : (b + 1) * size, h * lanes : (h + 1) * lanes]
            finish(2 * j, carry_a + part(0, 0))
            finish(2 * j + 1, carry_b + part(1, 0) + part(0, 1))
            carry_a = part(2, 0) + part(1, 1)
            carry_b = part(2, 1)
        carry[0:size, :] = carry_a
        carry[size : 2 * size, :] = carry_b
        return 0

    lax.fori_loop(0, count_y // (2 * pairs), step, 0)
    size = 3 * wide
    finish(count_y, carry[0:size, :])
    finish(count_y + 1, carry[size : 2 * size, :])

    span = gram.shape[1]
    straight, turned = 0.0, 0.0
    for x in range(count_x):
        part = gram[x * chan_out : (x + 1) * chan_out, :]
        part = jnp.concatenate([part, jnp.zeros((chan_out, 2 * lanes - span), f32)], axis=1)
        straight = straight + part
        turned = turned + (pltpu.roll(part, 2 * lanes - chan * x, 1) if x else part)
    spot = iota((chan_out, lanes), 1)
    tight = 0.0
    group = 3 * chan
    for b in range(3):
        for e in range(3):
            shift = (b * depth + e * wide) - (b * 3 + e) * group
            part = pltpu.roll(turned, 2 * lanes - shift, 1)[:, :lanes] if shift else turned[:, :lanes]
            tight = jnp.where(spot // group == b * 3 + e, part, tight)
    part = pltpu.roll(straight, 2 * lanes + 9 * group - 3 * wide, 1)[:, :lanes]
    tight = jnp.where(spot == 9 * group, part, tight)
    coarse = tight.astype(bf16)
    wpart[...] = tight
    sides = jnp.concatenate(split(tight), axis=0)
    wframe[...] = sides

    ends = [field[0:wide, :], field[(count_y + 1) * wide : (count_y + 2) * wide, :]]
    rows_out[...] = jnp.concatenate([end[chan : chan + own] for end in ends], axis=0)
    tall = cols.shape[0]
    outer[(count_y + 2) * wide :, :] = jnp.zeros((outer.shape[0] - (count_y + 2) * wide, lanes), f32)
    planes = [outer[pl.ds(r, tall, stride=wide), :].astype(bf16) for r in range(wide)]
    row = iota((wide * lanes, lanes), 0)
    spot = iota((wide * lanes, lanes), 1)
    want = jnp.where(spot < wide, spot * lanes + lanes - 1, (spot - wide) * lanes)
    chosen = ((row == want) & (spot < 2 * wide)).astype(f32).astype(bf16)
    found = dot(jnp.concatenate(planes, axis=1), chosen)
    cols[...] = found
    found = found.astype(bf16)
    zero = jnp.zeros((8, lanes), f32)
    for ref, odd in ((sent_0, 0), (sent_1, 1)):
        high = even != (odd == 1)
        for c in range(chan):
            low_plane, high_plane = [
                field[pl.ds(wide + x * chan + c, count_y, stride=wide), :]
                for x in (0, count_x + 1)
            ]
            plane = jnp.where(high, high_plane, low_plane)
            ref[c * count_y : (c + 1) * count_y, :] = plane.astype(bf16)
        low_frame, high_frame = [
            jnp.concatenate([end[x * chan : (x + 1) * chan] for end in ends] + [zero], axis=0)
            for x in (0, count_x + 1)
        ]
        ref[body : body + 16, :] = jnp.where(high, high_frame, low_frame).astype(bf16)
        ref[body + 16 : body + 16 + tall, :] = found
        ref[body + 16 + tall :, :] = sides


def x_kernel(alone, wpart, wframe, rows, cols, got_0, got_1, far, wsum, sent_0, sent_1, cols_out):
    tall = cols.shape[0]
    chan_out = wpart.shape[0]
    own = rows.shape[0] // 2
    body = got_0.shape[0] - 16 - tall - 2 * chan_out
    chan = 4
    wide = own + 2 * chan
    if alone:
        total = joined(jnp.concatenate(split(wpart[...]), axis=0))
    else:
        total = joined(wframe[...]) + joined(far[...])
        sides = [ref[body + 16 + tall :, :] for ref in (got_0, got_1)]
        total = total + (joined(sides[0]) + joined(sides[1]))
    wsum[...] = total
    sides = jnp.concatenate(split(total), axis=0)
    spot = iota((tall, lanes), 1)
    found = cols[...]
    one = got_0[body : body + 16 + tall, :].astype(f32)
    two = got_1[body : body + 16 + tall, :].astype(f32)
    from_low, from_high = pick("gx", two, one), pick("gx", one, two)
    for part, turn, start in ((from_low, lanes - own, chan), (from_high, own, own)):
        part = pltpu.roll(part[16:], turn, 1)
        near = (spot >= start) & (spot < start + chan)
        near = near | ((spot >= wide + start) & (spot < wide + start + chan))
        found = found + jnp.where(near, part, 0.0)
    cols_out[...] = found
    count_y = body // chan
    mid = jnp.zeros((own - 2 * chan, lanes), f32)
    both = []
    for at, line in ((0, 0), (1, count_y + 1)):
        more = [from_low[at * chan : (at + 1) * chan], mid, from_high[at * chan : (at + 1) * chan]]
        total = rows[at * own : (at + 1) * own, :] + jnp.concatenate(more, axis=0)
        extra = jnp.broadcast_to(found[line : line + 1], (16, lanes))
        both.append(jnp.concatenate([total, extra], axis=0))
    sent_0[0 : own + 16, :] = pick("gy", both[1], both[0]).astype(bf16)
    sent_1[0 : own + 16, :] = pick("gy", both[0], both[1]).astype(bf16)
    for ref in (sent_0, sent_1):
        ref[own + 16 :, :] = sides


def y_kernel(alone, count_y, wsum, cols, got_0, got_1, far, wout, frame, rows):
    tall = cols.shape[0]
    chan_out = wsum.shape[0]
    top = got_0.shape[0] - 2 * chan_out
    one, two = got_0[0:top, :].astype(f32), got_1[0:top, :].astype(f32)
    above, below = pick("gy", two, one), pick("gy", one, two)
    rows[...] = jnp.concatenate([above[0 : top - 16], below[0 : top - 16]], axis=0)
    if alone:
        total = joined(jnp.concatenate(split(wsum[...]), axis=0))
    else:
        total = joined(jnp.concatenate(split(wsum[...]), axis=0)) + joined(far[...])
        total = total + (joined(got_0[top:, :]) + joined(got_1[top:, :]))
    wout[...] = total
    frame[tall:, :] = jnp.concatenate(split(total), axis=0)
    row = iota((tall, lanes), 0)
    found = cols[...]
    found = found + jnp.where(row == 1, above[top - 16 : top - 15], 0.0)
    found = found + jnp.where(row == count_y, below[top - 16 : top - 15], 0.0)
    frame[0:tall, :] = found.astype(bf16)


def grad_kernel(field, got_0, got_1, grad):
    chan, count_x, count_y, _ = grad.shape
    wide = chan * (count_x + 2)
    for x in range(count_x):
        for c in range(chan):
            plane = field[pl.ds(wide + (x + 1) * chan + c, count_y, stride=wide), :]
            place = slice(c * count_y, (c + 1) * count_y)
            if x == 0:
                plane = plane + pick("gx", got_1[place, :].astype(f32), got_0[place, :].astype(f32))
            if x == count_x - 1:
                plane = plane + pick("gx", got_0[place, :].astype(f32), got_1[place, :].astype(f32))
            grad[c, x] = plane


def final_kernel(grad, wsum, rows, frame, out, wout, bout):
    chan, count_x, count_y, _ = grad.shape
    chan_out = wsum.shape[0]
    own = chan * count_x
    wide = own + 2 * chan
    tall = frame.shape[0] - 2 * chan_out
    total = joined(jnp.concatenate(split(wsum[...]), axis=0)) + joined(frame[tall:, :])
    total = jnp.concatenate([total, jnp.zeros((lanes - chan_out, lanes), f32)], axis=0)
    total = total.T
    for a in range(3):
        for be in range(9):
            at = (be * 3 + a) * chan
            wout[a * 9 + be] = total[at : at + chan, :chan_out]
    bout[...] = total[27 * chan : 27 * chan + 1, :chan_out]
    spot = iota((count_y, lanes), 1)
    row = iota((count_y, lanes), 0)
    cols = frame[0:tall, :].astype(f32)[1 : count_y + 1]
    first, final = rows[0:own, :], rows[own : 2 * own, :]
    for x in range(count_x):
        for c in range(chan):
            at = x * chan + c
            r = chan + at
            more = jnp.where(spot == lanes - 1, cols[:, r : r + 1], 0.0)
            more = jnp.where(spot == 0, cols[:, wide + r : wide + r + 1], more)
            more = more + jnp.where(row == 0, first[at : at + 1], 0.0)
            more = more + jnp.where(row == count_y - 1, final[at : at + 1], 0.0)
            out[c, x] = grad[c, x] + more


def call(kernel, outs, scratch=(), cost=None):
    return pl.pallas_call(
        kernel,
        out_shape=outs,
        scratch_shapes=list(scratch),
        cost_estimate=cost,
        compiler_params=pltpu.CompilerParams(vmem_limit_bytes=limit),
    )


def on_device(cells, weight, bias, cotangent):
    chan, count_x, count_y, count_z = cells.shape
    chan_out = weight.shape[0]
    own = chan * count_x
    wide = own + 2 * chan
    depth = 3 * wide + 8
    shape = jax.ShapeDtypeStruct

    kernel = weight.transpose(0, 3, 4, 2, 1)
    placed = jnp.stack(
        [
            jnp.pad(kernel, ((0, 0), (0, 0), (0, 0), (x, count_x - 1 - x), (0, 0)))
            for x in range(count_x)
        ]
    ).reshape(count_x * chan_out, 3, 3 * wide)
    coarse = lax.reduce_precision(bias, 8, 7)
    middle = lax.reduce_precision(bias - coarse, 8, 7)
    fine = bias - coarse - middle
    pieces = jnp.stack([coarse, middle, fine], axis=1).astype(bf16)
    pieces = jnp.pad(jnp.tile(pieces, (count_x, 1))[:, None], ((0, 0), (0, 2), (0, 5)))
    wbig = jnp.concatenate([placed, pieces], axis=2).reshape(count_x * chan_out, 3 * depth)
    wback = placed.reshape(count_x * chan_out, 9 * wide).T

    own_block = shape((own, lanes), bf16)
    edges, row_0, row_1 = call(
        pack_kernel,
        [shape((2 * own, lanes), bf16), own_block, own_block],
        [pltpu.VMEM((2 * own, lanes), f32)],
    )(cells)
    pool_x, pool_y, pool_z = cotangent.shape[1:]
    pooled_rows = shape((pool_y * pool_x * chan_out, lanes), f32)
    spread = call(spread_kernel, pooled_rows)(cotangent)
    edges = swapped(edges, "gz", 0)
    row_1 = swapped(jnp.concatenate([row_1, edges]), "gy", 1)
    row_0 = swapped(jnp.concatenate([row_0, edges]), "gy", 0)
    body = chan * count_y
    bundle = shape((body + 32, lanes), bf16)
    side = shape((own, lanes), f32)
    face_0, face_1, left, right, rows = call(
        bundle_kernel, [bundle, bundle, side, side, shape((2 * own, lanes), f32)]
    )(cells, edges, row_0, row_1)
    face_1, face_0 = swapped(face_1, "gx", 1), swapped(face_0, "gx", 0)

    tall = 80
    bundle = shape((body + 16 + tall + 2 * chan_out, lanes), bf16)
    sums, field, face_0, face_1, wpart, wframe, rows, cols = call(
        main_kernel,
        [
            pooled_rows,
            shape(((count_y + 2) * wide, lanes), f32),
            bundle,
            bundle,
            shape((chan_out, lanes), f32),
            shape((2 * chan_out, lanes), bf16),
            shape((2 * own, lanes), f32),
            shape((tall, lanes), f32),
        ],
        [
            pltpu.VMEM(((count_y + 2) * wide, lanes), f32),
            pltpu.VMEM(((count_y + 2) * depth, lanes), bf16),
            pltpu.VMEM((wide, lanes), f32),
            pltpu.VMEM((wide, lanes), f32),
            pltpu.VMEM((tall * wide, lanes), f32),
            pltpu.VMEM((6 * wide, lanes), f32),
            pltpu.VMEM((count_x * chan_out, 3 * depth), f32),
        ],
    )(cells, face_0, face_1, rows, left, right, spread, wbig, wback)

    alone_x = lax.axis_size("gx") != 4
    alone_y = lax.axis_size("gy") != 4
    if alone_x:
        wpart, far = lax.psum(wpart, "gx"), wframe
    else:
        far = swapped(wframe, "gx", 2)
    face_1, face_0 = swapped(face_1, "gx", 1), swapped(face_0, "gx", 0)
    pooled = call(pool_kernel, shape(cotangent.shape, bf16))(sums)
    rows_out = shape((own + 16 + 2 * chan_out, lanes), bf16)
    wsum, row_0, row_1, cols = call(
        functools.partial(x_kernel, alone_x),
        [shape((chan_out, lanes), f32), rows_out, rows_out, shape((tall, lanes), f32)],
    )(wpart, wframe, rows, cols, face_0, face_1, far)
    grad = call(grad_kernel, shape(cells.shape, f32))(field, face_0, face_1)
    if alone_y:
        far, wsum = wframe, lax.psum(wsum, "gy")
    else:
        far = swapped(row_0[own + 16 :], "gy", 2)
    row_1, row_0 = swapped(row_1, "gy", 1), swapped(row_0, "gy", 0)
    wsum, frame, rows = call(
        functools.partial(y_kernel, alone_y, count_y),
        [
            shape((chan_out, lanes), f32),
            shape((tall + 2 * chan_out, lanes), bf16),
            shape((2 * own, lanes), f32),
        ],
    )(wsum, cols, row_0, row_1, far)
    frame = swapped(frame, "gz", 0)
    input_grad, wsum, bias_grad = call(
        final_kernel,
        [
            shape(cells.shape, f32),
            shape((27, chan, chan_out), f32),
            shape((1, chan_out), f32),
        ],
    )(grad, wsum, rows, frame)
    weight_grad = wsum.reshape(3, 3, 3, chan, chan_out).transpose(4, 3, 0, 1, 2)
    return (pooled, weight_grad, bias_grad.reshape(chan_out), input_grad)


def solution(mesh):
    in_specs = (P(None, "gx", "gy", "gz"), P(), P(), P(None, "gx", "gy", "gz"))
    out_specs = (P(None, "gx", "gy", "gz"), P(), P(), P(None, "gx", "gy", "gz"))
    return jax.shard_map(
        on_device, mesh=mesh, in_specs=in_specs, out_specs=out_specs, check_vma=False
    )
```

```python
import functools

import jax
import jax.numpy as jnp
import numpy as np
from jax import lax
from jax.experimental import pallas as pl
from jax.experimental.pallas import tpu as pltpu
from jax.sharding import PartitionSpec as P

axes = ("gx", "gy", "gz")
f32, bf16 = jnp.float32, jnp.bfloat16
log_scale = 0.07
lanes = 128
limit = 48 * 1024 * 1024


def dot(a, b, contract=((1,), (0,))):
    return lax.dot_general(a, b, (contract, ((), ())), preferred_element_type=f32)


def iota(shape, dim):
    return lax.broadcasted_iota(jnp.int32, shape, dim)


def swapped(array, axis, pairing):
    count = lax.axis_size(axis)
    pairs = []
    for i in range(count):
        if pairing == 2:
            partner = i + count // 2
        else:
            partner = i + 1 if i % 2 == pairing else i - 1
        pairs.append((i, partner % count))
    return lax.ppermute(array, axis, pairs)


def is_even(axis):
    return lax.rem(lax.axis_index(axis), 2) == 0


def pick(axis, if_even, if_odd):
    return jnp.where(is_even(axis), if_even, if_odd)


def split(value):
    coarse = value.astype(bf16)
    return coarse, (value - coarse.astype(f32)).astype(bf16)


def joined(pair):
    half = pair.shape[0] // 2
    return pair[:half].astype(f32) + pair[half:].astype(f32)


def pack_kernel(cells, edges, sent_0, sent_1, rows):
    chan, count_x, count_y, _ = cells.shape
    count = chan * count_x
    planes = [cells[c, x] for x in range(count_x) for c in range(chan)]
    wide = jnp.concatenate(planes, axis=1)
    row = iota((2 * count, count * lanes), 0)
    lane = iota((2 * count, count * lanes), 1)
    want = jnp.where(row < count, row * lanes, (row - count) * lanes + lanes - 1)
    chosen = (lane == want).astype(f32).astype(bf16)
    found = dot(chosen, wide, ((1,), (1,)))
    found = jnp.concatenate([found, jnp.zeros((2 * count, lanes - count_y), f32)], axis=1)
    edges[...] = pltpu.roll(found, 1, 1).astype(bf16)
    for at, plane in enumerate(planes):
        wide_plane = plane.astype(f32)
        rows[at : at + 1, :] = wide_plane[0:1]
        rows[count + at : count + at + 1, :] = wide_plane[count_y - 1 : count_y]
    first, last = rows[0:count, :], rows[count : 2 * count, :]
    sent_0[...] = pick("gy", last, first).astype(bf16)
    sent_1[...] = pick("gy", first, last).astype(bf16)


def bundle_kernel(cells, edges, got_0, got_1, sent_0, sent_1, left, right, rows):
    chan, count_x, count_y, _ = cells.shape
    own = chan * count_x
    above = pick("gy", got_1[...].astype(f32), got_0[...].astype(f32))
    below = pick("gy", got_0[...].astype(f32), got_1[...].astype(f32))
    spot = iota((2 * own, lanes), 1)
    before = pltpu.roll(above[own:], count_y, 1)
    after = pltpu.roll(below[own:], lanes - count_y, 1)
    whole = jnp.where(
        spot == 0, before, jnp.where(spot == count_y + 1, after, edges[...].astype(f32))
    )
    right[...] = whole[0:own]
    left[...] = whole[own : 2 * own]
    rows_above, rows_below = above[0:own], below[0:own]
    rows[0:own, :] = rows_above
    rows[own : 2 * own, :] = rows_below
    zero = jnp.zeros((8, lanes), f32)
    body = chan * count_y
    frames = []
    for x in (0, count_x - 1):
        at = slice(x * chan, x * chan + chan)
        frame = [rows_above[at], rows_below[at], zero]
        frame += [whole[own + x * chan : own + (x + 1) * chan], whole[at], zero]
        frames.append(jnp.concatenate(frame, axis=0))
    even = is_even("gx")
    for ref, odd in ((sent_0, 0), (sent_1, 1)):
        high = even != (odd == 1)
        x = jnp.where(high, count_x - 1, 0)
        for c in range(chan):
            ref[c * count_y : (c + 1) * count_y, :] = cells[c, x]
        ref[body : body + 32, :] = jnp.where(high, frames[1], frames[0]).astype(bf16)


def spread_kernel(cot, spread):
    chan_out, pool_x, pool_y, pool_z = cot.shape
    twice = jnp.where(
        iota((pool_z, lanes), 1) // 2 == iota((pool_z, lanes), 0), 0.125, 0.0
    ).astype(bf16)
    for o in range(chan_out):
        part = dot(cot[o].reshape(pool_x * pool_y, pool_z), twice)
        for x in range(pool_x):
            spread[pl.ds(x * chan_out + o, pool_y, stride=pool_x * chan_out), :] = part[
                x * pool_y : (x + 1) * pool_y
            ]


def pool_kernel(sums, pooled):
    chan_out, pool_x, pool_y, pool_z = pooled.shape
    halves = jnp.where(
        iota((2 * lanes, pool_z), 0) % lanes // 2 == iota((2 * lanes, pool_z), 1), 0.125, 0.0
    ).astype(bf16)
    for o in range(0, chan_out, 4):
        rows = 4 * pool_x * pool_y
        part = sums[o * pool_x * pool_y : o * pool_x * pool_y + rows, :]
        mean = dot(jnp.concatenate(split(part), axis=1), halves) + log_scale * float(np.log(2.0))
        pooled[o : o + 4] = mean.astype(bf16).reshape(4, pool_x, pool_y, pool_z)


def main_kernel(
    cells, got_0, got_1, rows_in, left_in, right_in, spread, wbig, wback,
    sums, field, sent_0, sent_1, wpart, wframe, rows_out, cols,
    stage, patches, left, right, carry, gram, deltas,
):
    chan, count_x, count_y, _ = cells.shape
    pool_x, pool_y = count_x // 2, count_y // 2
    chan_out = wbig.shape[0] // count_x
    own = chan * count_x
    wide = own + 2 * chan
    depth = 3 * wide + 8
    body = chan * count_y
    lane = iota((wide, lanes), 1)
    even = is_even("gx")

    def got(up, start, size):
        one = got_0[start : start + size, :].astype(f32)
        two = got_1[start : start + size, :].astype(f32)
        return jnp.where(even, one, two) if up else jnp.where(even, two, one)

    for x in range(count_x + 2):
        for c in range(chan):
            if x == 0:
                plane = got(False, c * count_y, count_y)
            elif x == count_x + 1:
                plane = got(True, c * count_y, count_y)
            else:
                plane = cells[c, x - 1]
            stage[pl.ds(wide + x * chan + c, count_y, stride=wide), :] = plane.astype(f32)
    rest_low, rest_high = got(False, body, 32), got(True, body, 32)
    for base, top, at in ((0, 0, 0), ((count_y + 1) * wide, own, chan)):
        stage[base : base + chan, :] = rest_low[at : at + chan]
        stage[base + chan : base + chan + own, :] = rows_in[top : top + own, :]
        stage[base + chan + own : base + wide, :] = rest_high[at : at + chan]
    for ref, mine, at in ((left, left_in, 16), (right, right_in, 16 + chan)):
        ref[0:chan, :] = rest_low[at : at + chan]
        ref[chan : chan + own, :] = mine[...]
        ref[chan + own : wide, :] = rest_high[at : at + chan]
    left_cols, right_cols = left[...], right[...]
    for y in range(count_y + 2):
        mid = stage[y * wide : (y + 1) * wide, :]
        low_col = pltpu.roll(left_cols, (lanes - y) % lanes, 1)
        high_col = pltpu.roll(right_cols, (lanes - 1 - y) % lanes, 1)
        before = jnp.where(lane == 0, low_col, pltpu.roll(mid, 1, 1))
        after = jnp.where(lane == lanes - 1, high_col, pltpu.roll(mid, lanes - 1, 1))
        whole = jnp.concatenate([before, mid, after, jnp.ones((8, lanes), f32)], axis=0)
        patches[y * depth : (y + 1) * depth, :] = whole.astype(bf16)

    carry[...] = jnp.zeros_like(carry)
    gram[...] = jnp.zeros_like(gram)
    cols[...] = jnp.zeros_like(cols)
    pairs = 4
    steps = count_y // (2 * pairs)
    size = 3 * wide
    inside, outside = lane != lanes - 1, lane != 0

    def finish(y, whole):
        first, last = whole[0:wide], whole[2 * wide : 3 * wide]
        inner = (
            whole[wide : 2 * wide]
            + jnp.where(inside, pltpu.roll(first, lanes - 1, 1), 0.0)
            + jnp.where(outside, pltpu.roll(last, 1, 1), 0.0)
        )
        field[pl.ds(pl.multiple_of(y * wide, 8), wide), :] = inner
        here = lane == y
        cols[0:wide, :] = jnp.where(here, pltpu.roll(first, y, 1), cols[0:wide, :])
        cols[wide : 2 * wide, :] = jnp.where(
            here, pltpu.roll(last, y + 1, 1), cols[wide : 2 * wide, :]
        )

    def block_of(j):
        return jnp.concatenate(
            [
                patches[pl.ds(pl.multiple_of((2 * j + h) * depth, 16), 3 * depth), :]
                for h in range(2)
            ],
            axis=1,
        )

    def forward(i, k):
        j = i * pairs + k
        preact = dot(wbig[...], block_of(j))
        slope = jnp.tanh(5.0 * preact)
        linear = jnp.maximum(preact, 0.3 * preact)
        factor = 1.0 + jnp.abs(slope)
        here = spread[pl.ds(pl.multiple_of(j * pool_x * chan_out, 8), pool_x * chan_out), :]
        slope = 0.65 + 0.35 * slope
        delta = []
        for x in range(pool_x):
            top, mid = 2 * x * chan_out, (2 * x + 1) * chan_out
            end = mid + chan_out
            times = here[x * chan_out : (x + 1) * chan_out]
            times = jnp.concatenate([times, times], axis=1)
            delta.append((slope[top:mid] * times).astype(bf16))
            delta.append((slope[mid:end] * times).astype(bf16))
            total = linear[top:mid] + linear[mid:end]
            total = total[:, :lanes] + total[:, lanes:]
            prod = factor[top:mid] * factor[mid:end]
            prod = prod[:, :lanes] * prod[:, lanes:]
            total = total - log_scale * jnp.log(prod)
            sums[pl.ds(x * pool_y + j, chan_out, stride=pool_x * pool_y), :] = total
        slot = lax.rem(i, 2)
        deltas[slot, :, 2 * k * lanes : 2 * (k + 1) * lanes] = jnp.concatenate(delta, axis=0)

    def backward(i, k):
        j = i * pairs + k
        parts = dot(wback[...], deltas[lax.rem(i, 2), :, 2 * k * lanes : 2 * (k + 1) * lanes])
        part = lambda b, h: parts[b * size : (b + 1) * size, h * lanes : (h + 1) * lanes]
        finish(2 * j, carry[0:size, :] + part(0, 0))
        finish(2 * j + 1, carry[size : 2 * size, :] + part(1, 0) + part(0, 1))
        carry[0:size, :] = part(2, 0) + part(1, 1)
        carry[size : 2 * size, :] = part(2, 1)

    def weigh(i):
        blocks = jnp.concatenate([block_of(i * pairs + k) for k in range(pairs)], axis=1)
        gram[...] += dot(deltas[lax.rem(i, 2)], blocks, ((1,), (1,)))

    def step(i, _):
        weigh(i - 1)
        for k in range(pairs):
            forward(i, k)
            backward(i - 1, k)
        return 0

    for k in range(pairs):
        forward(jnp.int32(0), k)
    lax.fori_loop(1, steps, step, 0)
    last_step = jnp.int32(steps - 1)
    weigh(last_step)
    for k in range(pairs):
        backward(last_step, k)
    finish(count_y, carry[0:size, :])
    finish(count_y + 1, carry[size : 2 * size, :])

    span = gram.shape[1]
    straight, turned = 0.0, 0.0
    for x in range(count_x):
        part = gram[x * chan_out : (x + 1) * chan_out, :]
        part = jnp.concatenate([part, jnp.zeros((chan_out, 2 * lanes - span), f32)], axis=1)
        straight = straight + part
        turned = turned + (pltpu.roll(part, 2 * lanes - chan * x, 1) if x else part)
    spot = iota((chan_out, lanes), 1)
    tight = 0.0
    group = 3 * chan
    for b in range(3):
        for e in range(3):
            shift = (b * depth + e * wide) - (b * 3 + e) * group
            part = pltpu.roll(turned, 2 * lanes - shift, 1)[:, :lanes] if shift else turned[:, :lanes]
            tight = jnp.where(spot // group == b * 3 + e, part, tight)
    part = pltpu.roll(straight, 2 * lanes + 9 * group - 3 * wide, 1)[:, :lanes]
    tight = jnp.where(spot == 9 * group, part, tight)
    coarse = tight.astype(bf16)
    wpart[...] = tight
    sides = jnp.concatenate(split(tight), axis=0)
    wframe[...] = sides

    ends = [field[0:wide, :], field[(count_y + 1) * wide : (count_y + 2) * wide, :]]
    rows_out[...] = jnp.concatenate([end[chan : chan + own] for end in ends], axis=0)
    tall = cols.shape[0]
    found = cols[...].astype(bf16)
    zero = jnp.zeros((8, lanes), f32)
    for ref, odd in ((sent_0, 0), (sent_1, 1)):
        high = even != (odd == 1)
        for c in range(chan):
            low_plane, high_plane = [
                field[pl.ds(wide + x * chan + c, count_y, stride=wide), :]
                for x in (0, count_x + 1)
            ]
            plane = jnp.where(high, high_plane, low_plane)
            ref[c * count_y : (c + 1) * count_y, :] = plane.astype(bf16)
        low_frame, high_frame = [
            jnp.concatenate([end[x * chan : (x + 1) * chan] for end in ends] + [zero], axis=0)
            for x in (0, count_x + 1)
        ]
        ref[body : body + 16, :] = jnp.where(high, high_frame, low_frame).astype(bf16)
        ref[body + 16 : body + 16 + tall, :] = found
        ref[body + 16 + tall :, :] = sides


def x_kernel(alone, wpart, wframe, rows, cols, got_0, got_1, far, wsum, sent_0, sent_1, cols_out):
    tall = cols.shape[0]
    chan_out = wpart.shape[0]
    own = rows.shape[0] // 2
    body = got_0.shape[0] - 16 - tall - 2 * chan_out
    chan = 4
    wide = own + 2 * chan
    if alone:
        total = joined(jnp.concatenate(split(wpart[...]), axis=0))
    else:
        total = joined(wframe[...]) + joined(far[...])
        sides = [ref[body + 16 + tall :, :] for ref in (got_0, got_1)]
        total = total + (joined(sides[0]) + joined(sides[1]))
    wsum[...] = total
    sides = jnp.concatenate(split(total), axis=0)
    one = got_0[body : body + 16 + tall, :].astype(f32)
    two = got_1[body : body + 16 + tall, :].astype(f32)
    from_low, from_high = pick("gx", two, one), pick("gx", one, two)
    mid = jnp.zeros((own - 2 * chan, lanes), f32)
    found = []
    for top in (0, wide):
        more = [from_low[16 + top + chan + own : 16 + top + wide], mid]
        more.append(from_high[16 + top : 16 + top + chan])
        found.append(cols[top + chan : top + chan + own, :] + jnp.concatenate(more, axis=0))
    found = jnp.concatenate(found, axis=0)
    cols_out[...] = found
    both = []
    for at in (0, 1):
        more = [from_low[at * chan : (at + 1) * chan], mid, from_high[at * chan : (at + 1) * chan]]
        total = rows[at * own : (at + 1) * own, :] + jnp.concatenate(more, axis=0)
        both.append(total)
    sent_0[0:own, :] = pick("gy", both[1], both[0]).astype(bf16)
    sent_1[0:own, :] = pick("gy", both[0], both[1]).astype(bf16)
    for ref in (sent_0, sent_1):
        ref[own : 3 * own, :] = found.astype(bf16)
        ref[3 * own :, :] = sides


def y_kernel(alone, count_y, wsum, cols, got_0, got_1, far, wout, frame, rows):
    tall = cols.shape[0]
    chan_out = wsum.shape[0]
    top = got_0.shape[0] - 2 * chan_out
    one, two = got_0[0:top, :].astype(f32), got_1[0:top, :].astype(f32)
    above, below = pick("gy", two, one), pick("gy", one, two)
    rows[...] = jnp.concatenate([above[: top - tall], below[: top - tall]], axis=0)
    if alone:
        total = joined(jnp.concatenate(split(wsum[...]), axis=0))
    else:
        total = joined(jnp.concatenate(split(wsum[...]), axis=0)) + joined(far[...])
        total = total + (joined(got_0[top:, :]) + joined(got_1[top:, :]))
    wout[...] = total
    frame[tall:, :] = jnp.concatenate(split(total), axis=0)
    spot = iota((tall, lanes), 1)
    above = pltpu.roll(above[top - tall :], lanes - count_y, 1)
    below = pltpu.roll(below[top - tall :], count_y, 1)
    found = cols[...]
    found = found + jnp.where(spot == 1, above, jnp.where(spot == count_y, below, 0.0))
    frame[0:tall, :] = found.astype(bf16)


def grad_kernel(field, got_0, got_1, grad):
    chan, count_x, count_y, _ = grad.shape
    wide = chan * (count_x + 2)
    for x in range(count_x):
        for c in range(chan):
            plane = field[pl.ds(wide + (x + 1) * chan + c, count_y, stride=wide), :]
            place = slice(c * count_y, (c + 1) * count_y)
            if x == 0:
                plane = plane + pick("gx", got_1[place, :].astype(f32), got_0[place, :].astype(f32))
            if x == count_x - 1:
                plane = plane + pick("gx", got_0[place, :].astype(f32), got_1[place, :].astype(f32))
            grad[c, x] = plane


def final_kernel(grad, wsum, rows, frame, out, wout, bout):
    chan, count_x, count_y, _ = grad.shape
    chan_out = wsum.shape[0]
    own = chan * count_x
    wide = own + 2 * chan
    tall = frame.shape[0] - 2 * chan_out
    total = joined(jnp.concatenate(split(wsum[...]), axis=0)) + joined(frame[tall:, :])
    columns = pltpu.roll(frame[0:tall, :].astype(f32), lanes - 1, 1)
    rest = jnp.zeros((lanes - chan_out - tall, lanes), f32)
    total = jnp.concatenate([total, columns, rest], axis=0)
    total = total.T
    for a in range(3):
        for be in range(9):
            at = (be * 3 + a) * chan
            wout[a * 9 + be] = total[at : at + chan, :chan_out]
    bout[...] = total[27 * chan : 27 * chan + 1, :chan_out]
    spot = iota((count_y, lanes), 1)
    row = iota((count_y, lanes), 0)
    columns = total[0:count_y]
    first, final = rows[0:own, :], rows[own : 2 * own, :]
    for x in range(count_x):
        for c in range(chan):
            at = x * chan + c
            r = chan_out + at
            more = jnp.where(spot == lanes - 1, columns[:, r : r + 1], 0.0)
            more = jnp.where(spot == 0, columns[:, own + r : own + r + 1], more)
            more = more + jnp.where(row == 0, first[at : at + 1], 0.0)
            more = more + jnp.where(row == count_y - 1, final[at : at + 1], 0.0)
            out[c, x] = grad[c, x] + more


def call(kernel, outs, scratch=(), cost=None):
    return pl.pallas_call(
        kernel,
        out_shape=outs,
        scratch_shapes=list(scratch),
        cost_estimate=cost,
        compiler_params=pltpu.CompilerParams(vmem_limit_bytes=limit),
    )


def on_device(cells, weight, bias, cotangent):
    chan, count_x, count_y, count_z = cells.shape
    chan_out = weight.shape[0]
    own = chan * count_x
    wide = own + 2 * chan
    depth = 3 * wide + 8
    shape = jax.ShapeDtypeStruct

    kernel = weight.transpose(0, 3, 4, 2, 1)
    placed = jnp.stack(
        [
            jnp.pad(kernel, ((0, 0), (0, 0), (0, 0), (x, count_x - 1 - x), (0, 0)))
            for x in range(count_x)
        ]
    ).reshape(count_x * chan_out, 3, 3 * wide)
    coarse = lax.reduce_precision(bias, 8, 7)
    middle = lax.reduce_precision(bias - coarse, 8, 7)
    fine = bias - coarse - middle
    pieces = jnp.stack([coarse, middle, fine], axis=1).astype(bf16)
    pieces = jnp.pad(jnp.tile(pieces, (count_x, 1))[:, None], ((0, 0), (0, 2), (0, 5)))
    wbig = jnp.concatenate([placed, pieces], axis=2).reshape(count_x * chan_out, 3 * depth)
    wback = placed.reshape(count_x * chan_out, 9 * wide).T

    own_block = shape((own, lanes), bf16)
    edges, row_0, row_1 = call(
        pack_kernel,
        [shape((2 * own, lanes), bf16), own_block, own_block],
        [pltpu.VMEM((2 * own, lanes), f32)],
    )(cells)
    pool_x, pool_y, pool_z = cotangent.shape[1:]
    pooled_rows = shape((pool_y * pool_x * chan_out, lanes), f32)
    spread = call(spread_kernel, pooled_rows)(cotangent)
    edges = swapped(edges, "gz", 0)
    row_1 = swapped(jnp.concatenate([row_1, edges]), "gy", 1)
    row_0 = swapped(jnp.concatenate([row_0, edges]), "gy", 0)
    body = chan * count_y
    bundle = shape((body + 32, lanes), bf16)
    side = shape((own, lanes), f32)
    face_0, face_1, left, right, rows = call(
        bundle_kernel, [bundle, bundle, side, side, shape((2 * own, lanes), f32)]
    )(cells, edges, row_0, row_1)
    face_1, face_0 = swapped(face_1, "gx", 1), swapped(face_0, "gx", 0)

    tall = 2 * wide
    bundle = shape((body + 16 + tall + 2 * chan_out, lanes), bf16)
    sums, field, face_0, face_1, wpart, wframe, rows, cols = call(
        main_kernel,
        [
            pooled_rows,
            shape(((count_y + 2) * wide, lanes), f32),
            bundle,
            bundle,
            shape((chan_out, lanes), f32),
            shape((2 * chan_out, lanes), bf16),
            shape((2 * own, lanes), f32),
            shape((tall, lanes), f32),
        ],
        [
            pltpu.VMEM(((count_y + 2) * wide, lanes), f32),
            pltpu.VMEM(((count_y + 2) * depth, lanes), bf16),
            pltpu.VMEM((wide, lanes), f32),
            pltpu.VMEM((wide, lanes), f32),
            pltpu.VMEM((6 * wide, lanes), f32),
            pltpu.VMEM((count_x * chan_out, 3 * depth), f32),
            pltpu.VMEM((2, count_x * chan_out, 8 * lanes), bf16),
        ],
    )(cells, face_0, face_1, rows, left, right, spread, wbig, wback)

    alone_x = lax.axis_size("gx") != 4
    alone_y = lax.axis_size("gy") != 4
    if alone_x:
        wpart, far = lax.psum(wpart, "gx"), wframe
    else:
        far = swapped(wframe, "gx", 2)
    face_1, face_0 = swapped(face_1, "gx", 1), swapped(face_0, "gx", 0)
    pooled = call(pool_kernel, shape(cotangent.shape, bf16))(sums)
    rows_out = shape((3 * own + 2 * chan_out, lanes), bf16)
    wsum, row_0, row_1, cols = call(
        functools.partial(x_kernel, alone_x),
        [shape((chan_out, lanes), f32), rows_out, rows_out, shape((2 * own, lanes), f32)],
    )(wpart, wframe, rows, cols, face_0, face_1, far)
    grad = call(grad_kernel, shape(cells.shape, f32))(field, face_0, face_1)
    if alone_y:
        far, wsum = wframe, lax.psum(wsum, "gy")
    else:
        far = swapped(row_0[3 * own :], "gy", 2)
    row_1, row_0 = swapped(row_1, "gy", 1), swapped(row_0, "gy", 0)
    wsum, frame, rows = call(
        functools.partial(y_kernel, alone_y, count_y),
        [
            shape((chan_out, lanes), f32),
            shape((2 * own + 2 * chan_out, lanes), bf16),
            shape((2 * own, lanes), f32),
        ],
    )(wsum, cols, row_0, row_1, far)
    frame = swapped(frame, "gz", 0)
    input_grad, wsum, bias_grad = call(
        final_kernel,
        [
            shape(cells.shape, f32),
            shape((27, chan, chan_out), f32),
            shape((1, chan_out), f32),
        ],
    )(grad, wsum, rows, frame)
    weight_grad = wsum.reshape(3, 3, 3, chan, chan_out).transpose(4, 3, 0, 1, 2)
    return (pooled, weight_grad, bias_grad.reshape(chan_out), input_grad)


def solution(mesh):
    in_specs = (P(None, "gx", "gy", "gz"), P(), P(), P(None, "gx", "gy", "gz"))
    out_specs = (P(None, "gx", "gy", "gz"), P(), P(), P(None, "gx", "gy", "gz"))
    return jax.shard_map(
        on_device, mesh=mesh, in_specs=in_specs, out_specs=out_specs, check_vma=False
    )
```

```python
import functools

import jax
import jax.numpy as jnp
import numpy as np
from jax import lax
from jax.experimental import pallas as pl
from jax.experimental.pallas import tpu as pltpu
from jax.sharding import PartitionSpec as P

axes = ("gx", "gy", "gz")
f32, bf16 = jnp.float32, jnp.bfloat16
log_scale = 0.07
lanes = 128
limit = 48 * 1024 * 1024


def dot(a, b, contract=((1,), (0,))):
    return lax.dot_general(a, b, (contract, ((), ())), preferred_element_type=f32)


def iota(shape, dim):
    return lax.broadcasted_iota(jnp.int32, shape, dim)


def aligned(start, tile):
    return start if isinstance(start, int) else pl.multiple_of(start, tile)


def swapped(array, axis, pairing):
    count = lax.axis_size(axis)
    pairs = []
    for i in range(count):
        if pairing == 2:
            partner = i + count // 2
        else:
            partner = i + 1 if i % 2 == pairing else i - 1
        pairs.append((i, partner % count))
    return lax.ppermute(array, axis, pairs)


def is_even(axis):
    return lax.rem(lax.axis_index(axis), 2) == 0


def pick(axis, if_even, if_odd):
    return jnp.where(is_even(axis), if_even, if_odd)


def split(value):
    coarse = value.astype(bf16)
    return coarse, (value - coarse.astype(f32)).astype(bf16)


def joined(pair):
    half = pair.shape[0] // 2
    return pair[:half].astype(f32) + pair[half:].astype(f32)


def pack_kernel(cells, edges, sent_0, sent_1, rows):
    chan, count_x, count_y, _ = cells.shape
    count = chan * count_x
    planes = [cells[c, x] for x in range(count_x) for c in range(chan)]
    wide = jnp.concatenate(planes, axis=1)
    row = iota((2 * count, count * lanes), 0)
    lane = iota((2 * count, count * lanes), 1)
    want = jnp.where(row < count, row * lanes, (row - count) * lanes + lanes - 1)
    chosen = (lane == want).astype(f32).astype(bf16)
    found = dot(chosen, wide, ((1,), (1,)))
    found = jnp.concatenate([found, jnp.zeros((2 * count, lanes - count_y), f32)], axis=1)
    edges[...] = pltpu.roll(found, 1, 1).astype(bf16)
    for at, plane in enumerate(planes):
        wide_plane = plane.astype(f32)
        rows[at : at + 1, :] = wide_plane[0:1]
        rows[count + at : count + at + 1, :] = wide_plane[count_y - 1 : count_y]
    first, last = rows[0:count, :], rows[count : 2 * count, :]
    sent_0[...] = pick("gy", last, first).astype(bf16)
    sent_1[...] = pick("gy", first, last).astype(bf16)


def bundle_kernel(cells, edges, got_0, got_1, sent_0, sent_1, left, right, rows):
    chan, count_x, count_y, _ = cells.shape
    own = chan * count_x
    above = pick("gy", got_1[...].astype(f32), got_0[...].astype(f32))
    below = pick("gy", got_0[...].astype(f32), got_1[...].astype(f32))
    spot = iota((2 * own, lanes), 1)
    before = pltpu.roll(above[own:], count_y, 1)
    after = pltpu.roll(below[own:], lanes - count_y, 1)
    whole = jnp.where(
        spot == 0, before, jnp.where(spot == count_y + 1, after, edges[...].astype(f32))
    )
    right[...] = whole[0:own]
    left[...] = whole[own : 2 * own]
    rows_above, rows_below = above[0:own], below[0:own]
    rows[0:own, :] = rows_above
    rows[own : 2 * own, :] = rows_below
    zero = jnp.zeros((8, lanes), f32)
    body = chan * count_y
    frames = []
    for x in (0, count_x - 1):
        at = slice(x * chan, x * chan + chan)
        frame = [rows_above[at], rows_below[at], zero]
        frame += [whole[own + x * chan : own + (x + 1) * chan], whole[at], zero]
        frames.append(jnp.concatenate(frame, axis=0))
    even = is_even("gx")
    for ref, odd in ((sent_0, 0), (sent_1, 1)):
        high = even != (odd == 1)
        x = jnp.where(high, count_x - 1, 0)
        for c in range(chan):
            ref[c * count_y : (c + 1) * count_y, :] = cells[c, x]
        ref[body : body + 32, :] = jnp.where(high, frames[1], frames[0]).astype(bf16)


def spread_kernel(cot, spread):
    chan_out, pool_x, pool_y, pool_z = cot.shape
    twice = jnp.where(
        iota((pool_z, lanes), 1) // 2 == iota((pool_z, lanes), 0), 0.125, 0.0
    ).astype(bf16)
    for o in range(chan_out):
        part = dot(cot[o].reshape(pool_x * pool_y, pool_z), twice)
        for x in range(pool_x):
            spread[pl.ds(x * chan_out + o, pool_y, stride=pool_x * chan_out), :] = part[
                x * pool_y : (x + 1) * pool_y
            ]


def pool_kernel(sums, pooled):
    chan_out, pool_x, pool_y, pool_z = pooled.shape
    halves = jnp.where(
        iota((2 * lanes, pool_z), 0) % lanes // 2 == iota((2 * lanes, pool_z), 1), 0.125, 0.0
    ).astype(bf16)
    for o in range(0, chan_out, 4):
        rows = 4 * pool_x * pool_y
        part = sums[o * pool_x * pool_y : o * pool_x * pool_y + rows, :]
        mean = dot(jnp.concatenate(split(part), axis=1), halves) + log_scale * float(np.log(2.0))
        pooled[o : o + 4] = mean.astype(bf16).reshape(4, pool_x, pool_y, pool_z)


def main_kernel(
    cells, got_0, got_1, rows_in, left_in, right_in, spread, wbig, wback,
    sums, field, sent_0, sent_1, wpart, wframe, rows_out, cols,
    stage, patches, left, right, carry, gram, delta_a, delta_b,
):
    chan, count_x, count_y, _ = cells.shape
    pool_x, pool_y = count_x // 2, count_y // 2
    chan_out = wbig.shape[0] // count_x
    own = chan * count_x
    wide = own + 2 * chan
    depth = 3 * wide + 8
    body = chan * count_y
    lane = iota((wide, lanes), 1)
    even = is_even("gx")

    def got(up, start, size):
        one = got_0[start : start + size, :].astype(f32)
        two = got_1[start : start + size, :].astype(f32)
        return jnp.where(even, one, two) if up else jnp.where(even, two, one)

    for x in range(count_x + 2):
        for c in range(chan):
            if x == 0:
                plane = got(False, c * count_y, count_y)
            elif x == count_x + 1:
                plane = got(True, c * count_y, count_y)
            else:
                plane = cells[c, x - 1]
            stage[pl.ds(wide + x * chan + c, count_y, stride=wide), :] = plane.astype(f32)
    rest_low, rest_high = got(False, body, 32), got(True, body, 32)
    for base, top, at in ((0, 0, 0), ((count_y + 1) * wide, own, chan)):
        stage[base : base + chan, :] = rest_low[at : at + chan]
        stage[base + chan : base + chan + own, :] = rows_in[top : top + own, :]
        stage[base + chan + own : base + wide, :] = rest_high[at : at + chan]
    for ref, mine, at in ((left, left_in, 16), (right, right_in, 16 + chan)):
        ref[0:chan, :] = rest_low[at : at + chan]
        ref[chan : chan + own, :] = mine[...]
        ref[chan + own : wide, :] = rest_high[at : at + chan]
    left_cols, right_cols = left[...], right[...]
    for y in range(count_y + 2):
        mid = stage[y * wide : (y + 1) * wide, :]
        low_col = pltpu.roll(left_cols, (lanes - y) % lanes, 1)
        high_col = pltpu.roll(right_cols, (lanes - 1 - y) % lanes, 1)
        before = jnp.where(lane == 0, low_col, pltpu.roll(mid, 1, 1))
        after = jnp.where(lane == lanes - 1, high_col, pltpu.roll(mid, lanes - 1, 1))
        whole = jnp.concatenate([before, mid, after, jnp.ones((8, lanes), f32)], axis=0)
        patches[y * depth : (y + 1) * depth, :] = whole.astype(bf16)

    carry[...] = jnp.zeros_like(carry)
    gram[...] = jnp.zeros_like(gram)
    cols[...] = jnp.zeros_like(cols)
    pairs = 4
    steps = count_y // (2 * pairs)
    size = 3 * wide
    inside, outside = lane != lanes - 1, lane != 0

    def finish(y, whole, edge):
        first, last = whole[0:wide], whole[2 * wide : 3 * wide]
        inner = (
            whole[wide : 2 * wide]
            + jnp.where(inside, pltpu.roll(first, lanes - 1, 1), 0.0)
            + jnp.where(outside, pltpu.roll(last, 1, 1), 0.0)
        )
        field[pl.ds(aligned(y * wide, 8), wide), :] = inner
        here = lane == y
        edge[0] = jnp.where(here, pltpu.roll(first, y, 1), edge[0])
        edge[1] = jnp.where(here, pltpu.roll(last, y + 1, 1), edge[1])

    def block_of(j):
        return jnp.concatenate(
            [
                patches[pl.ds(aligned((2 * j + h) * depth, 16), 3 * depth), :]
                for h in range(2)
            ],
            axis=1,
        )

    def forward(i, k, ref):
        j = i * pairs + k
        preact = dot(wbig[...], block_of(j))
        slope = jnp.tanh(5.0 * preact)
        linear = jnp.maximum(preact, 0.3 * preact)
        factor = 1.0 + jnp.abs(slope)
        here = spread[pl.ds(aligned(j * pool_x * chan_out, 8), pool_x * chan_out), :]
        slope = 0.65 + 0.35 * slope
        delta = []
        for x in range(pool_x):
            top, mid = 2 * x * chan_out, (2 * x + 1) * chan_out
            end = mid + chan_out
            times = here[x * chan_out : (x + 1) * chan_out]
            times = jnp.concatenate([times, times], axis=1)
            delta.append((slope[top:mid] * times).astype(bf16))
            delta.append((slope[mid:end] * times).astype(bf16))
            total = linear[top:mid] + linear[mid:end]
            total = total[:, :lanes] + total[:, lanes:]
            prod = factor[top:mid] * factor[mid:end]
            prod = prod[:, :lanes] * prod[:, lanes:]
            total = total - log_scale * jnp.log(prod)
            sums[pl.ds(x * pool_y + j, chan_out, stride=pool_x * pool_y), :] = total
        ref[:, 2 * k * lanes : 2 * (k + 1) * lanes] = jnp.concatenate(delta, axis=0)

    def backward(i, k, ref, held, edge):
        j = i * pairs + k
        parts = dot(wback[...], ref[:, 2 * k * lanes : 2 * (k + 1) * lanes])
        part = lambda b, h: parts[b * size : (b + 1) * size, h * lanes : (h + 1) * lanes]
        finish(2 * j, held[0] + part(0, 0), edge)
        finish(2 * j + 1, held[1] + part(1, 0) + part(0, 1), edge)
        held[0] = part(2, 0) + part(1, 1)
        held[1] = part(2, 1)

    def weigh(i, ref):
        blocks = jnp.concatenate([block_of(i * pairs + k) for k in range(pairs)], axis=1)
        return dot(ref[...], blocks, ((1,), (1,)))

    def opened():
        return (
            [carry[0:size, :], carry[size : 2 * size, :]],
            [cols[0:wide, :], cols[wide : 2 * wide, :]],
        )

    def closed(held, edge):
        carry[0:size, :] = held[0]
        carry[size : 2 * size, :] = held[1]
        cols[0:wide, :] = edge[0]
        cols[wide : 2 * wide, :] = edge[1]

    def step(t, _):
        held, edge = opened()
        total = gram[...] + weigh(2 * t, delta_a)
        for k in range(pairs):
            forward(2 * t + 1, k, delta_b)
            backward(2 * t, k, delta_a, held, edge)
        total = total + weigh(2 * t + 1, delta_b)
        for k in range(pairs):
            forward(2 * t + 2, k, delta_a)
            backward(2 * t + 1, k, delta_b, held, edge)
        gram[...] = total
        closed(held, edge)
        return 0

    for k in range(pairs):
        forward(0, k, delta_a)
    lax.fori_loop(0, steps // 2 - 1, step, 0)
    held, edge = opened()
    total = gram[...] + weigh(steps - 2, delta_a)
    for k in range(pairs):
        forward(steps - 1, k, delta_b)
        backward(steps - 2, k, delta_a, held, edge)
    gram[...] = total + weigh(steps - 1, delta_b)
    for k in range(pairs):
        backward(steps - 1, k, delta_b, held, edge)
    finish(count_y, held[0], edge)
    finish(count_y + 1, held[1], edge)
    closed(held, edge)

    span = gram.shape[1]
    straight, turned = 0.0, 0.0
    for x in range(count_x):
        part = gram[x * chan_out : (x + 1) * chan_out, :]
        part = jnp.concatenate([part, jnp.zeros((chan_out, 2 * lanes - span), f32)], axis=1)
        straight = straight + part
        turned = turned + (pltpu.roll(part, 2 * lanes - chan * x, 1) if x else part)
    spot = iota((chan_out, lanes), 1)
    tight = 0.0
    group = 3 * chan
    for b in range(3):
        for e in range(3):
            shift = (b * depth + e * wide) - (b * 3 + e) * group
            part = pltpu.roll(turned, 2 * lanes - shift, 1)[:, :lanes] if shift else turned[:, :lanes]
            tight = jnp.where(spot // group == b * 3 + e, part, tight)
    part = pltpu.roll(straight, 2 * lanes + 9 * group - 3 * wide, 1)[:, :lanes]
    tight = jnp.where(spot == 9 * group, part, tight)
    coarse = tight.astype(bf16)
    wpart[...] = tight
    sides = jnp.concatenate(split(tight), axis=0)
    wframe[...] = sides

    ends = [field[0:wide, :], field[(count_y + 1) * wide : (count_y + 2) * wide, :]]
    rows_out[...] = jnp.concatenate([end[chan : chan + own] for end in ends], axis=0)
    tall = cols.shape[0]
    found = cols[...].astype(bf16)
    zero = jnp.zeros((8, lanes), f32)
    for ref, odd in ((sent_0, 0), (sent_1, 1)):
        high = even != (odd == 1)
        for c in range(chan):
            low_plane, high_plane = [
                field[pl.ds(wide + x * chan + c, count_y, stride=wide), :]
                for x in (0, count_x + 1)
            ]
            plane = jnp.where(high, high_plane, low_plane)
            ref[c * count_y : (c + 1) * count_y, :] = plane.astype(bf16)
        low_frame, high_frame = [
            jnp.concatenate([end[x * chan : (x + 1) * chan] for end in ends] + [zero], axis=0)
            for x in (0, count_x + 1)
        ]
        ref[body : body + 16, :] = jnp.where(high, high_frame, low_frame).astype(bf16)
        ref[body + 16 : body + 16 + tall, :] = found
        ref[body + 16 + tall :, :] = sides


def x_kernel(alone, wpart, wframe, rows, cols, got_0, got_1, far, wsum, sent_0, sent_1, cols_out):
    tall = cols.shape[0]
    chan_out = wpart.shape[0]
    own = rows.shape[0] // 2
    body = got_0.shape[0] - 16 - tall - 2 * chan_out
    chan = 4
    wide = own + 2 * chan
    if alone:
        total = joined(jnp.concatenate(split(wpart[...]), axis=0))
    else:
        total = joined(wframe[...]) + joined(far[...])
        sides = [ref[body + 16 + tall :, :] for ref in (got_0, got_1)]
        total = total + (joined(sides[0]) + joined(sides[1]))
    wsum[...] = total
    sides = jnp.concatenate(split(total), axis=0)
    one = got_0[body : body + 16 + tall, :].astype(f32)
    two = got_1[body : body + 16 + tall, :].astype(f32)
    from_low, from_high = pick("gx", two, one), pick("gx", one, two)
    mid = jnp.zeros((own - 2 * chan, lanes), f32)
    found = []
    for top in (0, wide):
        more = [from_low[16 + top + chan + own : 16 + top + wide], mid]
        more.append(from_high[16 + top : 16 + top + chan])
        found.append(cols[top + chan : top + chan + own, :] + jnp.concatenate(more, axis=0))
    found = jnp.concatenate(found, axis=0)
    cols_out[...] = found
    both = []
    for at in (0, 1):
        more = [from_low[at * chan : (at + 1) * chan], mid, from_high[at * chan : (at + 1) * chan]]
        total = rows[at * own : (at + 1) * own, :] + jnp.concatenate(more, axis=0)
        both.append(total)
    sent_0[0:own, :] = pick("gy", both[1], both[0]).astype(bf16)
    sent_1[0:own, :] = pick("gy", both[0], both[1]).astype(bf16)
    for ref in (sent_0, sent_1):
        ref[own : 3 * own, :] = found.astype(bf16)
        ref[3 * own :, :] = sides


def y_kernel(alone, count_y, wsum, cols, got_0, got_1, far, wout, frame, rows):
    tall = cols.shape[0]
    chan_out = wsum.shape[0]
    top = got_0.shape[0] - 2 * chan_out
    one, two = got_0[0:top, :].astype(f32), got_1[0:top, :].astype(f32)
    above, below = pick("gy", two, one), pick("gy", one, two)
    rows[...] = jnp.concatenate([above[: top - tall], below[: top - tall]], axis=0)
    if alone:
        total = joined(jnp.concatenate(split(wsum[...]), axis=0))
    else:
        total = joined(jnp.concatenate(split(wsum[...]), axis=0)) + joined(far[...])
        total = total + (joined(got_0[top:, :]) + joined(got_1[top:, :]))
    wout[...] = total
    frame[tall:, :] = jnp.concatenate(split(total), axis=0)
    spot = iota((tall, lanes), 1)
    above = pltpu.roll(above[top - tall :], lanes - count_y, 1)
    below = pltpu.roll(below[top - tall :], count_y, 1)
    found = cols[...]
    found = found + jnp.where(spot == 1, above, jnp.where(spot == count_y, below, 0.0))
    frame[0:tall, :] = found.astype(bf16)


def grad_kernel(field, got_0, got_1, grad):
    chan, count_x, count_y, _ = grad.shape
    wide = chan * (count_x + 2)
    for x in range(count_x):
        for c in range(chan):
            plane = field[pl.ds(wide + (x + 1) * chan + c, count_y, stride=wide), :]
            place = slice(c * count_y, (c + 1) * count_y)
            if x == 0:
                plane = plane + pick("gx", got_1[place, :].astype(f32), got_0[place, :].astype(f32))
            if x == count_x - 1:
                plane = plane + pick("gx", got_0[place, :].astype(f32), got_1[place, :].astype(f32))
            grad[c, x] = plane


def final_kernel(grad, wsum, rows, frame, out, wout, bout):
    chan, count_x, count_y, _ = grad.shape
    chan_out = wsum.shape[0]
    own = chan * count_x
    wide = own + 2 * chan
    tall = frame.shape[0] - 2 * chan_out
    total = joined(jnp.concatenate(split(wsum[...]), axis=0)) + joined(frame[tall:, :])
    columns = pltpu.roll(frame[0:tall, :].astype(f32), lanes - 1, 1)
    rest = jnp.zeros((lanes - chan_out - tall, lanes), f32)
    total = jnp.concatenate([total, columns, rest], axis=0)
    total = total.T
    for a in range(3):
        for be in range(9):
            at = (be * 3 + a) * chan
            wout[a * 9 + be] = total[at : at + chan, :chan_out]
    bout[...] = total[27 * chan : 27 * chan + 1, :chan_out]
    spot = iota((count_y, lanes), 1)
    row = iota((count_y, lanes), 0)
    columns = total[0:count_y]
    first, final = rows[0:own, :], rows[own : 2 * own, :]
    for x in range(count_x):
        for c in range(chan):
            at = x * chan + c
            r = chan_out + at
            more = jnp.where(spot == lanes - 1, columns[:, r : r + 1], 0.0)
            more = jnp.where(spot == 0, columns[:, own + r : own + r + 1], more)
            more = more + jnp.where(row == 0, first[at : at + 1], 0.0)
            more = more + jnp.where(row == count_y - 1, final[at : at + 1], 0.0)
            out[c, x] = grad[c, x] + more


def call(kernel, outs, scratch=(), cost=None):
    return pl.pallas_call(
        kernel,
        out_shape=outs,
        scratch_shapes=list(scratch),
        cost_estimate=cost,
        compiler_params=pltpu.CompilerParams(vmem_limit_bytes=limit),
    )


def on_device(cells, weight, bias, cotangent):
    chan, count_x, count_y, count_z = cells.shape
    chan_out = weight.shape[0]
    own = chan * count_x
    wide = own + 2 * chan
    depth = 3 * wide + 8
    shape = jax.ShapeDtypeStruct

    kernel = weight.transpose(0, 3, 4, 2, 1)
    placed = jnp.stack(
        [
            jnp.pad(kernel, ((0, 0), (0, 0), (0, 0), (x, count_x - 1 - x), (0, 0)))
            for x in range(count_x)
        ]
    ).reshape(count_x * chan_out, 3, 3 * wide)
    coarse = lax.reduce_precision(bias, 8, 7)
    middle = lax.reduce_precision(bias - coarse, 8, 7)
    fine = bias - coarse - middle
    pieces = jnp.stack([coarse, middle, fine], axis=1).astype(bf16)
    pieces = jnp.pad(jnp.tile(pieces, (count_x, 1))[:, None], ((0, 0), (0, 2), (0, 5)))
    wbig = jnp.concatenate([placed, pieces], axis=2).reshape(count_x * chan_out, 3 * depth)
    wback = placed.reshape(count_x * chan_out, 9 * wide).T

    own_block = shape((own, lanes), bf16)
    edges, row_0, row_1 = call(
        pack_kernel,
        [shape((2 * own, lanes), bf16), own_block, own_block],
        [pltpu.VMEM((2 * own, lanes), f32)],
    )(cells)
    pool_x, pool_y, pool_z = cotangent.shape[1:]
    pooled_rows = shape((pool_y * pool_x * chan_out, lanes), f32)
    spread = call(spread_kernel, pooled_rows)(cotangent)
    edges = swapped(edges, "gz", 0)
    row_1 = swapped(jnp.concatenate([row_1, edges]), "gy", 1)
    row_0 = swapped(jnp.concatenate([row_0, edges]), "gy", 0)
    body = chan * count_y
    bundle = shape((body + 32, lanes), bf16)
    side = shape((own, lanes), f32)
    face_0, face_1, left, right, rows = call(
        bundle_kernel, [bundle, bundle, side, side, shape((2 * own, lanes), f32)]
    )(cells, edges, row_0, row_1)
    face_1, face_0 = swapped(face_1, "gx", 1), swapped(face_0, "gx", 0)

    tall = 2 * wide
    bundle = shape((body + 16 + tall + 2 * chan_out, lanes), bf16)
    sums, field, face_0, face_1, wpart, wframe, rows, cols = call(
        main_kernel,
        [
            pooled_rows,
            shape(((count_y + 2) * wide, lanes), f32),
            bundle,
            bundle,
            shape((chan_out, lanes), f32),
            shape((2 * chan_out, lanes), bf16),
            shape((2 * own, lanes), f32),
            shape((tall, lanes), f32),
        ],
        [
            pltpu.VMEM(((count_y + 2) * wide, lanes), f32),
            pltpu.VMEM(((count_y + 2) * depth, lanes), bf16),
            pltpu.VMEM((wide, lanes), f32),
            pltpu.VMEM((wide, lanes), f32),
            pltpu.VMEM((6 * wide, lanes), f32),
            pltpu.VMEM((count_x * chan_out, 3 * depth), f32),
            pltpu.VMEM((count_x * chan_out, 8 * lanes), bf16),
            pltpu.VMEM((count_x * chan_out, 8 * lanes), bf16),
        ],
    )(cells, face_0, face_1, rows, left, right, spread, wbig, wback)

    alone_x = lax.axis_size("gx") != 4
    alone_y = lax.axis_size("gy") != 4
    if alone_x:
        wpart, far = lax.psum(wpart, "gx"), wframe
    else:
        far = swapped(wframe, "gx", 2)
    face_1, face_0 = swapped(face_1, "gx", 1), swapped(face_0, "gx", 0)
    pooled = call(pool_kernel, shape(cotangent.shape, bf16))(sums)
    rows_out = shape((3 * own + 2 * chan_out, lanes), bf16)
    wsum, row_0, row_1, cols = call(
        functools.partial(x_kernel, alone_x),
        [shape((chan_out, lanes), f32), rows_out, rows_out, shape((2 * own, lanes), f32)],
    )(wpart, wframe, rows, cols, face_0, face_1, far)
    grad = call(grad_kernel, shape(cells.shape, f32))(field, face_0, face_1)
    if alone_y:
        far, wsum = wframe, lax.psum(wsum, "gy")
    else:
        far = swapped(row_0[3 * own :], "gy", 2)
    row_1, row_0 = swapped(row_1, "gy", 1), swapped(row_0, "gy", 0)
    wsum, frame, rows = call(
        functools.partial(y_kernel, alone_y, count_y),
        [
            shape((chan_out, lanes), f32),
            shape((2 * own + 2 * chan_out, lanes), bf16),
            shape((2 * own, lanes), f32),
        ],
    )(wsum, cols, row_0, row_1, far)
    frame = swapped(frame, "gz", 0)
    input_grad, wsum, bias_grad = call(
        final_kernel,
        [
            shape(cells.shape, f32),
            shape((27, chan, chan_out), f32),
            shape((1, chan_out), f32),
        ],
    )(grad, wsum, rows, frame)
    weight_grad = wsum.reshape(3, 3, 3, chan, chan_out).transpose(4, 3, 0, 1, 2)
    return (pooled, weight_grad, bias_grad.reshape(chan_out), input_grad)


def solution(mesh):
    in_specs = (P(None, "gx", "gy", "gz"), P(), P(), P(None, "gx", "gy", "gz"))
    out_specs = (P(None, "gx", "gy", "gz"), P(), P(), P(None, "gx", "gy", "gz"))
    return jax.shard_map(
        on_device, mesh=mesh, in_specs=in_specs, out_specs=out_specs, check_vma=False
    )
```

```python
import functools

import jax
import jax.numpy as jnp
import numpy as np
from jax import lax
from jax.experimental import pallas as pl
from jax.experimental.pallas import tpu as pltpu
from jax.sharding import PartitionSpec as P

axes = ("gx", "gy", "gz")
f32, bf16 = jnp.float32, jnp.bfloat16
log_scale = 0.07
lanes = 128
limit = 48 * 1024 * 1024


def dot(a, b, contract=((1,), (0,))):
    return lax.dot_general(a, b, (contract, ((), ())), preferred_element_type=f32)


def iota(shape, dim):
    return lax.broadcasted_iota(jnp.int32, shape, dim)


def aligned(start, tile):
    return start if isinstance(start, int) else pl.multiple_of(start, tile)


def swapped(array, axis, pairing):
    count = lax.axis_size(axis)
    pairs = []
    for i in range(count):
        if pairing == 2:
            partner = i + count // 2
        else:
            partner = i + 1 if i % 2 == pairing else i - 1
        pairs.append((i, partner % count))
    return lax.ppermute(array, axis, pairs)


def is_even(axis):
    return lax.rem(lax.axis_index(axis), 2) == 0


def pick(axis, if_even, if_odd):
    return jnp.where(is_even(axis), if_even, if_odd)


def split(value):
    coarse = value.astype(bf16)
    return coarse, (value - coarse.astype(f32)).astype(bf16)


def joined(pair):
    half = pair.shape[0] // 2
    return pair[:half].astype(f32) + pair[half:].astype(f32)


def pack_kernel(cells, edges, sent_0, sent_1, rows):
    chan, count_x, count_y, _ = cells.shape
    count = chan * count_x
    planes = [cells[c, x] for x in range(count_x) for c in range(chan)]
    wide = jnp.concatenate(planes, axis=1)
    row = iota((2 * count, count * lanes), 0)
    lane = iota((2 * count, count * lanes), 1)
    want = jnp.where(row < count, row * lanes, (row - count) * lanes + lanes - 1)
    chosen = (lane == want).astype(f32).astype(bf16)
    found = dot(chosen, wide, ((1,), (1,)))
    found = jnp.concatenate([found, jnp.zeros((2 * count, lanes - count_y), f32)], axis=1)
    edges[...] = pltpu.roll(found, 1, 1).astype(bf16)
    for at, plane in enumerate(planes):
        wide_plane = plane.astype(f32)
        rows[at : at + 1, :] = wide_plane[0:1]
        rows[count + at : count + at + 1, :] = wide_plane[count_y - 1 : count_y]
    first, last = rows[0:count, :], rows[count : 2 * count, :]
    sent_0[...] = pick("gy", last, first).astype(bf16)
    sent_1[...] = pick("gy", first, last).astype(bf16)


def bundle_kernel(cells, edges, got_0, got_1, sent_0, sent_1, left, right, rows):
    chan, count_x, count_y, _ = cells.shape
    own = chan * count_x
    above = pick("gy", got_1[...].astype(f32), got_0[...].astype(f32))
    below = pick("gy", got_0[...].astype(f32), got_1[...].astype(f32))
    spot = iota((2 * own, lanes), 1)
    before = pltpu.roll(above[own:], count_y, 1)
    after = pltpu.roll(below[own:], lanes - count_y, 1)
    whole = jnp.where(
        spot == 0, before, jnp.where(spot == count_y + 1, after, edges[...].astype(f32))
    )
    right[...] = whole[0:own]
    left[...] = whole[own : 2 * own]
    rows_above, rows_below = above[0:own], below[0:own]
    rows[0:own, :] = rows_above
    rows[own : 2 * own, :] = rows_below
    zero = jnp.zeros((8, lanes), f32)
    body = chan * count_y
    frames = []
    for x in (0, count_x - 1):
        at = slice(x * chan, x * chan + chan)
        frame = [rows_above[at], rows_below[at], zero]
        frame += [whole[own + x * chan : own + (x + 1) * chan], whole[at], zero]
        frames.append(jnp.concatenate(frame, axis=0))
    even = is_even("gx")
    for ref, odd in ((sent_0, 0), (sent_1, 1)):
        high = even != (odd == 1)
        x = jnp.where(high, count_x - 1, 0)
        for c in range(chan):
            ref[c * count_y : (c + 1) * count_y, :] = cells[c, x]
        ref[body : body + 32, :] = jnp.where(high, frames[1], frames[0]).astype(bf16)


def spread_kernel(cot, spread):
    chan_out, pool_x, pool_y, pool_z = cot.shape
    twice = jnp.where(
        iota((pool_z, lanes), 1) // 2 == iota((pool_z, lanes), 0), 0.125, 0.0
    ).astype(bf16)
    for o in range(chan_out):
        part = dot(cot[o].reshape(pool_x * pool_y, pool_z), twice)
        for x in range(pool_x):
            spread[pl.ds(x * chan_out + o, pool_y, stride=pool_x * chan_out), :] = part[
                x * pool_y : (x + 1) * pool_y
            ]


def pool_kernel(sums, pooled):
    chan_out, pool_x, pool_y, pool_z = pooled.shape
    halves = jnp.where(
        iota((2 * lanes, pool_z), 0) % lanes // 2 == iota((2 * lanes, pool_z), 1), 0.125, 0.0
    ).astype(bf16)
    for o in range(0, chan_out, 4):
        rows = 4 * pool_x * pool_y
        part = sums[o * pool_x * pool_y : o * pool_x * pool_y + rows, :]
        mean = dot(jnp.concatenate(split(part), axis=1), halves) + log_scale * float(np.log(2.0))
        pooled[o : o + 4] = mean.astype(bf16).reshape(4, pool_x, pool_y, pool_z)


def main_kernel(
    cells, got_0, got_1, rows_in, left_in, right_in, spread, wbig, wback,
    sums, field, face_0, face_1, sent_0, sent_1, wpart, wframe, rows_out, cols,
    stage, patches, left, right, carry, gram, delta_a, delta_b,
):
    chan, count_x, count_y, _ = cells.shape
    pool_x, pool_y = count_x // 2, count_y // 2
    chan_out = wbig.shape[0] // count_x
    own = chan * count_x
    wide = own + 2 * chan
    depth = 3 * wide + 8
    body = chan * count_y
    lane = iota((wide, lanes), 1)
    even = is_even("gx")

    def got(up, start, size):
        one = got_0[start : start + size, :].astype(f32)
        two = got_1[start : start + size, :].astype(f32)
        return jnp.where(even, one, two) if up else jnp.where(even, two, one)

    for x in range(count_x + 2):
        for c in range(chan):
            if x == 0:
                plane = got(False, c * count_y, count_y)
            elif x == count_x + 1:
                plane = got(True, c * count_y, count_y)
            else:
                plane = cells[c, x - 1]
            stage[pl.ds(wide + x * chan + c, count_y, stride=wide), :] = plane.astype(f32)
    rest_low, rest_high = got(False, body, 32), got(True, body, 32)
    for base, top, at in ((0, 0, 0), ((count_y + 1) * wide, own, chan)):
        stage[base : base + chan, :] = rest_low[at : at + chan]
        stage[base + chan : base + chan + own, :] = rows_in[top : top + own, :]
        stage[base + chan + own : base + wide, :] = rest_high[at : at + chan]
    for ref, mine, at in ((left, left_in, 16), (right, right_in, 16 + chan)):
        ref[0:chan, :] = rest_low[at : at + chan]
        ref[chan : chan + own, :] = mine[...]
        ref[chan + own : wide, :] = rest_high[at : at + chan]
    left_cols, right_cols = left[...], right[...]
    for y in range(count_y + 2):
        mid = stage[y * wide : (y + 1) * wide, :]
        low_col = pltpu.roll(left_cols, (lanes - y) % lanes, 1)
        high_col = pltpu.roll(right_cols, (lanes - 1 - y) % lanes, 1)
        before = jnp.where(lane == 0, low_col, pltpu.roll(mid, 1, 1))
        after = jnp.where(lane == lanes - 1, high_col, pltpu.roll(mid, lanes - 1, 1))
        whole = jnp.concatenate([before, mid, after, jnp.ones((8, lanes), f32)], axis=0)
        patches[y * depth : (y + 1) * depth, :] = whole.astype(bf16)

    carry[...] = jnp.zeros_like(carry)
    gram[...] = jnp.zeros_like(gram)
    cols[...] = jnp.zeros_like(cols)
    pairs = 4
    steps = count_y // (2 * pairs)
    size = 3 * wide
    inside, outside = lane != lanes - 1, lane != 0

    def finish(y, whole, edge):
        first, last = whole[0:wide], whole[2 * wide : 3 * wide]
        inner = (
            whole[wide : 2 * wide]
            + jnp.where(inside, pltpu.roll(first, lanes - 1, 1), 0.0)
            + jnp.where(outside, pltpu.roll(last, 1, 1), 0.0)
        )
        field[pl.ds(aligned(y * wide, 8), wide), :] = inner
        here = lane == y
        edge[0] = jnp.where(here, pltpu.roll(first, y, 1), edge[0])
        edge[1] = jnp.where(here, pltpu.roll(last, y + 1, 1), edge[1])

    def block_of(j):
        return jnp.concatenate(
            [
                patches[pl.ds(aligned((2 * j + h) * depth, 16), 3 * depth), :]
                for h in range(2)
            ],
            axis=1,
        )

    def forward(i, k, ref):
        j = i * pairs + k
        preact = dot(wbig[...], block_of(j))
        slope = jnp.tanh(5.0 * preact)
        linear = jnp.maximum(preact, 0.3 * preact)
        factor = 1.0 + jnp.abs(slope)
        here = spread[pl.ds(aligned(j * pool_x * chan_out, 8), pool_x * chan_out), :]
        slope = 0.65 + 0.35 * slope
        delta = []
        for x in range(pool_x):
            top, mid = 2 * x * chan_out, (2 * x + 1) * chan_out
            end = mid + chan_out
            times = here[x * chan_out : (x + 1) * chan_out]
            times = jnp.concatenate([times, times], axis=1)
            delta.append((slope[top:mid] * times).astype(bf16))
            delta.append((slope[mid:end] * times).astype(bf16))
            total = linear[top:mid] + linear[mid:end]
            total = total[:, :lanes] + total[:, lanes:]
            prod = factor[top:mid] * factor[mid:end]
            prod = prod[:, :lanes] * prod[:, lanes:]
            total = total - log_scale * jnp.log(prod)
            sums[pl.ds(x * pool_y + j, chan_out, stride=pool_x * pool_y), :] = total
        ref[:, 2 * k * lanes : 2 * (k + 1) * lanes] = jnp.concatenate(delta, axis=0)

    def backward(i, k, ref, held, edge):
        j = i * pairs + k
        parts = dot(wback[...], ref[:, 2 * k * lanes : 2 * (k + 1) * lanes])
        part = lambda b, h: parts[b * size : (b + 1) * size, h * lanes : (h + 1) * lanes]
        finish(2 * j, held[0] + part(0, 0), edge)
        finish(2 * j + 1, held[1] + part(1, 0) + part(0, 1), edge)
        held[0] = part(2, 0) + part(1, 1)
        held[1] = part(2, 1)

    def weigh(i, ref):
        blocks = jnp.concatenate([block_of(i * pairs + k) for k in range(pairs)], axis=1)
        return dot(ref[...], blocks, ((1,), (1,)))

    def opened():
        return (
            [carry[0:size, :], carry[size : 2 * size, :]],
            [cols[0:wide, :], cols[wide : 2 * wide, :]],
        )

    def closed(held, edge):
        carry[0:size, :] = held[0]
        carry[size : 2 * size, :] = held[1]
        cols[0:wide, :] = edge[0]
        cols[wide : 2 * wide, :] = edge[1]

    def step(t, _):
        held, edge = opened()
        total = gram[...] + weigh(2 * t, delta_a)
        for k in range(pairs):
            forward(2 * t + 1, k, delta_b)
            backward(2 * t, k, delta_a, held, edge)
        total = total + weigh(2 * t + 1, delta_b)
        for k in range(pairs):
            forward(2 * t + 2, k, delta_a)
            backward(2 * t + 1, k, delta_b, held, edge)
        gram[...] = total
        closed(held, edge)
        return 0

    for k in range(pairs):
        forward(0, k, delta_a)
    lax.fori_loop(0, steps // 2 - 1, step, 0)
    held, edge = opened()
    total = gram[...] + weigh(steps - 2, delta_a)
    for k in range(pairs):
        forward(steps - 1, k, delta_b)
        backward(steps - 2, k, delta_a, held, edge)
    gram[...] = total + weigh(steps - 1, delta_b)
    for k in range(pairs):
        backward(steps - 1, k, delta_b, held, edge)
    finish(count_y, held[0], edge)
    finish(count_y + 1, held[1], edge)
    closed(held, edge)

    span = gram.shape[1]
    straight, turned = 0.0, 0.0
    for x in range(count_x):
        part = gram[x * chan_out : (x + 1) * chan_out, :]
        part = jnp.concatenate([part, jnp.zeros((chan_out, 2 * lanes - span), f32)], axis=1)
        straight = straight + part
        turned = turned + (pltpu.roll(part, 2 * lanes - chan * x, 1) if x else part)
    spot = iota((chan_out, lanes), 1)
    tight = 0.0
    group = 3 * chan
    for b in range(3):
        for e in range(3):
            shift = (b * depth + e * wide) - (b * 3 + e) * group
            part = pltpu.roll(turned, 2 * lanes - shift, 1)[:, :lanes] if shift else turned[:, :lanes]
            tight = jnp.where(spot // group == b * 3 + e, part, tight)
    part = pltpu.roll(straight, 2 * lanes + 9 * group - 3 * wide, 1)[:, :lanes]
    tight = jnp.where(spot == 9 * group, part, tight)
    coarse = tight.astype(bf16)
    wpart[...] = tight
    sides = jnp.concatenate(split(tight), axis=0)
    wframe[...] = sides

    ends = [field[0:wide, :], field[(count_y + 1) * wide : (count_y + 2) * wide, :]]
    rows_out[...] = jnp.concatenate([end[chan : chan + own] for end in ends], axis=0)
    tall = cols.shape[0]
    found = cols[...].astype(bf16)
    zero = jnp.zeros((8, lanes), f32)
    for face, ref, odd in ((face_0, sent_0, 0), (face_1, sent_1, 1)):
        high = even != (odd == 1)
        for c in range(chan):
            low_plane, high_plane = [
                field[pl.ds(wide + x * chan + c, count_y, stride=wide), :]
                for x in (0, count_x + 1)
            ]
            plane = jnp.where(high, high_plane, low_plane)
            face[c * count_y : (c + 1) * count_y, :] = plane.astype(bf16)
        low_frame, high_frame = [
            jnp.concatenate([end[x * chan : (x + 1) * chan] for end in ends] + [zero], axis=0)
            for x in (0, count_x + 1)
        ]
        ref[0:16, :] = jnp.where(high, high_frame, low_frame).astype(bf16)
        ref[16 : 16 + tall, :] = found
        ref[16 + tall :, :] = sides


def x_kernel(alone, wpart, wframe, rows, cols, got_0, got_1, far, frame, rows_out):
    tall = cols.shape[0]
    own = rows.shape[0] // 2
    wide = tall // 2
    chan = (wide - own) // 2
    if alone:
        total = wpart[...]
    else:
        total = joined(wframe[...]) + joined(far[...])
        total = total + (joined(got_0[16 + tall :, :]) + joined(got_1[16 + tall :, :]))
    frame[2 * own :, :] = jnp.concatenate(split(total), axis=0)
    one, two = got_0[0 : 16 + tall, :].astype(f32), got_1[0 : 16 + tall, :].astype(f32)
    from_low, from_high = pick("gx", two, one), pick("gx", one, two)
    mid = jnp.zeros((own - 2 * chan, lanes), f32)
    found = []
    for top in (0, wide):
        more = [from_low[16 + top + chan + own : 16 + top + wide], mid]
        more.append(from_high[16 + top : 16 + top + chan])
        found.append(cols[top + chan : top + chan + own, :] + jnp.concatenate(more, axis=0))
    frame[0 : 2 * own, :] = jnp.concatenate(found, axis=0).astype(bf16)
    for at in (0, 1):
        more = [from_low[at * chan : (at + 1) * chan], mid, from_high[at * chan : (at + 1) * chan]]
        place = slice(at * own, (at + 1) * own)
        rows_out[place, :] = rows[place, :] + jnp.concatenate(more, axis=0)


def z_kernel(count_y, mine, got, rows, sent_0, sent_1, wframe):
    own = rows.shape[0] // 2
    total = joined(mine[2 * own :, :]) + joined(got[2 * own :, :])
    sides = jnp.concatenate(split(total), axis=0)
    wframe[...] = sides
    last = got[0:own, :].astype(f32)
    first = got[own : 2 * own, :].astype(f32)
    spot = iota((own, lanes), 1)
    both = []
    for at, line in ((0, 0), (1, count_y + 1)):
        more = jnp.where(spot == lanes - 1, pltpu.roll(last, lanes - 1 - line, 1), 0.0)
        turned = pltpu.roll(first, lanes - line, 1) if line else first
        more = jnp.where(spot == 0, turned, more)
        both.append(rows[at * own : (at + 1) * own, :] + more)
    sent_0[0:own, :] = pick("gy", both[1], both[0]).astype(bf16)
    sent_1[0:own, :] = pick("gy", both[0], both[1]).astype(bf16)
    for ref in (sent_0, sent_1):
        ref[own:, :] = sides


def grad_kernel(field, face_0, face_1, got, grad, ends):
    chan, count_x, count_y, _ = grad.shape
    own = chan * count_x
    wide = own + 2 * chan
    spot = iota((count_y, lanes), 1)
    columns = pltpu.roll(got[0 : 2 * own, :].astype(f32), lanes - 1, 1)
    columns = jnp.concatenate([columns, jnp.zeros((lanes - 2 * own, lanes), f32)], axis=0)
    columns = columns.T[0:count_y]
    for x in range(count_x):
        for c in range(chan):
            at = x * chan + c
            plane = field[pl.ds(wide + chan + at, count_y, stride=wide), :]
            place = slice(c * count_y, (c + 1) * count_y)
            if x == 0:
                plane = plane + pick("gx", face_1[place, :].astype(f32), face_0[place, :].astype(f32))
            if x == count_x - 1:
                plane = plane + pick("gx", face_0[place, :].astype(f32), face_1[place, :].astype(f32))
            more = jnp.where(spot == lanes - 1, columns[:, at : at + 1], 0.0)
            plane = plane + jnp.where(spot == 0, columns[:, own + at : own + at + 1], more)
            grad[c, x] = plane
            ends[0, c, x] = plane[0:8]
            ends[1, c, x] = plane[count_y - 8 : count_y]


def final_kernel(whole, ends, mine, got_0, got_1, far, out, wout, bout, tiles, sems):
    chan, count_x, count_y, _ = whole.shape
    own = chan * count_x
    chan_out = mine.shape[0] // 2
    row = iota((8, lanes), 0)
    one, two = got_0[0:own, :].astype(f32), got_1[0:own, :].astype(f32)
    above, below = pick("gy", two, one), pick("gy", one, two)
    copies = []
    for side, more, line in ((0, above, 0), (1, below, 7)):
        for x in range(count_x):
            for c in range(chan):
                at = x * chan + c
                extra = jnp.where(row == line, more[at : at + 1], 0.0)
                tiles[side, c, x] = ends[side, c, x] + extra
        copies.append(
            pltpu.make_async_copy(
                tiles.at[side],
                out.at[:, :, pl.ds(side * (count_y - 8), 8), :],
                sems.at[side],
            )
        )
        copies[-1].start()
    total = joined(mine[...]) + joined(far[...])
    total = total + (joined(got_0[own:, :]) + joined(got_1[own:, :]))
    total = jnp.concatenate([total, jnp.zeros((lanes - chan_out, lanes), f32)], axis=0)
    total = total.T
    for a in range(3):
        for be in range(9):
            at = (be * 3 + a) * chan
            wout[a * 9 + be] = total[at : at + chan, :chan_out]
    bout[...] = total[27 * chan : 27 * chan + 1, :chan_out]
    for copy in copies:
        copy.wait()


def call(kernel, outs, scratch=(), cost=None, **rest):
    return pl.pallas_call(
        kernel,
        out_shape=outs,
        **rest,
        scratch_shapes=list(scratch),
        cost_estimate=cost,
        compiler_params=pltpu.CompilerParams(vmem_limit_bytes=limit),
    )


def on_device(cells, weight, bias, cotangent):
    chan, count_x, count_y, count_z = cells.shape
    chan_out = weight.shape[0]
    own = chan * count_x
    wide = own + 2 * chan
    depth = 3 * wide + 8
    shape = jax.ShapeDtypeStruct

    kernel = weight.transpose(0, 3, 4, 2, 1)
    placed = jnp.stack(
        [
            jnp.pad(kernel, ((0, 0), (0, 0), (0, 0), (x, count_x - 1 - x), (0, 0)))
            for x in range(count_x)
        ]
    ).reshape(count_x * chan_out, 3, 3 * wide)
    coarse = lax.reduce_precision(bias, 8, 7)
    middle = lax.reduce_precision(bias - coarse, 8, 7)
    fine = bias - coarse - middle
    pieces = jnp.stack([coarse, middle, fine], axis=1).astype(bf16)
    pieces = jnp.pad(jnp.tile(pieces, (count_x, 1))[:, None], ((0, 0), (0, 2), (0, 5)))
    wbig = jnp.concatenate([placed, pieces], axis=2).reshape(count_x * chan_out, 3 * depth)
    wback = placed.reshape(count_x * chan_out, 9 * wide).T

    own_block = shape((own, lanes), bf16)
    edges, row_0, row_1 = call(
        pack_kernel,
        [shape((2 * own, lanes), bf16), own_block, own_block],
        [pltpu.VMEM((2 * own, lanes), f32)],
    )(cells)
    pool_x, pool_y, pool_z = cotangent.shape[1:]
    pooled_rows = shape((pool_y * pool_x * chan_out, lanes), f32)
    spread = call(spread_kernel, pooled_rows)(cotangent)
    edges = swapped(edges, "gz", 0)
    row_1 = swapped(jnp.concatenate([row_1, edges]), "gy", 1)
    row_0 = swapped(jnp.concatenate([row_0, edges]), "gy", 0)
    body = chan * count_y
    bundle = shape((body + 32, lanes), bf16)
    side = shape((own, lanes), f32)
    face_0, face_1, left, right, rows = call(
        bundle_kernel, [bundle, bundle, side, side, shape((2 * own, lanes), f32)]
    )(cells, edges, row_0, row_1)
    face_1, face_0 = swapped(face_1, "gx", 1), swapped(face_0, "gx", 0)

    tall = 2 * wide
    bundle = shape((16 + tall + 2 * chan_out, lanes), bf16)
    face = shape((body, lanes), bf16)
    sums, field, face_0, face_1, row_0, row_1, wpart, wframe, rows, cols = call(
        main_kernel,
        [
            pooled_rows,
            shape(((count_y + 2) * wide, lanes), f32),
            face,
            face,
            bundle,
            bundle,
            shape((chan_out, lanes), f32),
            shape((2 * chan_out, lanes), bf16),
            shape((2 * own, lanes), f32),
            shape((tall, lanes), f32),
        ],
        [
            pltpu.VMEM(((count_y + 2) * wide, lanes), f32),
            pltpu.VMEM(((count_y + 2) * depth, lanes), bf16),
            pltpu.VMEM((wide, lanes), f32),
            pltpu.VMEM((wide, lanes), f32),
            pltpu.VMEM((6 * wide, lanes), f32),
            pltpu.VMEM((count_x * chan_out, 3 * depth), f32),
            pltpu.VMEM((count_x * chan_out, 8 * lanes), bf16),
            pltpu.VMEM((count_x * chan_out, 8 * lanes), bf16),
        ],
    )(cells, face_0, face_1, rows, left, right, spread, wbig, wback)

    alone = lax.axis_size("gx") != 4
    if alone:
        wpart, far = lax.psum(wpart, "gx"), wframe
    else:
        far = swapped(wframe, "gx", 2)
    row_1, row_0 = swapped(row_1, "gx", 1), swapped(row_0, "gx", 0)
    face_1, face_0 = swapped(face_1, "gx", 1), swapped(face_0, "gx", 0)
    pooled = call(pool_kernel, shape(cotangent.shape, bf16))(sums)
    mine, rows = call(
        functools.partial(x_kernel, alone),
        [shape((2 * own + 2 * chan_out, lanes), bf16), shape((2 * own, lanes), f32)],
    )(wpart, wframe, rows, cols, row_0, row_1, far)
    frame = swapped(mine, "gz", 0)
    bundle = shape((own + 2 * chan_out, lanes), bf16)
    row_0, row_1, mine = call(
        functools.partial(z_kernel, count_y),
        [bundle, bundle, shape((2 * chan_out, lanes), bf16)],
    )(mine, frame, rows)
    row_1, row_0 = swapped(row_1, "gy", 1), swapped(row_0, "gy", 0)
    far = swapped(mine, "gy", 2)
    tiles = (2, chan, count_x, 8, lanes)
    grad, ends = call(grad_kernel, [shape(cells.shape, f32), shape(tiles, f32)])(
        field, face_0, face_1, frame
    )
    vmem, anywhere = pl.BlockSpec(memory_space=pltpu.VMEM), pl.BlockSpec(memory_space=pl.ANY)
    input_grad, wsum, bias_grad = call(
        final_kernel,
        [
            shape(cells.shape, f32),
            shape((27, chan, chan_out), f32),
            shape((1, chan_out), f32),
        ],
        [pltpu.VMEM(tiles, f32), pltpu.SemaphoreType.DMA((2,))],
        in_specs=[anywhere] + [vmem] * 5,
        out_specs=[anywhere, vmem, vmem],
        input_output_aliases={0: 0},
    )(grad, ends, mine, row_0, row_1, far)
    weight_grad = wsum.reshape(3, 3, 3, chan, chan_out).transpose(4, 3, 0, 1, 2)
    return (pooled, weight_grad, bias_grad.reshape(chan_out), input_grad)


def solution(mesh):
    in_specs = (P(None, "gx", "gy", "gz"), P(), P(), P(None, "gx", "gy", "gz"))
    out_specs = (P(None, "gx", "gy", "gz"), P(), P(), P(None, "gx", "gy", "gz"))
    return jax.shard_map(
        on_device, mesh=mesh, in_specs=in_specs, out_specs=out_specs, check_vma=False
    )
```

```python
import functools

import jax
import jax.numpy as jnp
import numpy as np
from jax import lax
from jax.experimental import pallas as pl
from jax.experimental.pallas import tpu as pltpu
from jax.sharding import PartitionSpec as P

axes = ("gx", "gy", "gz")
f32, bf16 = jnp.float32, jnp.bfloat16
log_scale = 0.07
lanes = 128
limit = 48 * 1024 * 1024


def dot(a, b, contract=((1,), (0,))):
    return lax.dot_general(a, b, (contract, ((), ())), preferred_element_type=f32)


def iota(shape, dim):
    return lax.broadcasted_iota(jnp.int32, shape, dim)


def aligned(start, tile):
    return start if isinstance(start, int) else pl.multiple_of(start, tile)


def swapped(array, axis, pairing):
    count = lax.axis_size(axis)
    pairs = []
    for i in range(count):
        if pairing == 2:
            partner = i + count // 2
        else:
            partner = i + 1 if i % 2 == pairing else i - 1
        pairs.append((i, partner % count))
    return lax.ppermute(array, axis, pairs)


def is_even(axis):
    return lax.rem(lax.axis_index(axis), 2) == 0


def pick(axis, if_even, if_odd):
    return jnp.where(is_even(axis), if_even, if_odd)


def split(value):
    coarse = value.astype(bf16)
    return coarse, (value - coarse.astype(f32)).astype(bf16)


def joined(pair):
    half = pair.shape[0] // 2
    return pair[:half].astype(f32) + pair[half:].astype(f32)


def pack_kernel(cells, edges, sent_0, sent_1, rows):
    chan, count_x, count_y, _ = cells.shape
    count = chan * count_x
    row = iota((2 * count, count * lanes), 0)
    lane = iota((2 * count, count * lanes), 1)
    want = jnp.where(row < count, row * lanes, (row - count) * lanes + lanes - 1)
    chosen = (lane == want).astype(f32).astype(bf16)
    planes = [cells[c, x] for x in range(count_x) for c in range(chan)]
    wide = jnp.concatenate(planes, axis=1)
    found = dot(chosen, wide, ((1,), (1,)))
    found = jnp.concatenate([found, jnp.zeros((2 * count, lanes - count_y), f32)], axis=1)
    edges[...] = pltpu.roll(found, 1, 1).astype(bf16)
    for at, plane in enumerate(planes):
        wide_plane = plane.astype(f32)
        rows[at : at + 1, :] = wide_plane[0:1]
        rows[count + at : count + at + 1, :] = wide_plane[count_y - 1 : count_y]
    first, last = rows[0:count, :], rows[count : 2 * count, :]
    sent_0[...] = pick("gy", last, first).astype(bf16)
    sent_1[...] = pick("gy", first, last).astype(bf16)


def bundle_kernel(cells, edges, got_0, got_1, sent_0, sent_1, left, right, rows):
    chan, count_x, count_y, _ = cells.shape
    own = chan * count_x
    above = pick("gy", got_1[...].astype(f32), got_0[...].astype(f32))
    below = pick("gy", got_0[...].astype(f32), got_1[...].astype(f32))
    spot = iota((2 * own, lanes), 1)
    before = pltpu.roll(above[own:], count_y, 1)
    after = pltpu.roll(below[own:], lanes - count_y, 1)
    whole = jnp.where(
        spot == 0, before, jnp.where(spot == count_y + 1, after, edges[...].astype(f32))
    )
    right[...] = whole[0:own]
    left[...] = whole[own : 2 * own]
    rows_above, rows_below = above[0:own], below[0:own]
    rows[0:own, :] = rows_above
    rows[own : 2 * own, :] = rows_below
    zero = jnp.zeros((8, lanes), f32)
    body = chan * count_y
    frames = []
    for x in (0, count_x - 1):
        at = slice(x * chan, x * chan + chan)
        frame = [rows_above[at], rows_below[at], zero]
        frame += [whole[own + x * chan : own + (x + 1) * chan], whole[at], zero]
        frames.append(jnp.concatenate(frame, axis=0))
    even = is_even("gx")
    for ref, odd in ((sent_0, 0), (sent_1, 1)):
        high = even != (odd == 1)
        x = jnp.where(high, count_x - 1, 0)
        for c in range(chan):
            ref[c * count_y : (c + 1) * count_y, :] = cells[c, x]
        ref[body : body + 32, :] = jnp.where(high, frames[1], frames[0]).astype(bf16)


def spread_kernel(cot, spread):
    chan_out, pool_x, pool_y, pool_z = cot.shape
    twice = jnp.where(
        iota((pool_z, lanes), 1) // 2 == iota((pool_z, lanes), 0), 0.125, 0.0
    ).astype(bf16)
    for o in range(chan_out):
        part = dot(cot[o].reshape(pool_x * pool_y, pool_z), twice)
        for x in range(pool_x):
            spread[pl.ds(x * chan_out + o, pool_y, stride=pool_x * chan_out), :] = part[
                x * pool_y : (x + 1) * pool_y
            ]


def pool_kernel(sums, pooled):
    chan_out, pool_x, pool_y, pool_z = pooled.shape
    halves = jnp.where(
        iota((2 * lanes, pool_z), 0) % lanes // 2 == iota((2 * lanes, pool_z), 1), 0.125, 0.0
    ).astype(bf16)
    for o in range(0, chan_out, 4):
        rows = 4 * pool_x * pool_y
        part = sums[o * pool_x * pool_y : o * pool_x * pool_y + rows, :]
        mean = dot(jnp.concatenate(split(part), axis=1), halves) + log_scale * float(np.log(2.0))
        pooled[o : o + 4] = mean.astype(bf16).reshape(4, pool_x, pool_y, pool_z)


def main_kernel(
    cells, got_0, got_1, rows_in, left_in, right_in, spread, wbig, wback,
    sums, field, sent_0, sent_1, wpart, wframe, rows_out, cols,
    stage, patches, left, right, carry, gram, delta_a, delta_b,
):
    chan, count_x, count_y, _ = cells.shape
    pool_x, pool_y = count_x // 2, count_y // 2
    chan_out = wbig.shape[0] // count_x
    own = chan * count_x
    wide = own + 2 * chan
    depth = 3 * wide + 8
    body = chan * count_y
    lane = iota((wide, lanes), 1)
    even = is_even("gx")

    def got(up, start, size):
        one = got_0[start : start + size, :].astype(f32)
        two = got_1[start : start + size, :].astype(f32)
        return jnp.where(even, one, two) if up else jnp.where(even, two, one)

    for x in range(count_x + 2):
        for c in range(chan):
            if x == 0:
                plane = got(False, c * count_y, count_y)
            elif x == count_x + 1:
                plane = got(True, c * count_y, count_y)
            else:
                plane = cells[c, x - 1]
            stage[pl.ds(wide + x * chan + c, count_y, stride=wide), :] = plane.astype(f32)
    rest_low, rest_high = got(False, body, 32), got(True, body, 32)
    for base, top, at in ((0, 0, 0), ((count_y + 1) * wide, own, chan)):
        stage[base : base + chan, :] = rest_low[at : at + chan]
        stage[base + chan : base + chan + own, :] = rows_in[top : top + own, :]
        stage[base + chan + own : base + wide, :] = rest_high[at : at + chan]
    for ref, mine, at in ((left, left_in, 16), (right, right_in, 16 + chan)):
        ref[0:chan, :] = rest_low[at : at + chan]
        ref[chan : chan + own, :] = mine[...]
        ref[chan + own : wide, :] = rest_high[at : at + chan]
    left_cols, right_cols = left[...], right[...]
    for y in range(count_y + 2):
        mid = stage[y * wide : (y + 1) * wide, :]
        low_col = pltpu.roll(left_cols, (lanes - y) % lanes, 1)
        high_col = pltpu.roll(right_cols, (lanes - 1 - y) % lanes, 1)
        before = jnp.where(lane == 0, low_col, pltpu.roll(mid, 1, 1))
        after = jnp.where(lane == lanes - 1, high_col, pltpu.roll(mid, lanes - 1, 1))
        whole = jnp.concatenate([before, mid, after, jnp.ones((8, lanes), f32)], axis=0)
        patches[y * depth : (y + 1) * depth, :] = whole.astype(bf16)

    carry[...] = jnp.zeros_like(carry)
    gram[...] = jnp.zeros_like(gram)
    cols[...] = jnp.zeros_like(cols)
    pairs = 4
    steps = count_y // (2 * pairs)
    size = 3 * wide
    inside, outside = lane != lanes - 1, lane != 0

    def finish(y, whole, edge):
        first, last = whole[0:wide], whole[2 * wide : 3 * wide]
        inner = (
            whole[wide : 2 * wide]
            + jnp.where(inside, pltpu.roll(first, lanes - 1, 1), 0.0)
            + jnp.where(outside, pltpu.roll(last, 1, 1), 0.0)
        )
        field[pl.ds(aligned(y * wide, 8), wide), :] = inner
        here = lane == y
        edge[0] = jnp.where(here, pltpu.roll(first, y, 1), edge[0])
        edge[1] = jnp.where(here, pltpu.roll(last, y + 1, 1), edge[1])

    def block_of(j):
        return jnp.concatenate(
            [
                patches[pl.ds(aligned((2 * j + h) * depth, 16), 3 * depth), :]
                for h in range(2)
            ],
            axis=1,
        )

    def forward(i, k, ref):
        j = i * pairs + k
        preact = dot(wbig[...], block_of(j))
        slope = jnp.tanh(5.0 * preact)
        linear = jnp.maximum(preact, 0.3 * preact)
        factor = 1.0 + jnp.abs(slope)
        here = spread[pl.ds(aligned(j * pool_x * chan_out, 8), pool_x * chan_out), :]
        slope = 0.65 + 0.35 * slope
        delta = []
        for x in range(pool_x):
            top, mid = 2 * x * chan_out, (2 * x + 1) * chan_out
            end = mid + chan_out
            times = here[x * chan_out : (x + 1) * chan_out]
            times = jnp.concatenate([times, times], axis=1)
            delta.append((slope[top:mid] * times).astype(bf16))
            delta.append((slope[mid:end] * times).astype(bf16))
            total = linear[top:mid] + linear[mid:end]
            total = total[:, :lanes] + total[:, lanes:]
            prod = factor[top:mid] * factor[mid:end]
            prod = prod[:, :lanes] * prod[:, lanes:]
            total = total - log_scale * jnp.log(prod)
            sums[pl.ds(x * pool_y + j, chan_out, stride=pool_x * pool_y), :] = total
        ref[:, 2 * k * lanes : 2 * (k + 1) * lanes] = jnp.concatenate(delta, axis=0)

    def backward(i, k, ref, held, edge):
        j = i * pairs + k
        parts = dot(wback[...], ref[:, 2 * k * lanes : 2 * (k + 1) * lanes])
        part = lambda b, h: parts[b * size : (b + 1) * size, h * lanes : (h + 1) * lanes]
        finish(2 * j, held[0] + part(0, 0), edge)
        finish(2 * j + 1, held[1] + part(1, 0) + part(0, 1), edge)
        held[0] = part(2, 0) + part(1, 1)
        held[1] = part(2, 1)

    def weigh(i, ref):
        blocks = jnp.concatenate([block_of(i * pairs + k) for k in range(pairs)], axis=1)
        return dot(ref[...], blocks, ((1,), (1,)))

    def opened():
        return (
            [carry[0:size, :], carry[size : 2 * size, :]],
            [cols[0:wide, :], cols[wide : 2 * wide, :]],
        )

    def closed(held, edge):
        carry[0:size, :] = held[0]
        carry[size : 2 * size, :] = held[1]
        cols[0:wide, :] = edge[0]
        cols[wide : 2 * wide, :] = edge[1]

    def step(t, _):
        held, edge = opened()
        total = gram[...] + weigh(2 * t, delta_a)
        for k in range(pairs):
            forward(2 * t + 1, k, delta_b)
            backward(2 * t, k, delta_a, held, edge)
        total = total + weigh(2 * t + 1, delta_b)
        for k in range(pairs):
            forward(2 * t + 2, k, delta_a)
            backward(2 * t + 1, k, delta_b, held, edge)
        gram[...] = total
        closed(held, edge)
        return 0

    for k in range(pairs):
        forward(0, k, delta_a)
    lax.fori_loop(0, steps // 2 - 1, step, 0)
    held, edge = opened()
    total = gram[...] + weigh(steps - 2, delta_a)
    for k in range(pairs):
        forward(steps - 1, k, delta_b)
        backward(steps - 2, k, delta_a, held, edge)
    gram[...] = total + weigh(steps - 1, delta_b)
    for k in range(pairs):
        backward(steps - 1, k, delta_b, held, edge)
    finish(count_y, held[0], edge)
    finish(count_y + 1, held[1], edge)
    closed(held, edge)

    span = gram.shape[1]
    straight, turned = 0.0, 0.0
    for x in range(count_x):
        part = gram[x * chan_out : (x + 1) * chan_out, :]
        part = jnp.concatenate([part, jnp.zeros((chan_out, 2 * lanes - span), f32)], axis=1)
        straight = straight + part
        turned = turned + (pltpu.roll(part, 2 * lanes - chan * x, 1) if x else part)
    spot = iota((chan_out, lanes), 1)
    tight = 0.0
    group = 3 * chan
    for b in range(3):
        for e in range(3):
            shift = (b * depth + e * wide) - (b * 3 + e) * group
            part = pltpu.roll(turned, 2 * lanes - shift, 1)[:, :lanes] if shift else turned[:, :lanes]
            tight = jnp.where(spot // group == b * 3 + e, part, tight)
    part = pltpu.roll(straight, 2 * lanes + 9 * group - 3 * wide, 1)[:, :lanes]
    tight = jnp.where(spot == 9 * group, part, tight)
    coarse = tight.astype(bf16)
    wpart[...] = tight
    sides = jnp.concatenate(split(tight), axis=0)
    wframe[...] = sides

    ends = [field[0:wide, :], field[(count_y + 1) * wide : (count_y + 2) * wide, :]]
    rows_out[...] = jnp.concatenate([end[chan : chan + own] for end in ends], axis=0)
    tall = cols.shape[0]
    found = cols[...].astype(bf16)
    zero = jnp.zeros((8, lanes), f32)
    for ref, odd in ((sent_0, 0), (sent_1, 1)):
        high = even != (odd == 1)
        low_frame, high_frame = [
            jnp.concatenate([end[x * chan : (x + 1) * chan] for end in ends] + [zero], axis=0)
            for x in (0, count_x + 1)
        ]
        ref[0:16, :] = jnp.where(high, high_frame, low_frame).astype(bf16)
        ref[16 : 16 + tall, :] = found
        ref[16 + tall :, :] = sides


def face_kernel(chan, field, face_0, face_1):
    count_y = face_0.shape[0] // chan
    wide = field.shape[0] // (count_y + 2)
    even = is_even("gx")
    for c in range(chan):
        low, high = [
            field[pl.ds(wide + at + c, count_y, stride=wide), :] for at in (0, wide - chan)
        ]
        place = slice(c * count_y, (c + 1) * count_y)
        face_0[place, :] = jnp.where(even, high, low).astype(bf16)
        face_1[place, :] = jnp.where(even, low, high).astype(bf16)


def x_kernel(alone, wpart, wframe, rows, cols, got_0, got_1, far, frame, rows_out):
    tall = cols.shape[0]
    own = rows.shape[0] // 2
    wide = tall // 2
    chan = (wide - own) // 2
    if alone:
        total = wpart[...]
    else:
        total = joined(wframe[...]) + joined(far[16 + tall :, :])
        total = total + (joined(got_0[16 + tall :, :]) + joined(got_1[16 + tall :, :]))
    frame[2 * own :, :] = jnp.concatenate(split(total), axis=0)
    one, two = got_0[0 : 16 + tall, :].astype(f32), got_1[0 : 16 + tall, :].astype(f32)
    from_low, from_high = pick("gx", two, one), pick("gx", one, two)
    mid = jnp.zeros((own - 2 * chan, lanes), f32)
    found = []
    for top in (0, wide):
        more = [from_low[16 + top + chan + own : 16 + top + wide], mid]
        more.append(from_high[16 + top : 16 + top + chan])
        found.append(cols[top + chan : top + chan + own, :] + jnp.concatenate(more, axis=0))
    frame[0 : 2 * own, :] = jnp.concatenate(found, axis=0).astype(bf16)
    for at in (0, 1):
        more = [from_low[at * chan : (at + 1) * chan], mid, from_high[at * chan : (at + 1) * chan]]
        place = slice(at * own, (at + 1) * own)
        rows_out[place, :] = rows[place, :] + jnp.concatenate(more, axis=0)


def z_kernel(count_y, mine, got, rows, sent_0, sent_1, wframe):
    own = rows.shape[0] // 2
    total = joined(mine[2 * own :, :]) + joined(got[2 * own :, :])
    sides = jnp.concatenate(split(total), axis=0)
    wframe[...] = sides
    last = got[0:own, :].astype(f32)
    first = got[own : 2 * own, :].astype(f32)
    spot = iota((own, lanes), 1)
    both = []
    for at, line in ((0, 0), (1, count_y + 1)):
        more = jnp.where(spot == lanes - 1, pltpu.roll(last, lanes - 1 - line, 1), 0.0)
        turned = pltpu.roll(first, lanes - line, 1) if line else first
        more = jnp.where(spot == 0, turned, more)
        both.append(rows[at * own : (at + 1) * own, :] + more)
    sent_0[0:own, :] = pick("gy", both[1], both[0]).astype(bf16)
    sent_1[0:own, :] = pick("gy", both[0], both[1]).astype(bf16)
    for ref in (sent_0, sent_1):
        ref[own:, :] = sides


def grad_kernel(field, face_0, face_1, got, grad, ends):
    chan, count_x, count_y, _ = grad.shape
    own = chan * count_x
    wide = own + 2 * chan
    spot = iota((count_y, lanes), 1)
    columns = pltpu.roll(got[0 : 2 * own, :].astype(f32), lanes - 1, 1)
    columns = jnp.concatenate([columns, jnp.zeros((lanes - 2 * own, lanes), f32)], axis=0)
    columns = columns.T[0:count_y]
    for x in range(count_x):
        for c in range(chan):
            at = x * chan + c
            plane = field[pl.ds(wide + chan + at, count_y, stride=wide), :]
            place = slice(c * count_y, (c + 1) * count_y)
            if x == 0:
                plane = plane + pick("gx", face_1[place, :].astype(f32), face_0[place, :].astype(f32))
            if x == count_x - 1:
                plane = plane + pick("gx", face_0[place, :].astype(f32), face_1[place, :].astype(f32))
            more = jnp.where(spot == lanes - 1, columns[:, at : at + 1], 0.0)
            plane = plane + jnp.where(spot == 0, columns[:, own + at : own + at + 1], more)
            grad[c, x] = plane
            ends[0, c, x] = plane[0:8]
            ends[1, c, x] = plane[count_y - 8 : count_y]


def final_kernel(whole, ends, mine, got_0, got_1, far, out, wout, bout, tiles, wtile, btile, sems):
    chan, count_x, count_y, _ = whole.shape
    own = chan * count_x
    chan_out = mine.shape[0] // 2
    row = iota((8, lanes), 0)
    one, two = got_0[0:own, :].astype(f32), got_1[0:own, :].astype(f32)
    above, below = pick("gy", two, one), pick("gy", one, two)
    copies = []
    for side, more, line in ((0, above, 0), (1, below, 7)):
        for x in range(count_x):
            for c in range(chan):
                at = x * chan + c
                extra = jnp.where(row == line, more[at : at + 1], 0.0)
                tiles[side, c, x] = ends[side, c, x] + extra
        copies.append(
            pltpu.make_async_copy(
                tiles.at[side],
                out.at[:, :, pl.ds(side * (count_y - 8), 8), :],
                sems.at[side],
            )
        )
        copies[-1].start()
    total = joined(mine[...]) + joined(far[...])
    total = total + (joined(got_0[own:, :]) + joined(got_1[own:, :]))
    total = jnp.concatenate([total, jnp.zeros((lanes - chan_out, lanes), f32)], axis=0)
    total = total.T
    for a in range(3):
        for be in range(9):
            at = (be * 3 + a) * chan
            wtile[a * 9 + be] = total[at : at + chan, :chan_out]
    btile[...] = total[27 * chan : 27 * chan + 1, :chan_out]
    copies.append(pltpu.make_async_copy(wtile, wout, sems.at[2]))
    copies.append(pltpu.make_async_copy(btile, bout, sems.at[3]))
    copies[2].start()
    copies[3].start()
    for copy in copies:
        copy.wait()


def traffic(mib):
    return pl.CostEstimate(flops=0, bytes_accessed=mib << 20, transcendentals=0)


def call(kernel, outs, scratch=(), cost=None, **rest):
    return pl.pallas_call(
        kernel,
        out_shape=outs,
        **rest,
        scratch_shapes=list(scratch),
        cost_estimate=cost,
        compiler_params=pltpu.CompilerParams(vmem_limit_bytes=limit),
    )


def on_device(cells, weight, bias, cotangent):
    chan, count_x, count_y, count_z = cells.shape
    chan_out = weight.shape[0]
    own = chan * count_x
    wide = own + 2 * chan
    depth = 3 * wide + 8
    shape = jax.ShapeDtypeStruct

    kernel = weight.transpose(0, 3, 4, 2, 1)
    placed = jnp.stack(
        [
            jnp.pad(kernel, ((0, 0), (0, 0), (0, 0), (x, count_x - 1 - x), (0, 0)))
            for x in range(count_x)
        ]
    ).reshape(count_x * chan_out, 3, 3 * wide)
    coarse = lax.reduce_precision(bias, 8, 7)
    middle = lax.reduce_precision(bias - coarse, 8, 7)
    fine = bias - coarse - middle
    pieces = jnp.stack([coarse, middle, fine], axis=1).astype(bf16)
    pieces = jnp.pad(jnp.tile(pieces, (count_x, 1))[:, None], ((0, 0), (0, 2), (0, 5)))
    wbig = jnp.concatenate([placed, pieces], axis=2).reshape(count_x * chan_out, 3 * depth)
    wback = placed.reshape(count_x * chan_out, 9 * wide).T

    own_block = shape((own, lanes), bf16)
    edges, row_0, row_1 = call(
        pack_kernel,
        [shape((2 * own, lanes), bf16), own_block, own_block],
        [
            pltpu.VMEM((2 * own, lanes), f32),
        ],
    )(cells)
    pool_x, pool_y, pool_z = cotangent.shape[1:]
    pooled_rows = shape((pool_y * pool_x * chan_out, lanes), f32)
    spread = call(spread_kernel, pooled_rows)(cotangent)
    edges = swapped(edges, "gz", 0)
    row_1 = swapped(jnp.concatenate([row_1, edges]), "gy", 1)
    row_0 = swapped(jnp.concatenate([row_0, edges]), "gy", 0)
    body = chan * count_y
    bundle = shape((body + 32, lanes), bf16)
    side = shape((own, lanes), f32)
    face_0, face_1, left, right, rows = call(
        bundle_kernel, [bundle, bundle, side, side, shape((2 * own, lanes), f32)]
    )(cells, edges, row_0, row_1)
    face_1, face_0 = swapped(face_1, "gx", 1), swapped(face_0, "gx", 0)

    tall = 2 * wide
    bundle = shape((16 + tall + 2 * chan_out, lanes), bf16)
    face = shape((body, lanes), bf16)
    sums, field, row_0, row_1, wpart, wframe, rows, cols = call(
        main_kernel,
        [
            pooled_rows,
            shape(((count_y + 2) * wide, lanes), f32),
            bundle,
            bundle,
            shape((chan_out, lanes), f32),
            shape((2 * chan_out, lanes), bf16),
            shape((2 * own, lanes), f32),
            shape((tall, lanes), f32),
        ],
        [
            pltpu.VMEM(((count_y + 2) * wide, lanes), f32),
            pltpu.VMEM(((count_y + 2) * depth, lanes), bf16),
            pltpu.VMEM((wide, lanes), f32),
            pltpu.VMEM((wide, lanes), f32),
            pltpu.VMEM((6 * wide, lanes), f32),
            pltpu.VMEM((count_x * chan_out, 3 * depth), f32),
            pltpu.VMEM((count_x * chan_out, 8 * lanes), bf16),
            pltpu.VMEM((count_x * chan_out, 8 * lanes), bf16),
        ],
    )(cells, face_0, face_1, rows, left, right, spread, wbig, wback)

    alone = lax.axis_size("gx") != 4
    if alone:
        wpart, far = lax.psum(wpart, "gx"), row_0
    else:
        far = swapped(row_0, "gx", 2)
    row_1, row_0 = swapped(row_1, "gx", 1), swapped(row_0, "gx", 0)
    face_0, face_1 = call(functools.partial(face_kernel, chan), [face, face], cost=traffic(2))(field)
    face_1, face_0 = swapped(face_1, "gx", 1), swapped(face_0, "gx", 0)
    pooled = call(pool_kernel, shape(cotangent.shape, bf16), cost=traffic(8))(sums)
    mine, rows = call(
        functools.partial(x_kernel, alone),
        [shape((2 * own + 2 * chan_out, lanes), bf16), shape((2 * own, lanes), f32)],
    )(wpart, wframe, rows, cols, row_0, row_1, far)
    frame = swapped(mine, "gz", 0)
    bundle = shape((own + 2 * chan_out, lanes), bf16)
    row_0, row_1, mine = call(
        functools.partial(z_kernel, count_y),
        [bundle, bundle, shape((2 * chan_out, lanes), bf16)],
    )(mine, frame, rows)
    row_1, row_0 = swapped(row_1, "gy", 1), swapped(row_0, "gy", 0)
    far = swapped(mine, "gy", 2)
    tiles = (2, chan, count_x, 8, lanes)
    grad, ends = call(grad_kernel, [shape(cells.shape, f32), shape(tiles, f32)], cost=traffic(8))(
        field, face_0, face_1, frame
    )
    vmem, anywhere = pl.BlockSpec(memory_space=pltpu.VMEM), pl.BlockSpec(memory_space=pl.ANY)
    input_grad, wsum, bias_grad = call(
        final_kernel,
        [
            shape(cells.shape, f32),
            shape((27, chan, chan_out), f32),
            shape((1, chan_out), f32),
        ],
        [
            pltpu.VMEM(tiles, f32),
            pltpu.VMEM((27, chan, chan_out), f32),
            pltpu.VMEM((1, chan_out), f32),
            pltpu.SemaphoreType.DMA((4,)),
        ],
        in_specs=[anywhere] + [vmem] * 5,
        out_specs=[anywhere] * 3,
        input_output_aliases={0: 0},
    )(grad, ends, mine, row_0, row_1, far)
    weight_grad = wsum.reshape(3, 3, 3, chan, chan_out).transpose(4, 3, 0, 1, 2)
    return (pooled, weight_grad, bias_grad.reshape(chan_out), input_grad)


def solution(mesh):
    in_specs = (P(None, "gx", "gy", "gz"), P(), P(), P(None, "gx", "gy", "gz"))
    out_specs = (P(None, "gx", "gy", "gz"), P(), P(), P(None, "gx", "gy", "gz"))
    return jax.shard_map(
        on_device, mesh=mesh, in_specs=in_specs, out_specs=out_specs, check_vma=False
    )
```

```python
import functools

import jax
import jax.numpy as jnp
import numpy as np
from jax import lax
from jax.experimental import pallas as pl
from jax.experimental.pallas import tpu as pltpu
from jax.sharding import PartitionSpec as P

axes = ("gx", "gy", "gz")
f32, bf16 = jnp.float32, jnp.bfloat16
log_scale = 0.07
lanes = 128
limit = 48 * 1024 * 1024


def dot(a, b, contract=((1,), (0,))):
    return lax.dot_general(a, b, (contract, ((), ())), preferred_element_type=f32)


def iota(shape, dim):
    return lax.broadcasted_iota(jnp.int32, shape, dim)


def aligned(start, tile):
    return start if isinstance(start, int) else pl.multiple_of(start, tile)


def swapped(array, axis, pairing):
    count = lax.axis_size(axis)
    pairs = []
    for i in range(count):
        if pairing == 2:
            partner = i + count // 2
        else:
            partner = i + 1 if i % 2 == pairing else i - 1
        pairs.append((i, partner % count))
    return lax.ppermute(array, axis, pairs)


def is_even(axis):
    return lax.rem(lax.axis_index(axis), 2) == 0


def pick(axis, if_even, if_odd):
    return jnp.where(is_even(axis), if_even, if_odd)


def split(value):
    coarse = value.astype(bf16)
    return coarse, (value - coarse.astype(f32)).astype(bf16)


def joined(pair):
    half = pair.shape[0] // 2
    return pair[:half].astype(f32) + pair[half:].astype(f32)


def pack_kernel(cells, edges, sent_0, sent_1, rows):
    chan, count_x, count_y, _ = cells.shape
    count = chan * count_x
    row = iota((2 * count, count * lanes), 0)
    lane = iota((2 * count, count * lanes), 1)
    want = jnp.where(row < count, row * lanes, (row - count) * lanes + lanes - 1)
    chosen = (lane == want).astype(f32).astype(bf16)
    planes = [cells[c, x] for x in range(count_x) for c in range(chan)]
    wide = jnp.concatenate(planes, axis=1)
    found = dot(chosen, wide, ((1,), (1,)))
    found = jnp.concatenate([found, jnp.zeros((2 * count, lanes - count_y), f32)], axis=1)
    edges[...] = pltpu.roll(found, 1, 1).astype(bf16)
    for at, plane in enumerate(planes):
        wide_plane = plane.astype(f32)
        rows[at : at + 1, :] = wide_plane[0:1]
        rows[count + at : count + at + 1, :] = wide_plane[count_y - 1 : count_y]
    first, last = rows[0:count, :], rows[count : 2 * count, :]
    sent_0[...] = pick("gy", last, first).astype(bf16)
    sent_1[...] = pick("gy", first, last).astype(bf16)


def bundle_kernel(cells, edges, got_0, got_1, sent_0, sent_1, left, right, rows):
    chan, count_x, count_y, _ = cells.shape
    own = chan * count_x
    above = pick("gy", got_1[...].astype(f32), got_0[...].astype(f32))
    below = pick("gy", got_0[...].astype(f32), got_1[...].astype(f32))
    spot = iota((2 * own, lanes), 1)
    before = pltpu.roll(above[own:], count_y, 1)
    after = pltpu.roll(below[own:], lanes - count_y, 1)
    whole = jnp.where(
        spot == 0, before, jnp.where(spot == count_y + 1, after, edges[...].astype(f32))
    )
    right[...] = whole[0:own]
    left[...] = whole[own : 2 * own]
    rows_above, rows_below = above[0:own], below[0:own]
    rows[0:own, :] = rows_above
    rows[own : 2 * own, :] = rows_below
    zero = jnp.zeros((8, lanes), f32)
    body = chan * count_y
    frames = []
    for x in (0, count_x - 1):
        at = slice(x * chan, x * chan + chan)
        frame = [rows_above[at], rows_below[at], zero]
        frame += [whole[own + x * chan : own + (x + 1) * chan], whole[at], zero]
        frames.append(jnp.concatenate(frame, axis=0))
    even = is_even("gx")
    for ref, odd in ((sent_0, 0), (sent_1, 1)):
        high = even != (odd == 1)
        x = jnp.where(high, count_x - 1, 0)
        for c in range(chan):
            ref[c * count_y : (c + 1) * count_y, :] = cells[c, x]
        ref[body : body + 32, :] = jnp.where(high, frames[1], frames[0]).astype(bf16)


def spread_kernel(cot, spread):
    chan_out, pool_x, pool_y, pool_z = cot.shape
    twice = jnp.where(
        iota((pool_z, lanes), 1) // 2 == iota((pool_z, lanes), 0), 0.125, 0.0
    ).astype(bf16)
    for o in range(chan_out):
        part = dot(cot[o].reshape(pool_x * pool_y, pool_z), twice)
        for x in range(pool_x):
            spread[pl.ds(x * chan_out + o, pool_y, stride=pool_x * chan_out), :] = part[
                x * pool_y : (x + 1) * pool_y
            ]


def pool_kernel(sums, pooled):
    chan_out, pool_x, pool_y, pool_z = pooled.shape
    halves = jnp.where(
        iota((2 * lanes, pool_z), 0) % lanes // 2 == iota((2 * lanes, pool_z), 1), 0.125, 0.0
    ).astype(bf16)
    for o in range(0, chan_out, 4):
        rows = 4 * pool_x * pool_y
        part = sums[o * pool_x * pool_y : o * pool_x * pool_y + rows, :]
        mean = dot(jnp.concatenate(split(part), axis=1), halves) + log_scale * float(np.log(2.0))
        pooled[o : o + 4] = mean.astype(bf16).reshape(4, pool_x, pool_y, pool_z)


def shifted(mid, left, right, y):
    lane = iota(mid.shape, 1)
    low = pltpu.roll(left, (lanes - y) % lanes, 1)
    high = pltpu.roll(right, (lanes - 1 - y) % lanes, 1)
    before = jnp.where(lane == 0, low, pltpu.roll(mid, 1, 1))
    after = jnp.where(lane == lanes - 1, high, pltpu.roll(mid, lanes - 1, 1))
    return [before, mid, after]


def own_kernel(cells, rows, left, right, inner, stage):
    chan, count_x, count_y, _ = cells.shape
    own = chan * count_x
    for x in range(count_x):
        for c in range(chan):
            plane = cells[c, x].astype(f32)
            stage[pl.ds(own + x * chan + c, count_y, stride=own), :] = plane
    stage[0:own, :] = rows[0:own, :]
    stage[(count_y + 1) * own : (count_y + 2) * own, :] = rows[own : 2 * own, :]
    left_cols, right_cols = left[...], right[...]
    for y in range(count_y + 2):
        whole = shifted(stage[y * own : (y + 1) * own, :], left_cols, right_cols, y)
        whole = jnp.concatenate(whole, axis=0)
        inner[y * 3 * own : (y + 1) * 3 * own, :] = whole.astype(bf16)


def main_kernel(
    count_x, got_0, got_1, inner, spread, wbig, wback,
    sums, field, sent_0, sent_1, wpart, wframe, rows_out, cols,
    stage, patches, carry, gram, delta_a, delta_b,
):
    pool_x = count_x // 2
    chan_out = wbig.shape[0] // count_x
    pool_y = spread.shape[0] // (pool_x * chan_out)
    count_y = 2 * pool_y
    own = inner.shape[0] // (3 * (count_y + 2))
    chan = own // count_x
    wide = own + 2 * chan
    outside_rows = 2 * chan
    depth = 3 * outside_rows + 8
    body = chan * count_y
    lane = iota((wide, lanes), 1)
    even = is_even("gx")

    def got(up, start, size):
        one = got_0[start : start + size, :].astype(f32)
        two = got_1[start : start + size, :].astype(f32)
        return jnp.where(even, one, two) if up else jnp.where(even, two, one)

    for side in range(2):
        for c in range(chan):
            plane = got(side == 1, c * count_y, count_y)
            at = outside_rows + side * chan + c
            stage[pl.ds(at, count_y, stride=outside_rows), :] = plane
    rest_low, rest_high = got(False, body, 32), got(True, body, 32)
    both = lambda at: jnp.concatenate(
        [rest_low[at : at + chan], rest_high[at : at + chan]], axis=0
    )
    stage[0:outside_rows, :] = both(0)
    end = (count_y + 1) * outside_rows
    stage[end : end + outside_rows, :] = both(chan)
    left_cols, right_cols = both(16), both(16 + chan)
    for y in range(count_y + 2):
        mid = stage[y * outside_rows : (y + 1) * outside_rows, :]
        whole = shifted(mid, left_cols, right_cols, y) + [jnp.ones((8, lanes), f32)]
        patches[y * depth : (y + 1) * depth, :] = jnp.concatenate(whole, axis=0).astype(bf16)

    carry[...] = jnp.zeros_like(carry)
    gram[...] = jnp.zeros_like(gram)
    cols[...] = jnp.zeros_like(cols)
    pairs = 4
    steps = count_y // (2 * pairs)
    size = 3 * wide
    inside, outside = lane != lanes - 1, lane != 0

    def finish(y, whole, edge):
        first, last = whole[0:wide], whole[2 * wide : 3 * wide]
        inner = (
            whole[wide : 2 * wide]
            + jnp.where(inside, pltpu.roll(first, lanes - 1, 1), 0.0)
            + jnp.where(outside, pltpu.roll(last, 1, 1), 0.0)
        )
        field[pl.ds(aligned(y * wide, 8), wide), :] = inner
        here = lane == y
        edge[0] = jnp.where(here, pltpu.roll(first, y, 1), edge[0])
        edge[1] = jnp.where(here, pltpu.roll(last, y + 1, 1), edge[1])

    def block_of(j):
        columns = []
        for h in range(2):
            y = 2 * j + h
            near = inner[pl.ds(aligned(y * 3 * own, 16), 9 * own), :]
            rest = patches[pl.ds(aligned(y * depth, 16), 3 * depth), :]
            columns.append(jnp.concatenate([near, rest], axis=0))
        return jnp.concatenate(columns, axis=1)

    def forward(i, k, ref):
        j = i * pairs + k
        preact = dot(wbig[...], block_of(j))
        slope = jnp.tanh(5.0 * preact)
        linear = jnp.maximum(preact, 0.3 * preact)
        factor = 1.0 + jnp.abs(slope)
        here = spread[pl.ds(aligned(j * pool_x * chan_out, 8), pool_x * chan_out), :]
        slope = 0.65 + 0.35 * slope
        delta = []
        for x in range(pool_x):
            top, mid = 2 * x * chan_out, (2 * x + 1) * chan_out
            end = mid + chan_out
            times = here[x * chan_out : (x + 1) * chan_out]
            times = jnp.concatenate([times, times], axis=1)
            delta.append((slope[top:mid] * times).astype(bf16))
            delta.append((slope[mid:end] * times).astype(bf16))
            total = linear[top:mid] + linear[mid:end]
            total = total[:, :lanes] + total[:, lanes:]
            prod = factor[top:mid] * factor[mid:end]
            prod = prod[:, :lanes] * prod[:, lanes:]
            total = total - log_scale * jnp.log(prod)
            sums[pl.ds(x * pool_y + j, chan_out, stride=pool_x * pool_y), :] = total
        ref[:, 2 * k * lanes : 2 * (k + 1) * lanes] = jnp.concatenate(delta, axis=0)

    def backward(i, k, ref, held, edge):
        j = i * pairs + k
        parts = dot(wback[...], ref[:, 2 * k * lanes : 2 * (k + 1) * lanes])
        part = lambda b, h: parts[b * size : (b + 1) * size, h * lanes : (h + 1) * lanes]
        finish(2 * j, held[0] + part(0, 0), edge)
        finish(2 * j + 1, held[1] + part(1, 0) + part(0, 1), edge)
        held[0] = part(2, 0) + part(1, 1)
        held[1] = part(2, 1)

    def weigh(i, ref):
        blocks = jnp.concatenate([block_of(i * pairs + k) for k in range(pairs)], axis=1)
        return dot(ref[...], blocks, ((1,), (1,)))

    def opened():
        return (
            [carry[0:size, :], carry[size : 2 * size, :]],
            [cols[0:wide, :], cols[wide : 2 * wide, :]],
        )

    def closed(held, edge):
        carry[0:size, :] = held[0]
        carry[size : 2 * size, :] = held[1]
        cols[0:wide, :] = edge[0]
        cols[wide : 2 * wide, :] = edge[1]

    def step(t, _):
        held, edge = opened()
        total = gram[...] + weigh(2 * t, delta_a)
        for k in range(pairs):
            forward(2 * t + 1, k, delta_b)
            backward(2 * t, k, delta_a, held, edge)
        total = total + weigh(2 * t + 1, delta_b)
        for k in range(pairs):
            forward(2 * t + 2, k, delta_a)
            backward(2 * t + 1, k, delta_b, held, edge)
        gram[...] = total
        closed(held, edge)
        return 0

    for k in range(pairs):
        forward(0, k, delta_a)
    lax.fori_loop(0, steps // 2 - 1, step, 0)
    held, edge = opened()
    total = gram[...] + weigh(steps - 2, delta_a)
    for k in range(pairs):
        forward(steps - 1, k, delta_b)
        backward(steps - 2, k, delta_a, held, edge)
    gram[...] = total + weigh(steps - 1, delta_b)
    for k in range(pairs):
        backward(steps - 1, k, delta_b, held, edge)
    finish(count_y, held[0], edge)
    finish(count_y + 1, held[1], edge)
    closed(held, edge)

    span = gram.shape[1]
    spot = iota((chan_out, 2 * lanes), 1)
    first = 9 * own
    turn = lambda part, shift: pltpu.roll(part, (2 * lanes - shift) % (2 * lanes), 1)
    straight, turned, extra = 0.0, 0.0, 0.0
    for x in range(count_x):
        part = gram[x * chan_out : (x + 1) * chan_out, :]
        part = jnp.concatenate([part, jnp.zeros((chan_out, 2 * lanes - span), f32)], axis=1)
        straight = straight + part
        moved = turn(part, chan * (x - 1)) if x != 1 else part
        a = spot % own // chan
        turned = turned + jnp.where((a + x >= 1) & (a + x <= count_x), moved, 0.0)
        if x == 0:
            extra = extra + jnp.where((spot - first) % outside_rows < chan, part, 0.0)
        if x == count_x - 1:
            extra = extra + jnp.where((spot - first) % outside_rows >= chan, part, 0.0)
    group = 3 * chan
    tight = jnp.zeros((chan_out, 2 * lanes), f32)
    for b in range(3):
        for e in range(3):
            at = (b * 3 + e) * group
            here = spot // group == b * 3 + e
            value = turn(turned, b * 3 * own + e * own - at)
            source = first + b * depth + e * outside_rows
            low, high = turn(extra, source - at), turn(extra, source - at - chan)
            a = (spot - at) // chan
            value = value + jnp.where(a == 0, low, 0.0) + jnp.where(a == 2, high, 0.0)
            tight = jnp.where(here, value, tight)
    bias_at = first + 3 * outside_rows
    tight = jnp.where(spot == 9 * group, turn(straight, bias_at - 9 * group), tight)
    tight = tight[:, :lanes]
    wpart[...] = tight
    sides = jnp.concatenate(split(tight), axis=0)
    wframe[...] = sides

    ends = [field[0:wide, :], field[(count_y + 1) * wide : (count_y + 2) * wide, :]]
    rows_out[...] = jnp.concatenate([end[chan : chan + own] for end in ends], axis=0)
    tall = cols.shape[0]
    found = cols[...].astype(bf16)
    zero = jnp.zeros((8, lanes), f32)
    for ref, odd in ((sent_0, 0), (sent_1, 1)):
        high = even != (odd == 1)
        low_frame, high_frame = [
            jnp.concatenate([end[x * chan : (x + 1) * chan] for end in ends] + [zero], axis=0)
            for x in (0, count_x + 1)
        ]
        ref[0:16, :] = jnp.where(high, high_frame, low_frame).astype(bf16)
        ref[16 : 16 + tall, :] = found
        ref[16 + tall :, :] = sides


def face_kernel(chan, field, face_0, face_1):
    count_y = face_0.shape[0] // chan
    wide = field.shape[0] // (count_y + 2)
    even = is_even("gx")
    for c in range(chan):
        low, high = [
            field[pl.ds(wide + at + c, count_y, stride=wide), :] for at in (0, wide - chan)
        ]
        place = slice(c * count_y, (c + 1) * count_y)
        face_0[place, :] = jnp.where(even, high, low).astype(bf16)
        face_1[place, :] = jnp.where(even, low, high).astype(bf16)


def x_kernel(alone, wpart, wframe, rows, cols, got_0, got_1, far, frame, rows_out):
    tall = cols.shape[0]
    own = rows.shape[0] // 2
    wide = tall // 2
    chan = (wide - own) // 2
    if alone:
        total = wpart[...]
    else:
        total = joined(wframe[...]) + joined(far[16 + tall :, :])
        total = total + (joined(got_0[16 + tall :, :]) + joined(got_1[16 + tall :, :]))
    frame[2 * own :, :] = jnp.concatenate(split(total), axis=0)
    one, two = got_0[0 : 16 + tall, :].astype(f32), got_1[0 : 16 + tall, :].astype(f32)
    from_low, from_high = pick("gx", two, one), pick("gx", one, two)
    mid = jnp.zeros((own - 2 * chan, lanes), f32)
    found = []
    for top in (0, wide):
        more = [from_low[16 + top + chan + own : 16 + top + wide], mid]
        more.append(from_high[16 + top : 16 + top + chan])
        found.append(cols[top + chan : top + chan + own, :] + jnp.concatenate(more, axis=0))
    frame[0 : 2 * own, :] = jnp.concatenate(found, axis=0).astype(bf16)
    for at in (0, 1):
        more = [from_low[at * chan : (at + 1) * chan], mid, from_high[at * chan : (at + 1) * chan]]
        place = slice(at * own, (at + 1) * own)
        rows_out[place, :] = rows[place, :] + jnp.concatenate(more, axis=0)


def z_kernel(count_y, mine, got, rows, sent_0, sent_1, wframe):
    own = rows.shape[0] // 2
    total = joined(mine[2 * own :, :]) + joined(got[2 * own :, :])
    sides = jnp.concatenate(split(total), axis=0)
    wframe[...] = sides
    last = got[0:own, :].astype(f32)
    first = got[own : 2 * own, :].astype(f32)
    spot = iota((own, lanes), 1)
    both = []
    for at, line in ((0, 0), (1, count_y + 1)):
        more = jnp.where(spot == lanes - 1, pltpu.roll(last, lanes - 1 - line, 1), 0.0)
        turned = pltpu.roll(first, lanes - line, 1) if line else first
        more = jnp.where(spot == 0, turned, more)
        both.append(rows[at * own : (at + 1) * own, :] + more)
    sent_0[0:own, :] = pick("gy", both[1], both[0]).astype(bf16)
    sent_1[0:own, :] = pick("gy", both[0], both[1]).astype(bf16)
    for ref in (sent_0, sent_1):
        ref[own:, :] = sides


def grad_kernel(field, face_0, face_1, got, grad, ends):
    chan, count_x, count_y, _ = grad.shape
    own = chan * count_x
    wide = own + 2 * chan
    spot = iota((count_y, lanes), 1)
    columns = pltpu.roll(got[0 : 2 * own, :].astype(f32), lanes - 1, 1)
    columns = jnp.concatenate([columns, jnp.zeros((lanes - 2 * own, lanes), f32)], axis=0)
    columns = columns.T[0:count_y]
    for x in range(count_x):
        for c in range(chan):
            at = x * chan + c
            plane = field[pl.ds(wide + chan + at, count_y, stride=wide), :]
            place = slice(c * count_y, (c + 1) * count_y)
            if x == 0:
                plane = plane + pick("gx", face_1[place, :].astype(f32), face_0[place, :].astype(f32))
            if x == count_x - 1:
                plane = plane + pick("gx", face_0[place, :].astype(f32), face_1[place, :].astype(f32))
            more = jnp.where(spot == lanes - 1, columns[:, at : at + 1], 0.0)
            plane = plane + jnp.where(spot == 0, columns[:, own + at : own + at + 1], more)
            grad[c, x] = plane
            ends[0, c, x] = plane[0:8]
            ends[1, c, x] = plane[count_y - 8 : count_y]


def final_kernel(whole, ends, mine, got_0, got_1, far, out, wout, bout, tiles, wtile, btile, sems):
    chan, count_x, count_y, _ = whole.shape
    own = chan * count_x
    chan_out = mine.shape[0] // 2
    row = iota((8, lanes), 0)
    one, two = got_0[0:own, :].astype(f32), got_1[0:own, :].astype(f32)
    above, below = pick("gy", two, one), pick("gy", one, two)
    copies = []
    for side, more, line in ((0, above, 0), (1, below, 7)):
        for x in range(count_x):
            for c in range(chan):
                at = x * chan + c
                extra = jnp.where(row == line, more[at : at + 1], 0.0)
                tiles[side, c, x] = ends[side, c, x] + extra
        copies.append(
            pltpu.make_async_copy(
                tiles.at[side],
                out.at[:, :, pl.ds(side * (count_y - 8), 8), :],
                sems.at[side],
            )
        )
        copies[-1].start()
    total = joined(mine[...]) + joined(far[...])
    total = total + (joined(got_0[own:, :]) + joined(got_1[own:, :]))
    total = jnp.concatenate([total, jnp.zeros((lanes - chan_out, lanes), f32)], axis=0)
    total = total.T
    for a in range(3):
        for be in range(9):
            at = (be * 3 + a) * chan
            wtile[a * 9 + be] = total[at : at + chan, :chan_out]
    btile[...] = total[27 * chan : 27 * chan + 1, :chan_out]
    copies.append(pltpu.make_async_copy(wtile, wout, sems.at[2]))
    copies.append(pltpu.make_async_copy(btile, bout, sems.at[3]))
    copies[2].start()
    copies[3].start()
    for copy in copies:
        copy.wait()


def traffic(mib):
    return pl.CostEstimate(flops=0, bytes_accessed=mib << 20, transcendentals=0)


def call(kernel, outs, scratch=(), cost=None, **rest):
    return pl.pallas_call(
        kernel,
        out_shape=outs,
        **rest,
        scratch_shapes=list(scratch),
        cost_estimate=cost,
        compiler_params=pltpu.CompilerParams(vmem_limit_bytes=limit),
    )


def on_device(cells, weight, bias, cotangent):
    chan, count_x, count_y, count_z = cells.shape
    chan_out = weight.shape[0]
    own = chan * count_x
    wide = own + 2 * chan
    depth = 6 * chan + 8
    shape = jax.ShapeDtypeStruct

    kernel = weight.transpose(0, 3, 4, 2, 1)
    placed = jnp.stack(
        [
            jnp.pad(kernel, ((0, 0), (0, 0), (0, 0), (x, count_x - 1 - x), (0, 0)))
            for x in range(count_x)
        ]
    ).reshape(count_x * chan_out, 3, 3, count_x + 2, chan)
    coarse = lax.reduce_precision(bias, 8, 7)
    middle = lax.reduce_precision(bias - coarse, 8, 7)
    fine = bias - coarse - middle
    pieces = jnp.stack([coarse, middle, fine], axis=1).astype(bf16)
    pieces = jnp.pad(jnp.tile(pieces, (count_x, 1))[:, None], ((0, 0), (0, 2), (0, 5)))
    near = placed[:, :, :, 1 : count_x + 1].reshape(count_x * chan_out, 9 * own)
    rest = jnp.concatenate([placed[:, :, :, :1], placed[:, :, :, count_x + 1 :]], axis=3)
    rest = jnp.concatenate([rest.reshape(count_x * chan_out, 3, 6 * chan), pieces], axis=2)
    wbig = jnp.concatenate([near, rest.reshape(count_x * chan_out, 3 * depth)], axis=1)
    wback = placed.reshape(count_x * chan_out, 9 * wide).T

    own_block = shape((own, lanes), bf16)
    edges, row_0, row_1 = call(
        pack_kernel,
        [shape((2 * own, lanes), bf16), own_block, own_block],
        [
            pltpu.VMEM((2 * own, lanes), f32),
        ],
    )(cells)
    pool_x, pool_y, pool_z = cotangent.shape[1:]
    pooled_rows = shape((pool_y * pool_x * chan_out, lanes), f32)
    spread = call(spread_kernel, pooled_rows)(cotangent)
    edges = swapped(edges, "gz", 0)
    row_1 = swapped(jnp.concatenate([row_1, edges]), "gy", 1)
    row_0 = swapped(jnp.concatenate([row_0, edges]), "gy", 0)
    body = chan * count_y
    bundle = shape((body + 32, lanes), bf16)
    side = shape((own, lanes), f32)
    face_0, face_1, left, right, rows = call(
        bundle_kernel, [bundle, bundle, side, side, shape((2 * own, lanes), f32)]
    )(cells, edges, row_0, row_1)
    face_1, face_0 = swapped(face_1, "gx", 1), swapped(face_0, "gx", 0)
    inner = call(
        own_kernel,
        shape(((count_y + 2) * 3 * own, lanes), bf16),
        [pltpu.VMEM(((count_y + 2) * own, lanes), f32)],
        traffic(4),
    )(cells, rows, left, right)

    tall = 2 * wide
    bundle = shape((16 + tall + 2 * chan_out, lanes), bf16)
    face = shape((body, lanes), bf16)
    sums, field, row_0, row_1, wpart, wframe, rows, cols = call(
        functools.partial(main_kernel, count_x),
        [
            pooled_rows,
            shape(((count_y + 2) * wide, lanes), f32),
            bundle,
            bundle,
            shape((chan_out, lanes), f32),
            shape((2 * chan_out, lanes), bf16),
            shape((2 * own, lanes), f32),
            shape((tall, lanes), f32),
        ],
        [
            pltpu.VMEM(((count_y + 2) * 2 * chan, lanes), f32),
            pltpu.VMEM(((count_y + 2) * depth, lanes), bf16),
            pltpu.VMEM((6 * wide, lanes), f32),
            pltpu.VMEM((count_x * chan_out, 9 * own + 3 * depth), f32),
            pltpu.VMEM((count_x * chan_out, 8 * lanes), bf16),
            pltpu.VMEM((count_x * chan_out, 8 * lanes), bf16),
        ],
    )(face_0, face_1, inner, spread, wbig, wback)

    alone = lax.axis_size("gx") != 4
    if alone:
        wpart, far = lax.psum(wpart, "gx"), row_0
    else:
        far = swapped(row_0, "gx", 2)
    row_1, row_0 = swapped(row_1, "gx", 1), swapped(row_0, "gx", 0)
    face_0, face_1 = call(functools.partial(face_kernel, chan), [face, face], cost=traffic(2))(field)
    face_1, face_0 = swapped(face_1, "gx", 1), swapped(face_0, "gx", 0)
    pooled = call(pool_kernel, shape(cotangent.shape, bf16), cost=traffic(8))(sums)
    mine, rows = call(
        functools.partial(x_kernel, alone),
        [shape((2 * own + 2 * chan_out, lanes), bf16), shape((2 * own, lanes), f32)],
    )(wpart, wframe, rows, cols, row_0, row_1, far)
    frame = swapped(mine, "gz", 0)
    bundle = shape((own + 2 * chan_out, lanes), bf16)
    row_0, row_1, mine = call(
        functools.partial(z_kernel, count_y),
        [bundle, bundle, shape((2 * chan_out, lanes), bf16)],
    )(mine, frame, rows)
    row_1, row_0 = swapped(row_1, "gy", 1), swapped(row_0, "gy", 0)
    far = swapped(mine, "gy", 2)
    tiles = (2, chan, count_x, 8, lanes)
    grad, ends = call(grad_kernel, [shape(cells.shape, f32), shape(tiles, f32)], cost=traffic(8))(
        field, face_0, face_1, frame
    )
    vmem, anywhere = pl.BlockSpec(memory_space=pltpu.VMEM), pl.BlockSpec(memory_space=pl.ANY)
    input_grad, wsum, bias_grad = call(
        final_kernel,
        [
            shape(cells.shape, f32),
            shape((27, chan, chan_out), f32),
            shape((1, chan_out), f32),
        ],
        [
            pltpu.VMEM(tiles, f32),
            pltpu.VMEM((27, chan, chan_out), f32),
            pltpu.VMEM((1, chan_out), f32),
            pltpu.SemaphoreType.DMA((4,)),
        ],
        in_specs=[anywhere] + [vmem] * 5,
        out_specs=[anywhere] * 3,
        input_output_aliases={0: 0},
    )(grad, ends, mine, row_0, row_1, far)
    weight_grad = wsum.reshape(3, 3, 3, chan, chan_out).transpose(4, 3, 0, 1, 2)
    return (pooled, weight_grad, bias_grad.reshape(chan_out), input_grad)


def solution(mesh):
    in_specs = (P(None, "gx", "gy", "gz"), P(), P(), P(None, "gx", "gy", "gz"))
    out_specs = (P(None, "gx", "gy", "gz"), P(), P(), P(None, "gx", "gy", "gz"))
    return jax.shard_map(
        on_device, mesh=mesh, in_specs=in_specs, out_specs=out_specs, check_vma=False
    )
```

```python
import functools

import jax
import jax.numpy as jnp
import numpy as np
from jax import lax
from jax.experimental import pallas as pl
from jax.experimental.pallas import tpu as pltpu
from jax.sharding import PartitionSpec as P

axes = ("gx", "gy", "gz")
f32, bf16 = jnp.float32, jnp.bfloat16
log_scale = 0.07
lanes = 128
limit = 48 * 1024 * 1024


def dot(a, b, contract=((1,), (0,))):
    return lax.dot_general(a, b, (contract, ((), ())), preferred_element_type=f32)


def iota(shape, dim):
    return lax.broadcasted_iota(jnp.int32, shape, dim)


def aligned(start, tile):
    return start if isinstance(start, int) else pl.multiple_of(start, tile)


def swapped(array, axis, pairing):
    count = lax.axis_size(axis)
    pairs = []
    for i in range(count):
        if pairing == 2:
            partner = i + count // 2
        else:
            partner = i + 1 if i % 2 == pairing else i - 1
        pairs.append((i, partner % count))
    return lax.ppermute(array, axis, pairs)


def is_even(axis):
    return lax.rem(lax.axis_index(axis), 2) == 0


def pick(axis, if_even, if_odd):
    return jnp.where(is_even(axis), if_even, if_odd)


def split(value):
    coarse = value.astype(bf16)
    return coarse, (value - coarse.astype(f32)).astype(bf16)


def joined(pair):
    half = pair.shape[0] // 2
    return pair[:half].astype(f32) + pair[half:].astype(f32)


def pack_kernel(cells, edges, rows):
    chan, count_x, count_y, _ = cells.shape
    count = chan * count_x
    row = iota((2 * count, count * lanes), 0)
    lane = iota((2 * count, count * lanes), 1)
    want = jnp.where(row < count, row * lanes, (row - count) * lanes + lanes - 1)
    chosen = (lane == want).astype(f32).astype(bf16)
    planes = [cells[c, x] for x in range(count_x) for c in range(chan)]
    wide = jnp.concatenate(planes, axis=1)
    found = dot(chosen, wide, ((1,), (1,)))
    found = jnp.concatenate([found, jnp.zeros((2 * count, lanes - count_y), f32)], axis=1)
    edges[...] = pltpu.roll(found, 1, 1).astype(bf16)
    for at, plane in enumerate(planes):
        wide_plane = plane.astype(f32)
        rows[at : at + 1, :] = wide_plane[0:1]
        rows[count + at : count + at + 1, :] = wide_plane[count_y - 1 : count_y]


def bundle_kernel(cells, edges, sent_0, sent_1, left, right):
    chan, count_x, count_y, _ = cells.shape
    own = chan * count_x
    whole = edges[...].astype(f32)
    right[...] = whole[0:own]
    left[...] = whole[own : 2 * own]
    zero = jnp.zeros((8, lanes), f32)
    body = chan * count_y
    frames = []
    for x in (0, count_x - 1):
        at = slice(x * chan, x * chan + chan)
        frames.append(jnp.concatenate([whole[own + x * chan :][:chan], whole[at], zero], axis=0))
    even = is_even("gx")
    for ref, odd in ((sent_0, 0), (sent_1, 1)):
        high = even != (odd == 1)
        x = jnp.where(high, count_x - 1, 0)
        for c in range(chan):
            ref[c * count_y : (c + 1) * count_y, :] = cells[c, x]
        ref[body : body + 16, :] = jnp.where(high, frames[1], frames[0]).astype(bf16)


def from_sides(got_0, got_1, start, size):
    one = got_0[start : start + size, :].astype(f32)
    two = got_1[start : start + size, :].astype(f32)
    return pick("gx", two, one), pick("gx", one, two)


def rows_kernel(chan, rows, left, right, got_0, got_1, sent_0, sent_1):
    own = rows.shape[0] // 2
    body = got_0.shape[0] - 16
    count_y = body // chan
    low, high = from_sides(got_0, got_1, body, 16)
    edges = []
    for ref, at in ((left, 0), (right, chan)):
        edges += [ref[...], low[at : at + chan], high[at : at + chan]]
    edges.append(jnp.zeros((8, lanes), f32))
    low, high = from_sides(got_0, got_1, 0, body)
    both = []
    for at, line in ((0, 0), (own, count_y - 1)):
        outer = [
            plane[c * count_y + line : c * count_y + line + 1]
            for plane in (low, high)
            for c in range(chan)
        ]
        both.append(jnp.concatenate([rows[at : at + own, :]] + outer + edges, axis=0))
    sent_0[...] = pick("gy", both[1], both[0]).astype(bf16)
    sent_1[...] = pick("gy", both[0], both[1]).astype(bf16)


def spread_kernel(cot, spread):
    chan_out, pool_x, pool_y, pool_z = cot.shape
    twice = jnp.where(
        iota((pool_z, lanes), 1) // 2 == iota((pool_z, lanes), 0), 0.125, 0.0
    ).astype(bf16)
    for o in range(chan_out):
        part = dot(cot[o].reshape(pool_x * pool_y, pool_z), twice)
        for x in range(pool_x):
            spread[pl.ds(x * chan_out + o, pool_y, stride=pool_x * chan_out), :] = part[
                x * pool_y : (x + 1) * pool_y
            ]


def pool_kernel(edge, sums, outer_sums, pooled):
    chan_out, pool_x, pool_y, pool_z = pooled.shape
    halves = jnp.where(
        iota((2 * lanes, pool_z), 0) % lanes // 2 == iota((2 * lanes, pool_z), 1), 0.125, 0.0
    ).astype(bf16)
    for o in range(0, chan_out, 4):
        rows = 4 * pool_x * pool_y
        part = sums[o * pool_x * pool_y : o * pool_x * pool_y + rows, :]
        at = iota((rows, lanes), 0) % pool_y
        near = (at >= edge) & (at < pool_y - edge)
        part = jnp.where(near, part, outer_sums[o * pool_x * pool_y : o * pool_x * pool_y + rows, :])
        mean = dot(jnp.concatenate(split(part), axis=1), halves) + log_scale * float(np.log(2.0))
        pooled[o : o + 4] = mean.astype(bf16).reshape(4, pool_x, pool_y, pool_z)


def shifted(mid, left, right, y):
    lane = iota(mid.shape, 1)
    low = pltpu.roll(left, (lanes - y) % lanes, 1)
    high = pltpu.roll(right, (lanes - 1 - y) % lanes, 1)
    before = jnp.where(lane == 0, low, pltpu.roll(mid, 1, 1))
    after = jnp.where(lane == lanes - 1, high, pltpu.roll(mid, lanes - 1, 1))
    return [before, mid, after]


def own_kernel(cells, left, right, inner, stage):
    chan, count_x, count_y, _ = cells.shape
    own = chan * count_x
    for x in range(count_x):
        for c in range(chan):
            plane = cells[c, x].astype(f32)
            stage[pl.ds(own + x * chan + c, count_y, stride=own), :] = plane
    left_cols, right_cols = left[...], right[...]
    for y in range(1, count_y + 1):
        whole = shifted(stage[y * own : (y + 1) * own, :], left_cols, right_cols, y)
        whole = jnp.concatenate(whole, axis=0)
        inner[y * 3 * own : (y + 1) * 3 * own, :] = whole.astype(bf16)


pairs = 4


def sizes_of(count_x, inner, spread, wbig):
    pool_x = count_x // 2
    chan_out = wbig.shape[0] // count_x
    pool_y = spread.shape[0] // (pool_x * chan_out)
    own = inner.shape[0] // (3 * (2 * pool_y + 2))
    return pool_x, chan_out, pool_y, own, own // count_x


def worker(count_x, pool_x, chan_out, pool_y, own, chan, near_of, rest_of, refs):
    spread, wbig, wback, sums, field = refs
    wide = own + 2 * chan
    size = 3 * wide
    lane = iota((wide, lanes), 1)
    inside, outside = lane != lanes - 1, lane != 0

    def finish(y, whole, edge):
        first, last = whole[0:wide], whole[2 * wide : 3 * wide]
        inner = (
            whole[wide : 2 * wide]
            + jnp.where(inside, pltpu.roll(first, lanes - 1, 1), 0.0)
            + jnp.where(outside, pltpu.roll(last, 1, 1), 0.0)
        )
        field[pl.ds(aligned(y * wide, 8), wide), :] = inner
        here = lane == y
        edge[0] = jnp.where(here, pltpu.roll(first, y, 1), edge[0])
        edge[1] = jnp.where(here, pltpu.roll(last, y + 1, 1), edge[1])

    def block_of(j):
        columns = [
            jnp.concatenate([near_of(2 * j + h), rest_of(2 * j + h)], axis=0) for h in range(2)
        ]
        return jnp.concatenate(columns, axis=1)

    def forward(i, k, ref):
        j = i * pairs + k
        preact = dot(wbig[...], block_of(j))
        slope = jnp.tanh(5.0 * preact)
        linear = jnp.maximum(preact, 0.3 * preact)
        factor = 1.0 + jnp.abs(slope)
        here = spread[pl.ds(aligned(j * pool_x * chan_out, 8), pool_x * chan_out), :]
        slope = 0.65 + 0.35 * slope
        delta = []
        for x in range(pool_x):
            top, mid = 2 * x * chan_out, (2 * x + 1) * chan_out
            end = mid + chan_out
            times = here[x * chan_out : (x + 1) * chan_out]
            times = jnp.concatenate([times, times], axis=1)
            delta.append((slope[top:mid] * times).astype(bf16))
            delta.append((slope[mid:end] * times).astype(bf16))
            total = linear[top:mid] + linear[mid:end]
            total = total[:, :lanes] + total[:, lanes:]
            prod = factor[top:mid] * factor[mid:end]
            prod = prod[:, :lanes] * prod[:, lanes:]
            total = total - log_scale * jnp.log(prod)
            sums[pl.ds(x * pool_y + j, chan_out, stride=pool_x * pool_y), :] = total
        ref[:, 2 * k * lanes : 2 * (k + 1) * lanes] = jnp.concatenate(delta, axis=0)

    def backward(i, k, ref, held, edge):
        j = i * pairs + k
        parts = dot(wback[...], ref[:, 2 * k * lanes : 2 * (k + 1) * lanes])
        part = lambda b, h: parts[b * size : (b + 1) * size, h * lanes : (h + 1) * lanes]
        finish(2 * j, held[0] + part(0, 0), edge)
        finish(2 * j + 1, held[1] + part(1, 0) + part(0, 1), edge)
        held[0] = part(2, 0) + part(1, 1)
        held[1] = part(2, 1)

    def weigh(i, ref):
        blocks = jnp.concatenate([block_of(i * pairs + k) for k in range(pairs)], axis=1)
        return dot(ref[...], blocks, ((1,), (1,)))

    return finish, forward, backward, weigh


def inner_kernel(
    count_x, got_0, got_1, inner, spread, wbig, wback,
    sums, field, patches, cols, gram, stage, carry, delta_a, delta_b,
):
    shape = sizes_of(count_x, inner, spread, wbig)
    pool_x, chan_out, pool_y, own, chan = shape
    count_y = 2 * pool_y
    wide = own + 2 * chan
    size = 3 * wide
    outside_rows = 2 * chan
    depth = 3 * outside_rows + 8
    body = chan * count_y
    for side, planes in enumerate(from_sides(got_0, got_1, 0, body)):
        for c in range(chan):
            at = outside_rows + side * chan + c
            plane = planes[c * count_y : (c + 1) * count_y]
            stage[pl.ds(at, count_y, stride=outside_rows), :] = plane
    low, high = from_sides(got_0, got_1, body, 16)
    left_cols, right_cols = [
        jnp.concatenate([low[at : at + chan], high[at : at + chan]], axis=0) for at in (0, chan)
    ]
    for y in range(1, count_y + 1):
        mid = stage[y * outside_rows : (y + 1) * outside_rows, :]
        whole = shifted(mid, left_cols, right_cols, y) + [jnp.ones((8, lanes), f32)]
        patches[y * depth : (y + 1) * depth, :] = jnp.concatenate(whole, axis=0).astype(bf16)

    def near_of(y):
        return inner[pl.ds(aligned(y * 3 * own, 16), 9 * own), :]

    def rest_of(y):
        return patches[pl.ds(aligned(y * depth, 16), 3 * depth), :]

    finish, forward, backward, weigh = worker(
        count_x, *shape, near_of, rest_of, (spread, wbig, wback, sums, field)
    )
    carry[...] = jnp.zeros_like(carry)
    gram[...] = jnp.zeros_like(gram)
    cols[...] = jnp.zeros_like(cols)

    def opened():
        return (
            [carry[0:size, :], carry[size : 2 * size, :]],
            [cols[0:wide, :], cols[wide : 2 * wide, :]],
        )

    def closed(held, edge):
        carry[0:size, :] = held[0]
        carry[size : 2 * size, :] = held[1]
        cols[0:wide, :] = edge[0]
        cols[wide : 2 * wide, :] = edge[1]

    def both(at):
        held, edge = opened()
        total = gram[...] + weigh(at, delta_a)
        for k in range(pairs):
            forward(at + 1, k, delta_b)
            backward(at, k, delta_a, held, edge)
        return held, edge, total + weigh(at + 1, delta_b)

    def step(t, _):
        at = 2 * t + 1
        held, edge, total = both(at)
        for k in range(pairs):
            forward(at + 2, k, delta_a)
            backward(at + 1, k, delta_b, held, edge)
        gram[...] = total
        closed(held, edge)
        return 0

    steps = count_y // (2 * pairs)
    for k in range(pairs):
        forward(1, k, delta_a)
    lax.fori_loop(0, steps // 2 - 2, step, 0)
    held, edge, total = both(steps - 3)
    gram[...] = total
    for k in range(pairs):
        backward(steps - 2, k, delta_b, held, edge)
    end = (steps - 1) * 2 * pairs
    finish(end, held[0], edge)
    finish(end + 1, held[1], edge)
    closed(held, edge)


def main_kernel(
    count_x, row_0, row_1, inner, patches, inner_cols, inner_gram, spread, wbig, wback,
    sums, field, sent_0, sent_1, wpart, wframe, rows_out, cols,
    near, rest, gram, delta_a, delta_b,
):
    shape = sizes_of(count_x, inner, spread, wbig)
    pool_x, chan_out, pool_y, own, chan = shape
    count_y = 2 * pool_y
    wide = own + 2 * chan
    size = 3 * wide
    outside_rows = 2 * chan
    depth = 3 * outside_rows + 8
    even = is_even("gx")
    span_y = 2 * pairs
    top = span_y + 2
    start = count_y - span_y
    for ref, source, height in ((near, inner, 3 * own), (rest, patches, depth)):
        ref[height : top * height, :] = source[height : top * height, :]
        last = (2 * top - 1) * height
        ref[top * height : last, :] = source[start * height : (count_y + 1) * height, :]
    one, two = row_0[...].astype(f32), row_1[...].astype(f32)
    above, below = pick("gy", two, one), pick("gy", one, two)
    for at, got, line in ((0, above, count_y), (2 * top - 1, below, 1)):
        left, right = got[wide : 2 * wide], got[2 * wide : 3 * wide]
        whole = jnp.concatenate(shifted(got[:own], left[:own], right[:own], line), axis=0)
        near[at * 3 * own : (at + 1) * 3 * own, :] = whole.astype(bf16)
        whole = shifted(got[own:wide], left[own:], right[own:], line)
        whole = jnp.concatenate(whole + [jnp.ones((8, lanes), f32)], axis=0)
        rest[at * depth : (at + 1) * depth, :] = whole.astype(bf16)

    def place(y):
        return y if y < top else y - start + top

    def near_of(y):
        return near[place(y) * 3 * own : (place(y) + 3) * 3 * own, :]

    def rest_of(y):
        return rest[place(y) * depth : (place(y) + 3) * depth, :]

    finish, forward, backward, weigh = worker(
        count_x, *shape, near_of, rest_of, (spread, wbig, wback, sums, field)
    )
    final = count_y // span_y - 1
    zero = jnp.zeros((size, lanes), f32)
    held, edge = [zero, zero], [inner_cols[0:wide, :], inner_cols[wide : 2 * wide, :]]
    extra = [jnp.zeros((wide, lanes), f32)] * 2
    for k in range(pairs):
        forward(0, k, delta_a)
    for k in range(pairs):
        forward(final, k, delta_b)
        backward(0, k, delta_a, held, extra)
    total = inner_gram[...] + weigh(0, delta_a)
    finish(span_y, held[0], extra)
    finish(span_y + 1, held[1], extra)
    held = [zero, zero]
    for k in range(pairs):
        backward(final, k, delta_b, held, extra)
    gram[...] = total + weigh(final, delta_b)
    finish(count_y, held[0], extra)
    finish(count_y + 1, held[1], extra)
    cols[0:wide, :] = edge[0] + extra[0]
    cols[wide : 2 * wide, :] = edge[1] + extra[1]

    span = gram.shape[1]
    spot = iota((chan_out, 2 * lanes), 1)
    first = 9 * own
    turn = lambda part, shift: pltpu.roll(part, (2 * lanes - shift) % (2 * lanes), 1)
    straight, turned, extra = 0.0, 0.0, 0.0
    for x in range(count_x):
        part = gram[x * chan_out : (x + 1) * chan_out, :]
        part = jnp.concatenate([part, jnp.zeros((chan_out, 2 * lanes - span), f32)], axis=1)
        straight = straight + part
        moved = turn(part, chan * (x - 1)) if x != 1 else part
        a = spot % own // chan
        turned = turned + jnp.where((a + x >= 1) & (a + x <= count_x), moved, 0.0)
        if x == 0:
            extra = extra + jnp.where((spot - first) % outside_rows < chan, part, 0.0)
        if x == count_x - 1:
            extra = extra + jnp.where((spot - first) % outside_rows >= chan, part, 0.0)
    group = 3 * chan
    tight = jnp.zeros((chan_out, 2 * lanes), f32)
    for b in range(3):
        for e in range(3):
            at = (b * 3 + e) * group
            here = spot // group == b * 3 + e
            value = turn(turned, b * 3 * own + e * own - at)
            source = first + b * depth + e * outside_rows
            low, high = turn(extra, source - at), turn(extra, source - at - chan)
            a = (spot - at) // chan
            value = value + jnp.where(a == 0, low, 0.0) + jnp.where(a == 2, high, 0.0)
            tight = jnp.where(here, value, tight)
    bias_at = first + 3 * outside_rows
    tight = jnp.where(spot == 9 * group, turn(straight, bias_at - 9 * group), tight)
    tight = tight[:, :lanes]
    wpart[...] = tight
    sides = jnp.concatenate(split(tight), axis=0)
    wframe[...] = sides

    ends = [field[0:wide, :], field[(count_y + 1) * wide : (count_y + 2) * wide, :]]
    rows_out[...] = jnp.concatenate([end[chan : chan + own] for end in ends], axis=0)
    tall = cols.shape[0]
    found = cols[...].astype(bf16)
    zero = jnp.zeros((8, lanes), f32)
    for ref, odd in ((sent_0, 0), (sent_1, 1)):
        high = even != (odd == 1)
        low_frame, high_frame = [
            jnp.concatenate([end[x * chan : (x + 1) * chan] for end in ends] + [zero], axis=0)
            for x in (0, count_x + 1)
        ]
        ref[0:16, :] = jnp.where(high, high_frame, low_frame).astype(bf16)
        ref[16 : 16 + tall, :] = found
        ref[16 + tall :, :] = sides


def plane_of(field, outer_field, at, wide, count_y):
    row = iota((count_y, lanes), 0) + 1
    span_y = 2 * pairs
    place = pl.ds(wide + at, count_y, stride=wide)
    near = (row >= span_y) & (row < count_y - span_y + 2)
    far = (row < span_y + 2) | (row >= count_y - span_y)
    return jnp.where(near, field[place, :], 0.0) + jnp.where(far, outer_field[place, :], 0.0)


def face_kernel(chan, field, outer_field, face_0, face_1):
    count_y = face_0.shape[0] // chan
    wide = field.shape[0] // (count_y + 2)
    even = is_even("gx")
    for c in range(chan):
        low, high = [
            plane_of(field, outer_field, at + c, wide, count_y) for at in (0, wide - chan)
        ]
        place = slice(c * count_y, (c + 1) * count_y)
        face_0[place, :] = jnp.where(even, high, low).astype(bf16)
        face_1[place, :] = jnp.where(even, low, high).astype(bf16)


def x_kernel(alone, wpart, wframe, rows, cols, got_0, got_1, far, frame, rows_out):
    tall = cols.shape[0]
    own = rows.shape[0] // 2
    wide = tall // 2
    chan = (wide - own) // 2
    if alone:
        total = wpart[...]
    else:
        total = joined(wframe[...]) + joined(far[16 + tall :, :])
        total = total + (joined(got_0[16 + tall :, :]) + joined(got_1[16 + tall :, :]))
    frame[2 * own :, :] = jnp.concatenate(split(total), axis=0)
    one, two = got_0[0 : 16 + tall, :].astype(f32), got_1[0 : 16 + tall, :].astype(f32)
    from_low, from_high = pick("gx", two, one), pick("gx", one, two)
    mid = jnp.zeros((own - 2 * chan, lanes), f32)
    found = []
    for top in (0, wide):
        more = [from_low[16 + top + chan + own : 16 + top + wide], mid]
        more.append(from_high[16 + top : 16 + top + chan])
        found.append(cols[top + chan : top + chan + own, :] + jnp.concatenate(more, axis=0))
    frame[0 : 2 * own, :] = jnp.concatenate(found, axis=0).astype(bf16)
    for at in (0, 1):
        more = [from_low[at * chan : (at + 1) * chan], mid, from_high[at * chan : (at + 1) * chan]]
        place = slice(at * own, (at + 1) * own)
        rows_out[place, :] = rows[place, :] + jnp.concatenate(more, axis=0)


def z_kernel(count_y, mine, got, rows, sent_0, sent_1, wframe):
    own = rows.shape[0] // 2
    total = joined(mine[2 * own :, :]) + joined(got[2 * own :, :])
    sides = jnp.concatenate(split(total), axis=0)
    wframe[...] = sides
    last = got[0:own, :].astype(f32)
    first = got[own : 2 * own, :].astype(f32)
    spot = iota((own, lanes), 1)
    both = []
    for at, line in ((0, 0), (1, count_y + 1)):
        more = jnp.where(spot == lanes - 1, pltpu.roll(last, lanes - 1 - line, 1), 0.0)
        turned = pltpu.roll(first, lanes - line, 1) if line else first
        more = jnp.where(spot == 0, turned, more)
        both.append(rows[at * own : (at + 1) * own, :] + more)
    sent_0[0:own, :] = pick("gy", both[1], both[0]).astype(bf16)
    sent_1[0:own, :] = pick("gy", both[0], both[1]).astype(bf16)
    for ref in (sent_0, sent_1):
        ref[own:, :] = sides


def grad_kernel(field, outer_field, face_0, face_1, got, grad, ends):
    chan, count_x, count_y, _ = grad.shape
    own = chan * count_x
    wide = own + 2 * chan
    spot = iota((count_y, lanes), 1)
    columns = pltpu.roll(got[0 : 2 * own, :].astype(f32), lanes - 1, 1)
    columns = jnp.concatenate([columns, jnp.zeros((lanes - 2 * own, lanes), f32)], axis=0)
    columns = columns.T[0:count_y]
    for x in range(count_x):
        for c in range(chan):
            at = x * chan + c
            plane = plane_of(field, outer_field, chan + at, wide, count_y)
            place = slice(c * count_y, (c + 1) * count_y)
            if x == 0:
                plane = plane + pick("gx", face_1[place, :].astype(f32), face_0[place, :].astype(f32))
            if x == count_x - 1:
                plane = plane + pick("gx", face_0[place, :].astype(f32), face_1[place, :].astype(f32))
            more = jnp.where(spot == lanes - 1, columns[:, at : at + 1], 0.0)
            plane = plane + jnp.where(spot == 0, columns[:, own + at : own + at + 1], more)
            grad[c, x] = plane
            ends[0, c, x] = plane[0:8]
            ends[1, c, x] = plane[count_y - 8 : count_y]


def final_kernel(whole, ends, mine, got_0, got_1, far, out, wout, bout, tiles, wtile, btile, sems):
    chan, count_x, count_y, _ = whole.shape
    own = chan * count_x
    chan_out = mine.shape[0] // 2
    row = iota((8, lanes), 0)
    one, two = got_0[0:own, :].astype(f32), got_1[0:own, :].astype(f32)
    above, below = pick("gy", two, one), pick("gy", one, two)
    copies = []
    for side, more, line in ((0, above, 0), (1, below, 7)):
        for x in range(count_x):
            for c in range(chan):
                at = x * chan + c
                extra = jnp.where(row == line, more[at : at + 1], 0.0)
                tiles[side, c, x] = ends[side, c, x] + extra
        copies.append(
            pltpu.make_async_copy(
                tiles.at[side],
                out.at[:, :, pl.ds(side * (count_y - 8), 8), :],
                sems.at[side],
            )
        )
        copies[-1].start()
    total = joined(mine[...]) + joined(far[...])
    total = total + (joined(got_0[own:, :]) + joined(got_1[own:, :]))
    total = jnp.concatenate([total, jnp.zeros((lanes - chan_out, lanes), f32)], axis=0)
    total = total.T
    for a in range(3):
        for be in range(9):
            at = (be * 3 + a) * chan
            wtile[a * 9 + be] = total[at : at + chan, :chan_out]
    btile[...] = total[27 * chan : 27 * chan + 1, :chan_out]
    copies.append(pltpu.make_async_copy(wtile, wout, sems.at[2]))
    copies.append(pltpu.make_async_copy(btile, bout, sems.at[3]))
    copies[2].start()
    copies[3].start()
    for copy in copies:
        copy.wait()


def traffic(mib):
    return pl.CostEstimate(flops=0, bytes_accessed=mib << 20, transcendentals=0)


def call(kernel, outs, scratch=(), cost=None, **rest):
    return pl.pallas_call(
        kernel,
        out_shape=outs,
        **rest,
        scratch_shapes=list(scratch),
        cost_estimate=cost,
        compiler_params=pltpu.CompilerParams(vmem_limit_bytes=limit),
    )


def on_device(cells, weight, bias, cotangent):
    chan, count_x, count_y, count_z = cells.shape
    chan_out = weight.shape[0]
    own = chan * count_x
    wide = own + 2 * chan
    depth = 6 * chan + 8
    shape = jax.ShapeDtypeStruct

    kernel = weight.transpose(0, 3, 4, 2, 1)
    placed = jnp.stack(
        [
            jnp.pad(kernel, ((0, 0), (0, 0), (0, 0), (x, count_x - 1 - x), (0, 0)))
            for x in range(count_x)
        ]
    ).reshape(count_x * chan_out, 3, 3, count_x + 2, chan)
    coarse = lax.reduce_precision(bias, 8, 7)
    middle = lax.reduce_precision(bias - coarse, 8, 7)
    fine = bias - coarse - middle
    pieces = jnp.stack([coarse, middle, fine], axis=1).astype(bf16)
    pieces = jnp.pad(jnp.tile(pieces, (count_x, 1))[:, None], ((0, 0), (0, 2), (0, 5)))
    near = placed[:, :, :, 1 : count_x + 1].reshape(count_x * chan_out, 9 * own)
    rest = jnp.concatenate([placed[:, :, :, :1], placed[:, :, :, count_x + 1 :]], axis=3)
    rest = jnp.concatenate([rest.reshape(count_x * chan_out, 3, 6 * chan), pieces], axis=2)
    wbig = jnp.concatenate([near, rest.reshape(count_x * chan_out, 3 * depth)], axis=1)
    wback = placed.reshape(count_x * chan_out, 9 * wide).T

    edges, rows = call(
        pack_kernel, [shape((2 * own, lanes), bf16), shape((2 * own, lanes), f32)]
    )(cells)
    pool_x, pool_y, pool_z = cotangent.shape[1:]
    pooled_rows = shape((pool_y * pool_x * chan_out, lanes), f32)
    spread = call(spread_kernel, pooled_rows)(cotangent)
    edges = swapped(edges, "gz", 0)
    body = chan * count_y
    bundle = shape((body + 16, lanes), bf16)
    side = shape((own, lanes), f32)
    face_0, face_1, left, right = call(bundle_kernel, [bundle, bundle, side, side])(cells, edges)
    face_1, face_0 = swapped(face_1, "gx", 1), swapped(face_0, "gx", 0)
    inner = call(
        own_kernel,
        shape(((count_y + 2) * 3 * own, lanes), bf16),
        [pltpu.VMEM(((count_y + 2) * own, lanes), f32)],
        traffic(4),
    )(cells, left, right)
    bundle = shape((3 * wide + 8, lanes), bf16)
    row_0, row_1 = call(functools.partial(rows_kernel, chan), [bundle, bundle])(
        rows, left, right, face_0, face_1
    )
    row_1, row_0 = swapped(row_1, "gy", 1), swapped(row_0, "gy", 0)

    tall = 2 * wide
    all_field = shape(((count_y + 2) * wide, lanes), f32)
    all_gram = shape((count_x * chan_out, 9 * own + 3 * depth), f32)
    deltas = [pltpu.VMEM((count_x * chan_out, 8 * lanes), bf16)] * 2
    sums, field, patches, cols, gram = call(
        functools.partial(inner_kernel, count_x),
        [
            pooled_rows,
            all_field,
            shape(((count_y + 2) * depth, lanes), bf16),
            shape((tall, lanes), f32),
            all_gram,
        ],
        [
            pltpu.VMEM(((count_y + 2) * 2 * chan, lanes), f32),
            pltpu.VMEM((6 * wide, lanes), f32),
        ]
        + deltas,
        traffic(16),
    )(face_0, face_1, inner, spread, wbig, wback)

    bundle = shape((16 + tall + 2 * chan_out, lanes), bf16)
    face = shape((body, lanes), bf16)
    outer_sums, outer_field, row_0, row_1, wpart, wframe, rows, cols = call(
        functools.partial(main_kernel, count_x),
        [
            pooled_rows,
            all_field,
            bundle,
            bundle,
            shape((chan_out, lanes), f32),
            shape((2 * chan_out, lanes), bf16),
            shape((2 * own, lanes), f32),
            shape((tall, lanes), f32),
        ],
        [
            pltpu.VMEM((4 * (pairs + 1) * 3 * own, lanes), bf16),
            pltpu.VMEM((4 * (pairs + 1) * depth, lanes), bf16),
            pltpu.VMEM((count_x * chan_out, 9 * own + 3 * depth), f32),
        ]
        + deltas,
    )(row_0, row_1, inner, patches, cols, gram, spread, wbig, wback)

    alone = lax.axis_size("gx") != 4
    if alone:
        wpart, far = lax.psum(wpart, "gx"), row_0
    else:
        far = swapped(row_0, "gx", 2)
    row_1, row_0 = swapped(row_1, "gx", 1), swapped(row_0, "gx", 0)
    face_0, face_1 = call(functools.partial(face_kernel, chan), [face, face], cost=traffic(2))(
        field, outer_field
    )
    face_1, face_0 = swapped(face_1, "gx", 1), swapped(face_0, "gx", 0)
    pooled = call(
        functools.partial(pool_kernel, pairs), shape(cotangent.shape, bf16), cost=traffic(8)
    )(sums, outer_sums)
    mine, rows = call(
        functools.partial(x_kernel, alone),
        [shape((2 * own + 2 * chan_out, lanes), bf16), shape((2 * own, lanes), f32)],
    )(wpart, wframe, rows, cols, row_0, row_1, far)
    frame = swapped(mine, "gz", 0)
    bundle = shape((own + 2 * chan_out, lanes), bf16)
    row_0, row_1, mine = call(
        functools.partial(z_kernel, count_y),
        [bundle, bundle, shape((2 * chan_out, lanes), bf16)],
    )(mine, frame, rows)
    row_1, row_0 = swapped(row_1, "gy", 1), swapped(row_0, "gy", 0)
    far = swapped(mine, "gy", 2)
    tiles = (2, chan, count_x, 8, lanes)
    grad, ends = call(grad_kernel, [shape(cells.shape, f32), shape(tiles, f32)], cost=traffic(8))(
        field, outer_field, face_0, face_1, frame
    )
    vmem, anywhere = pl.BlockSpec(memory_space=pltpu.VMEM), pl.BlockSpec(memory_space=pl.ANY)
    input_grad, wsum, bias_grad = call(
        final_kernel,
        [
            shape(cells.shape, f32),
            shape((27, chan, chan_out), f32),
            shape((1, chan_out), f32),
        ],
        [
            pltpu.VMEM(tiles, f32),
            pltpu.VMEM((27, chan, chan_out), f32),
            pltpu.VMEM((1, chan_out), f32),
            pltpu.SemaphoreType.DMA((4,)),
        ],
        in_specs=[anywhere] + [vmem] * 5,
        out_specs=[anywhere] * 3,
        input_output_aliases={0: 0},
    )(grad, ends, mine, row_0, row_1, far)
    weight_grad = wsum.reshape(3, 3, 3, chan, chan_out).transpose(4, 3, 0, 1, 2)
    return (pooled, weight_grad, bias_grad.reshape(chan_out), input_grad)


def solution(mesh):
    in_specs = (P(None, "gx", "gy", "gz"), P(), P(), P(None, "gx", "gy", "gz"))
    out_specs = (P(None, "gx", "gy", "gz"), P(), P(), P(None, "gx", "gy", "gz"))
    return jax.shard_map(
        on_device, mesh=mesh, in_specs=in_specs, out_specs=out_specs, check_vma=False
    )
```

```python
import functools

import jax
import jax.numpy as jnp
import numpy as np
from jax import lax
from jax.experimental import pallas as pl
from jax.experimental.pallas import tpu as pltpu
from jax.sharding import PartitionSpec as P

axes = ("gx", "gy", "gz")
f32, bf16 = jnp.float32, jnp.bfloat16
log_scale = 0.07
lanes = 128
limit = 48 * 1024 * 1024


def dot(a, b, contract=((1,), (0,))):
    return lax.dot_general(a, b, (contract, ((), ())), preferred_element_type=f32)


def iota(shape, dim):
    return lax.broadcasted_iota(jnp.int32, shape, dim)


def aligned(start, tile):
    return start if isinstance(start, int) else pl.multiple_of(start, tile)


def swapped(array, axis, pairing):
    count = lax.axis_size(axis)
    pairs = []
    for i in range(count):
        if pairing == 2:
            partner = i + count // 2
        else:
            partner = i + 1 if i % 2 == pairing else i - 1
        pairs.append((i, partner % count))
    return lax.ppermute(array, axis, pairs)


def is_even(axis):
    return lax.rem(lax.axis_index(axis), 2) == 0


def pick(axis, if_even, if_odd):
    return jnp.where(is_even(axis), if_even, if_odd)


def split(value):
    coarse = value.astype(bf16)
    return coarse, (value - coarse.astype(f32)).astype(bf16)


def joined(pair):
    half = pair.shape[0] // 2
    return pair[:half].astype(f32) + pair[half:].astype(f32)


def pack_kernel(cells, edges, rows):
    chan, count_x, count_y, _ = cells.shape
    count = chan * count_x
    row = iota((2 * count, count * lanes), 0)
    lane = iota((2 * count, count * lanes), 1)
    want = jnp.where(row < count, row * lanes, (row - count) * lanes + lanes - 1)
    chosen = (lane == want).astype(f32).astype(bf16)
    planes = [cells[c, x] for x in range(count_x) for c in range(chan)]
    wide = jnp.concatenate(planes, axis=1)
    found = dot(chosen, wide, ((1,), (1,)))
    found = jnp.concatenate([found, jnp.zeros((2 * count, lanes - count_y), f32)], axis=1)
    edges[...] = pltpu.roll(found, 1, 1).astype(bf16)
    for at, plane in enumerate(planes):
        wide_plane = plane.astype(f32)
        rows[at : at + 1, :] = wide_plane[0:1]
        rows[count + at : count + at + 1, :] = wide_plane[count_y - 1 : count_y]


def bundle_kernel(cells, edges, sent_0, sent_1, left, right):
    chan, count_x, count_y, _ = cells.shape
    own = chan * count_x
    whole = edges[...].astype(f32)
    right[...] = whole[0:own]
    left[...] = whole[own : 2 * own]
    zero = jnp.zeros((8, lanes), f32)
    body = chan * count_y
    frames = []
    for x in (0, count_x - 1):
        at = slice(x * chan, x * chan + chan)
        frames.append(jnp.concatenate([whole[own + x * chan :][:chan], whole[at], zero], axis=0))
    even = is_even("gx")
    for ref, odd in ((sent_0, 0), (sent_1, 1)):
        high = even != (odd == 1)
        x = jnp.where(high, count_x - 1, 0)
        for c in range(chan):
            ref[c * count_y : (c + 1) * count_y, :] = cells[c, x]
        ref[body : body + 16, :] = jnp.where(high, frames[1], frames[0]).astype(bf16)


def from_sides(got_0, got_1, start, size):
    one = got_0[start : start + size, :].astype(f32)
    two = got_1[start : start + size, :].astype(f32)
    return pick("gx", two, one), pick("gx", one, two)


def rows_kernel(chan, rows, left, right, got_0, got_1, inner, spread, sent_0, sent_1):
    own = rows.shape[0] // 2
    body = got_0.shape[0] - 16
    count_y = body // chan
    low, high = from_sides(got_0, got_1, body, 16)
    edges = []
    for ref, at in ((left, 0), (right, chan)):
        edges += [ref[...], low[at : at + chan], high[at : at + chan]]
    edges.append(jnp.zeros((8, lanes), f32))
    low, high = from_sides(got_0, got_1, 0, body)
    both = []
    for at, line in ((0, 0), (own, count_y - 1)):
        outer = [
            plane[c * count_y + line : c * count_y + line + 1]
            for plane in (low, high)
            for c in range(chan)
        ]
        both.append(jnp.concatenate([rows[at : at + own, :]] + outer + edges, axis=0))
    sent_0[...] = pick("gy", both[1], both[0]).astype(bf16)
    sent_1[...] = pick("gy", both[0], both[1]).astype(bf16)


def spread_kernel(cot, spread):
    chan_out, pool_x, pool_y, pool_z = cot.shape
    twice = jnp.where(
        iota((pool_z, lanes), 1) // 2 == iota((pool_z, lanes), 0), 0.125, 0.0
    ).astype(bf16)
    for o in range(chan_out):
        part = dot(cot[o].reshape(pool_x * pool_y, pool_z), twice)
        for x in range(pool_x):
            spread[pl.ds(x * chan_out + o, pool_y, stride=pool_x * chan_out), :] = part[
                x * pool_y : (x + 1) * pool_y
            ]


def pool_kernel(edge, sums, outer_sums, pooled):
    chan_out, pool_x, pool_y, pool_z = pooled.shape
    halves = jnp.where(
        iota((2 * lanes, pool_z), 0) % lanes // 2 == iota((2 * lanes, pool_z), 1), 0.125, 0.0
    ).astype(bf16)
    for o in range(0, chan_out, 4):
        rows = 4 * pool_x * pool_y
        part = sums[o * pool_x * pool_y : o * pool_x * pool_y + rows, :]
        at = iota((rows, lanes), 0) % pool_y
        near = (at >= edge) & (at < pool_y - edge)
        part = jnp.where(near, part, outer_sums[o * pool_x * pool_y : o * pool_x * pool_y + rows, :])
        mean = dot(jnp.concatenate(split(part), axis=1), halves) + log_scale * float(np.log(2.0))
        pooled[o : o + 4] = mean.astype(bf16).reshape(4, pool_x, pool_y, pool_z)


def shifted(mid, left, right, y):
    lane = iota(mid.shape, 1)
    low = pltpu.roll(left, (lanes - y) % lanes, 1)
    high = pltpu.roll(right, (lanes - 1 - y) % lanes, 1)
    before = jnp.where(lane == 0, low, pltpu.roll(mid, 1, 1))
    after = jnp.where(lane == lanes - 1, high, pltpu.roll(mid, lanes - 1, 1))
    return [before, mid, after]


def own_kernel(cells, left, right, inner, stage):
    chan, count_x, count_y, _ = cells.shape
    own = chan * count_x
    for x in range(count_x):
        for c in range(chan):
            plane = cells[c, x].astype(f32)
            stage[pl.ds(own + x * chan + c, count_y, stride=own), :] = plane
    left_cols, right_cols = left[...], right[...]
    for y in range(1, count_y + 1):
        whole = shifted(stage[y * own : (y + 1) * own, :], left_cols, right_cols, y)
        whole = jnp.concatenate(whole, axis=0)
        inner[y * 3 * own : (y + 1) * 3 * own, :] = whole.astype(bf16)


pairs = 4


def sizes_of(count_x, inner, spread, wbig):
    pool_x = count_x // 2
    chan_out = wbig.shape[0] // count_x
    pool_y = spread.shape[0] // (pool_x * chan_out)
    own = inner.shape[0] // (3 * (2 * pool_y + 2))
    return pool_x, chan_out, pool_y, own, own // count_x


def worker(count_x, pool_x, chan_out, pool_y, own, chan, near_of, rest_of, refs):
    spread, wbig, wback, sums, field = refs
    wide = own + 2 * chan
    size = 3 * wide
    lane = iota((wide, lanes), 1)
    inside, outside = lane != lanes - 1, lane != 0

    def finish(y, whole, edge):
        first, last = whole[0:wide], whole[2 * wide : 3 * wide]
        inner = (
            whole[wide : 2 * wide]
            + jnp.where(inside, pltpu.roll(first, lanes - 1, 1), 0.0)
            + jnp.where(outside, pltpu.roll(last, 1, 1), 0.0)
        )
        field[pl.ds(aligned(y * wide, 8), wide), :] = inner
        here = lane == y
        edge[0] = jnp.where(here, pltpu.roll(first, y, 1), edge[0])
        edge[1] = jnp.where(here, pltpu.roll(last, y + 1, 1), edge[1])

    def block_of(j):
        columns = [
            jnp.concatenate([near_of(2 * j + h), rest_of(2 * j + h)], axis=0) for h in range(2)
        ]
        return jnp.concatenate(columns, axis=1)

    def forward(i, k, ref):
        j = i * pairs + k
        preact = dot(wbig[...], block_of(j))
        slope = jnp.tanh(5.0 * preact)
        linear = jnp.maximum(preact, 0.3 * preact)
        factor = 1.0 + jnp.abs(slope)
        here = spread[pl.ds(aligned(j * pool_x * chan_out, 8), pool_x * chan_out), :]
        slope = 0.65 + 0.35 * slope
        delta = []
        for x in range(pool_x):
            top, mid = 2 * x * chan_out, (2 * x + 1) * chan_out
            end = mid + chan_out
            times = here[x * chan_out : (x + 1) * chan_out]
            times = jnp.concatenate([times, times], axis=1)
            delta.append((slope[top:mid] * times).astype(bf16))
            delta.append((slope[mid:end] * times).astype(bf16))
            total = linear[top:mid] + linear[mid:end]
            total = total[:, :lanes] + total[:, lanes:]
            prod = factor[top:mid] * factor[mid:end]
            prod = prod[:, :lanes] * prod[:, lanes:]
            total = total - log_scale * jnp.log(prod)
            sums[pl.ds(x * pool_y + j, chan_out, stride=pool_x * pool_y), :] = total
        ref[:, 2 * k * lanes : 2 * (k + 1) * lanes] = jnp.concatenate(delta, axis=0)

    def backward(i, k, ref, held, edge):
        j = i * pairs + k
        parts = dot(wback[...], ref[:, 2 * k * lanes : 2 * (k + 1) * lanes])
        part = lambda b, h: parts[b * size : (b + 1) * size, h * lanes : (h + 1) * lanes]
        finish(2 * j, held[0] + part(0, 0), edge)
        finish(2 * j + 1, held[1] + part(1, 0) + part(0, 1), edge)
        held[0] = part(2, 0) + part(1, 1)
        held[1] = part(2, 1)

    def weigh(i, ref):
        blocks = jnp.concatenate([block_of(i * pairs + k) for k in range(pairs)], axis=1)
        return dot(ref[...], blocks, ((1,), (1,)))

    return finish, forward, backward, weigh


def inner_kernel(
    count_x, got_0, got_1, inner, spread, wbig, wback,
    sums, field, patches, cols, gram, stage, carry, delta_a, delta_b,
):
    shape = sizes_of(count_x, inner, spread, wbig)
    pool_x, chan_out, pool_y, own, chan = shape
    count_y = 2 * pool_y
    wide = own + 2 * chan
    size = 3 * wide
    outside_rows = 2 * chan
    depth = 3 * outside_rows + 8
    body = chan * count_y
    for side, planes in enumerate(from_sides(got_0, got_1, 0, body)):
        for c in range(chan):
            at = outside_rows + side * chan + c
            plane = planes[c * count_y : (c + 1) * count_y]
            stage[pl.ds(at, count_y, stride=outside_rows), :] = plane
    low, high = from_sides(got_0, got_1, body, 16)
    left_cols, right_cols = [
        jnp.concatenate([low[at : at + chan], high[at : at + chan]], axis=0) for at in (0, chan)
    ]
    for y in range(1, count_y + 1):
        mid = stage[y * outside_rows : (y + 1) * outside_rows, :]
        whole = shifted(mid, left_cols, right_cols, y) + [jnp.ones((8, lanes), f32)]
        patches[y * depth : (y + 1) * depth, :] = jnp.concatenate(whole, axis=0).astype(bf16)

    def near_of(y):
        return inner[pl.ds(aligned(y * 3 * own, 16), 9 * own), :]

    def rest_of(y):
        return patches[pl.ds(aligned(y * depth, 16), 3 * depth), :]

    finish, forward, backward, weigh = worker(
        count_x, *shape, near_of, rest_of, (spread, wbig, wback, sums, field)
    )
    carry[...] = jnp.zeros_like(carry)
    gram[...] = jnp.zeros_like(gram)
    cols[...] = jnp.zeros_like(cols)

    def opened():
        return (
            [carry[0:size, :], carry[size : 2 * size, :]],
            [cols[0:wide, :], cols[wide : 2 * wide, :]],
        )

    def closed(held, edge):
        carry[0:size, :] = held[0]
        carry[size : 2 * size, :] = held[1]
        cols[0:wide, :] = edge[0]
        cols[wide : 2 * wide, :] = edge[1]

    def both(at):
        held, edge = opened()
        total = gram[...] + weigh(at, delta_a)
        for k in range(pairs):
            forward(at + 1, k, delta_b)
            backward(at, k, delta_a, held, edge)
        return held, edge, total + weigh(at + 1, delta_b)

    def step(t, _):
        at = 2 * t + 1
        held, edge, total = both(at)
        for k in range(pairs):
            forward(at + 2, k, delta_a)
            backward(at + 1, k, delta_b, held, edge)
        gram[...] = total
        closed(held, edge)
        return 0

    steps = count_y // (2 * pairs)
    for k in range(pairs):
        forward(1, k, delta_a)
    lax.fori_loop(0, steps // 2 - 2, step, 0)
    held, edge, total = both(steps - 3)
    gram[...] = total
    for k in range(pairs):
        backward(steps - 2, k, delta_b, held, edge)
    end = (steps - 1) * 2 * pairs
    finish(end, held[0], edge)
    finish(end + 1, held[1], edge)
    closed(held, edge)


def main_kernel(
    count_x, row_0, row_1, inner, patches, inner_cols, inner_gram, spread, wbig, wback,
    sums, field, sent_0, sent_1, wpart, wframe, rows_out, cols,
    near, rest, gram, delta_a, delta_b,
):
    shape = sizes_of(count_x, inner, spread, wbig)
    pool_x, chan_out, pool_y, own, chan = shape
    count_y = 2 * pool_y
    wide = own + 2 * chan
    size = 3 * wide
    outside_rows = 2 * chan
    depth = 3 * outside_rows + 8
    even = is_even("gx")
    span_y = 2 * pairs
    top = span_y + 2
    start = count_y - span_y
    for ref, source, height in ((near, inner, 3 * own), (rest, patches, depth)):
        ref[height : top * height, :] = source[height : top * height, :]
        last = (2 * top - 1) * height
        ref[top * height : last, :] = source[start * height : (count_y + 1) * height, :]
    one, two = row_0[...].astype(f32), row_1[...].astype(f32)
    above, below = pick("gy", two, one), pick("gy", one, two)
    for at, got, line in ((0, above, count_y), (2 * top - 1, below, 1)):
        left, right = got[wide : 2 * wide], got[2 * wide : 3 * wide]
        whole = jnp.concatenate(shifted(got[:own], left[:own], right[:own], line), axis=0)
        near[at * 3 * own : (at + 1) * 3 * own, :] = whole.astype(bf16)
        whole = shifted(got[own:wide], left[own:], right[own:], line)
        whole = jnp.concatenate(whole + [jnp.ones((8, lanes), f32)], axis=0)
        rest[at * depth : (at + 1) * depth, :] = whole.astype(bf16)

    def place(y):
        return y if y < top else y - start + top

    def near_of(y):
        return near[place(y) * 3 * own : (place(y) + 3) * 3 * own, :]

    def rest_of(y):
        return rest[place(y) * depth : (place(y) + 3) * depth, :]

    finish, forward, backward, weigh = worker(
        count_x, *shape, near_of, rest_of, (spread, wbig, wback, sums, field)
    )
    final = count_y // span_y - 1
    zero = jnp.zeros((size, lanes), f32)
    held, edge = [zero, zero], [inner_cols[0:wide, :], inner_cols[wide : 2 * wide, :]]
    extra = [jnp.zeros((wide, lanes), f32)] * 2
    for k in range(pairs):
        forward(0, k, delta_a)
    for k in range(pairs):
        forward(final, k, delta_b)
        backward(0, k, delta_a, held, extra)
    total = inner_gram[...] + weigh(0, delta_a)
    finish(span_y, held[0], extra)
    finish(span_y + 1, held[1], extra)
    held = [zero, zero]
    for k in range(pairs):
        backward(final, k, delta_b, held, extra)
    gram[...] = total + weigh(final, delta_b)
    finish(count_y, held[0], extra)
    finish(count_y + 1, held[1], extra)
    cols[0:wide, :] = edge[0] + extra[0]
    cols[wide : 2 * wide, :] = edge[1] + extra[1]

    span = gram.shape[1]
    spot = iota((chan_out, 2 * lanes), 1)
    first = 9 * own
    turn = lambda part, shift: pltpu.roll(part, (2 * lanes - shift) % (2 * lanes), 1)
    straight, turned, extra = 0.0, 0.0, 0.0
    for x in range(count_x):
        part = gram[x * chan_out : (x + 1) * chan_out, :]
        part = jnp.concatenate([part, jnp.zeros((chan_out, 2 * lanes - span), f32)], axis=1)
        straight = straight + part
        moved = turn(part, chan * (x - 1)) if x != 1 else part
        a = spot % own // chan
        turned = turned + jnp.where((a + x >= 1) & (a + x <= count_x), moved, 0.0)
        if x == 0:
            extra = extra + jnp.where((spot - first) % outside_rows < chan, part, 0.0)
        if x == count_x - 1:
            extra = extra + jnp.where((spot - first) % outside_rows >= chan, part, 0.0)
    group = 3 * chan
    tight = jnp.zeros((chan_out, 2 * lanes), f32)
    for b in range(3):
        for e in range(3):
            at = (b * 3 + e) * group
            here = spot // group == b * 3 + e
            value = turn(turned, b * 3 * own + e * own - at)
            source = first + b * depth + e * outside_rows
            low, high = turn(extra, source - at), turn(extra, source - at - chan)
            a = (spot - at) // chan
            value = value + jnp.where(a == 0, low, 0.0) + jnp.where(a == 2, high, 0.0)
            tight = jnp.where(here, value, tight)
    bias_at = first + 3 * outside_rows
    tight = jnp.where(spot == 9 * group, turn(straight, bias_at - 9 * group), tight)
    tight = tight[:, :lanes]
    wpart[...] = tight
    sides = jnp.concatenate(split(tight), axis=0)
    wframe[...] = sides

    ends = [field[0:wide, :], field[(count_y + 1) * wide : (count_y + 2) * wide, :]]
    rows_out[...] = jnp.concatenate([end[chan : chan + own] for end in ends], axis=0)
    zero = jnp.zeros((8, lanes), f32)
    for ref, odd in ((sent_0, 0), (sent_1, 1)):
        high = even != (odd == 1)
        low_frame, high_frame = [
            jnp.concatenate(
                [end[x * chan : (x + 1) * chan] for end in ends]
                + [cols[top + x * chan : top + (x + 1) * chan, :] for top in (0, wide)],
                axis=0,
            )
            for x in (0, count_x + 1)
        ]
        ref[0:16, :] = jnp.where(high, high_frame, low_frame).astype(bf16)
        ref[16:, :] = sides


def plane_of(field, outer_field, at, wide, count_y):
    row = iota((count_y, lanes), 0) + 1
    span_y = 2 * pairs
    place = pl.ds(wide + at, count_y, stride=wide)
    near = (row >= span_y) & (row < count_y - span_y + 2)
    far = (row < span_y + 2) | (row >= count_y - span_y)
    return jnp.where(near, field[place, :], 0.0) + jnp.where(far, outer_field[place, :], 0.0)


def face_kernel(chan, field, outer_field, face_0, face_1):
    count_y = face_0.shape[0] // chan
    wide = field.shape[0] // (count_y + 2)
    even = is_even("gx")
    for c in range(chan):
        low, high = [
            plane_of(field, outer_field, at + c, wide, count_y) for at in (0, wide - chan)
        ]
        place = slice(c * count_y, (c + 1) * count_y)
        face_0[place, :] = jnp.where(even, high, low).astype(bf16)
        face_1[place, :] = jnp.where(even, low, high).astype(bf16)


def x_kernel(alone, wpart, wframe, rows, cols, got_0, got_1, far, frame, rows_out):
    own = rows.shape[0] // 2
    wide = cols.shape[0] // 2
    chan = (wide - own) // 2
    if alone:
        total = wpart[...]
    else:
        total = joined(wframe[...]) + joined(far[16:, :])
        total = total + (joined(got_0[16:, :]) + joined(got_1[16:, :]))
    frame[2 * own :, :] = jnp.concatenate(split(total), axis=0)
    one, two = got_0[0:16, :].astype(f32), got_1[0:16, :].astype(f32)
    from_low, from_high = pick("gx", two, one), pick("gx", one, two)
    mid = jnp.zeros((own - 2 * chan, lanes), f32)
    found = []
    for top, at in ((0, 2 * chan), (wide, 3 * chan)):
        more = [from_low[at : at + chan], mid, from_high[at : at + chan]]
        found.append(cols[top + chan : top + chan + own, :] + jnp.concatenate(more, axis=0))
    frame[0 : 2 * own, :] = jnp.concatenate(found, axis=0).astype(bf16)
    for at in (0, 1):
        more = [from_low[at * chan : (at + 1) * chan], mid, from_high[at * chan : (at + 1) * chan]]
        place = slice(at * own, (at + 1) * own)
        rows_out[place, :] = rows[place, :] + jnp.concatenate(more, axis=0)


def z_kernel(count_y, mine, got, rows, sent_0, sent_1, wframe):
    own = rows.shape[0] // 2
    total = joined(mine[2 * own :, :]) + joined(got[2 * own :, :])
    sides = jnp.concatenate(split(total), axis=0)
    wframe[...] = sides
    last = got[0:own, :].astype(f32)
    first = got[own : 2 * own, :].astype(f32)
    spot = iota((own, lanes), 1)
    both = []
    for at, line in ((0, 0), (1, count_y + 1)):
        more = jnp.where(spot == lanes - 1, pltpu.roll(last, lanes - 1 - line, 1), 0.0)
        turned = pltpu.roll(first, lanes - line, 1) if line else first
        more = jnp.where(spot == 0, turned, more)
        both.append(rows[at * own : (at + 1) * own, :] + more)
    sent_0[0:own, :] = pick("gy", both[1], both[0]).astype(bf16)
    sent_1[0:own, :] = pick("gy", both[0], both[1]).astype(bf16)
    for ref in (sent_0, sent_1):
        ref[own:, :] = sides


def grad_kernel(field, outer_field, face_0, face_1, got, grad, ends):
    chan, count_x, count_y, _ = grad.shape
    own = chan * count_x
    wide = own + 2 * chan
    spot = iota((count_y, lanes), 1)
    columns = pltpu.roll(got[0 : 2 * own, :].astype(f32), lanes - 1, 1)
    columns = jnp.concatenate([columns, jnp.zeros((lanes - 2 * own, lanes), f32)], axis=0)
    columns = columns.T[0:count_y]
    for x in range(count_x):
        for c in range(chan):
            at = x * chan + c
            plane = plane_of(field, outer_field, chan + at, wide, count_y)
            place = slice(c * count_y, (c + 1) * count_y)
            if x == 0:
                plane = plane + pick("gx", face_1[place, :].astype(f32), face_0[place, :].astype(f32))
            if x == count_x - 1:
                plane = plane + pick("gx", face_0[place, :].astype(f32), face_1[place, :].astype(f32))
            more = jnp.where(spot == lanes - 1, columns[:, at : at + 1], 0.0)
            plane = plane + jnp.where(spot == 0, columns[:, own + at : own + at + 1], more)
            grad[c, x] = plane
            ends[0, c, x] = plane[0:8]
            ends[1, c, x] = plane[count_y - 8 : count_y]


def final_kernel(whole, ends, mine, got_0, got_1, far, out, wout, bout, tiles, wtile, btile, sems):
    chan, count_x, count_y, _ = whole.shape
    own = chan * count_x
    chan_out = mine.shape[0] // 2
    row = iota((8, lanes), 0)
    one, two = got_0[0:own, :].astype(f32), got_1[0:own, :].astype(f32)
    above, below = pick("gy", two, one), pick("gy", one, two)
    copies = []
    for side, more, line in ((0, above, 0), (1, below, 7)):
        for x in range(count_x):
            for c in range(chan):
                at = x * chan + c
                extra = jnp.where(row == line, more[at : at + 1], 0.0)
                tiles[side, c, x] = ends[side, c, x] + extra
        copies.append(
            pltpu.make_async_copy(
                tiles.at[side],
                out.at[:, :, pl.ds(side * (count_y - 8), 8), :],
                sems.at[side],
            )
        )
        copies[-1].start()
    total = joined(mine[...]) + joined(far[...])
    total = total + (joined(got_0[own:, :]) + joined(got_1[own:, :]))
    total = jnp.concatenate([total, jnp.zeros((lanes - chan_out, lanes), f32)], axis=0)
    total = total.T
    for a in range(3):
        for be in range(9):
            at = (be * 3 + a) * chan
            wtile[a * 9 + be] = total[at : at + chan, :chan_out]
    btile[...] = total[27 * chan : 27 * chan + 1, :chan_out]
    copies.append(pltpu.make_async_copy(wtile, wout, sems.at[2]))
    copies.append(pltpu.make_async_copy(btile, bout, sems.at[3]))
    copies[2].start()
    copies[3].start()
    for copy in copies:
        copy.wait()


def traffic(mib):
    return pl.CostEstimate(flops=0, bytes_accessed=mib << 20, transcendentals=0)


def call(kernel, outs, scratch=(), cost=None, **rest):
    return pl.pallas_call(
        kernel,
        out_shape=outs,
        **rest,
        scratch_shapes=list(scratch),
        cost_estimate=cost,
        compiler_params=pltpu.CompilerParams(vmem_limit_bytes=limit),
    )


def on_device(cells, weight, bias, cotangent):
    chan, count_x, count_y, count_z = cells.shape
    chan_out = weight.shape[0]
    own = chan * count_x
    wide = own + 2 * chan
    depth = 6 * chan + 8
    shape = jax.ShapeDtypeStruct

    kernel = weight.transpose(0, 3, 4, 2, 1)
    placed = jnp.stack(
        [
            jnp.pad(kernel, ((0, 0), (0, 0), (0, 0), (x, count_x - 1 - x), (0, 0)))
            for x in range(count_x)
        ]
    ).reshape(count_x * chan_out, 3, 3, count_x + 2, chan)
    coarse = lax.reduce_precision(bias, 8, 7)
    middle = lax.reduce_precision(bias - coarse, 8, 7)
    fine = bias - coarse - middle
    pieces = jnp.stack([coarse, middle, fine], axis=1).astype(bf16)
    pieces = jnp.pad(jnp.tile(pieces, (count_x, 1))[:, None], ((0, 0), (0, 2), (0, 5)))
    near = placed[:, :, :, 1 : count_x + 1].reshape(count_x * chan_out, 9 * own)
    rest = jnp.concatenate([placed[:, :, :, :1], placed[:, :, :, count_x + 1 :]], axis=3)
    rest = jnp.concatenate([rest.reshape(count_x * chan_out, 3, 6 * chan), pieces], axis=2)
    wbig = jnp.concatenate([near, rest.reshape(count_x * chan_out, 3 * depth)], axis=1)
    wback = placed.reshape(count_x * chan_out, 9 * wide).T

    edges, rows = call(
        pack_kernel, [shape((2 * own, lanes), bf16), shape((2 * own, lanes), f32)]
    )(cells)
    pool_x, pool_y, pool_z = cotangent.shape[1:]
    pooled_rows = shape((pool_y * pool_x * chan_out, lanes), f32)
    spread = call(spread_kernel, pooled_rows)(cotangent)
    edges = swapped(edges, "gz", 0)
    body = chan * count_y
    bundle = shape((body + 16, lanes), bf16)
    side = shape((own, lanes), f32)
    face_0, face_1, left, right = call(bundle_kernel, [bundle, bundle, side, side])(cells, edges)
    face_1, face_0 = swapped(face_1, "gx", 1), swapped(face_0, "gx", 0)
    inner = call(
        own_kernel,
        shape(((count_y + 2) * 3 * own, lanes), bf16),
        [pltpu.VMEM(((count_y + 2) * own, lanes), f32)],
        traffic(4),
    )(cells, left, right)
    bundle = shape((3 * wide + 8, lanes), bf16)
    vmem, anywhere = pl.BlockSpec(memory_space=pltpu.VMEM), pl.BlockSpec(memory_space=pl.ANY)
    row_0, row_1 = call(
        functools.partial(rows_kernel, chan),
        [bundle, bundle],
        in_specs=[vmem] * 5 + [anywhere] * 2,
    )(rows, left, right, face_0, face_1, inner, spread)
    row_1, row_0 = swapped(row_1, "gy", 1), swapped(row_0, "gy", 0)

    tall = 2 * wide
    all_field = shape(((count_y + 2) * wide, lanes), f32)
    all_gram = shape((count_x * chan_out, 9 * own + 3 * depth), f32)
    deltas = [pltpu.VMEM((count_x * chan_out, 8 * lanes), bf16)] * 2
    sums, field, patches, cols, gram = call(
        functools.partial(inner_kernel, count_x),
        [
            pooled_rows,
            all_field,
            shape(((count_y + 2) * depth, lanes), bf16),
            shape((tall, lanes), f32),
            all_gram,
        ],
        [
            pltpu.VMEM(((count_y + 2) * 2 * chan, lanes), f32),
            pltpu.VMEM((6 * wide, lanes), f32),
        ]
        + deltas,
        traffic(16),
    )(face_0, face_1, inner, spread, wbig, wback)

    bundle = shape((16 + 2 * chan_out, lanes), bf16)
    face = shape((body, lanes), bf16)
    outer_sums, outer_field, row_0, row_1, wpart, wframe, rows, cols = call(
        functools.partial(main_kernel, count_x),
        [
            pooled_rows,
            all_field,
            bundle,
            bundle,
            shape((chan_out, lanes), f32),
            shape((2 * chan_out, lanes), bf16),
            shape((2 * own, lanes), f32),
            shape((tall, lanes), f32),
        ],
        [
            pltpu.VMEM((4 * (pairs + 1) * 3 * own, lanes), bf16),
            pltpu.VMEM((4 * (pairs + 1) * depth, lanes), bf16),
            pltpu.VMEM((count_x * chan_out, 9 * own + 3 * depth), f32),
        ]
        + deltas,
    )(row_0, row_1, inner, patches, cols, gram, spread, wbig, wback)

    alone = lax.axis_size("gx") != 4
    if alone:
        wpart, far = lax.psum(wpart, "gx"), row_0
    else:
        far = swapped(row_0, "gx", 2)
    row_1, row_0 = swapped(row_1, "gx", 1), swapped(row_0, "gx", 0)
    face_0, face_1 = call(functools.partial(face_kernel, chan), [face, face], cost=traffic(2))(
        field, outer_field
    )
    face_1, face_0 = swapped(face_1, "gx", 1), swapped(face_0, "gx", 0)
    pooled = call(
        functools.partial(pool_kernel, pairs), shape(cotangent.shape, bf16), cost=traffic(8)
    )(sums, outer_sums)
    mine, rows = call(
        functools.partial(x_kernel, alone),
        [shape((2 * own + 2 * chan_out, lanes), bf16), shape((2 * own, lanes), f32)],
    )(wpart, wframe, rows, cols, row_0, row_1, far)
    frame = swapped(mine, "gz", 0)
    bundle = shape((own + 2 * chan_out, lanes), bf16)
    row_0, row_1, mine = call(
        functools.partial(z_kernel, count_y),
        [bundle, bundle, shape((2 * chan_out, lanes), bf16)],
    )(mine, frame, rows)
    row_1, row_0 = swapped(row_1, "gy", 1), swapped(row_0, "gy", 0)
    far = swapped(mine, "gy", 2)
    tiles = (2, chan, count_x, 8, lanes)
    grad, ends = call(grad_kernel, [shape(cells.shape, f32), shape(tiles, f32)], cost=traffic(8))(
        field, outer_field, face_0, face_1, frame
    )
    input_grad, wsum, bias_grad = call(
        final_kernel,
        [
            shape(cells.shape, f32),
            shape((27, chan, chan_out), f32),
            shape((1, chan_out), f32),
        ],
        [
            pltpu.VMEM(tiles, f32),
            pltpu.VMEM((27, chan, chan_out), f32),
            pltpu.VMEM((1, chan_out), f32),
            pltpu.SemaphoreType.DMA((4,)),
        ],
        in_specs=[anywhere] + [vmem] * 5,
        out_specs=[anywhere] * 3,
        input_output_aliases={0: 0},
    )(grad, ends, mine, row_0, row_1, far)
    weight_grad = wsum.reshape(3, 3, 3, chan, chan_out).transpose(4, 3, 0, 1, 2)
    return (pooled, weight_grad, bias_grad.reshape(chan_out), input_grad)


def solution(mesh):
    in_specs = (P(None, "gx", "gy", "gz"), P(), P(), P(None, "gx", "gy", "gz"))
    out_specs = (P(None, "gx", "gy", "gz"), P(), P(), P(None, "gx", "gy", "gz"))
    return jax.shard_map(
        on_device, mesh=mesh, in_specs=in_specs, out_specs=out_specs, check_vma=False
    )
```

```python
import functools

import jax
import jax.numpy as jnp
import numpy as np
from jax import lax
from jax.experimental import pallas as pl
from jax.experimental.pallas import tpu as pltpu
from jax.sharding import PartitionSpec as P

axes = ("gx", "gy", "gz")
f32, bf16 = jnp.float32, jnp.bfloat16
log_scale = 0.07
lanes = 128
limit = 48 * 1024 * 1024


def dot(a, b, contract=((1,), (0,))):
    return lax.dot_general(a, b, (contract, ((), ())), preferred_element_type=f32)


def iota(shape, dim):
    return lax.broadcasted_iota(jnp.int32, shape, dim)


def aligned(start, tile):
    return start if isinstance(start, int) else pl.multiple_of(start, tile)


def swapped(array, axis, pairing):
    count = lax.axis_size(axis)
    pairs = []
    for i in range(count):
        if pairing == 2:
            partner = i + count // 2
        else:
            partner = i + 1 if i % 2 == pairing else i - 1
        pairs.append((i, partner % count))
    return lax.ppermute(array, axis, pairs)


def is_even(axis):
    return lax.rem(lax.axis_index(axis), 2) == 0


def pick(axis, if_even, if_odd):
    return jnp.where(is_even(axis), if_even, if_odd)


def split(value):
    coarse = value.astype(bf16)
    return coarse, (value - coarse.astype(f32)).astype(bf16)


def joined(pair):
    half = pair.shape[0] // 2
    return pair[:half].astype(f32) + pair[half:].astype(f32)


def pack_kernel(cells, edges, rows):
    chan, count_x, count_y, _ = cells.shape
    count = chan * count_x
    row = iota((2 * count, count * lanes), 0)
    lane = iota((2 * count, count * lanes), 1)
    want = jnp.where(row < count, row * lanes, (row - count) * lanes + lanes - 1)
    chosen = (lane == want).astype(f32).astype(bf16)
    planes = [cells[c, x] for x in range(count_x) for c in range(chan)]
    wide = jnp.concatenate(planes, axis=1)
    found = dot(chosen, wide, ((1,), (1,)))
    found = jnp.concatenate([found, jnp.zeros((2 * count, lanes - count_y), f32)], axis=1)
    edges[...] = pltpu.roll(found, 1, 1).astype(bf16)
    for at, plane in enumerate(planes):
        wide_plane = plane.astype(f32)
        rows[at : at + 1, :] = wide_plane[0:1]
        rows[count + at : count + at + 1, :] = wide_plane[count_y - 1 : count_y]


def bundle_kernel(cells, edges, sent_0, sent_1, left, right):
    chan, count_x, count_y, _ = cells.shape
    own = chan * count_x
    whole = edges[...].astype(f32)
    right[...] = whole[0:own]
    left[...] = whole[own : 2 * own]
    zero = jnp.zeros((8, lanes), f32)
    body = chan * count_y
    frames = []
    for x in (0, count_x - 1):
        at = slice(x * chan, x * chan + chan)
        frames.append(jnp.concatenate([whole[own + x * chan :][:chan], whole[at], zero], axis=0))
    even = is_even("gx")
    for ref, odd in ((sent_0, 0), (sent_1, 1)):
        high = even != (odd == 1)
        x = jnp.where(high, count_x - 1, 0)
        for c in range(chan):
            ref[c * count_y : (c + 1) * count_y, :] = cells[c, x]
        ref[body : body + 16, :] = jnp.where(high, frames[1], frames[0]).astype(bf16)


def from_sides(got_0, got_1, start, size):
    one = got_0[start : start + size, :].astype(f32)
    two = got_1[start : start + size, :].astype(f32)
    return pick("gx", two, one), pick("gx", one, two)


def rows_kernel(chan, rows, left, right, got_0, got_1, inner, spread, sent_0, sent_1):
    own = rows.shape[0] // 2
    body = got_0.shape[0] - 16
    count_y = body // chan
    low, high = from_sides(got_0, got_1, body, 16)
    edges = []
    for ref, at in ((left, 0), (right, chan)):
        edges += [ref[...], low[at : at + chan], high[at : at + chan]]
    edges.append(jnp.zeros((8, lanes), f32))
    low, high = from_sides(got_0, got_1, 0, body)
    both = []
    for at, line in ((0, 0), (own, count_y - 1)):
        outer = [
            plane[c * count_y + line : c * count_y + line + 1]
            for plane in (low, high)
            for c in range(chan)
        ]
        both.append(jnp.concatenate([rows[at : at + own, :]] + outer + edges, axis=0))
    sent_0[...] = pick("gy", both[1], both[0]).astype(bf16)
    sent_1[...] = pick("gy", both[0], both[1]).astype(bf16)


def spread_kernel(cot, spread):
    chan_out, pool_x, pool_y, pool_z = cot.shape
    twice = jnp.where(
        iota((pool_z, lanes), 1) // 2 == iota((pool_z, lanes), 0), 0.125, 0.0
    ).astype(bf16)
    for o in range(chan_out):
        part = dot(cot[o].reshape(pool_x * pool_y, pool_z), twice)
        for x in range(pool_x):
            spread[pl.ds(x * chan_out + o, pool_y, stride=pool_x * chan_out), :] = part[
                x * pool_y : (x + 1) * pool_y
            ]


def pool_kernel(edge, sums, outer_sums, pooled):
    chan_out, pool_x, pool_y, pool_z = pooled.shape
    halves = jnp.where(
        iota((2 * lanes, pool_z), 0) % lanes // 2 == iota((2 * lanes, pool_z), 1), 0.125, 0.0
    ).astype(bf16)
    for o in range(0, chan_out, 4):
        rows = 4 * pool_x * pool_y
        part = sums[o * pool_x * pool_y : o * pool_x * pool_y + rows, :]
        at = iota((rows, lanes), 0) % pool_y
        near = (at >= edge) & (at < pool_y - edge)
        part = jnp.where(near, part, outer_sums[o * pool_x * pool_y : o * pool_x * pool_y + rows, :])
        mean = dot(jnp.concatenate(split(part), axis=1), halves) + log_scale * float(np.log(2.0))
        pooled[o : o + 4] = mean.astype(bf16).reshape(4, pool_x, pool_y, pool_z)


def shifted(mid, left, right, y):
    lane = iota(mid.shape, 1)
    low = pltpu.roll(left, (lanes - y) % lanes, 1)
    high = pltpu.roll(right, (lanes - 1 - y) % lanes, 1)
    before = jnp.where(lane == 0, low, pltpu.roll(mid, 1, 1))
    after = jnp.where(lane == lanes - 1, high, pltpu.roll(mid, lanes - 1, 1))
    return [before, mid, after]


def own_kernel(cells, left, right, inner, stage):
    chan, count_x, count_y, _ = cells.shape
    own = chan * count_x
    for x in range(count_x):
        for c in range(chan):
            plane = cells[c, x].astype(f32)
            stage[pl.ds(own + x * chan + c, count_y, stride=own), :] = plane
    left_cols, right_cols = left[...], right[...]
    for y in range(1, count_y + 1):
        whole = shifted(stage[y * own : (y + 1) * own, :], left_cols, right_cols, y)
        whole = jnp.concatenate(whole, axis=0)
        inner[y * 3 * own : (y + 1) * 3 * own, :] = whole.astype(bf16)


pairs = 4


def sizes_of(count_x, inner, spread, wbig):
    pool_x = count_x // 2
    chan_out = wbig.shape[0] // count_x
    pool_y = spread.shape[0] // (pool_x * chan_out)
    own = inner.shape[0] // (3 * (2 * pool_y + 2))
    return pool_x, chan_out, pool_y, own, own // count_x


def worker(count_x, pool_x, chan_out, pool_y, own, chan, near_of, rest_of, refs):
    spread, wbig, wback, sums, field = refs
    wide = own + 2 * chan
    size = 3 * wide
    lane = iota((wide, lanes), 1)
    inside, outside = lane != lanes - 1, lane != 0

    def finish(y, whole, edge):
        first, last = whole[0:wide], whole[2 * wide : 3 * wide]
        inner = (
            whole[wide : 2 * wide]
            + jnp.where(inside, pltpu.roll(first, lanes - 1, 1), 0.0)
            + jnp.where(outside, pltpu.roll(last, 1, 1), 0.0)
        )
        field[pl.ds(aligned(y * wide, 8), wide), :] = inner
        here = lane == y
        edge[0] = jnp.where(here, pltpu.roll(first, y, 1), edge[0])
        edge[1] = jnp.where(here, pltpu.roll(last, y + 1, 1), edge[1])

    def block_of(j):
        columns = [
            jnp.concatenate([near_of(2 * j + h), rest_of(2 * j + h)], axis=0) for h in range(2)
        ]
        return jnp.concatenate(columns, axis=1)

    def forward(i, k, ref):
        j = i * pairs + k
        preact = dot(wbig[...], block_of(j))
        slope = jnp.tanh(5.0 * preact)
        linear = jnp.maximum(preact, 0.3 * preact)
        factor = 1.0 + jnp.abs(slope)
        here = spread[pl.ds(aligned(j * pool_x * chan_out, 8), pool_x * chan_out), :]
        slope = 0.65 + 0.35 * slope
        delta = []
        for x in range(pool_x):
            top, mid = 2 * x * chan_out, (2 * x + 1) * chan_out
            end = mid + chan_out
            times = here[x * chan_out : (x + 1) * chan_out]
            times = jnp.concatenate([times, times], axis=1)
            delta.append((slope[top:mid] * times).astype(bf16))
            delta.append((slope[mid:end] * times).astype(bf16))
            total = linear[top:mid] + linear[mid:end]
            total = total[:, :lanes] + total[:, lanes:]
            prod = factor[top:mid] * factor[mid:end]
            prod = prod[:, :lanes] * prod[:, lanes:]
            total = total - log_scale * jnp.log(prod)
            sums[pl.ds(x * pool_y + j, chan_out, stride=pool_x * pool_y), :] = total
        ref[:, 2 * k * lanes : 2 * (k + 1) * lanes] = jnp.concatenate(delta, axis=0)

    def backward(i, k, ref, held, edge):
        j = i * pairs + k
        parts = dot(wback[...], ref[:, 2 * k * lanes : 2 * (k + 1) * lanes])
        part = lambda b, h: parts[b * size : (b + 1) * size, h * lanes : (h + 1) * lanes]
        finish(2 * j, held[0] + part(0, 0), edge)
        finish(2 * j + 1, held[1] + part(1, 0) + part(0, 1), edge)
        held[0] = part(2, 0) + part(1, 1)
        held[1] = part(2, 1)

    def weigh(i, ref):
        blocks = jnp.concatenate([block_of(i * pairs + k) for k in range(pairs)], axis=1)
        return dot(ref[...], blocks, ((1,), (1,)))

    return finish, forward, backward, weigh


def inner_kernel(
    count_x, got_0, got_1, inner, spread, wbig, wback,
    sums, field, patches, cols, gram, stage, carry, delta_a, delta_b,
):
    shape = sizes_of(count_x, inner, spread, wbig)
    pool_x, chan_out, pool_y, own, chan = shape
    count_y = 2 * pool_y
    wide = own + 2 * chan
    size = 3 * wide
    outside_rows = 2 * chan
    depth = 3 * outside_rows + 8
    body = chan * count_y
    for side, planes in enumerate(from_sides(got_0, got_1, 0, body)):
        for c in range(chan):
            at = outside_rows + side * chan + c
            plane = planes[c * count_y : (c + 1) * count_y]
            stage[pl.ds(at, count_y, stride=outside_rows), :] = plane
    low, high = from_sides(got_0, got_1, body, 16)
    left_cols, right_cols = [
        jnp.concatenate([low[at : at + chan], high[at : at + chan]], axis=0) for at in (0, chan)
    ]
    for y in range(1, count_y + 1):
        mid = stage[y * outside_rows : (y + 1) * outside_rows, :]
        whole = shifted(mid, left_cols, right_cols, y) + [jnp.ones((8, lanes), f32)]
        patches[y * depth : (y + 1) * depth, :] = jnp.concatenate(whole, axis=0).astype(bf16)

    def near_of(y):
        return inner[pl.ds(aligned(y * 3 * own, 16), 9 * own), :]

    def rest_of(y):
        return patches[pl.ds(aligned(y * depth, 16), 3 * depth), :]

    finish, forward, backward, weigh = worker(
        count_x, *shape, near_of, rest_of, (spread, wbig, wback, sums, field)
    )
    carry[...] = jnp.zeros_like(carry)
    gram[...] = jnp.zeros_like(gram)
    cols[...] = jnp.zeros_like(cols)

    def opened():
        return (
            [carry[0:size, :], carry[size : 2 * size, :]],
            [cols[0:wide, :], cols[wide : 2 * wide, :]],
        )

    def closed(held, edge):
        carry[0:size, :] = held[0]
        carry[size : 2 * size, :] = held[1]
        cols[0:wide, :] = edge[0]
        cols[wide : 2 * wide, :] = edge[1]

    def both(at):
        held, edge = opened()
        total = gram[...] + weigh(at, delta_a)
        for k in range(pairs):
            forward(at + 1, k, delta_b)
            backward(at, k, delta_a, held, edge)
        return held, edge, total + weigh(at + 1, delta_b)

    def step(t, _):
        at = 2 * t + 1
        held, edge, total = both(at)
        for k in range(pairs):
            forward(at + 2, k, delta_a)
            backward(at + 1, k, delta_b, held, edge)
        gram[...] = total
        closed(held, edge)
        return 0

    steps = count_y // (2 * pairs)
    for k in range(pairs):
        forward(1, k, delta_a)
    lax.fori_loop(0, steps // 2 - 2, step, 0)
    held, edge, total = both(steps - 3)
    gram[...] = total
    for k in range(pairs):
        backward(steps - 2, k, delta_b, held, edge)
    end = (steps - 1) * 2 * pairs
    finish(end, held[0], edge)
    finish(end + 1, held[1], edge)
    closed(held, edge)


def main_kernel(
    count_x, row_1, row_0, inner, patches, inner_cols, inner_gram, spread, wbig, wback,
    sums, field, sent_0, sent_1, wpart, wframe, rows_out, cols,
    near, rest, gram, delta_a, delta_b,
):
    shape = sizes_of(count_x, inner, spread, wbig)
    pool_x, chan_out, pool_y, own, chan = shape
    count_y = 2 * pool_y
    wide = own + 2 * chan
    size = 3 * wide
    outside_rows = 2 * chan
    depth = 3 * outside_rows + 8
    even = is_even("gx")
    span_y = 2 * pairs
    top = span_y + 2
    start = count_y - span_y
    for ref, source, height in ((near, inner, 3 * own), (rest, patches, depth)):
        ref[height : top * height, :] = source[height : top * height, :]
        last = (2 * top - 1) * height
        ref[top * height : last, :] = source[start * height : (count_y + 1) * height, :]
    one, two = row_0[...].astype(f32), row_1[...].astype(f32)
    above, below = pick("gy", two, one), pick("gy", one, two)
    for at, got, line in ((0, above, count_y), (2 * top - 1, below, 1)):
        left, right = got[wide : 2 * wide], got[2 * wide : 3 * wide]
        whole = jnp.concatenate(shifted(got[:own], left[:own], right[:own], line), axis=0)
        near[at * 3 * own : (at + 1) * 3 * own, :] = whole.astype(bf16)
        whole = shifted(got[own:wide], left[own:], right[own:], line)
        whole = jnp.concatenate(whole + [jnp.ones((8, lanes), f32)], axis=0)
        rest[at * depth : (at + 1) * depth, :] = whole.astype(bf16)

    def place(y):
        return y if y < top else y - start + top

    def near_of(y):
        return near[place(y) * 3 * own : (place(y) + 3) * 3 * own, :]

    def rest_of(y):
        return rest[place(y) * depth : (place(y) + 3) * depth, :]

    finish, forward, backward, weigh = worker(
        count_x, *shape, near_of, rest_of, (spread, wbig, wback, sums, field)
    )
    final = count_y // span_y - 1
    zero = jnp.zeros((size, lanes), f32)
    held, edge = [zero, zero], [inner_cols[0:wide, :], inner_cols[wide : 2 * wide, :]]
    extra = [jnp.zeros((wide, lanes), f32)] * 2
    for k in range(pairs):
        forward(0, k, delta_a)
    for k in range(pairs):
        forward(final, k, delta_b)
        backward(0, k, delta_a, held, extra)
    total = inner_gram[...] + weigh(0, delta_a)
    finish(span_y, held[0], extra)
    finish(span_y + 1, held[1], extra)
    held = [zero, zero]
    for k in range(pairs):
        backward(final, k, delta_b, held, extra)
    gram[...] = total + weigh(final, delta_b)
    finish(count_y, held[0], extra)
    finish(count_y + 1, held[1], extra)
    cols[0:wide, :] = edge[0] + extra[0]
    cols[wide : 2 * wide, :] = edge[1] + extra[1]

    span = gram.shape[1]
    spot = iota((chan_out, 2 * lanes), 1)
    first = 9 * own
    turn = lambda part, shift: pltpu.roll(part, (2 * lanes - shift) % (2 * lanes), 1)
    straight, turned, extra = 0.0, 0.0, 0.0
    for x in range(count_x):
        part = gram[x * chan_out : (x + 1) * chan_out, :]
        part = jnp.concatenate([part, jnp.zeros((chan_out, 2 * lanes - span), f32)], axis=1)
        straight = straight + part
        moved = turn(part, chan * (x - 1)) if x != 1 else part
        a = spot % own // chan
        turned = turned + jnp.where((a + x >= 1) & (a + x <= count_x), moved, 0.0)
        if x == 0:
            extra = extra + jnp.where((spot - first) % outside_rows < chan, part, 0.0)
        if x == count_x - 1:
            extra = extra + jnp.where((spot - first) % outside_rows >= chan, part, 0.0)
    group = 3 * chan
    tight = jnp.zeros((chan_out, 2 * lanes), f32)
    for b in range(3):
        for e in range(3):
            at = (b * 3 + e) * group
            here = spot // group == b * 3 + e
            value = turn(turned, b * 3 * own + e * own - at)
            source = first + b * depth + e * outside_rows
            low, high = turn(extra, source - at), turn(extra, source - at - chan)
            a = (spot - at) // chan
            value = value + jnp.where(a == 0, low, 0.0) + jnp.where(a == 2, high, 0.0)
            tight = jnp.where(here, value, tight)
    bias_at = first + 3 * outside_rows
    tight = jnp.where(spot == 9 * group, turn(straight, bias_at - 9 * group), tight)
    tight = tight[:, :lanes]
    wpart[...] = tight
    sides = jnp.concatenate(split(tight), axis=0)
    wframe[...] = sides

    ends = [field[0:wide, :], field[(count_y + 1) * wide : (count_y + 2) * wide, :]]
    rows_out[...] = jnp.concatenate([end[chan : chan + own] for end in ends], axis=0)
    zero = jnp.zeros((8, lanes), f32)
    for ref, odd in ((sent_0, 0), (sent_1, 1)):
        high = even != (odd == 1)
        low_frame, high_frame = [
            jnp.concatenate(
                [end[x * chan : (x + 1) * chan] for end in ends]
                + [cols[top + x * chan : top + (x + 1) * chan, :] for top in (0, wide)],
                axis=0,
            )
            for x in (0, count_x + 1)
        ]
        ref[0:16, :] = jnp.where(high, high_frame, low_frame).astype(bf16)
        ref[16:, :] = sides


def plane_of(field, outer_field, at, wide, count_y):
    row = iota((count_y, lanes), 0) + 1
    span_y = 2 * pairs
    place = pl.ds(wide + at, count_y, stride=wide)
    near = (row >= span_y) & (row < count_y - span_y + 2)
    far = (row < span_y + 2) | (row >= count_y - span_y)
    return jnp.where(near, field[place, :], 0.0) + jnp.where(far, outer_field[place, :], 0.0)


def face_kernel(chan, field, outer_field, face_0, face_1):
    count_y = face_0.shape[0] // chan
    wide = field.shape[0] // (count_y + 2)
    even = is_even("gx")
    for c in range(chan):
        low, high = [
            plane_of(field, outer_field, at + c, wide, count_y) for at in (0, wide - chan)
        ]
        place = slice(c * count_y, (c + 1) * count_y)
        face_0[place, :] = jnp.where(even, high, low).astype(bf16)
        face_1[place, :] = jnp.where(even, low, high).astype(bf16)


def x_kernel(alone, wpart, wframe, rows, cols, got_0, got_1, far, frame, rows_out):
    own = rows.shape[0] // 2
    wide = cols.shape[0] // 2
    chan = (wide - own) // 2
    if alone:
        total = wpart[...]
    else:
        total = joined(wframe[...]) + joined(far[16:, :])
        total = total + (joined(got_0[16:, :]) + joined(got_1[16:, :]))
    frame[2 * own :, :] = jnp.concatenate(split(total), axis=0)
    one, two = got_0[0:16, :].astype(f32), got_1[0:16, :].astype(f32)
    from_low, from_high = pick("gx", two, one), pick("gx", one, two)
    mid = jnp.zeros((own - 2 * chan, lanes), f32)
    found = []
    for top, at in ((0, 2 * chan), (wide, 3 * chan)):
        more = [from_low[at : at + chan], mid, from_high[at : at + chan]]
        found.append(cols[top + chan : top + chan + own, :] + jnp.concatenate(more, axis=0))
    frame[0 : 2 * own, :] = jnp.concatenate(found, axis=0).astype(bf16)
    for at in (0, 1):
        more = [from_low[at * chan : (at + 1) * chan], mid, from_high[at * chan : (at + 1) * chan]]
        place = slice(at * own, (at + 1) * own)
        rows_out[place, :] = rows[place, :] + jnp.concatenate(more, axis=0)


def z_kernel(count_y, mine, got, rows, sent_0, sent_1, wframe):
    own = rows.shape[0] // 2
    total = joined(mine[2 * own :, :]) + joined(got[2 * own :, :])
    sides = jnp.concatenate(split(total), axis=0)
    wframe[...] = sides
    last = got[0:own, :].astype(f32)
    first = got[own : 2 * own, :].astype(f32)
    spot = iota((own, lanes), 1)
    both = []
    for at, line in ((0, 0), (1, count_y + 1)):
        more = jnp.where(spot == lanes - 1, pltpu.roll(last, lanes - 1 - line, 1), 0.0)
        turned = pltpu.roll(first, lanes - line, 1) if line else first
        more = jnp.where(spot == 0, turned, more)
        both.append(rows[at * own : (at + 1) * own, :] + more)
    sent_0[0:own, :] = pick("gy", both[1], both[0]).astype(bf16)
    sent_1[0:own, :] = pick("gy", both[0], both[1]).astype(bf16)
    for ref in (sent_0, sent_1):
        ref[own:, :] = sides


def grad_kernel(field, outer_field, face_0, face_1, got, grad, ends):
    chan, count_x, count_y, _ = grad.shape
    own = chan * count_x
    wide = own + 2 * chan
    spot = iota((count_y, lanes), 1)
    columns = pltpu.roll(got[0 : 2 * own, :].astype(f32), lanes - 1, 1)
    columns = jnp.concatenate([columns, jnp.zeros((lanes - 2 * own, lanes), f32)], axis=0)
    columns = columns.T[0:count_y]
    for x in range(count_x):
        for c in range(chan):
            at = x * chan + c
            plane = plane_of(field, outer_field, chan + at, wide, count_y)
            place = slice(c * count_y, (c + 1) * count_y)
            if x == 0:
                plane = plane + pick("gx", face_1[place, :].astype(f32), face_0[place, :].astype(f32))
            if x == count_x - 1:
                plane = plane + pick("gx", face_0[place, :].astype(f32), face_1[place, :].astype(f32))
            more = jnp.where(spot == lanes - 1, columns[:, at : at + 1], 0.0)
            plane = plane + jnp.where(spot == 0, columns[:, own + at : own + at + 1], more)
            grad[c, x] = plane
            ends[0, c, x] = plane[0:8]
            ends[1, c, x] = plane[count_y - 8 : count_y]


def final_kernel(whole, ends, mine, got_1, far, got_0, out, wout, bout, tiles, wtile, btile, sems):
    chan, count_x, count_y, _ = whole.shape
    own = chan * count_x
    chan_out = mine.shape[0] // 2
    row = iota((8, lanes), 0)
    one, two = got_0[0:own, :].astype(f32), got_1[0:own, :].astype(f32)
    above, below = pick("gy", two, one), pick("gy", one, two)
    copies = []
    for side, more, line in ((0, above, 0), (1, below, 7)):
        for x in range(count_x):
            for c in range(chan):
                at = x * chan + c
                extra = jnp.where(row == line, more[at : at + 1], 0.0)
                tiles[side, c, x] = ends[side, c, x] + extra
        copies.append(
            pltpu.make_async_copy(
                tiles.at[side],
                out.at[:, :, pl.ds(side * (count_y - 8), 8), :],
                sems.at[side],
            )
        )
        copies[-1].start()
    total = joined(mine[...]) + joined(far[own:, :])
    total = total + (joined(got_0[own:, :]) + joined(got_1[own:, :]))
    total = jnp.concatenate([total, jnp.zeros((lanes - chan_out, lanes), f32)], axis=0)
    total = total.T
    for a in range(3):
        for be in range(9):
            at = (be * 3 + a) * chan
            wtile[a * 9 + be] = total[at : at + chan, :chan_out]
    btile[...] = total[27 * chan : 27 * chan + 1, :chan_out]
    copies.append(pltpu.make_async_copy(wtile, wout, sems.at[2]))
    copies.append(pltpu.make_async_copy(btile, bout, sems.at[3]))
    copies[2].start()
    copies[3].start()
    for copy in copies:
        copy.wait()


def traffic(mib):
    return pl.CostEstimate(flops=0, bytes_accessed=mib << 20, transcendentals=0)


def call(kernel, outs, scratch=(), cost=None, **rest):
    return pl.pallas_call(
        kernel,
        out_shape=outs,
        **rest,
        scratch_shapes=list(scratch),
        cost_estimate=cost,
        compiler_params=pltpu.CompilerParams(vmem_limit_bytes=limit),
    )


def on_device(cells, weight, bias, cotangent):
    chan, count_x, count_y, count_z = cells.shape
    chan_out = weight.shape[0]
    own = chan * count_x
    wide = own + 2 * chan
    depth = 6 * chan + 8
    shape = jax.ShapeDtypeStruct

    kernel = weight.transpose(0, 3, 4, 2, 1)
    placed = jnp.stack(
        [
            jnp.pad(kernel, ((0, 0), (0, 0), (0, 0), (x, count_x - 1 - x), (0, 0)))
            for x in range(count_x)
        ]
    ).reshape(count_x * chan_out, 3, 3, count_x + 2, chan)
    coarse = lax.reduce_precision(bias, 8, 7)
    middle = lax.reduce_precision(bias - coarse, 8, 7)
    fine = bias - coarse - middle
    pieces = jnp.stack([coarse, middle, fine], axis=1).astype(bf16)
    pieces = jnp.pad(jnp.tile(pieces, (count_x, 1))[:, None], ((0, 0), (0, 2), (0, 5)))
    near = placed[:, :, :, 1 : count_x + 1].reshape(count_x * chan_out, 9 * own)
    rest = jnp.concatenate([placed[:, :, :, :1], placed[:, :, :, count_x + 1 :]], axis=3)
    rest = jnp.concatenate([rest.reshape(count_x * chan_out, 3, 6 * chan), pieces], axis=2)
    wbig = jnp.concatenate([near, rest.reshape(count_x * chan_out, 3 * depth)], axis=1)
    wback = placed.reshape(count_x * chan_out, 9 * wide).T

    edges, rows = call(
        pack_kernel, [shape((2 * own, lanes), bf16), shape((2 * own, lanes), f32)]
    )(cells)
    pool_x, pool_y, pool_z = cotangent.shape[1:]
    pooled_rows = shape((pool_y * pool_x * chan_out, lanes), f32)
    spread = call(spread_kernel, pooled_rows)(cotangent)
    edges = swapped(edges, "gz", 0)
    body = chan * count_y
    bundle = shape((body + 16, lanes), bf16)
    side = shape((own, lanes), f32)
    face_0, face_1, left, right = call(bundle_kernel, [bundle, bundle, side, side])(cells, edges)
    face_1, face_0 = swapped(face_1, "gx", 1), swapped(face_0, "gx", 0)
    inner = call(
        own_kernel,
        shape(((count_y + 2) * 3 * own, lanes), bf16),
        [pltpu.VMEM(((count_y + 2) * own, lanes), f32)],
        traffic(4),
    )(cells, left, right)
    bundle = shape((3 * wide + 8, lanes), bf16)
    vmem, anywhere = pl.BlockSpec(memory_space=pltpu.VMEM), pl.BlockSpec(memory_space=pl.ANY)
    row_0, row_1 = call(
        functools.partial(rows_kernel, chan),
        [bundle, bundle],
        in_specs=[vmem] * 5 + [anywhere] * 2,
    )(rows, left, right, face_0, face_1, inner, spread)
    row_1, row_0 = swapped(row_1, "gy", 1), swapped(row_0, "gy", 0)

    tall = 2 * wide
    all_field = shape(((count_y + 2) * wide, lanes), f32)
    all_gram = shape((count_x * chan_out, 9 * own + 3 * depth), f32)
    deltas = [pltpu.VMEM((count_x * chan_out, 8 * lanes), bf16)] * 2
    sums, field, patches, cols, gram = call(
        functools.partial(inner_kernel, count_x),
        [
            pooled_rows,
            all_field,
            shape(((count_y + 2) * depth, lanes), bf16),
            shape((tall, lanes), f32),
            all_gram,
        ],
        [
            pltpu.VMEM(((count_y + 2) * 2 * chan, lanes), f32),
            pltpu.VMEM((6 * wide, lanes), f32),
        ]
        + deltas,
        traffic(16),
    )(face_0, face_1, inner, spread, wbig, wback)

    bundle = shape((16 + 2 * chan_out, lanes), bf16)
    face = shape((body, lanes), bf16)
    outer_sums, outer_field, row_0, row_1, wpart, wframe, rows, cols = call(
        functools.partial(main_kernel, count_x),
        [
            pooled_rows,
            all_field,
            bundle,
            bundle,
            shape((chan_out, lanes), f32),
            shape((2 * chan_out, lanes), bf16),
            shape((2 * own, lanes), f32),
            shape((tall, lanes), f32),
        ],
        [
            pltpu.VMEM((4 * (pairs + 1) * 3 * own, lanes), bf16),
            pltpu.VMEM((4 * (pairs + 1) * depth, lanes), bf16),
            pltpu.VMEM((count_x * chan_out, 9 * own + 3 * depth), f32),
        ]
        + deltas,
    )(row_1, row_0, inner, patches, cols, gram, spread, wbig, wback)

    alone = lax.axis_size("gx") != 4
    if alone:
        wpart, far = lax.psum(wpart, "gx"), row_0
    else:
        far = swapped(row_0, "gx", 2)
    row_1, row_0 = swapped(row_1, "gx", 1), swapped(row_0, "gx", 0)
    face_0, face_1 = call(functools.partial(face_kernel, chan), [face, face], cost=traffic(2))(
        field, outer_field
    )
    face_1, face_0 = swapped(face_1, "gx", 1), swapped(face_0, "gx", 0)
    pooled = call(
        functools.partial(pool_kernel, pairs), shape(cotangent.shape, bf16), cost=traffic(8)
    )(sums, outer_sums)
    mine, rows = call(
        functools.partial(x_kernel, alone),
        [shape((2 * own + 2 * chan_out, lanes), bf16), shape((2 * own, lanes), f32)],
    )(wpart, wframe, rows, cols, row_0, row_1, far)
    frame = swapped(mine, "gz", 0)
    bundle = shape((own + 2 * chan_out, lanes), bf16)
    row_0, row_1, mine = call(
        functools.partial(z_kernel, count_y),
        [bundle, bundle, shape((2 * chan_out, lanes), bf16)],
    )(mine, frame, rows)
    far = swapped(row_1, "gy", 2)
    row_1, row_0 = swapped(row_1, "gy", 1), swapped(row_0, "gy", 0)
    tiles = (2, chan, count_x, 8, lanes)
    grad, ends = call(grad_kernel, [shape(cells.shape, f32), shape(tiles, f32)], cost=traffic(8))(
        field, outer_field, face_0, face_1, frame
    )
    input_grad, wsum, bias_grad = call(
        final_kernel,
        [
            shape(cells.shape, f32),
            shape((27, chan, chan_out), f32),
            shape((1, chan_out), f32),
        ],
        [
            pltpu.VMEM(tiles, f32),
            pltpu.VMEM((27, chan, chan_out), f32),
            pltpu.VMEM((1, chan_out), f32),
            pltpu.SemaphoreType.DMA((4,)),
        ],
        in_specs=[anywhere] + [vmem] * 5,
        out_specs=[anywhere] * 3,
        input_output_aliases={0: 0},
    )(grad, ends, mine, row_1, far, row_0)
    weight_grad = wsum.reshape(3, 3, 3, chan, chan_out).transpose(4, 3, 0, 1, 2)
    return (pooled, weight_grad, bias_grad.reshape(chan_out), input_grad)


def solution(mesh):
    in_specs = (P(None, "gx", "gy", "gz"), P(), P(), P(None, "gx", "gy", "gz"))
    out_specs = (P(None, "gx", "gy", "gz"), P(), P(), P(None, "gx", "gy", "gz"))
    return jax.shard_map(
        on_device, mesh=mesh, in_specs=in_specs, out_specs=out_specs, check_vma=False
    )
```

```python
import functools

import jax
import jax.numpy as jnp
import numpy as np
from jax import lax
from jax.experimental import pallas as pl
from jax.experimental.pallas import tpu as pltpu
from jax.sharding import PartitionSpec as P

axes = ("gx", "gy", "gz")
f32, bf16 = jnp.float32, jnp.bfloat16
log_scale = 0.07
lanes = 128
limit = 48 * 1024 * 1024


def dot(a, b, contract=((1,), (0,))):
    return lax.dot_general(a, b, (contract, ((), ())), preferred_element_type=f32)


def iota(shape, dim):
    return lax.broadcasted_iota(jnp.int32, shape, dim)


def aligned(start, tile):
    return start if isinstance(start, int) else pl.multiple_of(start, tile)


def swapped(array, axis, pairing):
    count = lax.axis_size(axis)
    pairs = []
    for i in range(count):
        if pairing == 2:
            partner = i + count // 2
        else:
            partner = i + 1 if i % 2 == pairing else i - 1
        pairs.append((i, partner % count))
    return lax.ppermute(array, axis, pairs)


def is_even(axis):
    return lax.rem(lax.axis_index(axis), 2) == 0


def pick(axis, if_even, if_odd):
    return jnp.where(is_even(axis), if_even, if_odd)


def split(value):
    coarse = value.astype(bf16)
    return coarse, (value - coarse.astype(f32)).astype(bf16)


def joined(pair):
    half = pair.shape[0] // 2
    return pair[:half].astype(f32) + pair[half:].astype(f32)


def pack_kernel(cells, edges, rows):
    chan, count_x, count_y, _ = cells.shape
    count = chan * count_x
    row = iota((2 * count, count * lanes), 0)
    lane = iota((2 * count, count * lanes), 1)
    want = jnp.where(row < count, row * lanes, (row - count) * lanes + lanes - 1)
    chosen = (lane == want).astype(f32).astype(bf16)
    planes = [cells[c, x] for x in range(count_x) for c in range(chan)]
    wide = jnp.concatenate(planes, axis=1)
    found = dot(chosen, wide, ((1,), (1,)))
    found = jnp.concatenate([found, jnp.zeros((2 * count, lanes - count_y), f32)], axis=1)
    edges[...] = pltpu.roll(found, 1, 1).astype(bf16)
    for at, plane in enumerate(planes):
        wide_plane = plane.astype(f32)
        rows[at : at + 1, :] = wide_plane[0:1]
        rows[count + at : count + at + 1, :] = wide_plane[count_y - 1 : count_y]


def bundle_kernel(cells, edges, sent_0, sent_1, left, right):
    chan, count_x, count_y, _ = cells.shape
    own = chan * count_x
    whole = edges[...].astype(f32)
    right[...] = whole[0:own]
    left[...] = whole[own : 2 * own]
    zero = jnp.zeros((8, lanes), f32)
    body = chan * count_y
    frames = []
    for x in (0, count_x - 1):
        at = slice(x * chan, x * chan + chan)
        frames.append(jnp.concatenate([whole[own + x * chan :][:chan], whole[at], zero], axis=0))
    even = is_even("gx")
    for ref, odd in ((sent_0, 0), (sent_1, 1)):
        high = even != (odd == 1)
        x = jnp.where(high, count_x - 1, 0)
        for c in range(chan):
            ref[c * count_y : (c + 1) * count_y, :] = cells[c, x]
        ref[body : body + 16, :] = jnp.where(high, frames[1], frames[0]).astype(bf16)


def from_sides(got_0, got_1, start, size):
    one = got_0[start : start + size, :].astype(f32)
    two = got_1[start : start + size, :].astype(f32)
    return pick("gx", two, one), pick("gx", one, two)


def rows_kernel(chan, rows, left, right, got_0, got_1, inner, spread, sent_0, sent_1):
    own = rows.shape[0] // 2
    body = got_0.shape[0] - 16
    count_y = body // chan
    low, high = from_sides(got_0, got_1, body, 16)
    edges = []
    for ref, at in ((left, 0), (right, chan)):
        edges += [ref[...], low[at : at + chan], high[at : at + chan]]
    edges.append(jnp.zeros((8, lanes), f32))
    low, high = from_sides(got_0, got_1, 0, body)
    both = []
    for at, line in ((0, 0), (own, count_y - 1)):
        outer = [
            plane[c * count_y + line : c * count_y + line + 1]
            for plane in (low, high)
            for c in range(chan)
        ]
        both.append(jnp.concatenate([rows[at : at + own, :]] + outer + edges, axis=0))
    sent_0[...] = pick("gy", both[1], both[0]).astype(bf16)
    sent_1[...] = pick("gy", both[0], both[1]).astype(bf16)


def spread_kernel(cot, spread):
    chan_out, pool_x, pool_y, pool_z = cot.shape
    twice = jnp.where(
        iota((pool_z, lanes), 1) // 2 == iota((pool_z, lanes), 0), 0.125, 0.0
    ).astype(bf16)
    for o in range(chan_out):
        part = dot(cot[o].reshape(pool_x * pool_y, pool_z), twice)
        for x in range(pool_x):
            spread[pl.ds(x * chan_out + o, pool_y, stride=pool_x * chan_out), :] = part[
                x * pool_y : (x + 1) * pool_y
            ]


def pool_kernel(edge, sums, outer_sums, pooled):
    chan_out, pool_x, pool_y, pool_z = pooled.shape
    halves = jnp.where(
        iota((2 * lanes, pool_z), 0) % lanes // 2 == iota((2 * lanes, pool_z), 1), 0.125, 0.0
    ).astype(bf16)
    for o in range(0, chan_out, 4):
        rows = 4 * pool_x * pool_y
        part = sums[o * pool_x * pool_y : o * pool_x * pool_y + rows, :]
        at = iota((rows, lanes), 0) % pool_y
        near = (at >= edge) & (at < pool_y - edge)
        part = jnp.where(near, part, outer_sums[o * pool_x * pool_y : o * pool_x * pool_y + rows, :])
        mean = dot(jnp.concatenate(split(part), axis=1), halves) + log_scale * float(np.log(2.0))
        pooled[o : o + 4] = mean.astype(bf16).reshape(4, pool_x, pool_y, pool_z)


def shifted(mid, left, right, y):
    lane = iota(mid.shape, 1)
    low = pltpu.roll(left, (lanes - y) % lanes, 1)
    high = pltpu.roll(right, (lanes - 1 - y) % lanes, 1)
    before = jnp.where(lane == 0, low, pltpu.roll(mid, 1, 1))
    after = jnp.where(lane == lanes - 1, high, pltpu.roll(mid, lanes - 1, 1))
    return [before, mid, after]


def own_kernel(cells, left, right, inner, stage):
    chan, count_x, count_y, _ = cells.shape
    own = chan * count_x
    for x in range(count_x):
        for c in range(chan):
            plane = cells[c, x].astype(f32)
            stage[pl.ds(own + x * chan + c, count_y, stride=own), :] = plane
    left_cols, right_cols = left[...], right[...]
    for y in range(1, count_y + 1):
        whole = shifted(stage[y * own : (y + 1) * own, :], left_cols, right_cols, y)
        whole = jnp.concatenate(whole, axis=0)
        inner[y * 3 * own : (y + 1) * 3 * own, :] = whole.astype(bf16)


pairs = 4


def sizes_of(count_x, inner, spread, wbig):
    pool_x = count_x // 2
    chan_out = wbig.shape[0] // count_x
    pool_y = spread.shape[0] // (pool_x * chan_out)
    own = inner.shape[0] // (3 * (2 * pool_y + 2))
    return pool_x, chan_out, pool_y, own, own // count_x


def worker(count_x, pool_x, chan_out, pool_y, own, chan, near_of, rest_of, refs):
    spread, wbig, wback, sums, field = refs
    wide = own + 2 * chan
    size = 3 * wide
    lane = iota((wide, lanes), 1)
    inside, outside = lane != lanes - 1, lane != 0

    def finish(y, whole, edge):
        first, last = whole[0:wide], whole[2 * wide : 3 * wide]
        inner = (
            whole[wide : 2 * wide]
            + jnp.where(inside, pltpu.roll(first, lanes - 1, 1), 0.0)
            + jnp.where(outside, pltpu.roll(last, 1, 1), 0.0)
        )
        field[pl.ds(aligned(y * wide, 8), wide), :] = inner
        here = lane == y
        edge[0] = jnp.where(here, pltpu.roll(first, y, 1), edge[0])
        edge[1] = jnp.where(here, pltpu.roll(last, y + 1, 1), edge[1])

    def block_of(j):
        columns = [
            jnp.concatenate([near_of(2 * j + h), rest_of(2 * j + h)], axis=0) for h in range(2)
        ]
        return jnp.concatenate(columns, axis=1)

    def forward(i, k, ref):
        j = i * pairs + k
        preact = dot(wbig[...], block_of(j))
        slope = jnp.tanh(5.0 * preact)
        linear = jnp.maximum(preact, 0.3 * preact)
        factor = 1.0 + jnp.abs(slope)
        here = spread[pl.ds(aligned(j * pool_x * chan_out, 8), pool_x * chan_out), :]
        slope = 0.65 + 0.35 * slope
        delta = []
        for x in range(pool_x):
            top, mid = 2 * x * chan_out, (2 * x + 1) * chan_out
            end = mid + chan_out
            times = here[x * chan_out : (x + 1) * chan_out]
            times = jnp.concatenate([times, times], axis=1)
            delta.append((slope[top:mid] * times).astype(bf16))
            delta.append((slope[mid:end] * times).astype(bf16))
            total = linear[top:mid] + linear[mid:end]
            total = total[:, :lanes] + total[:, lanes:]
            prod = factor[top:mid] * factor[mid:end]
            prod = prod[:, :lanes] * prod[:, lanes:]
            total = total - log_scale * jnp.log(prod)
            sums[pl.ds(x * pool_y + j, chan_out, stride=pool_x * pool_y), :] = total
        ref[:, 2 * k * lanes : 2 * (k + 1) * lanes] = jnp.concatenate(delta, axis=0)

    def backward(i, k, ref, held, edge):
        j = i * pairs + k
        parts = dot(wback[...], ref[:, 2 * k * lanes : 2 * (k + 1) * lanes])
        part = lambda b, h: parts[b * size : (b + 1) * size, h * lanes : (h + 1) * lanes]
        finish(2 * j, held[0] + part(0, 0), edge)
        finish(2 * j + 1, held[1] + part(1, 0) + part(0, 1), edge)
        held[0] = part(2, 0) + part(1, 1)
        held[1] = part(2, 1)

    def weigh(i, ref):
        blocks = jnp.concatenate([block_of(i * pairs + k) for k in range(pairs)], axis=1)
        return dot(ref[...], blocks, ((1,), (1,)))

    return finish, forward, backward, weigh


def inner_kernel(
    count_x, got_0, got_1, inner, spread, wbig, wback,
    sums, field, patches, cols, gram, stage, carry, delta_a, delta_b,
):
    shape = sizes_of(count_x, inner, spread, wbig)
    pool_x, chan_out, pool_y, own, chan = shape
    count_y = 2 * pool_y
    wide = own + 2 * chan
    size = 3 * wide
    outside_rows = 2 * chan
    depth = 3 * outside_rows + 8
    body = chan * count_y
    for side, planes in enumerate(from_sides(got_0, got_1, 0, body)):
        for c in range(chan):
            at = outside_rows + side * chan + c
            plane = planes[c * count_y : (c + 1) * count_y]
            stage[pl.ds(at, count_y, stride=outside_rows), :] = plane
    low, high = from_sides(got_0, got_1, body, 16)
    left_cols, right_cols = [
        jnp.concatenate([low[at : at + chan], high[at : at + chan]], axis=0) for at in (0, chan)
    ]
    for y in range(1, count_y + 1):
        mid = stage[y * outside_rows : (y + 1) * outside_rows, :]
        whole = shifted(mid, left_cols, right_cols, y) + [jnp.ones((8, lanes), f32)]
        patches[y * depth : (y + 1) * depth, :] = jnp.concatenate(whole, axis=0).astype(bf16)

    def near_of(y):
        return inner[pl.ds(aligned(y * 3 * own, 16), 9 * own), :]

    def rest_of(y):
        return patches[pl.ds(aligned(y * depth, 16), 3 * depth), :]

    finish, forward, backward, weigh = worker(
        count_x, *shape, near_of, rest_of, (spread, wbig, wback, sums, field)
    )
    carry[...] = jnp.zeros_like(carry)
    gram[...] = jnp.zeros_like(gram)
    cols[...] = jnp.zeros_like(cols)

    def opened():
        return (
            [carry[0:size, :], carry[size : 2 * size, :]],
            [cols[0:wide, :], cols[wide : 2 * wide, :]],
        )

    def closed(held, edge):
        carry[0:size, :] = held[0]
        carry[size : 2 * size, :] = held[1]
        cols[0:wide, :] = edge[0]
        cols[wide : 2 * wide, :] = edge[1]

    def both(at):
        held, edge = opened()
        total = gram[...] + weigh(at, delta_a)
        for k in range(pairs):
            forward(at + 1, k, delta_b)
            backward(at, k, delta_a, held, edge)
        return held, edge, total + weigh(at + 1, delta_b)

    def step(t, _):
        at = 2 * t + 1
        held, edge, total = both(at)
        for k in range(pairs):
            forward(at + 2, k, delta_a)
            backward(at + 1, k, delta_b, held, edge)
        gram[...] = total
        closed(held, edge)
        return 0

    steps = count_y // (2 * pairs)
    for k in range(pairs):
        forward(1, k, delta_a)
    lax.fori_loop(0, steps // 2 - 2, step, 0)
    held, edge, total = both(steps - 3)
    gram[...] = total
    for k in range(pairs):
        backward(steps - 2, k, delta_b, held, edge)
    end = (steps - 1) * 2 * pairs
    finish(end, held[0], edge)
    finish(end + 1, held[1], edge)
    closed(held, edge)


def main_kernel(
    count_x, row_1, row_0, inner, patches, inner_cols, inner_gram, spread, wbig, wback,
    sums, field, sent_0, sent_1, wpart, wframe, rows_out, cols,
    near, rest, gram, delta_a, delta_b,
):
    shape = sizes_of(count_x, inner, spread, wbig)
    pool_x, chan_out, pool_y, own, chan = shape
    count_y = 2 * pool_y
    wide = own + 2 * chan
    size = 3 * wide
    outside_rows = 2 * chan
    depth = 3 * outside_rows + 8
    even = is_even("gx")
    span_y = 2 * pairs
    top = span_y + 2
    start = count_y - span_y
    for ref, source, height in ((near, inner, 3 * own), (rest, patches, depth)):
        ref[height : top * height, :] = source[height : top * height, :]
        last = (2 * top - 1) * height
        ref[top * height : last, :] = source[start * height : (count_y + 1) * height, :]
    one, two = row_0[...].astype(f32), row_1[...].astype(f32)
    above, below = pick("gy", two, one), pick("gy", one, two)
    for at, got, line in ((0, above, count_y), (2 * top - 1, below, 1)):
        left, right = got[wide : 2 * wide], got[2 * wide : 3 * wide]
        whole = jnp.concatenate(shifted(got[:own], left[:own], right[:own], line), axis=0)
        near[at * 3 * own : (at + 1) * 3 * own, :] = whole.astype(bf16)
        whole = shifted(got[own:wide], left[own:], right[own:], line)
        whole = jnp.concatenate(whole + [jnp.ones((8, lanes), f32)], axis=0)
        rest[at * depth : (at + 1) * depth, :] = whole.astype(bf16)

    def place(y):
        return y if y < top else y - start + top

    def near_of(y):
        return near[place(y) * 3 * own : (place(y) + 3) * 3 * own, :]

    def rest_of(y):
        return rest[place(y) * depth : (place(y) + 3) * depth, :]

    finish, forward, backward, weigh = worker(
        count_x, *shape, near_of, rest_of, (spread, wbig, wback, sums, field)
    )
    final = count_y // span_y - 1
    zero = jnp.zeros((size, lanes), f32)
    held, edge = [zero, zero], [inner_cols[0:wide, :], inner_cols[wide : 2 * wide, :]]
    extra = [jnp.zeros((wide, lanes), f32)] * 2
    for k in range(pairs):
        forward(0, k, delta_a)
    for k in range(pairs):
        forward(final, k, delta_b)
        backward(0, k, delta_a, held, extra)
    total = inner_gram[...] + weigh(0, delta_a)
    finish(span_y, held[0], extra)
    finish(span_y + 1, held[1], extra)
    held = [zero, zero]
    for k in range(pairs):
        backward(final, k, delta_b, held, extra)
    gram[...] = total + weigh(final, delta_b)
    finish(count_y, held[0], extra)
    finish(count_y + 1, held[1], extra)
    cols[0:wide, :] = edge[0] + extra[0]
    cols[wide : 2 * wide, :] = edge[1] + extra[1]

    span = gram.shape[1]
    spot = iota((chan_out, 2 * lanes), 1)
    first = 9 * own
    turn = lambda part, shift: pltpu.roll(part, (2 * lanes - shift) % (2 * lanes), 1)
    straight, turned, extra = 0.0, 0.0, 0.0
    for x in range(count_x):
        part = gram[x * chan_out : (x + 1) * chan_out, :]
        part = jnp.concatenate([part, jnp.zeros((chan_out, 2 * lanes - span), f32)], axis=1)
        straight = straight + part
        moved = turn(part, chan * (x - 1)) if x != 1 else part
        a = spot % own // chan
        turned = turned + jnp.where((a + x >= 1) & (a + x <= count_x), moved, 0.0)
        if x == 0:
            extra = extra + jnp.where((spot - first) % outside_rows < chan, part, 0.0)
        if x == count_x - 1:
            extra = extra + jnp.where((spot - first) % outside_rows >= chan, part, 0.0)
    group = 3 * chan
    tight = jnp.zeros((chan_out, 2 * lanes), f32)
    for b in range(3):
        for e in range(3):
            at = (b * 3 + e) * group
            here = spot // group == b * 3 + e
            value = turn(turned, b * 3 * own + e * own - at)
            source = first + b * depth + e * outside_rows
            low, high = turn(extra, source - at), turn(extra, source - at - chan)
            a = (spot - at) // chan
            value = value + jnp.where(a == 0, low, 0.0) + jnp.where(a == 2, high, 0.0)
            tight = jnp.where(here, value, tight)
    bias_at = first + 3 * outside_rows
    tight = jnp.where(spot == 9 * group, turn(straight, bias_at - 9 * group), tight)
    tight = tight[:, :lanes]
    wpart[...] = tight
    sides = jnp.concatenate(split(tight), axis=0)
    wframe[...] = sides

    ends = [field[0:wide, :], field[(count_y + 1) * wide : (count_y + 2) * wide, :]]
    rows_out[...] = jnp.concatenate([end[chan : chan + own] for end in ends], axis=0)
    zero = jnp.zeros((8, lanes), f32)
    for ref, odd in ((sent_0, 0), (sent_1, 1)):
        high = even != (odd == 1)
        low_frame, high_frame = [
            jnp.concatenate(
                [end[x * chan : (x + 1) * chan] for end in ends]
                + [cols[top + x * chan : top + (x + 1) * chan, :] for top in (0, wide)],
                axis=0,
            )
            for x in (0, count_x + 1)
        ]
        ref[0:16, :] = jnp.where(high, high_frame, low_frame).astype(bf16)
        ref[16:, :] = sides


def plane_of(field, outer_field, at, wide, count_y):
    row = iota((count_y, lanes), 0) + 1
    span_y = 2 * pairs
    place = pl.ds(wide + at, count_y, stride=wide)
    near = (row >= span_y) & (row < count_y - span_y + 2)
    far = (row < span_y + 2) | (row >= count_y - span_y)
    return jnp.where(near, field[place, :], 0.0) + jnp.where(far, outer_field[place, :], 0.0)


def face_kernel(chan, field, outer_field, face_0, face_1):
    count_y = face_0.shape[0] // chan
    wide = field.shape[0] // (count_y + 2)
    even = is_even("gx")
    for c in range(chan):
        low, high = [
            plane_of(field, outer_field, at + c, wide, count_y) for at in (0, wide - chan)
        ]
        place = slice(c * count_y, (c + 1) * count_y)
        face_0[place, :] = jnp.where(even, high, low).astype(bf16)
        face_1[place, :] = jnp.where(even, low, high).astype(bf16)


def x_kernel(alone, wpart, wframe, rows, cols, got_0, got_1, far, frame, rows_out):
    own = rows.shape[0] // 2
    wide = cols.shape[0] // 2
    chan = (wide - own) // 2
    if alone:
        total = wpart[...]
    else:
        total = joined(wframe[...]) + joined(far[16:, :])
        total = total + (joined(got_0[16:, :]) + joined(got_1[16:, :]))
    frame[2 * own :, :] = jnp.concatenate(split(total), axis=0)
    one, two = got_0[0:16, :].astype(f32), got_1[0:16, :].astype(f32)
    from_low, from_high = pick("gx", two, one), pick("gx", one, two)
    mid = jnp.zeros((own - 2 * chan, lanes), f32)
    found = []
    for top, at in ((0, 2 * chan), (wide, 3 * chan)):
        more = [from_low[at : at + chan], mid, from_high[at : at + chan]]
        found.append(cols[top + chan : top + chan + own, :] + jnp.concatenate(more, axis=0))
    frame[0 : 2 * own, :] = jnp.concatenate(found, axis=0).astype(bf16)
    for at in (0, 1):
        more = [from_low[at * chan : (at + 1) * chan], mid, from_high[at * chan : (at + 1) * chan]]
        place = slice(at * own, (at + 1) * own)
        rows_out[place, :] = rows[place, :] + jnp.concatenate(more, axis=0)


def z_kernel(count_y, mine, got, rows, sent_0, sent_1, wframe):
    own = rows.shape[0] // 2
    total = joined(mine[2 * own :, :]) + joined(got[2 * own :, :])
    sides = jnp.concatenate(split(total), axis=0)
    wframe[...] = sides
    last = got[0:own, :].astype(f32)
    first = got[own : 2 * own, :].astype(f32)
    spot = iota((own, lanes), 1)
    both = []
    for at, line in ((0, 0), (1, count_y + 1)):
        more = jnp.where(spot == lanes - 1, pltpu.roll(last, lanes - 1 - line, 1), 0.0)
        turned = pltpu.roll(first, lanes - line, 1) if line else first
        more = jnp.where(spot == 0, turned, more)
        both.append(rows[at * own : (at + 1) * own, :] + more)
    sent_0[0:own, :] = pick("gy", both[1], both[0]).astype(bf16)
    sent_1[0:own, :] = pick("gy", both[0], both[1]).astype(bf16)
    for ref in (sent_0, sent_1):
        ref[own:, :] = sides


def grad_kernel(field, outer_field, face_0, face_1, got, grad, ends):
    chan, count_x, count_y, _ = grad.shape
    own = chan * count_x
    wide = own + 2 * chan
    spot = iota((count_y, lanes), 1)
    columns = pltpu.roll(got[0 : 2 * own, :].astype(f32), lanes - 1, 1)
    columns = jnp.concatenate([columns, jnp.zeros((lanes - 2 * own, lanes), f32)], axis=0)
    columns = columns.T[0:count_y]
    for x in range(count_x):
        for c in range(chan):
            at = x * chan + c
            plane = plane_of(field, outer_field, chan + at, wide, count_y)
            place = slice(c * count_y, (c + 1) * count_y)
            if x == 0:
                plane = plane + pick("gx", face_1[place, :].astype(f32), face_0[place, :].astype(f32))
            if x == count_x - 1:
                plane = plane + pick("gx", face_0[place, :].astype(f32), face_1[place, :].astype(f32))
            more = jnp.where(spot == lanes - 1, columns[:, at : at + 1], 0.0)
            plane = plane + jnp.where(spot == 0, columns[:, own + at : own + at + 1], more)
            grad[c, x] = plane
            ends[0, c, x] = plane[0:8]
            ends[1, c, x] = plane[count_y - 8 : count_y]


def final_kernel(whole, ends, mine, got_1, far, got_0, out, wout, bout, tiles, wtile, btile, sems):
    chan, count_x, count_y, _ = whole.shape
    own = chan * count_x
    chan_out = mine.shape[0] // 2
    row = iota((8, lanes), 0)
    one, two = got_0[0:own, :].astype(f32), got_1[0:own, :].astype(f32)
    above, below = pick("gy", two, one), pick("gy", one, two)
    copies = []
    for side, more, line in ((0, above, 0), (1, below, 7)):
        for x in range(count_x):
            for c in range(chan):
                at = x * chan + c
                extra = jnp.where(row == line, more[at : at + 1], 0.0)
                tiles[side, c, x] = ends[side, c, x] + extra
        copies.append(
            pltpu.make_async_copy(
                tiles.at[side],
                out.at[:, :, pl.ds(side * (count_y - 8), 8), :],
                sems.at[side],
            )
        )
        copies[-1].start()
    total = joined(mine[...]) + joined(far[...])
    total = total + (joined(got_0[own:, :]) + joined(got_1[own:, :]))
    total = jnp.concatenate([total, jnp.zeros((lanes - chan_out, lanes), f32)], axis=0)
    total = total.T
    for a in range(3):
        for be in range(9):
            at = (be * 3 + a) * chan
            wtile[a * 9 + be] = total[at : at + chan, :chan_out]
    btile[...] = total[27 * chan : 27 * chan + 1, :chan_out]
    copies.append(pltpu.make_async_copy(wtile, wout, sems.at[2]))
    copies.append(pltpu.make_async_copy(btile, bout, sems.at[3]))
    copies[2].start()
    copies[3].start()
    for copy in copies:
        copy.wait()


def traffic(mib):
    return pl.CostEstimate(flops=0, bytes_accessed=mib << 20, transcendentals=0)


def call(kernel, outs, scratch=(), cost=None, **rest):
    return pl.pallas_call(
        kernel,
        out_shape=outs,
        **rest,
        scratch_shapes=list(scratch),
        cost_estimate=cost,
        compiler_params=pltpu.CompilerParams(vmem_limit_bytes=limit),
    )


def on_device(cells, weight, bias, cotangent):
    chan, count_x, count_y, count_z = cells.shape
    chan_out = weight.shape[0]
    own = chan * count_x
    wide = own + 2 * chan
    depth = 6 * chan + 8
    shape = jax.ShapeDtypeStruct

    kernel = weight.transpose(0, 3, 4, 2, 1)
    placed = jnp.stack(
        [
            jnp.pad(kernel, ((0, 0), (0, 0), (0, 0), (x, count_x - 1 - x), (0, 0)))
            for x in range(count_x)
        ]
    ).reshape(count_x * chan_out, 3, 3, count_x + 2, chan)
    coarse = lax.reduce_precision(bias, 8, 7)
    middle = lax.reduce_precision(bias - coarse, 8, 7)
    fine = bias - coarse - middle
    pieces = jnp.stack([coarse, middle, fine], axis=1).astype(bf16)
    pieces = jnp.pad(jnp.tile(pieces, (count_x, 1))[:, None], ((0, 0), (0, 2), (0, 5)))
    near = placed[:, :, :, 1 : count_x + 1].reshape(count_x * chan_out, 9 * own)
    rest = jnp.concatenate([placed[:, :, :, :1], placed[:, :, :, count_x + 1 :]], axis=3)
    rest = jnp.concatenate([rest.reshape(count_x * chan_out, 3, 6 * chan), pieces], axis=2)
    wbig = jnp.concatenate([near, rest.reshape(count_x * chan_out, 3 * depth)], axis=1)
    wback = placed.reshape(count_x * chan_out, 9 * wide).T

    edges, rows = call(
        pack_kernel, [shape((2 * own, lanes), bf16), shape((2 * own, lanes), f32)]
    )(cells)
    pool_x, pool_y, pool_z = cotangent.shape[1:]
    pooled_rows = shape((pool_y * pool_x * chan_out, lanes), f32)
    spread = call(spread_kernel, pooled_rows)(cotangent)
    edges = swapped(edges, "gz", 0)
    body = chan * count_y
    bundle = shape((body + 16, lanes), bf16)
    side = shape((own, lanes), f32)
    face_0, face_1, left, right = call(bundle_kernel, [bundle, bundle, side, side])(cells, edges)
    face_1, face_0 = swapped(face_1, "gx", 1), swapped(face_0, "gx", 0)
    inner = call(
        own_kernel,
        shape(((count_y + 2) * 3 * own, lanes), bf16),
        [pltpu.VMEM(((count_y + 2) * own, lanes), f32)],
        traffic(4),
    )(cells, left, right)
    bundle = shape((3 * wide + 8, lanes), bf16)
    vmem, anywhere = pl.BlockSpec(memory_space=pltpu.VMEM), pl.BlockSpec(memory_space=pl.ANY)
    row_0, row_1 = call(
        functools.partial(rows_kernel, chan),
        [bundle, bundle],
        in_specs=[vmem] * 5 + [anywhere] * 2,
    )(rows, left, right, face_0, face_1, inner, spread)
    row_1, row_0 = swapped(row_1, "gy", 1), swapped(row_0, "gy", 0)

    tall = 2 * wide
    all_field = shape(((count_y + 2) * wide, lanes), f32)
    all_gram = shape((count_x * chan_out, 9 * own + 3 * depth), f32)
    deltas = [pltpu.VMEM((count_x * chan_out, 8 * lanes), bf16)] * 2
    sums, field, patches, cols, gram = call(
        functools.partial(inner_kernel, count_x),
        [
            pooled_rows,
            all_field,
            shape(((count_y + 2) * depth, lanes), bf16),
            shape((tall, lanes), f32),
            all_gram,
        ],
        [
            pltpu.VMEM(((count_y + 2) * 2 * chan, lanes), f32),
            pltpu.VMEM((6 * wide, lanes), f32),
        ]
        + deltas,
        traffic(16),
    )(face_0, face_1, inner, spread, wbig, wback)

    bundle = shape((16 + 2 * chan_out, lanes), bf16)
    face = shape((body, lanes), bf16)
    outer_sums, outer_field, row_0, row_1, wpart, wframe, rows, cols = call(
        functools.partial(main_kernel, count_x),
        [
            pooled_rows,
            all_field,
            bundle,
            bundle,
            shape((chan_out, lanes), f32),
            shape((2 * chan_out, lanes), bf16),
            shape((2 * own, lanes), f32),
            shape((tall, lanes), f32),
        ],
        [
            pltpu.VMEM((4 * (pairs + 1) * 3 * own, lanes), bf16),
            pltpu.VMEM((4 * (pairs + 1) * depth, lanes), bf16),
            pltpu.VMEM((count_x * chan_out, 9 * own + 3 * depth), f32),
        ]
        + deltas,
    )(row_1, row_0, inner, patches, cols, gram, spread, wbig, wback)

    alone = lax.axis_size("gx") != 4
    if alone:
        wpart, far = lax.psum(wpart, "gx"), row_0
    else:
        far = swapped(row_0, "gx", 2)
    row_1, row_0 = swapped(row_1, "gx", 1), swapped(row_0, "gx", 0)
    face_0, face_1 = call(functools.partial(face_kernel, chan), [face, face], cost=traffic(2))(
        field, outer_field
    )
    face_1, face_0 = swapped(face_1, "gx", 1), swapped(face_0, "gx", 0)
    pooled = call(
        functools.partial(pool_kernel, pairs), shape(cotangent.shape, bf16), cost=traffic(8)
    )(sums, outer_sums)
    mine, rows = call(
        functools.partial(x_kernel, alone),
        [shape((2 * own + 2 * chan_out, lanes), bf16), shape((2 * own, lanes), f32)],
    )(wpart, wframe, rows, cols, row_0, row_1, far)
    frame = swapped(mine, "gz", 0)
    bundle = shape((own + 2 * chan_out, lanes), bf16)
    row_0, row_1, mine = call(
        functools.partial(z_kernel, count_y),
        [bundle, bundle, shape((2 * chan_out, lanes), bf16)],
    )(mine, frame, rows)
    row_1, row_0 = swapped(row_1, "gy", 1), swapped(row_0, "gy", 0)
    far = swapped(mine, "gy", 2)
    tiles = (2, chan, count_x, 8, lanes)
    grad, ends = call(grad_kernel, [shape(cells.shape, f32), shape(tiles, f32)], cost=traffic(8))(
        field, outer_field, face_0, face_1, frame
    )
    input_grad, wsum, bias_grad = call(
        final_kernel,
        [
            shape(cells.shape, f32),
            shape((27, chan, chan_out), f32),
            shape((1, chan_out), f32),
        ],
        [
            pltpu.VMEM(tiles, f32),
            pltpu.VMEM((27, chan, chan_out), f32),
            pltpu.VMEM((1, chan_out), f32),
            pltpu.SemaphoreType.DMA((4,)),
        ],
        in_specs=[anywhere] + [vmem] * 5,
        out_specs=[anywhere] * 3,
        input_output_aliases={0: 0},
    )(grad, ends, mine, row_1, far, row_0)
    weight_grad = wsum.reshape(3, 3, 3, chan, chan_out).transpose(4, 3, 0, 1, 2)
    return (pooled, weight_grad, bias_grad.reshape(chan_out), input_grad)


def solution(mesh):
    in_specs = (P(None, "gx", "gy", "gz"), P(), P(), P(None, "gx", "gy", "gz"))
    out_specs = (P(None, "gx", "gy", "gz"), P(), P(), P(None, "gx", "gy", "gz"))
    return jax.shard_map(
        on_device, mesh=mesh, in_specs=in_specs, out_specs=out_specs, check_vma=False
    )
```

```python
import functools

import jax
import jax.numpy as jnp
import numpy as np
from jax import lax
from jax.experimental import pallas as pl
from jax.experimental.pallas import tpu as pltpu
from jax.sharding import PartitionSpec as P

axes = ("gx", "gy", "gz")
f32, bf16 = jnp.float32, jnp.bfloat16
log_scale = 0.07
lanes = 128
limit = 48 * 1024 * 1024


def dot(a, b, contract=((1,), (0,))):
    return lax.dot_general(a, b, (contract, ((), ())), preferred_element_type=f32)


def iota(shape, dim):
    return lax.broadcasted_iota(jnp.int32, shape, dim)


def aligned(start, tile):
    return start if isinstance(start, int) else pl.multiple_of(start, tile)


def swapped(array, axis, pairing):
    count = lax.axis_size(axis)
    pairs = []
    for i in range(count):
        if pairing == 2:
            partner = i + count // 2
        else:
            partner = i + 1 if i % 2 == pairing else i - 1
        pairs.append((i, partner % count))
    return lax.ppermute(array, axis, pairs)


def is_even(axis):
    return lax.rem(lax.axis_index(axis), 2) == 0


def pick(axis, if_even, if_odd):
    return jnp.where(is_even(axis), if_even, if_odd)


def split(value):
    coarse = value.astype(bf16)
    return coarse, (value - coarse.astype(f32)).astype(bf16)


def joined(pair):
    half = pair.shape[0] // 2
    return pair[:half].astype(f32) + pair[half:].astype(f32)


def pack_kernel(cells, edges, rows):
    chan, count_x, count_y, _ = cells.shape
    count = chan * count_x
    row = iota((2 * count, count * lanes), 0)
    lane = iota((2 * count, count * lanes), 1)
    want = jnp.where(row < count, row * lanes, (row - count) * lanes + lanes - 1)
    chosen = (lane == want).astype(f32).astype(bf16)
    planes = [cells[c, x] for x in range(count_x) for c in range(chan)]
    wide = jnp.concatenate(planes, axis=1)
    found = dot(chosen, wide, ((1,), (1,)))
    found = jnp.concatenate([found, jnp.zeros((2 * count, lanes - count_y), f32)], axis=1)
    edges[...] = pltpu.roll(found, 1, 1).astype(bf16)
    for at, plane in enumerate(planes):
        wide_plane = plane.astype(f32)
        rows[at : at + 1, :] = wide_plane[0:1]
        rows[count + at : count + at + 1, :] = wide_plane[count_y - 1 : count_y]


def bundle_kernel(cells, edges, sent_0, sent_1, left, right):
    chan, count_x, count_y, _ = cells.shape
    own = chan * count_x
    whole = edges[...].astype(f32)
    right[...] = whole[0:own]
    left[...] = whole[own : 2 * own]
    zero = jnp.zeros((8, lanes), f32)
    body = chan * count_y
    frames = []
    for x in (0, count_x - 1):
        at = slice(x * chan, x * chan + chan)
        frames.append(jnp.concatenate([whole[own + x * chan :][:chan], whole[at], zero], axis=0))
    even = is_even("gx")
    for ref, odd in ((sent_0, 0), (sent_1, 1)):
        high = even != (odd == 1)
        x = jnp.where(high, count_x - 1, 0)
        for c in range(chan):
            ref[c * count_y : (c + 1) * count_y, :] = cells[c, x]
        ref[body : body + 16, :] = jnp.where(high, frames[1], frames[0]).astype(bf16)


def from_sides(got_0, got_1, start, size):
    one = got_0[start : start + size, :].astype(f32)
    two = got_1[start : start + size, :].astype(f32)
    return pick("gx", two, one), pick("gx", one, two)


def rows_kernel(chan, rows, left, right, got_0, got_1, inner, spread, sent_0, sent_1):
    own = rows.shape[0] // 2
    body = got_0.shape[0] - 16
    count_y = body // chan
    low, high = from_sides(got_0, got_1, body, 16)
    edges = []
    for ref, at in ((left, 0), (right, chan)):
        edges += [ref[...], low[at : at + chan], high[at : at + chan]]
    edges.append(jnp.zeros((8, lanes), f32))
    low, high = from_sides(got_0, got_1, 0, body)
    both = []
    for at, line in ((0, 0), (own, count_y - 1)):
        outer = [
            plane[c * count_y + line : c * count_y + line + 1]
            for plane in (low, high)
            for c in range(chan)
        ]
        both.append(jnp.concatenate([rows[at : at + own, :]] + outer + edges, axis=0))
    sent_0[...] = pick("gy", both[1], both[0]).astype(bf16)
    sent_1[...] = pick("gy", both[0], both[1]).astype(bf16)


def spread_kernel(cot, spread):
    chan_out, pool_x, pool_y, pool_z = cot.shape
    twice = jnp.where(
        iota((pool_z, lanes), 1) // 2 == iota((pool_z, lanes), 0), 0.125, 0.0
    ).astype(bf16)
    for o in range(chan_out):
        part = dot(cot[o].reshape(pool_x * pool_y, pool_z), twice)
        for x in range(pool_x):
            spread[pl.ds(x * chan_out + o, pool_y, stride=pool_x * chan_out), :] = part[
                x * pool_y : (x + 1) * pool_y
            ]


def pool_kernel(edge, sums, outer_sums, pooled, token):
    token[...] = jnp.zeros_like(token)
    chan_out, pool_x, pool_y, pool_z = pooled.shape
    halves = jnp.where(
        iota((2 * lanes, pool_z), 0) % lanes // 2 == iota((2 * lanes, pool_z), 1), 0.125, 0.0
    ).astype(bf16)
    for o in range(0, chan_out, 4):
        rows = 4 * pool_x * pool_y
        part = sums[o * pool_x * pool_y : o * pool_x * pool_y + rows, :]
        at = iota((rows, lanes), 0) % pool_y
        near = (at >= edge) & (at < pool_y - edge)
        part = jnp.where(near, part, outer_sums[o * pool_x * pool_y : o * pool_x * pool_y + rows, :])
        mean = dot(jnp.concatenate(split(part), axis=1), halves) + log_scale * float(np.log(2.0))
        pooled[o : o + 4] = mean.astype(bf16).reshape(4, pool_x, pool_y, pool_z)


def shifted(mid, left, right, y):
    lane = iota(mid.shape, 1)
    low = pltpu.roll(left, (lanes - y) % lanes, 1)
    high = pltpu.roll(right, (lanes - 1 - y) % lanes, 1)
    before = jnp.where(lane == 0, low, pltpu.roll(mid, 1, 1))
    after = jnp.where(lane == lanes - 1, high, pltpu.roll(mid, lanes - 1, 1))
    return [before, mid, after]


def own_kernel(cells, left, right, inner, stage):
    chan, count_x, count_y, _ = cells.shape
    own = chan * count_x
    for x in range(count_x):
        for c in range(chan):
            plane = cells[c, x].astype(f32)
            stage[pl.ds(own + x * chan + c, count_y, stride=own), :] = plane
    left_cols, right_cols = left[...], right[...]
    for y in range(1, count_y + 1):
        whole = shifted(stage[y * own : (y + 1) * own, :], left_cols, right_cols, y)
        whole = jnp.concatenate(whole, axis=0)
        inner[y * 3 * own : (y + 1) * 3 * own, :] = whole.astype(bf16)


pairs = 4


def sizes_of(count_x, inner, spread, wbig):
    pool_x = count_x // 2
    chan_out = wbig.shape[0] // count_x
    pool_y = spread.shape[0] // (pool_x * chan_out)
    own = inner.shape[0] // (3 * (2 * pool_y + 2))
    return pool_x, chan_out, pool_y, own, own // count_x


def worker(count_x, pool_x, chan_out, pool_y, own, chan, near_of, rest_of, refs):
    spread, wbig, wback, sums, field = refs
    wide = own + 2 * chan
    size = 3 * wide
    lane = iota((wide, lanes), 1)
    inside, outside = lane != lanes - 1, lane != 0

    def finish(y, whole, edge):
        first, last = whole[0:wide], whole[2 * wide : 3 * wide]
        inner = (
            whole[wide : 2 * wide]
            + jnp.where(inside, pltpu.roll(first, lanes - 1, 1), 0.0)
            + jnp.where(outside, pltpu.roll(last, 1, 1), 0.0)
        )
        field[pl.ds(aligned(y * wide, 8), wide), :] = inner
        here = lane == y
        edge[0] = jnp.where(here, pltpu.roll(first, y, 1), edge[0])
        edge[1] = jnp.where(here, pltpu.roll(last, y + 1, 1), edge[1])

    def block_of(j):
        columns = [
            jnp.concatenate([near_of(2 * j + h), rest_of(2 * j + h)], axis=0) for h in range(2)
        ]
        return jnp.concatenate(columns, axis=1)

    def forward(i, k, ref):
        j = i * pairs + k
        preact = dot(wbig[...], block_of(j))
        slope = jnp.tanh(5.0 * preact)
        linear = jnp.maximum(preact, 0.3 * preact)
        factor = 1.0 + jnp.abs(slope)
        here = spread[pl.ds(aligned(j * pool_x * chan_out, 8), pool_x * chan_out), :]
        slope = 0.65 + 0.35 * slope
        delta = []
        for x in range(pool_x):
            top, mid = 2 * x * chan_out, (2 * x + 1) * chan_out
            end = mid + chan_out
            times = here[x * chan_out : (x + 1) * chan_out]
            times = jnp.concatenate([times, times], axis=1)
            delta.append((slope[top:mid] * times).astype(bf16))
            delta.append((slope[mid:end] * times).astype(bf16))
            total = linear[top:mid] + linear[mid:end]
            total = total[:, :lanes] + total[:, lanes:]
            prod = factor[top:mid] * factor[mid:end]
            prod = prod[:, :lanes] * prod[:, lanes:]
            total = total - log_scale * jnp.log(prod)
            sums[pl.ds(x * pool_y + j, chan_out, stride=pool_x * pool_y), :] = total
        ref[:, 2 * k * lanes : 2 * (k + 1) * lanes] = jnp.concatenate(delta, axis=0)

    def backward(i, k, ref, held, edge):
        j = i * pairs + k
        parts = dot(wback[...], ref[:, 2 * k * lanes : 2 * (k + 1) * lanes])
        part = lambda b, h: parts[b * size : (b + 1) * size, h * lanes : (h + 1) * lanes]
        finish(2 * j, held[0] + part(0, 0), edge)
        finish(2 * j + 1, held[1] + part(1, 0) + part(0, 1), edge)
        held[0] = part(2, 0) + part(1, 1)
        held[1] = part(2, 1)

    def weigh(i, ref):
        blocks = jnp.concatenate([block_of(i * pairs + k) for k in range(pairs)], axis=1)
        return dot(ref[...], blocks, ((1,), (1,)))

    return finish, forward, backward, weigh


def inner_kernel(
    count_x, got_0, got_1, inner, spread, wbig, wback,
    sums, field, patches, cols, gram, stage, carry, delta_a, delta_b,
):
    shape = sizes_of(count_x, inner, spread, wbig)
    pool_x, chan_out, pool_y, own, chan = shape
    count_y = 2 * pool_y
    wide = own + 2 * chan
    size = 3 * wide
    outside_rows = 2 * chan
    depth = 3 * outside_rows + 8
    body = chan * count_y
    for side, planes in enumerate(from_sides(got_0, got_1, 0, body)):
        for c in range(chan):
            at = outside_rows + side * chan + c
            plane = planes[c * count_y : (c + 1) * count_y]
            stage[pl.ds(at, count_y, stride=outside_rows), :] = plane
    low, high = from_sides(got_0, got_1, body, 16)
    left_cols, right_cols = [
        jnp.concatenate([low[at : at + chan], high[at : at + chan]], axis=0) for at in (0, chan)
    ]
    for y in range(1, count_y + 1):
        mid = stage[y * outside_rows : (y + 1) * outside_rows, :]
        whole = shifted(mid, left_cols, right_cols, y) + [jnp.ones((8, lanes), f32)]
        patches[y * depth : (y + 1) * depth, :] = jnp.concatenate(whole, axis=0).astype(bf16)

    def near_of(y):
        return inner[pl.ds(aligned(y * 3 * own, 16), 9 * own), :]

    def rest_of(y):
        return patches[pl.ds(aligned(y * depth, 16), 3 * depth), :]

    finish, forward, backward, weigh = worker(
        count_x, *shape, near_of, rest_of, (spread, wbig, wback, sums, field)
    )
    carry[...] = jnp.zeros_like(carry)
    gram[...] = jnp.zeros_like(gram)
    cols[...] = jnp.zeros_like(cols)

    def opened():
        return (
            [carry[0:size, :], carry[size : 2 * size, :]],
            [cols[0:wide, :], cols[wide : 2 * wide, :]],
        )

    def closed(held, edge):
        carry[0:size, :] = held[0]
        carry[size : 2 * size, :] = held[1]
        cols[0:wide, :] = edge[0]
        cols[wide : 2 * wide, :] = edge[1]

    def both(at):
        held, edge = opened()
        total = gram[...] + weigh(at, delta_a)
        for k in range(pairs):
            forward(at + 1, k, delta_b)
            backward(at, k, delta_a, held, edge)
        return held, edge, total + weigh(at + 1, delta_b)

    def step(t, _):
        at = 2 * t + 1
        held, edge, total = both(at)
        for k in range(pairs):
            forward(at + 2, k, delta_a)
            backward(at + 1, k, delta_b, held, edge)
        gram[...] = total
        closed(held, edge)
        return 0

    steps = count_y // (2 * pairs)
    for k in range(pairs):
        forward(1, k, delta_a)
    lax.fori_loop(0, steps // 2 - 2, step, 0)
    held, edge, total = both(steps - 3)
    gram[...] = total
    for k in range(pairs):
        backward(steps - 2, k, delta_b, held, edge)
    end = (steps - 1) * 2 * pairs
    finish(end, held[0], edge)
    finish(end + 1, held[1], edge)
    closed(held, edge)


def main_kernel(
    count_x, row_1, row_0, inner, patches, inner_cols, inner_gram, spread, wbig, wback,
    sums, field, sent_0, sent_1, wpart, wframe, rows_out, cols,
    near, rest, gram, delta_a, delta_b,
):
    shape = sizes_of(count_x, inner, spread, wbig)
    pool_x, chan_out, pool_y, own, chan = shape
    count_y = 2 * pool_y
    wide = own + 2 * chan
    size = 3 * wide
    outside_rows = 2 * chan
    depth = 3 * outside_rows + 8
    even = is_even("gx")
    span_y = 2 * pairs
    top = span_y + 2
    start = count_y - span_y
    for ref, source, height in ((near, inner, 3 * own), (rest, patches, depth)):
        ref[height : top * height, :] = source[height : top * height, :]
        last = (2 * top - 1) * height
        ref[top * height : last, :] = source[start * height : (count_y + 1) * height, :]
    one, two = row_0[...].astype(f32), row_1[...].astype(f32)
    above, below = pick("gy", two, one), pick("gy", one, two)
    for at, got, line in ((0, above, count_y), (2 * top - 1, below, 1)):
        left, right = got[wide : 2 * wide], got[2 * wide : 3 * wide]
        whole = jnp.concatenate(shifted(got[:own], left[:own], right[:own], line), axis=0)
        near[at * 3 * own : (at + 1) * 3 * own, :] = whole.astype(bf16)
        whole = shifted(got[own:wide], left[own:], right[own:], line)
        whole = jnp.concatenate(whole + [jnp.ones((8, lanes), f32)], axis=0)
        rest[at * depth : (at + 1) * depth, :] = whole.astype(bf16)

    def place(y):
        return y if y < top else y - start + top

    def near_of(y):
        return near[place(y) * 3 * own : (place(y) + 3) * 3 * own, :]

    def rest_of(y):
        return rest[place(y) * depth : (place(y) + 3) * depth, :]

    finish, forward, backward, weigh = worker(
        count_x, *shape, near_of, rest_of, (spread, wbig, wback, sums, field)
    )
    final = count_y // span_y - 1
    zero = jnp.zeros((size, lanes), f32)
    held, edge = [zero, zero], [inner_cols[0:wide, :], inner_cols[wide : 2 * wide, :]]
    extra = [jnp.zeros((wide, lanes), f32)] * 2
    for k in range(pairs):
        forward(0, k, delta_a)
    for k in range(pairs):
        forward(final, k, delta_b)
        backward(0, k, delta_a, held, extra)
    total = inner_gram[...] + weigh(0, delta_a)
    finish(span_y, held[0], extra)
    finish(span_y + 1, held[1], extra)
    held = [zero, zero]
    for k in range(pairs):
        backward(final, k, delta_b, held, extra)
    gram[...] = total + weigh(final, delta_b)
    finish(count_y, held[0], extra)
    finish(count_y + 1, held[1], extra)
    cols[0:wide, :] = edge[0] + extra[0]
    cols[wide : 2 * wide, :] = edge[1] + extra[1]

    span = gram.shape[1]
    spot = iota((chan_out, 2 * lanes), 1)
    first = 9 * own
    turn = lambda part, shift: pltpu.roll(part, (2 * lanes - shift) % (2 * lanes), 1)
    straight, turned, extra = 0.0, 0.0, 0.0
    for x in range(count_x):
        part = gram[x * chan_out : (x + 1) * chan_out, :]
        part = jnp.concatenate([part, jnp.zeros((chan_out, 2 * lanes - span), f32)], axis=1)
        straight = straight + part
        moved = turn(part, chan * (x - 1)) if x != 1 else part
        a = spot % own // chan
        turned = turned + jnp.where((a + x >= 1) & (a + x <= count_x), moved, 0.0)
        if x == 0:
            extra = extra + jnp.where((spot - first) % outside_rows < chan, part, 0.0)
        if x == count_x - 1:
            extra = extra + jnp.where((spot - first) % outside_rows >= chan, part, 0.0)
    group = 3 * chan
    tight = jnp.zeros((chan_out, 2 * lanes), f32)
    for b in range(3):
        for e in range(3):
            at = (b * 3 + e) * group
            here = spot // group == b * 3 + e
            value = turn(turned, b * 3 * own + e * own - at)
            source = first + b * depth + e * outside_rows
            low, high = turn(extra, source - at), turn(extra, source - at - chan)
            a = (spot - at) // chan
            value = value + jnp.where(a == 0, low, 0.0) + jnp.where(a == 2, high, 0.0)
            tight = jnp.where(here, value, tight)
    bias_at = first + 3 * outside_rows
    tight = jnp.where(spot == 9 * group, turn(straight, bias_at - 9 * group), tight)
    tight = tight[:, :lanes]
    wpart[...] = tight
    sides = jnp.concatenate(split(tight), axis=0)
    wframe[...] = sides

    ends = [field[0:wide, :], field[(count_y + 1) * wide : (count_y + 2) * wide, :]]
    rows_out[...] = jnp.concatenate([end[chan : chan + own] for end in ends], axis=0)
    zero = jnp.zeros((8, lanes), f32)
    for ref, odd in ((sent_0, 0), (sent_1, 1)):
        high = even != (odd == 1)
        low_frame, high_frame = [
            jnp.concatenate(
                [end[x * chan : (x + 1) * chan] for end in ends]
                + [cols[top + x * chan : top + (x + 1) * chan, :] for top in (0, wide)],
                axis=0,
            )
            for x in (0, count_x + 1)
        ]
        ref[0:16, :] = jnp.where(high, high_frame, low_frame).astype(bf16)
        ref[16:, :] = sides


def plane_of(field, outer_field, at, wide, count_y):
    row = iota((count_y, lanes), 0) + 1
    span_y = 2 * pairs
    place = pl.ds(wide + at, count_y, stride=wide)
    near = (row >= span_y) & (row < count_y - span_y + 2)
    far = (row < span_y + 2) | (row >= count_y - span_y)
    return jnp.where(near, field[place, :], 0.0) + jnp.where(far, outer_field[place, :], 0.0)


def face_kernel(chan, field, outer_field, face_0, face_1):
    count_y = face_0.shape[0] // chan
    wide = field.shape[0] // (count_y + 2)
    even = is_even("gx")
    for c in range(chan):
        low, high = [
            plane_of(field, outer_field, at + c, wide, count_y) for at in (0, wide - chan)
        ]
        place = slice(c * count_y, (c + 1) * count_y)
        face_0[place, :] = jnp.where(even, high, low).astype(bf16)
        face_1[place, :] = jnp.where(even, low, high).astype(bf16)


def x_kernel(alone, wpart, wframe, rows, cols, got_0, got_1, far, frame, rows_out):
    own = rows.shape[0] // 2
    wide = cols.shape[0] // 2
    chan = (wide - own) // 2
    if alone:
        total = wpart[...]
    else:
        total = joined(wframe[...]) + joined(far[16:, :])
        total = total + (joined(got_0[16:, :]) + joined(got_1[16:, :]))
    frame[2 * own :, :] = jnp.concatenate(split(total), axis=0)
    one, two = got_0[0:16, :].astype(f32), got_1[0:16, :].astype(f32)
    from_low, from_high = pick("gx", two, one), pick("gx", one, two)
    mid = jnp.zeros((own - 2 * chan, lanes), f32)
    found = []
    for top, at in ((0, 2 * chan), (wide, 3 * chan)):
        more = [from_low[at : at + chan], mid, from_high[at : at + chan]]
        found.append(cols[top + chan : top + chan + own, :] + jnp.concatenate(more, axis=0))
    frame[0 : 2 * own, :] = jnp.concatenate(found, axis=0).astype(bf16)
    for at in (0, 1):
        more = [from_low[at * chan : (at + 1) * chan], mid, from_high[at * chan : (at + 1) * chan]]
        place = slice(at * own, (at + 1) * own)
        rows_out[place, :] = rows[place, :] + jnp.concatenate(more, axis=0)


def z_kernel(count_y, mine, got, rows, token, sent_0, sent_1, wframe):
    own = rows.shape[0] // 2
    total = joined(mine[2 * own :, :]) + joined(got[2 * own :, :])
    sides = jnp.concatenate(split(total), axis=0)
    wframe[...] = sides
    last = got[0:own, :].astype(f32)
    first = got[own : 2 * own, :].astype(f32)
    spot = iota((own, lanes), 1)
    both = []
    for at, line in ((0, 0), (1, count_y + 1)):
        more = jnp.where(spot == lanes - 1, pltpu.roll(last, lanes - 1 - line, 1), 0.0)
        turned = pltpu.roll(first, lanes - line, 1) if line else first
        more = jnp.where(spot == 0, turned, more)
        both.append(rows[at * own : (at + 1) * own, :] + more)
    sent_0[0:own, :] = pick("gy", both[1], both[0]).astype(bf16)
    sent_1[0:own, :] = pick("gy", both[0], both[1]).astype(bf16)
    for ref in (sent_0, sent_1):
        ref[own:, :] = sides


def grad_kernel(field, outer_field, face_0, face_1, got, grad, ends):
    chan, count_x, count_y, _ = grad.shape
    own = chan * count_x
    wide = own + 2 * chan
    spot = iota((count_y, lanes), 1)
    columns = pltpu.roll(got[0 : 2 * own, :].astype(f32), lanes - 1, 1)
    columns = jnp.concatenate([columns, jnp.zeros((lanes - 2 * own, lanes), f32)], axis=0)
    columns = columns.T[0:count_y]
    for x in range(count_x):
        for c in range(chan):
            at = x * chan + c
            plane = plane_of(field, outer_field, chan + at, wide, count_y)
            place = slice(c * count_y, (c + 1) * count_y)
            if x == 0:
                plane = plane + pick("gx", face_1[place, :].astype(f32), face_0[place, :].astype(f32))
            if x == count_x - 1:
                plane = plane + pick("gx", face_0[place, :].astype(f32), face_1[place, :].astype(f32))
            more = jnp.where(spot == lanes - 1, columns[:, at : at + 1], 0.0)
            plane = plane + jnp.where(spot == 0, columns[:, own + at : own + at + 1], more)
            grad[c, x] = plane
            ends[0, c, x] = plane[0:8]
            ends[1, c, x] = plane[count_y - 8 : count_y]


def final_kernel(whole, ends, mine, got_0, got_1, far, out, wout, bout, tiles, wtile, btile, sems):
    chan, count_x, count_y, _ = whole.shape
    own = chan * count_x
    chan_out = mine.shape[0] // 2
    row = iota((8, lanes), 0)
    one, two = got_0[0:own, :].astype(f32), got_1[0:own, :].astype(f32)
    above, below = pick("gy", two, one), pick("gy", one, two)
    copies = []
    for side, more, line in ((0, above, 0), (1, below, 7)):
        for x in range(count_x):
            for c in range(chan):
                at = x * chan + c
                extra = jnp.where(row == line, more[at : at + 1], 0.0)
                tiles[side, c, x] = ends[side, c, x] + extra
        copies.append(
            pltpu.make_async_copy(
                tiles.at[side],
                out.at[:, :, pl.ds(side * (count_y - 8), 8), :],
                sems.at[side],
            )
        )
        copies[-1].start()
    total = joined(mine[...]) + joined(far[...])
    total = total + (joined(got_0[own:, :]) + joined(got_1[own:, :]))
    total = jnp.concatenate([total, jnp.zeros((lanes - chan_out, lanes), f32)], axis=0)
    total = total.T
    for a in range(3):
        for be in range(9):
            at = (be * 3 + a) * chan
            wtile[a * 9 + be] = total[at : at + chan, :chan_out]
    btile[...] = total[27 * chan : 27 * chan + 1, :chan_out]
    copies.append(pltpu.make_async_copy(wtile, wout, sems.at[2]))
    copies.append(pltpu.make_async_copy(btile, bout, sems.at[3]))
    copies[2].start()
    copies[3].start()
    for copy in copies:
        copy.wait()


def traffic(mib):
    return pl.CostEstimate(flops=0, bytes_accessed=mib << 20, transcendentals=0)


def call(kernel, outs, scratch=(), cost=None, **rest):
    return pl.pallas_call(
        kernel,
        out_shape=outs,
        **rest,
        scratch_shapes=list(scratch),
        cost_estimate=cost,
        compiler_params=pltpu.CompilerParams(vmem_limit_bytes=limit),
    )


def on_device(cells, weight, bias, cotangent):
    chan, count_x, count_y, count_z = cells.shape
    chan_out = weight.shape[0]
    own = chan * count_x
    wide = own + 2 * chan
    depth = 6 * chan + 8
    shape = jax.ShapeDtypeStruct

    kernel = weight.transpose(0, 3, 4, 2, 1)
    placed = jnp.stack(
        [
            jnp.pad(kernel, ((0, 0), (0, 0), (0, 0), (x, count_x - 1 - x), (0, 0)))
            for x in range(count_x)
        ]
    ).reshape(count_x * chan_out, 3, 3, count_x + 2, chan)
    coarse = lax.reduce_precision(bias, 8, 7)
    middle = lax.reduce_precision(bias - coarse, 8, 7)
    fine = bias - coarse - middle
    pieces = jnp.stack([coarse, middle, fine], axis=1).astype(bf16)
    pieces = jnp.pad(jnp.tile(pieces, (count_x, 1))[:, None], ((0, 0), (0, 2), (0, 5)))
    near = placed[:, :, :, 1 : count_x + 1].reshape(count_x * chan_out, 9 * own)
    rest = jnp.concatenate([placed[:, :, :, :1], placed[:, :, :, count_x + 1 :]], axis=3)
    rest = jnp.concatenate([rest.reshape(count_x * chan_out, 3, 6 * chan), pieces], axis=2)
    wbig = jnp.concatenate([near, rest.reshape(count_x * chan_out, 3 * depth)], axis=1)
    wback = placed.reshape(count_x * chan_out, 9 * wide).T

    edges, rows = call(
        pack_kernel, [shape((2 * own, lanes), bf16), shape((2 * own, lanes), f32)]
    )(cells)
    pool_x, pool_y, pool_z = cotangent.shape[1:]
    pooled_rows = shape((pool_y * pool_x * chan_out, lanes), f32)
    spread = call(spread_kernel, pooled_rows)(cotangent)
    edges = swapped(edges, "gz", 0)
    body = chan * count_y
    bundle = shape((body + 16, lanes), bf16)
    side = shape((own, lanes), f32)
    face_0, face_1, left, right = call(bundle_kernel, [bundle, bundle, side, side])(cells, edges)
    face_1, face_0 = swapped(face_1, "gx", 1), swapped(face_0, "gx", 0)
    inner = call(
        own_kernel,
        shape(((count_y + 2) * 3 * own, lanes), bf16),
        [pltpu.VMEM(((count_y + 2) * own, lanes), f32)],
        traffic(4),
    )(cells, left, right)
    bundle = shape((3 * wide + 8, lanes), bf16)
    vmem, anywhere = pl.BlockSpec(memory_space=pltpu.VMEM), pl.BlockSpec(memory_space=pl.ANY)
    row_0, row_1 = call(
        functools.partial(rows_kernel, chan),
        [bundle, bundle],
        in_specs=[vmem] * 5 + [anywhere] * 2,
    )(rows, left, right, face_0, face_1, inner, spread)
    row_1, row_0 = swapped(row_1, "gy", 1), swapped(row_0, "gy", 0)

    tall = 2 * wide
    all_field = shape(((count_y + 2) * wide, lanes), f32)
    all_gram = shape((count_x * chan_out, 9 * own + 3 * depth), f32)
    deltas = [pltpu.VMEM((count_x * chan_out, 8 * lanes), bf16)] * 2
    sums, field, patches, cols, gram = call(
        functools.partial(inner_kernel, count_x),
        [
            pooled_rows,
            all_field,
            shape(((count_y + 2) * depth, lanes), bf16),
            shape((tall, lanes), f32),
            all_gram,
        ],
        [
            pltpu.VMEM(((count_y + 2) * 2 * chan, lanes), f32),
            pltpu.VMEM((6 * wide, lanes), f32),
        ]
        + deltas,
        traffic(16),
    )(face_0, face_1, inner, spread, wbig, wback)

    bundle = shape((16 + 2 * chan_out, lanes), bf16)
    face = shape((body, lanes), bf16)
    outer_sums, outer_field, row_0, row_1, wpart, wframe, rows, cols = call(
        functools.partial(main_kernel, count_x),
        [
            pooled_rows,
            all_field,
            bundle,
            bundle,
            shape((chan_out, lanes), f32),
            shape((2 * chan_out, lanes), bf16),
            shape((2 * own, lanes), f32),
            shape((tall, lanes), f32),
        ],
        [
            pltpu.VMEM((4 * (pairs + 1) * 3 * own, lanes), bf16),
            pltpu.VMEM((4 * (pairs + 1) * depth, lanes), bf16),
            pltpu.VMEM((count_x * chan_out, 9 * own + 3 * depth), f32),
        ]
        + deltas,
    )(row_1, row_0, inner, patches, cols, gram, spread, wbig, wback)

    alone = lax.axis_size("gx") != 4
    if alone:
        wpart, far = lax.psum(wpart, "gx"), row_0
    else:
        far = swapped(row_0, "gx", 2)
    row_1, row_0 = swapped(row_1, "gx", 1), swapped(row_0, "gx", 0)
    face_0, face_1 = call(functools.partial(face_kernel, chan), [face, face], cost=traffic(2))(
        field, outer_field
    )
    face_1, face_0 = swapped(face_1, "gx", 1), swapped(face_0, "gx", 0)
    pooled, token = call(
        functools.partial(pool_kernel, pairs),
        [shape(cotangent.shape, bf16), shape((8, lanes), f32)],
        cost=traffic(8),
    )(sums, outer_sums)
    mine, rows = call(
        functools.partial(x_kernel, alone),
        [shape((2 * own + 2 * chan_out, lanes), bf16), shape((2 * own, lanes), f32)],
    )(wpart, wframe, rows, cols, row_0, row_1, far)
    frame = swapped(mine, "gz", 0)
    bundle = shape((own + 2 * chan_out, lanes), bf16)
    row_0, row_1, mine = call(
        functools.partial(z_kernel, count_y),
        [bundle, bundle, shape((2 * chan_out, lanes), bf16)],
        in_specs=[vmem] * 3 + [anywhere],
    )(mine, frame, rows, token)
    row_1, row_0 = swapped(row_1, "gy", 1), swapped(row_0, "gy", 0)
    far = swapped(mine, "gy", 2)
    tiles = (2, chan, count_x, 8, lanes)
    grad, ends = call(grad_kernel, [shape(cells.shape, f32), shape(tiles, f32)], cost=traffic(8))(
        field, outer_field, face_0, face_1, frame
    )
    input_grad, wsum, bias_grad = call(
        final_kernel,
        [
            shape(cells.shape, f32),
            shape((27, chan, chan_out), f32),
            shape((1, chan_out), f32),
        ],
        [
            pltpu.VMEM(tiles, f32),
            pltpu.VMEM((27, chan, chan_out), f32),
            pltpu.VMEM((1, chan_out), f32),
            pltpu.SemaphoreType.DMA((4,)),
        ],
        in_specs=[anywhere] + [vmem] * 5,
        out_specs=[anywhere] * 3,
        input_output_aliases={0: 0},
    )(grad, ends, mine, row_0, row_1, far)
    weight_grad = wsum.reshape(3, 3, 3, chan, chan_out).transpose(4, 3, 0, 1, 2)
    return (pooled, weight_grad, bias_grad.reshape(chan_out), input_grad)


def solution(mesh):
    in_specs = (P(None, "gx", "gy", "gz"), P(), P(), P(None, "gx", "gy", "gz"))
    out_specs = (P(None, "gx", "gy", "gz"), P(), P(), P(None, "gx", "gy", "gz"))
    return jax.shard_map(
        on_device, mesh=mesh, in_specs=in_specs, out_specs=out_specs, check_vma=False
    )
```

```python
import functools

import jax
import jax.numpy as jnp
import numpy as np
from jax import lax
from jax.experimental import pallas as pl
from jax.experimental.pallas import tpu as pltpu
from jax.sharding import PartitionSpec as P

axes = ("gx", "gy", "gz")
f32, bf16 = jnp.float32, jnp.bfloat16
log_scale = 0.07
lanes = 128
limit = 48 * 1024 * 1024


def dot(a, b, contract=((1,), (0,))):
    return lax.dot_general(a, b, (contract, ((), ())), preferred_element_type=f32)


def iota(shape, dim):
    return lax.broadcasted_iota(jnp.int32, shape, dim)


def aligned(start, tile):
    return start if isinstance(start, int) else pl.multiple_of(start, tile)


def swapped(array, axis, pairing):
    count = lax.axis_size(axis)
    pairs = []
    for i in range(count):
        if pairing == 2:
            partner = i + count // 2
        else:
            partner = i + 1 if i % 2 == pairing else i - 1
        pairs.append((i, partner % count))
    return lax.ppermute(array, axis, pairs)


def is_even(axis):
    return lax.rem(lax.axis_index(axis), 2) == 0


def pick(axis, if_even, if_odd):
    return jnp.where(is_even(axis), if_even, if_odd)


def split(value):
    coarse = value.astype(bf16)
    return coarse, (value - coarse.astype(f32)).astype(bf16)


def joined(pair):
    half = pair.shape[0] // 2
    return pair[:half].astype(f32) + pair[half:].astype(f32)


def pack_kernel(cells, edges, rows):
    chan, count_x, count_y, _ = cells.shape
    count = chan * count_x
    row = iota((2 * count, count * lanes), 0)
    lane = iota((2 * count, count * lanes), 1)
    want = jnp.where(row < count, row * lanes, (row - count) * lanes + lanes - 1)
    chosen = (lane == want).astype(f32).astype(bf16)
    planes = [cells[c, x] for x in range(count_x) for c in range(chan)]
    wide = jnp.concatenate(planes, axis=1)
    found = dot(chosen, wide, ((1,), (1,)))
    found = jnp.concatenate([found, jnp.zeros((2 * count, lanes - count_y), f32)], axis=1)
    edges[...] = pltpu.roll(found, 1, 1).astype(bf16)
    for at, plane in enumerate(planes):
        wide_plane = plane.astype(f32)
        rows[at : at + 1, :] = wide_plane[0:1]
        rows[count + at : count + at + 1, :] = wide_plane[count_y - 1 : count_y]


def bundle_kernel(cells, edges, sent_0, sent_1, left, right):
    chan, count_x, count_y, _ = cells.shape
    own = chan * count_x
    whole = edges[...].astype(f32)
    right[...] = whole[0:own]
    left[...] = whole[own : 2 * own]
    zero = jnp.zeros((8, lanes), f32)
    body = chan * count_y
    frames = []
    for x in (0, count_x - 1):
        at = slice(x * chan, x * chan + chan)
        frames.append(jnp.concatenate([whole[own + x * chan :][:chan], whole[at], zero], axis=0))
    even = is_even("gx")
    for ref, odd in ((sent_0, 0), (sent_1, 1)):
        high = even != (odd == 1)
        x = jnp.where(high, count_x - 1, 0)
        for c in range(chan):
            ref[c * count_y : (c + 1) * count_y, :] = cells[c, x]
        ref[body : body + 16, :] = jnp.where(high, frames[1], frames[0]).astype(bf16)


def from_sides(got_0, got_1, start, size):
    one = got_0[start : start + size, :].astype(f32)
    two = got_1[start : start + size, :].astype(f32)
    return pick("gx", two, one), pick("gx", one, two)


def rows_kernel(chan, rows, left, right, got_0, got_1, inner, spread, sent_0, sent_1):
    own = rows.shape[0] // 2
    body = got_0.shape[0] - 16
    count_y = body // chan
    low, high = from_sides(got_0, got_1, body, 16)
    edges = []
    for ref, at in ((left, 0), (right, chan)):
        edges += [ref[...], low[at : at + chan], high[at : at + chan]]
    edges.append(jnp.zeros((8, lanes), f32))
    low, high = from_sides(got_0, got_1, 0, body)
    both = []
    for at, line in ((0, 0), (own, count_y - 1)):
        outer = [
            plane[c * count_y + line : c * count_y + line + 1]
            for plane in (low, high)
            for c in range(chan)
        ]
        both.append(jnp.concatenate([rows[at : at + own, :]] + outer + edges, axis=0))
    sent_0[...] = pick("gy", both[1], both[0]).astype(bf16)
    sent_1[...] = pick("gy", both[0], both[1]).astype(bf16)


def spread_kernel(cot, spread):
    chan_out, pool_x, pool_y, pool_z = cot.shape
    twice = jnp.where(
        iota((pool_z, lanes), 1) // 2 == iota((pool_z, lanes), 0), 0.125, 0.0
    ).astype(bf16)
    for o in range(chan_out):
        part = dot(cot[o].reshape(pool_x * pool_y, pool_z), twice)
        for x in range(pool_x):
            spread[pl.ds(x * chan_out + o, pool_y, stride=pool_x * chan_out), :] = part[
                x * pool_y : (x + 1) * pool_y
            ]


def pool_kernel(edge, sums, outer_sums, pooled, token):
    token[...] = jnp.zeros_like(token)
    chan_out, pool_x, pool_y, pool_z = pooled.shape
    halves = jnp.where(
        iota((2 * lanes, pool_z), 0) % lanes // 2 == iota((2 * lanes, pool_z), 1), 0.125, 0.0
    ).astype(bf16)
    for o in range(0, chan_out, 4):
        rows = 4 * pool_x * pool_y
        part = sums[o * pool_x * pool_y : o * pool_x * pool_y + rows, :]
        at = iota((rows, lanes), 0) % pool_y
        near = (at >= edge) & (at < pool_y - edge)
        part = jnp.where(near, part, outer_sums[o * pool_x * pool_y : o * pool_x * pool_y + rows, :])
        mean = dot(jnp.concatenate(split(part), axis=1), halves) + log_scale * float(np.log(2.0))
        pooled[o : o + 4] = mean.astype(bf16).reshape(4, pool_x, pool_y, pool_z)


def shifted(mid, left, right, y):
    lane = iota(mid.shape, 1)
    low = pltpu.roll(left, (lanes - y) % lanes, 1)
    high = pltpu.roll(right, (lanes - 1 - y) % lanes, 1)
    before = jnp.where(lane == 0, low, pltpu.roll(mid, 1, 1))
    after = jnp.where(lane == lanes - 1, high, pltpu.roll(mid, lanes - 1, 1))
    return [before, mid, after]


def own_kernel(cells, left, right, inner, stage):
    chan, count_x, count_y, _ = cells.shape
    own = chan * count_x
    for x in range(count_x):
        for c in range(chan):
            plane = cells[c, x].astype(f32)
            stage[pl.ds(own + x * chan + c, count_y, stride=own), :] = plane
    left_cols, right_cols = left[...], right[...]
    for y in range(1, count_y + 1):
        whole = shifted(stage[y * own : (y + 1) * own, :], left_cols, right_cols, y)
        whole = jnp.concatenate(whole, axis=0)
        inner[y * 3 * own : (y + 1) * 3 * own, :] = whole.astype(bf16)


pairs = 4


def sizes_of(count_x, inner, spread, wbig):
    pool_x = count_x // 2
    chan_out = wbig.shape[0] // count_x
    pool_y = spread.shape[0] // (pool_x * chan_out)
    own = inner.shape[0] // (3 * (2 * pool_y + 2))
    return pool_x, chan_out, pool_y, own, own // count_x


def worker(count_x, pool_x, chan_out, pool_y, own, chan, near_of, rest_of, refs):
    spread, wbig, wback, sums, field = refs
    wide = own + 2 * chan
    size = 3 * wide
    lane = iota((wide, lanes), 1)
    inside, outside = lane != lanes - 1, lane != 0

    def finish(y, whole, edge):
        first, last = whole[0:wide], whole[2 * wide : 3 * wide]
        inner = (
            whole[wide : 2 * wide]
            + jnp.where(inside, pltpu.roll(first, lanes - 1, 1), 0.0)
            + jnp.where(outside, pltpu.roll(last, 1, 1), 0.0)
        )
        field[pl.ds(aligned(y * wide, 8), wide), :] = inner
        here = lane == y
        edge[0] = jnp.where(here, pltpu.roll(first, y, 1), edge[0])
        edge[1] = jnp.where(here, pltpu.roll(last, y + 1, 1), edge[1])

    def block_of(j):
        columns = [
            jnp.concatenate([near_of(2 * j + h), rest_of(2 * j + h)], axis=0) for h in range(2)
        ]
        return jnp.concatenate(columns, axis=1)

    def forward(i, k, ref):
        j = i * pairs + k
        preact = dot(wbig[...], block_of(j))
        slope = jnp.tanh(5.0 * preact)
        linear = jnp.maximum(preact, 0.3 * preact)
        factor = 1.0 + jnp.abs(slope)
        here = spread[pl.ds(aligned(j * pool_x * chan_out, 8), pool_x * chan_out), :]
        slope = 0.65 + 0.35 * slope
        delta = []
        for x in range(pool_x):
            top, mid = 2 * x * chan_out, (2 * x + 1) * chan_out
            end = mid + chan_out
            times = here[x * chan_out : (x + 1) * chan_out]
            times = jnp.concatenate([times, times], axis=1)
            delta.append((slope[top:mid] * times).astype(bf16))
            delta.append((slope[mid:end] * times).astype(bf16))
            total = linear[top:mid] + linear[mid:end]
            total = total[:, :lanes] + total[:, lanes:]
            prod = factor[top:mid] * factor[mid:end]
            prod = prod[:, :lanes] * prod[:, lanes:]
            total = total - log_scale * jnp.log(prod)
            sums[pl.ds(x * pool_y + j, chan_out, stride=pool_x * pool_y), :] = total
        ref[:, 2 * k * lanes : 2 * (k + 1) * lanes] = jnp.concatenate(delta, axis=0)

    def backward(i, k, ref, held, edge):
        j = i * pairs + k
        parts = dot(wback[...], ref[:, 2 * k * lanes : 2 * (k + 1) * lanes])
        part = lambda b, h: parts[b * size : (b + 1) * size, h * lanes : (h + 1) * lanes]
        finish(2 * j, held[0] + part(0, 0), edge)
        finish(2 * j + 1, held[1] + part(1, 0) + part(0, 1), edge)
        held[0] = part(2, 0) + part(1, 1)
        held[1] = part(2, 1)

    def weigh(i, ref):
        blocks = jnp.concatenate([block_of(i * pairs + k) for k in range(pairs)], axis=1)
        return dot(ref[...], blocks, ((1,), (1,)))

    return finish, forward, backward, weigh


def inner_kernel(
    count_x, got_0, got_1, inner, spread, wbig, wback,
    sums, field, patches, cols, gram, stage, carry, delta_a, delta_b,
):
    shape = sizes_of(count_x, inner, spread, wbig)
    pool_x, chan_out, pool_y, own, chan = shape
    count_y = 2 * pool_y
    wide = own + 2 * chan
    size = 3 * wide
    outside_rows = 2 * chan
    depth = 3 * outside_rows + 8
    body = chan * count_y
    for side, planes in enumerate(from_sides(got_0, got_1, 0, body)):
        for c in range(chan):
            at = outside_rows + side * chan + c
            plane = planes[c * count_y : (c + 1) * count_y]
            stage[pl.ds(at, count_y, stride=outside_rows), :] = plane
    low, high = from_sides(got_0, got_1, body, 16)
    left_cols, right_cols = [
        jnp.concatenate([low[at : at + chan], high[at : at + chan]], axis=0) for at in (0, chan)
    ]
    for y in range(1, count_y + 1):
        mid = stage[y * outside_rows : (y + 1) * outside_rows, :]
        whole = shifted(mid, left_cols, right_cols, y) + [jnp.ones((8, lanes), f32)]
        patches[y * depth : (y + 1) * depth, :] = jnp.concatenate(whole, axis=0).astype(bf16)

    def near_of(y):
        return inner[pl.ds(aligned(y * 3 * own, 16), 9 * own), :]

    def rest_of(y):
        return patches[pl.ds(aligned(y * depth, 16), 3 * depth), :]

    finish, forward, backward, weigh = worker(
        count_x, *shape, near_of, rest_of, (spread, wbig, wback, sums, field)
    )
    carry[...] = jnp.zeros_like(carry)
    gram[...] = jnp.zeros_like(gram)
    cols[...] = jnp.zeros_like(cols)

    def opened():
        return (
            [carry[0:size, :], carry[size : 2 * size, :]],
            [cols[0:wide, :], cols[wide : 2 * wide, :]],
        )

    def closed(held, edge):
        carry[0:size, :] = held[0]
        carry[size : 2 * size, :] = held[1]
        cols[0:wide, :] = edge[0]
        cols[wide : 2 * wide, :] = edge[1]

    def both(at):
        held, edge = opened()
        total = gram[...] + weigh(at, delta_a)
        for k in range(pairs):
            forward(at + 1, k, delta_b)
            backward(at, k, delta_a, held, edge)
        return held, edge, total + weigh(at + 1, delta_b)

    def step(t, _):
        at = 2 * t + 1
        held, edge, total = both(at)
        for k in range(pairs):
            forward(at + 2, k, delta_a)
            backward(at + 1, k, delta_b, held, edge)
        gram[...] = total
        closed(held, edge)
        return 0

    steps = count_y // (2 * pairs)
    for k in range(pairs):
        forward(1, k, delta_a)
    lax.fori_loop(0, steps // 2 - 2, step, 0)
    held, edge, total = both(steps - 3)
    gram[...] = total
    for k in range(pairs):
        backward(steps - 2, k, delta_b, held, edge)
    end = (steps - 1) * 2 * pairs
    finish(end, held[0], edge)
    finish(end + 1, held[1], edge)
    closed(held, edge)


def main_kernel(
    count_x, row_1, row_0, inner, patches, inner_cols, inner_gram, spread, wbig, wback,
    sums, field, sent_0, sent_1, wpart, wframe, rows_out, cols,
    near, rest, gram, delta_a, delta_b,
):
    shape = sizes_of(count_x, inner, spread, wbig)
    pool_x, chan_out, pool_y, own, chan = shape
    count_y = 2 * pool_y
    wide = own + 2 * chan
    size = 3 * wide
    outside_rows = 2 * chan
    depth = 3 * outside_rows + 8
    even = is_even("gx")
    span_y = 2 * pairs
    top = span_y + 2
    start = count_y - span_y
    for ref, source, height in ((near, inner, 3 * own), (rest, patches, depth)):
        ref[height : top * height, :] = source[height : top * height, :]
        last = (2 * top - 1) * height
        ref[top * height : last, :] = source[start * height : (count_y + 1) * height, :]
    one, two = row_0[...].astype(f32), row_1[...].astype(f32)
    above, below = pick("gy", two, one), pick("gy", one, two)
    for at, got, line in ((0, above, count_y), (2 * top - 1, below, 1)):
        left, right = got[wide : 2 * wide], got[2 * wide : 3 * wide]
        whole = jnp.concatenate(shifted(got[:own], left[:own], right[:own], line), axis=0)
        near[at * 3 * own : (at + 1) * 3 * own, :] = whole.astype(bf16)
        whole = shifted(got[own:wide], left[own:], right[own:], line)
        whole = jnp.concatenate(whole + [jnp.ones((8, lanes), f32)], axis=0)
        rest[at * depth : (at + 1) * depth, :] = whole.astype(bf16)

    def place(y):
        return y if y < top else y - start + top

    def near_of(y):
        return near[place(y) * 3 * own : (place(y) + 3) * 3 * own, :]

    def rest_of(y):
        return rest[place(y) * depth : (place(y) + 3) * depth, :]

    finish, forward, backward, weigh = worker(
        count_x, *shape, near_of, rest_of, (spread, wbig, wback, sums, field)
    )
    final = count_y // span_y - 1
    zero = jnp.zeros((size, lanes), f32)
    held, edge = [zero, zero], [inner_cols[0:wide, :], inner_cols[wide : 2 * wide, :]]
    extra = [jnp.zeros((wide, lanes), f32)] * 2
    for k in range(pairs):
        forward(0, k, delta_a)
    for k in range(pairs):
        forward(final, k, delta_b)
        backward(0, k, delta_a, held, extra)
    total = inner_gram[...] + weigh(0, delta_a)
    finish(span_y, held[0], extra)
    finish(span_y + 1, held[1], extra)
    held = [zero, zero]
    for k in range(pairs):
        backward(final, k, delta_b, held, extra)
    gram[...] = total + weigh(final, delta_b)
    finish(count_y, held[0], extra)
    finish(count_y + 1, held[1], extra)
    cols[0:wide, :] = edge[0] + extra[0]
    cols[wide : 2 * wide, :] = edge[1] + extra[1]

    span = gram.shape[1]
    spot = iota((chan_out, 2 * lanes), 1)
    first = 9 * own
    turn = lambda part, shift: pltpu.roll(part, (2 * lanes - shift) % (2 * lanes), 1)
    straight, turned, extra = 0.0, 0.0, 0.0
    for x in range(count_x):
        part = gram[x * chan_out : (x + 1) * chan_out, :]
        part = jnp.concatenate([part, jnp.zeros((chan_out, 2 * lanes - span), f32)], axis=1)
        straight = straight + part
        moved = turn(part, chan * (x - 1)) if x != 1 else part
        a = spot % own // chan
        turned = turned + jnp.where((a + x >= 1) & (a + x <= count_x), moved, 0.0)
        if x == 0:
            extra = extra + jnp.where((spot - first) % outside_rows < chan, part, 0.0)
        if x == count_x - 1:
            extra = extra + jnp.where((spot - first) % outside_rows >= chan, part, 0.0)
    group = 3 * chan
    tight = jnp.zeros((chan_out, 2 * lanes), f32)
    for b in range(3):
        for e in range(3):
            at = (b * 3 + e) * group
            here = spot // group == b * 3 + e
            value = turn(turned, b * 3 * own + e * own - at)
            source = first + b * depth + e * outside_rows
            low, high = turn(extra, source - at), turn(extra, source - at - chan)
            a = (spot - at) // chan
            value = value + jnp.where(a == 0, low, 0.0) + jnp.where(a == 2, high, 0.0)
            tight = jnp.where(here, value, tight)
    bias_at = first + 3 * outside_rows
    tight = jnp.where(spot == 9 * group, turn(straight, bias_at - 9 * group), tight)
    tight = tight[:, :lanes]
    wpart[...] = tight
    sides = jnp.concatenate(split(tight), axis=0)
    wframe[...] = sides

    ends = [field[0:wide, :], field[(count_y + 1) * wide : (count_y + 2) * wide, :]]
    rows_out[...] = jnp.concatenate([end[chan : chan + own] for end in ends], axis=0)
    zero = jnp.zeros((8, lanes), f32)
    for ref, odd in ((sent_0, 0), (sent_1, 1)):
        high = even != (odd == 1)
        low_frame, high_frame = [
            jnp.concatenate(
                [end[x * chan : (x + 1) * chan] for end in ends]
                + [cols[top + x * chan : top + (x + 1) * chan, :] for top in (0, wide)],
                axis=0,
            )
            for x in (0, count_x + 1)
        ]
        ref[0:16, :] = jnp.where(high, high_frame, low_frame).astype(bf16)
        ref[16:, :] = sides


def plane_of(field, outer_field, at, wide, count_y):
    row = iota((count_y, lanes), 0) + 1
    span_y = 2 * pairs
    place = pl.ds(wide + at, count_y, stride=wide)
    near = (row >= span_y) & (row < count_y - span_y + 2)
    far = (row < span_y + 2) | (row >= count_y - span_y)
    return jnp.where(near, field[place, :], 0.0) + jnp.where(far, outer_field[place, :], 0.0)


def face_kernel(chan, field, outer_field, face_0, face_1):
    count_y = face_0.shape[0] // chan
    wide = field.shape[0] // (count_y + 2)
    even = is_even("gx")
    for c in range(chan):
        low, high = [
            plane_of(field, outer_field, at + c, wide, count_y) for at in (0, wide - chan)
        ]
        place = slice(c * count_y, (c + 1) * count_y)
        face_0[place, :] = jnp.where(even, high, low).astype(bf16)
        face_1[place, :] = jnp.where(even, low, high).astype(bf16)


def x_kernel(alone, wpart, wframe, rows, cols, got_0, got_1, far, frame, rows_out):
    own = rows.shape[0] // 2
    wide = cols.shape[0] // 2
    chan = (wide - own) // 2
    if alone:
        total = wpart[...]
    else:
        total = joined(wframe[...]) + joined(far[16:, :])
        total = total + (joined(got_0[16:, :]) + joined(got_1[16:, :]))
    frame[2 * own :, :] = jnp.concatenate(split(total), axis=0)
    one, two = got_0[0:16, :].astype(f32), got_1[0:16, :].astype(f32)
    from_low, from_high = pick("gx", two, one), pick("gx", one, two)
    mid = jnp.zeros((own - 2 * chan, lanes), f32)
    found = []
    for top, at in ((0, 2 * chan), (wide, 3 * chan)):
        more = [from_low[at : at + chan], mid, from_high[at : at + chan]]
        found.append(cols[top + chan : top + chan + own, :] + jnp.concatenate(more, axis=0))
    frame[0 : 2 * own, :] = jnp.concatenate(found, axis=0).astype(bf16)
    for at in (0, 1):
        more = [from_low[at * chan : (at + 1) * chan], mid, from_high[at * chan : (at + 1) * chan]]
        place = slice(at * own, (at + 1) * own)
        rows_out[place, :] = rows[place, :] + jnp.concatenate(more, axis=0)


def z_kernel(count_y, mine, got, rows, token, sent_0, sent_1, wframe):
    own = rows.shape[0] // 2
    total = joined(mine[2 * own :, :]) + joined(got[2 * own :, :])
    sides = jnp.concatenate(split(total), axis=0)
    wframe[...] = sides
    last = got[0:own, :].astype(f32)
    first = got[own : 2 * own, :].astype(f32)
    spot = iota((own, lanes), 1)
    both = []
    for at, line in ((0, 0), (1, count_y + 1)):
        more = jnp.where(spot == lanes - 1, pltpu.roll(last, lanes - 1 - line, 1), 0.0)
        turned = pltpu.roll(first, lanes - line, 1) if line else first
        more = jnp.where(spot == 0, turned, more)
        both.append(rows[at * own : (at + 1) * own, :] + more)
    sent_0[0:own, :] = pick("gy", both[1], both[0]).astype(bf16)
    sent_1[0:own, :] = pick("gy", both[0], both[1]).astype(bf16)
    for ref in (sent_0, sent_1):
        ref[own:, :] = sides


def grad_kernel(field, outer_field, face_0, face_1, got, grad, ends):
    chan, count_x, count_y, _ = grad.shape
    own = chan * count_x
    wide = own + 2 * chan
    spot = iota((count_y, lanes), 1)
    columns = pltpu.roll(got[0 : 2 * own, :].astype(f32), lanes - 1, 1)
    columns = jnp.concatenate([columns, jnp.zeros((lanes - 2 * own, lanes), f32)], axis=0)
    columns = columns.T[0:count_y]
    for x in range(count_x):
        for c in range(chan):
            at = x * chan + c
            plane = plane_of(field, outer_field, chan + at, wide, count_y)
            place = slice(c * count_y, (c + 1) * count_y)
            if x == 0:
                plane = plane + pick("gx", face_1[place, :].astype(f32), face_0[place, :].astype(f32))
            if x == count_x - 1:
                plane = plane + pick("gx", face_0[place, :].astype(f32), face_1[place, :].astype(f32))
            more = jnp.where(spot == lanes - 1, columns[:, at : at + 1], 0.0)
            plane = plane + jnp.where(spot == 0, columns[:, own + at : own + at + 1], more)
            grad[c, x] = plane
            ends[0, c, x] = plane[0:8]
            ends[1, c, x] = plane[count_y - 8 : count_y]


def final_kernel(whole, ends, mine, got_1, far, got_0, out, wout, bout, tiles, wtile, btile, sems):
    chan, count_x, count_y, _ = whole.shape
    own = chan * count_x
    chan_out = mine.shape[0] // 2
    row = iota((8, lanes), 0)
    one, two = got_0[0:own, :].astype(f32), got_1[0:own, :].astype(f32)
    above, below = pick("gy", two, one), pick("gy", one, two)
    copies = []
    for side, more, line in ((0, above, 0), (1, below, 7)):
        for x in range(count_x):
            for c in range(chan):
                at = x * chan + c
                extra = jnp.where(row == line, more[at : at + 1], 0.0)
                tiles[side, c, x] = ends[side, c, x] + extra
        copies.append(
            pltpu.make_async_copy(
                tiles.at[side],
                out.at[:, :, pl.ds(side * (count_y - 8), 8), :],
                sems.at[side],
            )
        )
        copies[-1].start()
    total = joined(mine[...]) + joined(far[...])
    total = total + (joined(got_0[own:, :]) + joined(got_1[own:, :]))
    total = jnp.concatenate([total, jnp.zeros((lanes - chan_out, lanes), f32)], axis=0)
    total = total.T
    for a in range(3):
        for be in range(9):
            at = (be * 3 + a) * chan
            wtile[a * 9 + be] = total[at : at + chan, :chan_out]
    btile[...] = total[27 * chan : 27 * chan + 1, :chan_out]
    copies.append(pltpu.make_async_copy(wtile, wout, sems.at[2]))
    copies.append(pltpu.make_async_copy(btile, bout, sems.at[3]))
    copies[2].start()
    copies[3].start()
    for copy in copies:
        copy.wait()


def traffic(mib):
    return pl.CostEstimate(flops=0, bytes_accessed=mib << 20, transcendentals=0)


def call(kernel, outs, scratch=(), cost=None, **rest):
    return pl.pallas_call(
        kernel,
        out_shape=outs,
        **rest,
        scratch_shapes=list(scratch),
        cost_estimate=cost,
        compiler_params=pltpu.CompilerParams(vmem_limit_bytes=limit),
    )


def on_device(cells, weight, bias, cotangent):
    chan, count_x, count_y, count_z = cells.shape
    chan_out = weight.shape[0]
    own = chan * count_x
    wide = own + 2 * chan
    depth = 6 * chan + 8
    shape = jax.ShapeDtypeStruct

    kernel = weight.transpose(0, 3, 4, 2, 1)
    placed = jnp.stack(
        [
            jnp.pad(kernel, ((0, 0), (0, 0), (0, 0), (x, count_x - 1 - x), (0, 0)))
            for x in range(count_x)
        ]
    ).reshape(count_x * chan_out, 3, 3, count_x + 2, chan)
    coarse = lax.reduce_precision(bias, 8, 7)
    middle = lax.reduce_precision(bias - coarse, 8, 7)
    fine = bias - coarse - middle
    pieces = jnp.stack([coarse, middle, fine], axis=1).astype(bf16)
    pieces = jnp.pad(jnp.tile(pieces, (count_x, 1))[:, None], ((0, 0), (0, 2), (0, 5)))
    near = placed[:, :, :, 1 : count_x + 1].reshape(count_x * chan_out, 9 * own)
    rest = jnp.concatenate([placed[:, :, :, :1], placed[:, :, :, count_x + 1 :]], axis=3)
    rest = jnp.concatenate([rest.reshape(count_x * chan_out, 3, 6 * chan), pieces], axis=2)
    wbig = jnp.concatenate([near, rest.reshape(count_x * chan_out, 3 * depth)], axis=1)
    wback = placed.reshape(count_x * chan_out, 9 * wide).T

    edges, rows = call(
        pack_kernel, [shape((2 * own, lanes), bf16), shape((2 * own, lanes), f32)]
    )(cells)
    pool_x, pool_y, pool_z = cotangent.shape[1:]
    pooled_rows = shape((pool_y * pool_x * chan_out, lanes), f32)
    spread = call(spread_kernel, pooled_rows)(cotangent)
    edges = swapped(edges, "gz", 0)
    body = chan * count_y
    bundle = shape((body + 16, lanes), bf16)
    side = shape((own, lanes), f32)
    face_0, face_1, left, right = call(bundle_kernel, [bundle, bundle, side, side])(cells, edges)
    face_1, face_0 = swapped(face_1, "gx", 1), swapped(face_0, "gx", 0)
    inner = call(
        own_kernel,
        shape(((count_y + 2) * 3 * own, lanes), bf16),
        [pltpu.VMEM(((count_y + 2) * own, lanes), f32)],
        traffic(4),
    )(cells, left, right)
    bundle = shape((3 * wide + 8, lanes), bf16)
    vmem, anywhere = pl.BlockSpec(memory_space=pltpu.VMEM), pl.BlockSpec(memory_space=pl.ANY)
    row_0, row_1 = call(
        functools.partial(rows_kernel, chan),
        [bundle, bundle],
        in_specs=[vmem] * 5 + [anywhere] * 2,
    )(rows, left, right, face_0, face_1, inner, spread)
    row_1, row_0 = swapped(row_1, "gy", 1), swapped(row_0, "gy", 0)

    tall = 2 * wide
    all_field = shape(((count_y + 2) * wide, lanes), f32)
    all_gram = shape((count_x * chan_out, 9 * own + 3 * depth), f32)
    deltas = [pltpu.VMEM((count_x * chan_out, 8 * lanes), bf16)] * 2
    sums, field, patches, cols, gram = call(
        functools.partial(inner_kernel, count_x),
        [
            pooled_rows,
            all_field,
            shape(((count_y + 2) * depth, lanes), bf16),
            shape((tall, lanes), f32),
            all_gram,
        ],
        [
            pltpu.VMEM(((count_y + 2) * 2 * chan, lanes), f32),
            pltpu.VMEM((6 * wide, lanes), f32),
        ]
        + deltas,
        traffic(16),
    )(face_0, face_1, inner, spread, wbig, wback)

    bundle = shape((16 + 2 * chan_out, lanes), bf16)
    face = shape((body, lanes), bf16)
    outer_sums, outer_field, row_0, row_1, wpart, wframe, rows, cols = call(
        functools.partial(main_kernel, count_x),
        [
            pooled_rows,
            all_field,
            bundle,
            bundle,
            shape((chan_out, lanes), f32),
            shape((2 * chan_out, lanes), bf16),
            shape((2 * own, lanes), f32),
            shape((tall, lanes), f32),
        ],
        [
            pltpu.VMEM((4 * (pairs + 1) * 3 * own, lanes), bf16),
            pltpu.VMEM((4 * (pairs + 1) * depth, lanes), bf16),
            pltpu.VMEM((count_x * chan_out, 9 * own + 3 * depth), f32),
        ]
        + deltas,
    )(row_1, row_0, inner, patches, cols, gram, spread, wbig, wback)

    alone = lax.axis_size("gx") != 4
    if alone:
        wpart, far = lax.psum(wpart, "gx"), row_0
    else:
        far = swapped(row_0, "gx", 2)
    row_1, row_0 = swapped(row_1, "gx", 1), swapped(row_0, "gx", 0)
    face_0, face_1 = call(functools.partial(face_kernel, chan), [face, face], cost=traffic(2))(
        field, outer_field
    )
    face_1, face_0 = swapped(face_1, "gx", 1), swapped(face_0, "gx", 0)
    pooled, token = call(
        functools.partial(pool_kernel, pairs),
        [shape(cotangent.shape, bf16), shape((8, lanes), f32)],
        cost=traffic(8),
    )(sums, outer_sums)
    mine, rows = call(
        functools.partial(x_kernel, alone),
        [shape((2 * own + 2 * chan_out, lanes), bf16), shape((2 * own, lanes), f32)],
    )(wpart, wframe, rows, cols, row_0, row_1, far)
    frame = swapped(mine, "gz", 0)
    bundle = shape((own + 2 * chan_out, lanes), bf16)
    row_0, row_1, mine = call(
        functools.partial(z_kernel, count_y),
        [bundle, bundle, shape((2 * chan_out, lanes), bf16)],
        in_specs=[vmem] * 3 + [anywhere],
    )(mine, frame, rows, token)
    row_1, row_0 = swapped(row_1, "gy", 1), swapped(row_0, "gy", 0)
    far = swapped(mine, "gy", 2)
    tiles = (2, chan, count_x, 8, lanes)
    grad, ends = call(grad_kernel, [shape(cells.shape, f32), shape(tiles, f32)], cost=traffic(8))(
        field, outer_field, face_0, face_1, frame
    )
    input_grad, wsum, bias_grad = call(
        final_kernel,
        [
            shape(cells.shape, f32),
            shape((27, chan, chan_out), f32),
            shape((1, chan_out), f32),
        ],
        [
            pltpu.VMEM(tiles, f32),
            pltpu.VMEM((27, chan, chan_out), f32),
            pltpu.VMEM((1, chan_out), f32),
            pltpu.SemaphoreType.DMA((4,)),
        ],
        in_specs=[anywhere] + [vmem] * 5,
        out_specs=[anywhere] * 3,
        input_output_aliases={0: 0},
    )(grad, ends, mine, row_1, far, row_0)
    weight_grad = wsum.reshape(3, 3, 3, chan, chan_out).transpose(4, 3, 0, 1, 2)
    return (pooled, weight_grad, bias_grad.reshape(chan_out), input_grad)


def solution(mesh):
    in_specs = (P(None, "gx", "gy", "gz"), P(), P(), P(None, "gx", "gy", "gz"))
    out_specs = (P(None, "gx", "gy", "gz"), P(), P(), P(None, "gx", "gy", "gz"))
    return jax.shard_map(
        on_device, mesh=mesh, in_specs=in_specs, out_specs=out_specs, check_vma=False
    )
```

```python
import functools

import jax
import jax.numpy as jnp
import numpy as np
from jax import lax
from jax.experimental import pallas as pl
from jax.experimental.pallas import tpu as pltpu
from jax.sharding import PartitionSpec as P

axes = ("gx", "gy", "gz")
f32, bf16 = jnp.float32, jnp.bfloat16
log_scale = 0.07
lanes = 128
limit = 48 * 1024 * 1024


def dot(a, b, contract=((1,), (0,))):
    return lax.dot_general(a, b, (contract, ((), ())), preferred_element_type=f32)


def iota(shape, dim):
    return lax.broadcasted_iota(jnp.int32, shape, dim)


def aligned(start, tile):
    return start if isinstance(start, int) else pl.multiple_of(start, tile)


def swapped(array, axis, pairing):
    count = lax.axis_size(axis)
    pairs = []
    for i in range(count):
        if pairing == 2:
            partner = i + count // 2
        else:
            partner = i + 1 if i % 2 == pairing else i - 1
        pairs.append((i, partner % count))
    return lax.ppermute(array, axis, pairs)


def is_even(axis):
    return lax.rem(lax.axis_index(axis), 2) == 0


def pick(axis, if_even, if_odd):
    return jnp.where(is_even(axis), if_even, if_odd)


def split(value):
    coarse = value.astype(bf16)
    return coarse, (value - coarse.astype(f32)).astype(bf16)


def joined(pair):
    half = pair.shape[0] // 2
    return pair[:half].astype(f32) + pair[half:].astype(f32)


def pack_kernel(cells, edges, rows):
    chan, count_x, count_y, _ = cells.shape
    count = chan * count_x
    row = iota((2 * count, count * lanes), 0)
    lane = iota((2 * count, count * lanes), 1)
    want = jnp.where(row < count, row * lanes, (row - count) * lanes + lanes - 1)
    chosen = (lane == want).astype(f32).astype(bf16)
    planes = [cells[c, x] for x in range(count_x) for c in range(chan)]
    wide = jnp.concatenate(planes, axis=1)
    found = dot(chosen, wide, ((1,), (1,)))
    found = jnp.concatenate([found, jnp.zeros((2 * count, lanes - count_y), f32)], axis=1)
    edges[...] = pltpu.roll(found, 1, 1).astype(bf16)
    for at, plane in enumerate(planes):
        wide_plane = plane.astype(f32)
        rows[at : at + 1, :] = wide_plane[0:1]
        rows[count + at : count + at + 1, :] = wide_plane[count_y - 1 : count_y]


def bundle_kernel(cells, edges, sent_0, sent_1, left, right):
    chan, count_x, count_y, _ = cells.shape
    own = chan * count_x
    whole = edges[...].astype(f32)
    right[...] = whole[0:own]
    left[...] = whole[own : 2 * own]
    zero = jnp.zeros((8, lanes), f32)
    body = chan * count_y
    frames = []
    for x in (0, count_x - 1):
        at = slice(x * chan, x * chan + chan)
        frames.append(jnp.concatenate([whole[own + x * chan :][:chan], whole[at], zero], axis=0))
    even = is_even("gx")
    for ref, odd in ((sent_0, 0), (sent_1, 1)):
        high = even != (odd == 1)
        x = jnp.where(high, count_x - 1, 0)
        for c in range(chan):
            ref[c * count_y : (c + 1) * count_y, :] = cells[c, x]
        ref[body : body + 16, :] = jnp.where(high, frames[1], frames[0]).astype(bf16)


def from_sides(got_0, got_1, start, size):
    one = got_0[start : start + size, :].astype(f32)
    two = got_1[start : start + size, :].astype(f32)
    return pick("gx", two, one), pick("gx", one, two)


def rows_kernel(chan, got_1, got_0, rows, left, right, inner, spread, sent_0, sent_1):
    own = rows.shape[0] // 2
    body = got_0.shape[0] - 16
    count_y = body // chan
    low, high = from_sides(got_0, got_1, body, 16)
    edges = []
    for ref, at in ((left, 0), (right, chan)):
        edges += [ref[...], low[at : at + chan], high[at : at + chan]]
    edges.append(jnp.zeros((8, lanes), f32))
    low, high = from_sides(got_0, got_1, 0, body)
    both = []
    for at, line in ((0, 0), (own, count_y - 1)):
        outer = [
            plane[c * count_y + line : c * count_y + line + 1]
            for plane in (low, high)
            for c in range(chan)
        ]
        both.append(jnp.concatenate([rows[at : at + own, :]] + outer + edges, axis=0))
    sent_0[...] = pick("gy", both[1], both[0]).astype(bf16)
    sent_1[...] = pick("gy", both[0], both[1]).astype(bf16)


def spread_kernel(cot, spread):
    chan_out, pool_x, pool_y, pool_z = cot.shape
    twice = jnp.where(
        iota((pool_z, lanes), 1) // 2 == iota((pool_z, lanes), 0), 0.125, 0.0
    ).astype(bf16)
    for o in range(chan_out):
        part = dot(cot[o].reshape(pool_x * pool_y, pool_z), twice)
        for x in range(pool_x):
            spread[pl.ds(x * chan_out + o, pool_y, stride=pool_x * chan_out), :] = part[
                x * pool_y : (x + 1) * pool_y
            ]


def pool_kernel(edge, sums, outer_sums, pooled, token):
    token[...] = jnp.zeros_like(token)
    chan_out, pool_x, pool_y, pool_z = pooled.shape
    halves = jnp.where(
        iota((2 * lanes, pool_z), 0) % lanes // 2 == iota((2 * lanes, pool_z), 1), 0.125, 0.0
    ).astype(bf16)
    for o in range(0, chan_out, 4):
        rows = 4 * pool_x * pool_y
        part = sums[o * pool_x * pool_y : o * pool_x * pool_y + rows, :]
        at = iota((rows, lanes), 0) % pool_y
        near = (at >= edge) & (at < pool_y - edge)
        part = jnp.where(near, part, outer_sums[o * pool_x * pool_y : o * pool_x * pool_y + rows, :])
        mean = dot(jnp.concatenate(split(part), axis=1), halves) + log_scale * float(np.log(2.0))
        pooled[o : o + 4] = mean.astype(bf16).reshape(4, pool_x, pool_y, pool_z)


def shifted(mid, left, right, y):
    lane = iota(mid.shape, 1)
    low = pltpu.roll(left, (lanes - y) % lanes, 1)
    high = pltpu.roll(right, (lanes - 1 - y) % lanes, 1)
    before = jnp.where(lane == 0, low, pltpu.roll(mid, 1, 1))
    after = jnp.where(lane == lanes - 1, high, pltpu.roll(mid, lanes - 1, 1))
    return [before, mid, after]


def own_kernel(cells, left, right, inner, stage):
    chan, count_x, count_y, _ = cells.shape
    own = chan * count_x
    for x in range(count_x):
        for c in range(chan):
            plane = cells[c, x].astype(f32)
            stage[pl.ds(own + x * chan + c, count_y, stride=own), :] = plane
    left_cols, right_cols = left[...], right[...]
    for y in range(1, count_y + 1):
        whole = shifted(stage[y * own : (y + 1) * own, :], left_cols, right_cols, y)
        whole = jnp.concatenate(whole, axis=0)
        inner[y * 3 * own : (y + 1) * 3 * own, :] = whole.astype(bf16)


pairs = 4


def sizes_of(count_x, inner, spread, wbig):
    pool_x = count_x // 2
    chan_out = wbig.shape[0] // count_x
    pool_y = spread.shape[0] // (pool_x * chan_out)
    own = inner.shape[0] // (3 * (2 * pool_y + 2))
    return pool_x, chan_out, pool_y, own, own // count_x


def worker(count_x, pool_x, chan_out, pool_y, own, chan, near_of, rest_of, refs):
    spread, wbig, wback, sums, field = refs
    wide = own + 2 * chan
    size = 3 * wide
    lane = iota((wide, lanes), 1)
    inside, outside = lane != lanes - 1, lane != 0

    def finish(y, whole, edge):
        first, last = whole[0:wide], whole[2 * wide : 3 * wide]
        inner = (
            whole[wide : 2 * wide]
            + jnp.where(inside, pltpu.roll(first, lanes - 1, 1), 0.0)
            + jnp.where(outside, pltpu.roll(last, 1, 1), 0.0)
        )
        field[pl.ds(aligned(y * wide, 8), wide), :] = inner
        here = lane == y
        edge[0] = jnp.where(here, pltpu.roll(first, y, 1), edge[0])
        edge[1] = jnp.where(here, pltpu.roll(last, y + 1, 1), edge[1])

    def block_of(j):
        columns = [
            jnp.concatenate([near_of(2 * j + h), rest_of(2 * j + h)], axis=0) for h in range(2)
        ]
        return jnp.concatenate(columns, axis=1)

    def forward(i, k, ref):
        j = i * pairs + k
        preact = dot(wbig[...], block_of(j))
        slope = jnp.tanh(5.0 * preact)
        linear = jnp.maximum(preact, 0.3 * preact)
        factor = 1.0 + jnp.abs(slope)
        here = spread[pl.ds(aligned(j * pool_x * chan_out, 8), pool_x * chan_out), :]
        slope = 0.65 + 0.35 * slope
        delta = []
        for x in range(pool_x):
            top, mid = 2 * x * chan_out, (2 * x + 1) * chan_out
            end = mid + chan_out
            times = here[x * chan_out : (x + 1) * chan_out]
            times = jnp.concatenate([times, times], axis=1)
            delta.append((slope[top:mid] * times).astype(bf16))
            delta.append((slope[mid:end] * times).astype(bf16))
            total = linear[top:mid] + linear[mid:end]
            total = total[:, :lanes] + total[:, lanes:]
            prod = factor[top:mid] * factor[mid:end]
            prod = prod[:, :lanes] * prod[:, lanes:]
            total = total - log_scale * jnp.log(prod)
            sums[pl.ds(x * pool_y + j, chan_out, stride=pool_x * pool_y), :] = total
        ref[:, 2 * k * lanes : 2 * (k + 1) * lanes] = jnp.concatenate(delta, axis=0)

    def backward(i, k, ref, held, edge):
        j = i * pairs + k
        parts = dot(wback[...], ref[:, 2 * k * lanes : 2 * (k + 1) * lanes])
        part = lambda b, h: parts[b * size : (b + 1) * size, h * lanes : (h + 1) * lanes]
        finish(2 * j, held[0] + part(0, 0), edge)
        finish(2 * j + 1, held[1] + part(1, 0) + part(0, 1), edge)
        held[0] = part(2, 0) + part(1, 1)
        held[1] = part(2, 1)

    def weigh(i, ref):
        blocks = jnp.concatenate([block_of(i * pairs + k) for k in range(pairs)], axis=1)
        return dot(ref[...], blocks, ((1,), (1,)))

    return finish, forward, backward, weigh


def inner_kernel(
    count_x, got_0, got_1, inner, spread, wbig, wback,
    sums, field, patches, cols, gram, stage, carry, delta_a, delta_b,
):
    shape = sizes_of(count_x, inner, spread, wbig)
    pool_x, chan_out, pool_y, own, chan = shape
    count_y = 2 * pool_y
    wide = own + 2 * chan
    size = 3 * wide
    outside_rows = 2 * chan
    depth = 3 * outside_rows + 8
    body = chan * count_y
    for side, planes in enumerate(from_sides(got_0, got_1, 0, body)):
        for c in range(chan):
            at = outside_rows + side * chan + c
            plane = planes[c * count_y : (c + 1) * count_y]
            stage[pl.ds(at, count_y, stride=outside_rows), :] = plane
    low, high = from_sides(got_0, got_1, body, 16)
    left_cols, right_cols = [
        jnp.concatenate([low[at : at + chan], high[at : at + chan]], axis=0) for at in (0, chan)
    ]
    for y in range(1, count_y + 1):
        mid = stage[y * outside_rows : (y + 1) * outside_rows, :]
        whole = shifted(mid, left_cols, right_cols, y) + [jnp.ones((8, lanes), f32)]
        patches[y * depth : (y + 1) * depth, :] = jnp.concatenate(whole, axis=0).astype(bf16)

    def near_of(y):
        return inner[pl.ds(aligned(y * 3 * own, 16), 9 * own), :]

    def rest_of(y):
        return patches[pl.ds(aligned(y * depth, 16), 3 * depth), :]

    finish, forward, backward, weigh = worker(
        count_x, *shape, near_of, rest_of, (spread, wbig, wback, sums, field)
    )
    carry[...] = jnp.zeros_like(carry)
    gram[...] = jnp.zeros_like(gram)
    cols[...] = jnp.zeros_like(cols)

    def opened():
        return (
            [carry[0:size, :], carry[size : 2 * size, :]],
            [cols[0:wide, :], cols[wide : 2 * wide, :]],
        )

    def closed(held, edge):
        carry[0:size, :] = held[0]
        carry[size : 2 * size, :] = held[1]
        cols[0:wide, :] = edge[0]
        cols[wide : 2 * wide, :] = edge[1]

    def both(at):
        held, edge = opened()
        total = gram[...] + weigh(at, delta_a)
        for k in range(pairs):
            forward(at + 1, k, delta_b)
            backward(at, k, delta_a, held, edge)
        return held, edge, total + weigh(at + 1, delta_b)

    def step(t, _):
        at = 2 * t + 1
        held, edge, total = both(at)
        for k in range(pairs):
            forward(at + 2, k, delta_a)
            backward(at + 1, k, delta_b, held, edge)
        gram[...] = total
        closed(held, edge)
        return 0

    steps = count_y // (2 * pairs)
    for k in range(pairs):
        forward(1, k, delta_a)
    lax.fori_loop(0, steps // 2 - 2, step, 0)
    held, edge, total = both(steps - 3)
    gram[...] = total
    for k in range(pairs):
        backward(steps - 2, k, delta_b, held, edge)
    end = (steps - 1) * 2 * pairs
    finish(end, held[0], edge)
    finish(end + 1, held[1], edge)
    closed(held, edge)


def main_kernel(
    count_x, row_1, row_0, inner, patches, inner_cols, inner_gram, spread, wbig, wback,
    sums, field, sent_0, sent_1, wpart, wframe, rows_out, cols,
    near, rest, gram, delta_a, delta_b,
):
    shape = sizes_of(count_x, inner, spread, wbig)
    pool_x, chan_out, pool_y, own, chan = shape
    count_y = 2 * pool_y
    wide = own + 2 * chan
    size = 3 * wide
    outside_rows = 2 * chan
    depth = 3 * outside_rows + 8
    even = is_even("gx")
    span_y = 2 * pairs
    top = span_y + 2
    start = count_y - span_y
    for ref, source, height in ((near, inner, 3 * own), (rest, patches, depth)):
        ref[height : top * height, :] = source[height : top * height, :]
        last = (2 * top - 1) * height
        ref[top * height : last, :] = source[start * height : (count_y + 1) * height, :]
    one, two = row_0[...].astype(f32), row_1[...].astype(f32)
    above, below = pick("gy", two, one), pick("gy", one, two)
    for at, got, line in ((0, above, count_y), (2 * top - 1, below, 1)):
        left, right = got[wide : 2 * wide], got[2 * wide : 3 * wide]
        whole = jnp.concatenate(shifted(got[:own], left[:own], right[:own], line), axis=0)
        near[at * 3 * own : (at + 1) * 3 * own, :] = whole.astype(bf16)
        whole = shifted(got[own:wide], left[own:], right[own:], line)
        whole = jnp.concatenate(whole + [jnp.ones((8, lanes), f32)], axis=0)
        rest[at * depth : (at + 1) * depth, :] = whole.astype(bf16)

    def place(y):
        return y if y < top else y - start + top

    def near_of(y):
        return near[place(y) * 3 * own : (place(y) + 3) * 3 * own, :]

    def rest_of(y):
        return rest[place(y) * depth : (place(y) + 3) * depth, :]

    finish, forward, backward, weigh = worker(
        count_x, *shape, near_of, rest_of, (spread, wbig, wback, sums, field)
    )
    final = count_y // span_y - 1
    zero = jnp.zeros((size, lanes), f32)
    held, edge = [zero, zero], [inner_cols[0:wide, :], inner_cols[wide : 2 * wide, :]]
    extra = [jnp.zeros((wide, lanes), f32)] * 2
    for k in range(pairs):
        forward(0, k, delta_a)
    for k in range(pairs):
        forward(final, k, delta_b)
        backward(0, k, delta_a, held, extra)
    total = inner_gram[...] + weigh(0, delta_a)
    finish(span_y, held[0], extra)
    finish(span_y + 1, held[1], extra)
    held = [zero, zero]
    for k in range(pairs):
        backward(final, k, delta_b, held, extra)
    gram[...] = total + weigh(final, delta_b)
    finish(count_y, held[0], extra)
    finish(count_y + 1, held[1], extra)
    cols[0:wide, :] = edge[0] + extra[0]
    cols[wide : 2 * wide, :] = edge[1] + extra[1]

    span = gram.shape[1]
    spot = iota((chan_out, 2 * lanes), 1)
    first = 9 * own
    turn = lambda part, shift: pltpu.roll(part, (2 * lanes - shift) % (2 * lanes), 1)
    straight, turned, extra = 0.0, 0.0, 0.0
    for x in range(count_x):
        part = gram[x * chan_out : (x + 1) * chan_out, :]
        part = jnp.concatenate([part, jnp.zeros((chan_out, 2 * lanes - span), f32)], axis=1)
        straight = straight + part
        moved = turn(part, chan * (x - 1)) if x != 1 else part
        a = spot % own // chan
        turned = turned + jnp.where((a + x >= 1) & (a + x <= count_x), moved, 0.0)
        if x == 0:
            extra = extra + jnp.where((spot - first) % outside_rows < chan, part, 0.0)
        if x == count_x - 1:
            extra = extra + jnp.where((spot - first) % outside_rows >= chan, part, 0.0)
    group = 3 * chan
    tight = jnp.zeros((chan_out, 2 * lanes), f32)
    for b in range(3):
        for e in range(3):
            at = (b * 3 + e) * group
            here = spot // group == b * 3 + e
            value = turn(turned, b * 3 * own + e * own - at)
            source = first + b * depth + e * outside_rows
            low, high = turn(extra, source - at), turn(extra, source - at - chan)
            a = (spot - at) // chan
            value = value + jnp.where(a == 0, low, 0.0) + jnp.where(a == 2, high, 0.0)
            tight = jnp.where(here, value, tight)
    bias_at = first + 3 * outside_rows
    tight = jnp.where(spot == 9 * group, turn(straight, bias_at - 9 * group), tight)
    tight = tight[:, :lanes]
    wpart[...] = tight
    sides = jnp.concatenate(split(tight), axis=0)
    wframe[...] = sides

    ends = [field[0:wide, :], field[(count_y + 1) * wide : (count_y + 2) * wide, :]]
    rows_out[...] = jnp.concatenate([end[chan : chan + own] for end in ends], axis=0)
    zero = jnp.zeros((8, lanes), f32)
    for ref, odd in ((sent_0, 0), (sent_1, 1)):
        high = even != (odd == 1)
        low_frame, high_frame = [
            jnp.concatenate(
                [end[x * chan : (x + 1) * chan] for end in ends]
                + [cols[top + x * chan : top + (x + 1) * chan, :] for top in (0, wide)],
                axis=0,
            )
            for x in (0, count_x + 1)
        ]
        ref[0:16, :] = jnp.where(high, high_frame, low_frame).astype(bf16)
        ref[16:, :] = sides


def plane_of(field, outer_field, at, wide, count_y):
    row = iota((count_y, lanes), 0) + 1
    span_y = 2 * pairs
    place = pl.ds(wide + at, count_y, stride=wide)
    near = (row >= span_y) & (row < count_y - span_y + 2)
    far = (row < span_y + 2) | (row >= count_y - span_y)
    return jnp.where(near, field[place, :], 0.0) + jnp.where(far, outer_field[place, :], 0.0)


def face_kernel(chan, field, outer_field, face_0, face_1):
    count_y = face_0.shape[0] // chan
    wide = field.shape[0] // (count_y + 2)
    even = is_even("gx")
    for c in range(chan):
        low, high = [
            plane_of(field, outer_field, at + c, wide, count_y) for at in (0, wide - chan)
        ]
        place = slice(c * count_y, (c + 1) * count_y)
        face_0[place, :] = jnp.where(even, high, low).astype(bf16)
        face_1[place, :] = jnp.where(even, low, high).astype(bf16)


def x_kernel(alone, wpart, wframe, rows, cols, got_0, got_1, far, frame, rows_out):
    own = rows.shape[0] // 2
    wide = cols.shape[0] // 2
    chan = (wide - own) // 2
    if alone:
        total = wpart[...]
    else:
        total = joined(wframe[...]) + joined(far[16:, :])
        total = total + (joined(got_0[16:, :]) + joined(got_1[16:, :]))
    frame[2 * own :, :] = jnp.concatenate(split(total), axis=0)
    one, two = got_0[0:16, :].astype(f32), got_1[0:16, :].astype(f32)
    from_low, from_high = pick("gx", two, one), pick("gx", one, two)
    mid = jnp.zeros((own - 2 * chan, lanes), f32)
    found = []
    for top, at in ((0, 2 * chan), (wide, 3 * chan)):
        more = [from_low[at : at + chan], mid, from_high[at : at + chan]]
        found.append(cols[top + chan : top + chan + own, :] + jnp.concatenate(more, axis=0))
    frame[0 : 2 * own, :] = jnp.concatenate(found, axis=0).astype(bf16)
    for at in (0, 1):
        more = [from_low[at * chan : (at + 1) * chan], mid, from_high[at * chan : (at + 1) * chan]]
        place = slice(at * own, (at + 1) * own)
        rows_out[place, :] = rows[place, :] + jnp.concatenate(more, axis=0)


def z_kernel(count_y, mine, got, rows, token, sent_0, sent_1, wframe):
    own = rows.shape[0] // 2
    total = joined(mine[2 * own :, :]) + joined(got[2 * own :, :])
    sides = jnp.concatenate(split(total), axis=0)
    wframe[...] = sides
    last = got[0:own, :].astype(f32)
    first = got[own : 2 * own, :].astype(f32)
    spot = iota((own, lanes), 1)
    both = []
    for at, line in ((0, 0), (1, count_y + 1)):
        more = jnp.where(spot == lanes - 1, pltpu.roll(last, lanes - 1 - line, 1), 0.0)
        turned = pltpu.roll(first, lanes - line, 1) if line else first
        more = jnp.where(spot == 0, turned, more)
        both.append(rows[at * own : (at + 1) * own, :] + more)
    sent_0[0:own, :] = pick("gy", both[1], both[0]).astype(bf16)
    sent_1[0:own, :] = pick("gy", both[0], both[1]).astype(bf16)
    for ref in (sent_0, sent_1):
        ref[own:, :] = sides


def grad_kernel(field, outer_field, face_0, face_1, got, grad, ends):
    chan, count_x, count_y, _ = grad.shape
    own = chan * count_x
    wide = own + 2 * chan
    spot = iota((count_y, lanes), 1)
    columns = pltpu.roll(got[0 : 2 * own, :].astype(f32), lanes - 1, 1)
    columns = jnp.concatenate([columns, jnp.zeros((lanes - 2 * own, lanes), f32)], axis=0)
    columns = columns.T[0:count_y]
    for x in range(count_x):
        for c in range(chan):
            at = x * chan + c
            plane = plane_of(field, outer_field, chan + at, wide, count_y)
            place = slice(c * count_y, (c + 1) * count_y)
            if x == 0:
                plane = plane + pick("gx", face_1[place, :].astype(f32), face_0[place, :].astype(f32))
            if x == count_x - 1:
                plane = plane + pick("gx", face_0[place, :].astype(f32), face_1[place, :].astype(f32))
            more = jnp.where(spot == lanes - 1, columns[:, at : at + 1], 0.0)
            plane = plane + jnp.where(spot == 0, columns[:, own + at : own + at + 1], more)
            grad[c, x] = plane
            ends[0, c, x] = plane[0:8]
            ends[1, c, x] = plane[count_y - 8 : count_y]


def final_kernel(whole, ends, mine, got_1, far, got_0, out, wout, bout, tiles, wtile, btile, sems):
    chan, count_x, count_y, _ = whole.shape
    own = chan * count_x
    chan_out = mine.shape[0] // 2
    row = iota((8, lanes), 0)
    one, two = got_0[0:own, :].astype(f32), got_1[0:own, :].astype(f32)
    above, below = pick("gy", two, one), pick("gy", one, two)
    copies = []
    for side, more, line in ((0, above, 0), (1, below, 7)):
        for x in range(count_x):
            for c in range(chan):
                at = x * chan + c
                extra = jnp.where(row == line, more[at : at + 1], 0.0)
                tiles[side, c, x] = ends[side, c, x] + extra
        copies.append(
            pltpu.make_async_copy(
                tiles.at[side],
                out.at[:, :, pl.ds(side * (count_y - 8), 8), :],
                sems.at[side],
            )
        )
        copies[-1].start()
    total = joined(mine[...]) + joined(far[...])
    total = total + (joined(got_0[own:, :]) + joined(got_1[own:, :]))
    total = jnp.concatenate([total, jnp.zeros((lanes - chan_out, lanes), f32)], axis=0)
    total = total.T
    for a in range(3):
        for be in range(9):
            at = (be * 3 + a) * chan
            wtile[a * 9 + be] = total[at : at + chan, :chan_out]
    btile[...] = total[27 * chan : 27 * chan + 1, :chan_out]
    copies.append(pltpu.make_async_copy(wtile, wout, sems.at[2]))
    copies.append(pltpu.make_async_copy(btile, bout, sems.at[3]))
    copies[2].start()
    copies[3].start()
    for copy in copies:
        copy.wait()


def traffic(mib):
    return pl.CostEstimate(flops=0, bytes_accessed=mib << 20, transcendentals=0)


def call(kernel, outs, scratch=(), cost=None, **rest):
    return pl.pallas_call(
        kernel,
        out_shape=outs,
        **rest,
        scratch_shapes=list(scratch),
        cost_estimate=cost,
        compiler_params=pltpu.CompilerParams(vmem_limit_bytes=limit),
    )


def on_device(cells, weight, bias, cotangent):
    chan, count_x, count_y, count_z = cells.shape
    chan_out = weight.shape[0]
    own = chan * count_x
    wide = own + 2 * chan
    depth = 6 * chan + 8
    shape = jax.ShapeDtypeStruct

    kernel = weight.transpose(0, 3, 4, 2, 1)
    placed = jnp.stack(
        [
            jnp.pad(kernel, ((0, 0), (0, 0), (0, 0), (x, count_x - 1 - x), (0, 0)))
            for x in range(count_x)
        ]
    ).reshape(count_x * chan_out, 3, 3, count_x + 2, chan)
    coarse = lax.reduce_precision(bias, 8, 7)
    middle = lax.reduce_precision(bias - coarse, 8, 7)
    fine = bias - coarse - middle
    pieces = jnp.stack([coarse, middle, fine], axis=1).astype(bf16)
    pieces = jnp.pad(jnp.tile(pieces, (count_x, 1))[:, None], ((0, 0), (0, 2), (0, 5)))
    near = placed[:, :, :, 1 : count_x + 1].reshape(count_x * chan_out, 9 * own)
    rest = jnp.concatenate([placed[:, :, :, :1], placed[:, :, :, count_x + 1 :]], axis=3)
    rest = jnp.concatenate([rest.reshape(count_x * chan_out, 3, 6 * chan), pieces], axis=2)
    wbig = jnp.concatenate([near, rest.reshape(count_x * chan_out, 3 * depth)], axis=1)
    wback = placed.reshape(count_x * chan_out, 9 * wide).T

    edges, rows = call(
        pack_kernel, [shape((2 * own, lanes), bf16), shape((2 * own, lanes), f32)]
    )(cells)
    pool_x, pool_y, pool_z = cotangent.shape[1:]
    pooled_rows = shape((pool_y * pool_x * chan_out, lanes), f32)
    spread = call(spread_kernel, pooled_rows)(cotangent)
    edges = swapped(edges, "gz", 0)
    body = chan * count_y
    bundle = shape((body + 16, lanes), bf16)
    side = shape((own, lanes), f32)
    face_0, face_1, left, right = call(bundle_kernel, [bundle, bundle, side, side])(cells, edges)
    face_1, face_0 = swapped(face_1, "gx", 1), swapped(face_0, "gx", 0)
    inner = call(
        own_kernel,
        shape(((count_y + 2) * 3 * own, lanes), bf16),
        [pltpu.VMEM(((count_y + 2) * own, lanes), f32)],
        traffic(4),
    )(cells, left, right)
    bundle = shape((3 * wide + 8, lanes), bf16)
    vmem, anywhere = pl.BlockSpec(memory_space=pltpu.VMEM), pl.BlockSpec(memory_space=pl.ANY)
    row_0, row_1 = call(
        functools.partial(rows_kernel, chan),
        [bundle, bundle],
        in_specs=[vmem] * 5 + [anywhere] * 2,
    )(face_1, face_0, rows, left, right, inner, spread)
    row_1, row_0 = swapped(row_1, "gy", 1), swapped(row_0, "gy", 0)

    tall = 2 * wide
    all_field = shape(((count_y + 2) * wide, lanes), f32)
    all_gram = shape((count_x * chan_out, 9 * own + 3 * depth), f32)
    deltas = [pltpu.VMEM((count_x * chan_out, 8 * lanes), bf16)] * 2
    sums, field, patches, cols, gram = call(
        functools.partial(inner_kernel, count_x),
        [
            pooled_rows,
            all_field,
            shape(((count_y + 2) * depth, lanes), bf16),
            shape((tall, lanes), f32),
            all_gram,
        ],
        [
            pltpu.VMEM(((count_y + 2) * 2 * chan, lanes), f32),
            pltpu.VMEM((6 * wide, lanes), f32),
        ]
        + deltas,
        traffic(16),
    )(face_0, face_1, inner, spread, wbig, wback)

    bundle = shape((16 + 2 * chan_out, lanes), bf16)
    face = shape((body, lanes), bf16)
    outer_sums, outer_field, row_0, row_1, wpart, wframe, rows, cols = call(
        functools.partial(main_kernel, count_x),
        [
            pooled_rows,
            all_field,
            bundle,
            bundle,
            shape((chan_out, lanes), f32),
            shape((2 * chan_out, lanes), bf16),
            shape((2 * own, lanes), f32),
            shape((tall, lanes), f32),
        ],
        [
            pltpu.VMEM((4 * (pairs + 1) * 3 * own, lanes), bf16),
            pltpu.VMEM((4 * (pairs + 1) * depth, lanes), bf16),
            pltpu.VMEM((count_x * chan_out, 9 * own + 3 * depth), f32),
        ]
        + deltas,
    )(row_1, row_0, inner, patches, cols, gram, spread, wbig, wback)

    alone = lax.axis_size("gx") != 4
    if alone:
        wpart, far = lax.psum(wpart, "gx"), row_0
    else:
        far = swapped(row_0, "gx", 2)
    row_1, row_0 = swapped(row_1, "gx", 1), swapped(row_0, "gx", 0)
    face_0, face_1 = call(functools.partial(face_kernel, chan), [face, face], cost=traffic(2))(
        field, outer_field
    )
    face_1, face_0 = swapped(face_1, "gx", 1), swapped(face_0, "gx", 0)
    pooled, token = call(
        functools.partial(pool_kernel, pairs),
        [shape(cotangent.shape, bf16), shape((8, lanes), f32)],
        cost=traffic(8),
    )(sums, outer_sums)
    mine, rows = call(
        functools.partial(x_kernel, alone),
        [shape((2 * own + 2 * chan_out, lanes), bf16), shape((2 * own, lanes), f32)],
    )(wpart, wframe, rows, cols, row_0, row_1, far)
    frame = swapped(mine, "gz", 0)
    bundle = shape((own + 2 * chan_out, lanes), bf16)
    row_0, row_1, mine = call(
        functools.partial(z_kernel, count_y),
        [bundle, bundle, shape((2 * chan_out, lanes), bf16)],
        in_specs=[vmem] * 3 + [anywhere],
    )(mine, frame, rows, token)
    row_1, row_0 = swapped(row_1, "gy", 1), swapped(row_0, "gy", 0)
    far = swapped(mine, "gy", 2)
    tiles = (2, chan, count_x, 8, lanes)
    grad, ends = call(grad_kernel, [shape(cells.shape, f32), shape(tiles, f32)], cost=traffic(8))(
        field, outer_field, face_0, face_1, frame
    )
    input_grad, wsum, bias_grad = call(
        final_kernel,
        [
            shape(cells.shape, f32),
            shape((27, chan, chan_out), f32),
            shape((1, chan_out), f32),
        ],
        [
            pltpu.VMEM(tiles, f32),
            pltpu.VMEM((27, chan, chan_out), f32),
            pltpu.VMEM((1, chan_out), f32),
            pltpu.SemaphoreType.DMA((4,)),
        ],
        in_specs=[anywhere] + [vmem] * 5,
        out_specs=[anywhere] * 3,
        input_output_aliases={0: 0},
    )(grad, ends, mine, row_1, far, row_0)
    weight_grad = wsum.reshape(3, 3, 3, chan, chan_out).transpose(4, 3, 0, 1, 2)
    return (pooled, weight_grad, bias_grad.reshape(chan_out), input_grad)


def solution(mesh):
    in_specs = (P(None, "gx", "gy", "gz"), P(), P(), P(None, "gx", "gy", "gz"))
    out_specs = (P(None, "gx", "gy", "gz"), P(), P(), P(None, "gx", "gy", "gz"))
    return jax.shard_map(
        on_device, mesh=mesh, in_specs=in_specs, out_specs=out_specs, check_vma=False
    )
```
